32 devices in a mesh: groups: 2 (over x), tensor: 8 (over z, y), dp: 2 (over core).
Axes of the slice: x: 2, y: 2, z: 4, core: 2. Of those that a mesh axis runs over, the one named last changes fastest.
Arguments:
- attention_result: bfloat16 [4, 768, 8192], P(None, ('groups', 'dp'), 'tensor'), parts along dimension 1, may hold values from -6 to 6
- tenant: int32 [768], P(('groups', 'dp')), parts along dimension 0, may hold values from 0 to 127, as said below
- projection_weight: bfloat16 [8192, 8192], P('tensor'), may hold values from -0.0625 to 0.0625
- adapter_down_maps: bfloat16 [256, 64, 8192], P(('groups', 'dp'), None, 'tensor'), parts along dimension 0, may hold values from -0.0625 to 0.0625
- adapter_up_maps: bfloat16 [256, 64, 8192], P(('groups', 'dp'), None, 'tensor'), parts along dimension 0, may hold values from -0.75 to 0.75
Outputs:
- projected: bfloat16 [4, 768, 8192], P(None, ('groups', 'dp'), 'tensor'), parts along dimension 1
The draws below stay inside these ranges and needn't reach their ends.
There are 2 independent parts, one for each index of `groups`. The reference program is written for one: setup_inputs(seed, part) draws one part's arguments, and reference() takes and returns one part's arrays. A program takes and returns all parts, laid end to end along the dimension named above; an argument that names none is the same for every part. Nothing has to cross between parts.
Inputs may be any that keep to these rules, and one draw needn't show every extreme that they name: `tenant`: among the rows of one device (aligned blocks of 192 rows), at most 16 distinct adapters come from each owner's range of 64 consecutive ids; the first block names exactly 16 from every owner's range.
All inputs are finite; a program needn't handle non-finite values.
Results may differ from the reference program's by a relative error of at most 0.014.
Values may be sent and summed in bfloat16 or wider, within the bound.
No kernel may reach another device: no remote copies, remote signals or barrier semaphores. Data moves between devices by JAX's collectives and lax.ppermute only.
A program may use at most 128 MiB of HBM per device.

```python
import jax
import jax.numpy as jnp
from jax import lax

MODEL_DIM = 8192
ADAPTER_RANK = 64
STEPS = 4
ROWS_DEV = 192
ADAPT_DEV = 64
SLOTS = 16
ROWS = 384
ADAPTER_TOTAL = 128
N_TENSOR = 8


def draw_tenant(key, part):
    key = jax.random.fold_in(key, 7)
    owners = ADAPTER_TOTAL // ADAPT_DEV
    blocks = ROWS // ROWS_DEV
    pool_width = owners * SLOTS
    pieces = []
    for block_index in range(blocks):
        block_key = jax.random.fold_in(key, block_index)
        count_key, choose_key, first_key, second_key, order_key = jax.random.split(block_key, 5)
        counts = jax.random.randint(count_key, (owners,), SLOTS // 2, SLOTS + 1).astype(jnp.int32)
        if block_index == 0:
            counts = jnp.full((owners,), SLOTS, jnp.int32)
        adapter_pool = []
        for owner_index in range(owners):
            shuffled = jax.random.permutation(jax.random.fold_in(choose_key, owner_index), ADAPT_DEV)[:SLOTS]
            adapter_pool.append(shuffled.astype(jnp.int32) + owner_index * ADAPT_DEV)
        adapter_pool = jnp.concatenate(adapter_pool)
        live_slot = (jnp.arange(SLOTS)[None, :] < counts[:, None]).reshape(pool_width)
        position = jnp.cumsum(live_slot.astype(jnp.int32)) - 1
        live_total = jnp.sum(live_slot.astype(jnp.int32))
        target = jnp.where(live_slot, position, pool_width)
        packed = jnp.zeros((pool_width + 1,), jnp.int32).at[target].set(adapter_pool)[:pool_width]
        first_draw = jax.random.randint(first_key, (ROWS_DEV,), 0, live_total)
        second = jax.random.randint(second_key, (ROWS_DEV,), 0, first_draw + 1)
        row_index = jnp.arange(ROWS_DEV)
        chosen_slot = jnp.where(row_index < live_total, row_index, second)
        row_ids = packed[chosen_slot]
        pieces.append(row_ids[jax.random.permutation(order_key, ROWS_DEV)])
    return jnp.concatenate(pieces).astype(jnp.int32)


def shard_levels(rng, extent, cuts, least, largest):
    factor_of = 1.0
    for axis_at, shards_of in cuts:
        draws = jax.random.uniform(jax.random.fold_in(jax.random.fold_in(rng, 6), axis_at), (shards_of,), jnp.float32, least / len(cuts), largest / len(cuts))
        factor_of = factor_of * jnp.repeat(jnp.exp(draws), extent[axis_at] // shards_of).reshape((-1,) + (1,) * (len(extent) - 1 - axis_at))
    return factor_of


def gaussian(key, extent, spread, limit, cuts=(), dtype=jnp.bfloat16):
    loudness = shard_levels(key, extent, cuts, -0.22, 0.18) if cuts else 1.0
    result = jax.random.normal(key, extent, jnp.float32) * spread * loudness
    return jnp.minimum(jnp.maximum(result, -limit), limit).astype(dtype)


def setup_inputs(seed: int = 0, part: int = 0) -> dict:
    splits = jax.random.split(jax.random.key(seed), 6)
    part_splits = jax.random.split(jax.random.fold_in(splits[5], part), 6)
    attention_result = gaussian(part_splits[0], (STEPS, ROWS, MODEL_DIM), 1.0, 6.0, ((1, 2), (2, 8)))
    tenant = draw_tenant(jax.random.fold_in(jax.random.fold_in(splits[5], part), 71), part)
    projection_weight = gaussian(splits[2], (MODEL_DIM, MODEL_DIM), MODEL_DIM ** -0.5, 0.0625, ((0, 8),))
    adapter_down_maps = gaussian(part_splits[3], (ADAPTER_TOTAL, ADAPTER_RANK, MODEL_DIM), MODEL_DIM ** -0.5, 0.0625, ((0, 2), (2, 8)))
    adapter_up_maps = gaussian(part_splits[4], (ADAPTER_TOTAL, ADAPTER_RANK, MODEL_DIM), ADAPTER_RANK ** -0.5, 0.75, ((0, 2), (2, 8)))
    return dict(attention_result=attention_result, tenant=tenant, projection_weight=projection_weight, adapter_down_maps=adapter_down_maps, adapter_up_maps=adapter_up_maps)


def reference(attention_result, tenant, projection_weight, adapter_down_maps, adapter_up_maps):
    decode_step_count, count_of_rows, hidden_width = attention_result.shape
    shard_width = hidden_width // N_TENSOR
    flat_rows = attention_result.reshape(decode_step_count * count_of_rows, hidden_width)
    base_projected = jnp.zeros((decode_step_count * count_of_rows, hidden_width), jnp.float32)
    for shard_index in range(N_TENSOR):
        offset = shard_index * shard_width
        shard_term = jnp.dot(flat_rows[:, offset:offset + shard_width], projection_weight[offset:offset + shard_width], preferred_element_type=jnp.float32)
        rounded = lax.optimization_barrier(shard_term.astype(jnp.bfloat16))
        base_projected = base_projected + rounded.astype(jnp.float32)

    def single_row(row_item):
        row_inputs, adapter_number = row_item
        down_block_rows = adapter_down_maps[adapter_number]
        up_block_rows = adapter_up_maps[adapter_number]
        low_rank = jnp.dot(row_inputs.astype(jnp.float32), down_block_rows.astype(jnp.float32).T, precision=lax.Precision.HIGHEST)
        low_bf = low_rank.astype(jnp.bfloat16)
        return jnp.dot(low_bf, up_block_rows, preferred_element_type=jnp.float32)

    adapter_correction = lax.map(single_row, (jnp.transpose(attention_result, (1, 0, 2)), tenant))
    adapter_correction = jnp.transpose(adapter_correction, (1, 0, 2))
    grand_total = base_projected.reshape(decode_step_count, count_of_rows, hidden_width) + adapter_correction
    return grand_total.astype(jnp.bfloat16)
```

```python
import jax
import jax.numpy as jnp
import numpy as np
from jax import lax
from jax.experimental import pallas as pl
from jax.experimental.pallas import tpu as pltpu
from jax.sharding import PartitionSpec as P

SLOTS = 16
GROUP = 4


def copy_blocks(index, down, up):
    count = index.shape[0]

    def kernel(index_ref, down_ref, up_ref, down_out, up_out, sems):
        copies = []
        for s in range(count):
            for m, (src, dst) in enumerate(((down_ref, down_out), (up_ref, up_out))):
                copies.append(
                    pltpu.make_async_copy(src.at[index_ref[s]], dst.at[s], sems.at[m, s])
                )
        for copy in copies:
            copy.start()
        for copy in copies:
            copy.wait()

    shape = jax.ShapeDtypeStruct((count,) + down.shape[1:], down.dtype)
    return pl.pallas_call(
        kernel,
        out_shape=(shape, shape),
        in_specs=[
            pl.BlockSpec(memory_space=pltpu.SMEM),
            pl.BlockSpec(memory_space=pl.ANY),
            pl.BlockSpec(memory_space=pl.ANY),
        ],
        out_specs=(pl.BlockSpec(memory_space=pl.ANY), pl.BlockSpec(memory_space=pl.ANY)),
        scratch_shapes=[pltpu.SemaphoreType.DMA((2, count))],
        cost_estimate=pl.CostEstimate(
            flops=0, transcendentals=0, bytes_accessed=4 * count * down[0].size * 2
        ),
        name="copy_blocks",
    )(index, down, up)


def low_rank(rows, slot, maps):
    count, width = rows.shape
    rank = maps.shape[1]
    wide = GROUP * rank
    steps = maps.shape[0] // GROUP
    flat = maps.reshape(maps.shape[0] * rank, width)

    def kernel(rows_ref, slot_ref, maps_ref, out_ref, acc):
        i = pl.program_id(0)

        @pl.when(i == 0)
        def _():
            acc[...] = jnp.zeros_like(acc)

        scores = lax.dot_general(
            rows_ref[...], maps_ref[...], (((1,), (1,)), ((), ())),
            preferred_element_type=jnp.float32,
        )
        lane_slot = lax.broadcasted_iota(jnp.int32, (count, wide), 1) // rank + i * GROUP
        acc[...] += jnp.where(slot_ref[...] == lane_slot, scores, 0.0)

        @pl.when(i == steps - 1)
        def _():
            total = acc[:, 0:rank]
            for g in range(1, GROUP):
                total += acc[:, g * rank : (g + 1) * rank]
            out_ref[...] = total.astype(out_ref.dtype)

    return pl.pallas_call(
        kernel,
        grid=(steps,),
        out_shape=jax.ShapeDtypeStruct((count, rank), jnp.bfloat16),
        in_specs=[
            pl.BlockSpec((count, width), lambda i: (0, 0)),
            pl.BlockSpec((count, 1), lambda i: (0, 0)),
            pl.BlockSpec((wide, width), lambda i: (i, 0)),
        ],
        out_specs=pl.BlockSpec((count, rank), lambda i: (0, 0)),
        scratch_shapes=[pltpu.VMEM((count, wide), jnp.float32)],
        compiler_params=pltpu.CompilerParams(vmem_limit_bytes=32 * 2**20),
        cost_estimate=pl.CostEstimate(
            flops=2 * count * width * flat.shape[0],
            transcendentals=0,
            bytes_accessed=2 * (flat.size + rows.size),
        ),
        name="low_rank",
    )(rows, slot, flat)


def expand(low, slot, maps):
    count, rank = low.shape
    width = maps.shape[2]
    wide = GROUP * rank
    steps = maps.shape[0] // GROUP
    flat = maps.reshape(maps.shape[0] * rank, width)

    def kernel(low_ref, slot_ref, maps_ref, out_ref):
        i = pl.program_id(0)
        tiled = jnp.concatenate([low_ref[...]] * GROUP, axis=1)
        lane_slot = lax.broadcasted_iota(jnp.int32, (count, wide), 1) // rank + i * GROUP
        picked = jnp.where(slot_ref[...] == lane_slot, tiled, jnp.zeros_like(tiled))
        term = jnp.dot(picked, maps_ref[...], preferred_element_type=jnp.float32)

        @pl.when(i == 0)
        def _():
            out_ref[...] = term

        @pl.when(i > 0)
        def _():
            out_ref[...] += term

    return pl.pallas_call(
        kernel,
        grid=(steps,),
        out_shape=jax.ShapeDtypeStruct((count, width), jnp.float32),
        in_specs=[
            pl.BlockSpec((count, rank), lambda i: (0, 0)),
            pl.BlockSpec((count, 1), lambda i: (0, 0)),
            pl.BlockSpec((wide, width), lambda i: (i, 0)),
        ],
        out_specs=pl.BlockSpec((count, width), lambda i: (0, 0)),
        compiler_params=pltpu.CompilerParams(vmem_limit_bytes=32 * 2**20),
        cost_estimate=pl.CostEstimate(
            flops=2 * count * width * flat.shape[0],
            transcendentals=0,
            bytes_accessed=2 * flat.size + 4 * count * width,
        ),
        name="expand",
    )(low, slot, flat)


def line_plan(nz):
    order = np.zeros((nz, nz), np.int32)
    for z in range(nz):
        def need(j):
            if j == z:
                return (2 * nz, 0)
            return (nz - 1 - j + z, j) if j > z else (nz - 1 - z + j, nz - j)

        order[z] = sorted(range(nz), key=need)
    return order


def on_device(attention_result, tenant, projection_weight, adapter_down_maps, adapter_up_maps):
    steps, row_count, width = attention_result.shape
    local_adapters = adapter_down_maps.shape[0]
    owners = lax.axis_size("dp")
    me = lax.axis_index("dp")
    n = lax.axis_size("tensor")
    nz = n // 2
    place = lax.axis_index("tensor")
    z, y = place // 2, place % 2
    order = line_plan(nz)
    my_order = jnp.asarray(order)[z]
    out_width = projection_weight.shape[1] // n

    def swap_y(value):
        return lax.ppermute(value, "tensor", [(t, t ^ 1) for t in range(n)])

    def hop(value, h):
        pairs = []
        for side in range(2):
            pairs.append((h * 2 + side, (h + 1) * 2 + side))
            pairs.append(((nz - 1 - h) * 2 + side, (nz - 2 - h) * 2 + side))
        return lax.ppermute(value, "tensor", pairs)

    def slot_of(h, m):
        return list(order[h]).index(nz - 1 - m)

    def line_sum(blocks):
        arrived = {}
        for when in range(2 * nz - 3):
            for h in range(nz - 1):
                m = when - h
                if 0 <= m < nz - 1 - h:
                    value = blocks[slot_of(h, m)]
                    if h:
                        value = value.astype(jnp.float32) + arrived[h - 1, m].astype(jnp.float32)
                    arrived[h, m] = hop(value.astype(jnp.bfloat16), h)
        return [arrived[h, nz - 2 - h] for h in range(nz - 1)]

    rows = attention_result.reshape(steps * row_count, width)
    total_rows = steps * row_count
    first = total_rows // 6
    rows_a, rows_b = rows[:first], rows[first:]

    def weight_block(start, size):
        return lax.dynamic_slice(projection_weight, (0, start), (width, size))

    def dot(left, right):
        return jnp.dot(left, right, preferred_element_type=jnp.float32)

    sent_y = []
    for k in range(nz):
        partial = dot(rows_b, weight_block((my_order[k] * 2 + 1 - y) * out_width, out_width))
        sent_y.append(swap_y(partial.astype(jnp.bfloat16)))
    blocks_a = []
    for k in range(nz):
        blocks_a.append(dot(rows_a, weight_block(my_order[k] * 2 * out_width, 2 * out_width)))
        if k < nz - 1:
            blocks_a[k] = blocks_a[k].astype(jnp.bfloat16)
    arrived_a = line_sum(blocks_a)
    blocks_b = []
    for k in range(nz):
        partial = dot(rows_b, weight_block((my_order[k] * 2 + y) * out_width, out_width))
        partial = partial + sent_y[k].astype(jnp.float32)
        blocks_b.append(partial.astype(jnp.bfloat16) if k < nz - 1 else partial)
    arrived_b = line_sum(blocks_b)

    sum_a = blocks_a[nz - 1]
    for value in arrived_a:
        sum_a = sum_a + value.astype(jnp.float32)
    sum_a = sum_a.astype(jnp.bfloat16)
    away_a = lax.dynamic_slice(sum_a, (0, (1 - y) * out_width), (first, out_width))
    kept_a = lax.dynamic_slice(sum_a, (0, y * out_width), (first, out_width))
    other_a = swap_y(away_a)

    slot_range = jnp.arange(SLOTS, dtype=jnp.int32)
    ids = jnp.arange(local_adapters, dtype=jnp.int32)

    def slots(row_ids, owner):
        hit = row_ids[:, None] - owner * local_adapters == ids[None, :]
        used = jnp.any(hit, axis=0)
        position = jnp.sum(
            (used[None, :] & (ids[None, :] < ids[:, None])).astype(jnp.int32), axis=1
        )
        names = jnp.sum(
            jnp.where(used[None, :] & (position[None, :] == slot_range[:, None]), ids[None, :], 0),
            axis=1,
        )
        row_slot = jnp.sum(jnp.where(hit, position[None, :] + 1, 0), axis=1) - 1
        return names, row_slot

    downs, ups, row_slots = [], [], []
    for shift in range(owners):
        if shift == 0:
            names, row_slot = slots(tenant, me)
            down, up = copy_blocks(names, adapter_down_maps, adapter_up_maps)
        else:
            theirs = lax.ppermute(
                tenant, "dp", [(i, (i - shift) % owners) for i in range(owners)]
            )
            names, _ = slots(theirs, me)
            down, up = copy_blocks(names, adapter_down_maps, adapter_up_maps)
            onward = [(i, (i + shift) % owners) for i in range(owners)]
            down, up = lax.ppermute(down, "dp", onward), lax.ppermute(up, "dp", onward)
            _, row_slot = slots(tenant, (me - shift) % owners)
        downs.append(down)
        ups.append(up)
        row_slots.append(jnp.tile(row_slot, steps)[:, None])

    low = low_rank(rows, row_slots[0], downs[0]).astype(jnp.float32)
    for s in range(1, owners):
        low = low + low_rank(rows, row_slots[s], downs[s]).astype(jnp.float32)
    rank = low.shape[1]
    low = low.astype(jnp.bfloat16).reshape(total_rows * rank // 128, 128)
    bit = 1
    while bit < n:
        other = lax.ppermute(low, "tensor", [(t, t ^ bit) for t in range(n)])
        low = (low.astype(jnp.float32) + other.astype(jnp.float32)).astype(jnp.bfloat16)
        bit *= 2
    low = low.reshape(total_rows, rank)
    delta = expand(low, row_slots[0], ups[0])
    for s in range(1, owners):
        delta = delta + expand(low, row_slots[s], ups[s])

    head_b = lax.optimization_barrier(blocks_b[nz - 1] + delta[first:])
    out_b = head_b
    for value in arrived_b:
        out_b = out_b + value.astype(jnp.float32)
    out_a = kept_a.astype(jnp.float32) + other_a.astype(jnp.float32) + delta[:first]
    out = jnp.concatenate([out_a.astype(jnp.bfloat16), out_b.astype(jnp.bfloat16)], axis=0)
    return out.reshape(steps, row_count, out_width)


def solution(mesh):
    placed = (
        P(None, ("groups", "dp"), "tensor"),
        P(("groups", "dp")),
        P("tensor", None),
        P(("groups", "dp"), None, "tensor"),
        P(("groups", "dp"), None, "tensor"),
    )
    return jax.shard_map(
        on_device,
        mesh=mesh,
        in_specs=placed,
        out_specs=P(None, ("groups", "dp"), "tensor"),
        check_vma=False,
    )
```

```python
import jax
import jax.numpy as jnp
import numpy as np
from jax import lax
from jax.experimental import pallas as pl
from jax.experimental.pallas import tpu as pltpu
from jax.sharding import PartitionSpec as P

SLOTS = 16
GROUP = 4
VMEM = 32 * 2**20


def copy_blocks(index, down, up):
    count = index.shape[0]

    def kernel(index_ref, down_ref, up_ref, down_out, up_out, sems):
        copies = []
        for m, (src, dst) in enumerate(((down_ref, down_out), (up_ref, up_out))):
            for s in range(count):
                copies.append(
                    pltpu.make_async_copy(src.at[index_ref[s]], dst.at[s], sems.at[m, s])
                )
        for copy in copies:
            copy.start()
        for copy in copies:
            copy.wait()

    shape = jax.ShapeDtypeStruct((count,) + down.shape[1:], down.dtype)
    return pl.pallas_call(
        kernel,
        out_shape=(shape, shape),
        in_specs=[
            pl.BlockSpec(memory_space=pltpu.SMEM),
            pl.BlockSpec(memory_space=pl.ANY),
            pl.BlockSpec(memory_space=pl.ANY),
        ],
        out_specs=(pl.BlockSpec(memory_space=pltpu.VMEM), pl.BlockSpec(memory_space=pltpu.VMEM)),
        scratch_shapes=[pltpu.SemaphoreType.DMA((2, count))],
        compiler_params=pltpu.CompilerParams(vmem_limit_bytes=VMEM),
        cost_estimate=pl.CostEstimate(
            flops=0, transcendentals=0, bytes_accessed=4 * count * down[0].size * 2
        ),
        name="copy_blocks",
    )(index, down, up)


def low_rank(rows, slot, maps, index):
    count, width = rows.shape
    rank = maps.shape[1]
    wide = GROUP * rank
    steps = index.shape[0] // GROUP

    def kernel(index_ref, rows_ref, slot_ref, *refs):
        map_refs, out_ref, acc = refs[:GROUP], refs[GROUP], refs[GROUP + 1]
        i = pl.program_id(0)

        @pl.when(i == 0)
        def _():
            acc[...] = jnp.zeros_like(acc)

        blocks = jnp.concatenate([ref[0] for ref in map_refs], axis=0)
        scores = lax.dot_general(
            rows_ref[...], blocks, (((1,), (1,)), ((), ())),
            preferred_element_type=jnp.float32,
        )
        lane_slot = lax.broadcasted_iota(jnp.int32, (count, wide), 1) // rank + i * GROUP
        acc[...] += jnp.where(slot_ref[...] == lane_slot, scores, 0.0)

        @pl.when(i == steps - 1)
        def _():
            total = acc[:, 0:rank]
            for g in range(1, GROUP):
                total += acc[:, g * rank : (g + 1) * rank]
            out_ref[...] = total

    def map_spec(g):
        return pl.BlockSpec((1, rank, width), lambda i, index: (index[i * GROUP + g], 0, 0))

    return pl.pallas_call(
        kernel,
        grid_spec=pltpu.PrefetchScalarGridSpec(
            num_scalar_prefetch=1,
            grid=(steps,),
            in_specs=[
                pl.BlockSpec((count, width), lambda i, index: (0, 0)),
                pl.BlockSpec((count, 1), lambda i, index: (0, 0)),
            ]
            + [map_spec(g) for g in range(GROUP)],
            out_specs=pl.BlockSpec((count, rank), lambda i, index: (0, 0)),
            scratch_shapes=[pltpu.VMEM((count, wide), jnp.float32)],
        ),
        out_shape=jax.ShapeDtypeStruct((count, rank), jnp.float32),
        compiler_params=pltpu.CompilerParams(vmem_limit_bytes=VMEM),
        cost_estimate=pl.CostEstimate(
            flops=2 * count * width * rank * index.shape[0],
            transcendentals=0,
            bytes_accessed=2 * (index.shape[0] * rank * width + rows.size),
        ),
        name="low_rank",
    )(index, rows, slot, *[maps] * GROUP)


def expand(low, slot, maps, index, start=None):
    count, rank = low.shape
    width = maps.shape[2]
    wide = GROUP * rank
    steps = index.shape[0] // GROUP
    starts = [] if start is None else [start]

    def kernel(index_ref, low_ref, slot_ref, *refs):
        map_refs, out_ref = refs[:GROUP], refs[-1]
        i = pl.program_id(0)
        tiled = jnp.concatenate([low_ref[...]] * GROUP, axis=1)
        lane_slot = lax.broadcasted_iota(jnp.int32, (count, wide), 1) // rank + i * GROUP
        picked = jnp.where(slot_ref[...] == lane_slot, tiled, jnp.zeros_like(tiled))
        blocks = jnp.concatenate([ref[0] for ref in map_refs], axis=0)
        term = jnp.dot(picked, blocks, preferred_element_type=jnp.float32)

        @pl.when(i == 0)
        def _():
            out_ref[...] = term + refs[GROUP][...] if starts else term

        @pl.when(i > 0)
        def _():
            out_ref[...] += term

    def map_spec(g):
        return pl.BlockSpec((1, rank, width), lambda i, index: (index[i * GROUP + g], 0, 0))

    whole = pl.BlockSpec((count, width), lambda i, index: (0, 0))
    return pl.pallas_call(
        kernel,
        grid_spec=pltpu.PrefetchScalarGridSpec(
            num_scalar_prefetch=1,
            grid=(steps,),
            in_specs=[
                pl.BlockSpec((count, rank), lambda i, index: (0, 0)),
                pl.BlockSpec((count, 1), lambda i, index: (0, 0)),
            ]
            + [map_spec(g) for g in range(GROUP)]
            + [whole] * len(starts),
            out_specs=whole,
        ),
        out_shape=jax.ShapeDtypeStruct((count, width), jnp.float32),
        compiler_params=pltpu.CompilerParams(vmem_limit_bytes=VMEM),
        cost_estimate=pl.CostEstimate(
            flops=2 * count * width * rank * index.shape[0],
            transcendentals=0,
            bytes_accessed=2 * index.shape[0] * rank * width + 4 * count * width,
        ),
        name="expand",
    )(index, low, slot, *[maps] * GROUP, *starts)


def product(rows, row_at, row_tile, weight, at, size, adds=(), dtype=jnp.bfloat16):
    width = rows.shape[1]
    tile = min(512, size)
    steps = size // tile

    def kernel(at_ref, rows_ref, weight_ref, *refs):
        total = jnp.dot(rows_ref[...], weight_ref[...], preferred_element_type=jnp.float32)
        for ref in refs[:-1]:
            total += ref[...].astype(jnp.float32)
        refs[-1][...] = total.astype(dtype)

    return pl.pallas_call(
        kernel,
        grid_spec=pltpu.PrefetchScalarGridSpec(
            num_scalar_prefetch=1,
            grid=(steps,),
            in_specs=[
                pl.BlockSpec((row_tile, width), lambda i, at: (row_at, 0)),
                pl.BlockSpec((width, tile), lambda i, at: (0, at[0] * steps + i)),
            ]
            + [pl.BlockSpec((row_tile, tile), lambda i, at: (0, i)) for _ in adds],
            out_specs=pl.BlockSpec((row_tile, tile), lambda i, at: (0, i)),
        ),
        out_shape=jax.ShapeDtypeStruct((row_tile, size), dtype),
        compiler_params=pltpu.CompilerParams(vmem_limit_bytes=VMEM),
        cost_estimate=pl.CostEstimate(
            flops=2 * row_tile * width * size,
            transcendentals=0,
            bytes_accessed=2 * (row_tile * width + width * size + row_tile * size * (1 + len(adds))),
        ),
        name="product",
    )(jnp.reshape(at, (1,)), rows, weight, *adds)


def finish(head, arrived, tail):
    high, width = head.shape
    low = tail.shape[0]
    blocks = high // low

    def kernel(head_ref, *refs):
        tail_ref, out_ref = refs[-2], refs[-1]
        i = pl.program_id(0)

        @pl.when(i < blocks)
        def _():
            total = head_ref[...]
            for ref in refs[:-2]:
                total += ref[...].astype(jnp.float32)
            out_ref[...] = total.astype(out_ref.dtype)

        @pl.when(i == blocks)
        def _():
            out_ref[...] = tail_ref[...]

    spec = pl.BlockSpec((low, width), lambda i: (jnp.minimum(i, blocks - 1), 0))
    return pl.pallas_call(
        kernel,
        grid=(blocks + 1,),
        in_specs=[spec] * (1 + len(arrived)) + [pl.BlockSpec((low, width), lambda i: (0, 0))],
        out_specs=pl.BlockSpec((low, width), lambda i: (i, 0)),
        out_shape=jax.ShapeDtypeStruct((high + low, width), tail.dtype),
        compiler_params=pltpu.CompilerParams(vmem_limit_bytes=VMEM),
        cost_estimate=pl.CostEstimate(
            flops=high * width * len(arrived),
            transcendentals=0,
            bytes_accessed=high * width * (6 + 2 * len(arrived)),
        ),
        name="finish",
    )(head, *arrived, tail)


def line_plan(nz):
    order = np.zeros((nz, nz), np.int32)
    for z in range(nz):
        def need(j):
            if j == z:
                return (2 * nz, 0)
            return (nz - 1 - j + z, j) if j > z else (nz - 1 - z + j, nz - j)

        order[z] = sorted(range(nz), key=need)
    return order


def on_device(attention_result, tenant, projection_weight, adapter_down_maps, adapter_up_maps):
    steps, row_count, width = attention_result.shape
    local_adapters = adapter_down_maps.shape[0]
    owners = lax.axis_size("dp")
    me = lax.axis_index("dp")
    n = lax.axis_size("tensor")
    nz = n // 2
    place = lax.axis_index("tensor")
    z, y = place // 2, place % 2
    order = line_plan(nz)
    my_order = jnp.asarray(order)[z]
    out_width = projection_weight.shape[1] // n

    def swap_y(value):
        return lax.ppermute(value, "tensor", [(t, t ^ 1) for t in range(n)])

    def hop(value, h):
        pairs = []
        for side in range(2):
            pairs.append((h * 2 + side, (h + 1) * 2 + side))
            pairs.append(((nz - 1 - h) * 2 + side, (nz - 2 - h) * 2 + side))
        return lax.ppermute(value, "tensor", pairs)

    def slot_of(h, m):
        return list(order[h]).index(nz - 1 - m)

    def line_sum(blocks):
        arrived = {}
        for when in range(2 * nz - 3):
            for h in range(nz - 1):
                m = when - h
                if 0 <= m < nz - 1 - h:
                    value = blocks[slot_of(h, m)]
                    if h:
                        value = value.astype(jnp.float32) + arrived[h - 1, m].astype(jnp.float32)
                    arrived[h, m] = hop(value.astype(jnp.bfloat16), h)
        return [arrived[h, nz - 2 - h] for h in range(nz - 1)]

    rows = attention_result.reshape(steps * row_count, width)
    total_rows = steps * row_count
    few = total_rows // 6
    most = total_rows - few

    def product_a(at):
        return product(rows, most // few, few, projection_weight, at, 2 * out_width)

    def product_b(at, adds=(), dtype=jnp.bfloat16):
        return product(rows, 0, most, projection_weight, at, out_width, adds, dtype)

    sent_y = []
    for k in range(nz):
        sent_y.append(swap_y(product_b(my_order[k] * 2 + 1 - y)))
    blocks_a = [product_a(my_order[k]) for k in range(nz)]
    arrived_a = line_sum(blocks_a)
    blocks_b = [product_b(my_order[k] * 2 + y, [sent_y[k]]) for k in range(nz - 1)]
    arrived_b = line_sum(blocks_b)

    sum_a = blocks_a[nz - 1].astype(jnp.float32)
    for value in arrived_a:
        sum_a = sum_a + value.astype(jnp.float32)
    sum_a = sum_a.astype(jnp.bfloat16)
    away_a = lax.dynamic_slice(sum_a, (0, (1 - y) * out_width), (few, out_width))
    kept_a = lax.dynamic_slice(sum_a, (0, y * out_width), (few, out_width))
    other_a = swap_y(away_a)

    slot_range = jnp.arange(SLOTS, dtype=jnp.int32)
    ids = jnp.arange(local_adapters, dtype=jnp.int32)

    def slots(row_ids, owner):
        hit = row_ids[:, None] - owner * local_adapters == ids[None, :]
        used = jnp.any(hit, axis=0)
        position = jnp.sum(
            (used[None, :] & (ids[None, :] < ids[:, None])).astype(jnp.int32), axis=1
        )
        names = jnp.sum(
            jnp.where(used[None, :] & (position[None, :] == slot_range[:, None]), ids[None, :], 0),
            axis=1,
        )
        row_slot = jnp.sum(jnp.where(hit, position[None, :] + 1, 0), axis=1) - 1
        return names, row_slot

    held = []
    for shift in range(owners):
        names, row_slot = slots(tenant, (me - shift) % owners)
        if shift == 0:
            down, up = adapter_down_maps, adapter_up_maps
        else:
            theirs = lax.ppermute(
                tenant, "dp", [(i, (i - shift) % owners) for i in range(owners)]
            )
            down, up = copy_blocks(slots(theirs, me)[0], adapter_down_maps, adapter_up_maps)
            onward = [(i, (i + shift) % owners) for i in range(owners)]
            down, up = lax.ppermute(down, "dp", onward), lax.ppermute(up, "dp", onward)
            names = slot_range
        held.append((names, jnp.tile(row_slot, steps)[:, None], down, up))

    low = 0
    for names, row_slot, down, _ in held:
        low = low + low_rank(rows, row_slot, down, names)
    rank = low.shape[1]
    low = low.astype(jnp.bfloat16).reshape(total_rows * rank // 128, 128)
    bit = 1
    while bit < n:
        other = lax.ppermute(low, "tensor", [(t, t ^ bit) for t in range(n)])
        low = (low.astype(jnp.float32) + other.astype(jnp.float32)).astype(jnp.bfloat16)
        bit *= 2
    low = low.reshape(total_rows, rank)
    delta = None
    for names, row_slot, _, up in held:
        delta = expand(low, row_slot, up, names, delta)

    head_b = product_b(my_order[nz - 1] * 2 + y, [sent_y[nz - 1], delta], jnp.float32)
    out_a = kept_a.astype(jnp.float32) + other_a.astype(jnp.float32) + delta[most:]
    out = finish(head_b, arrived_b, out_a.astype(jnp.bfloat16))
    return out.reshape(steps, row_count, out_width)


def solution(mesh):
    placed = (
        P(None, ("groups", "dp"), "tensor"),
        P(("groups", "dp")),
        P("tensor", None),
        P(("groups", "dp"), None, "tensor"),
        P(("groups", "dp"), None, "tensor"),
    )
    return jax.shard_map(
        on_device,
        mesh=mesh,
        in_specs=placed,
        out_specs=P(None, ("groups", "dp"), "tensor"),
        check_vma=False,
    )
```

```python
import jax
import jax.numpy as jnp
import numpy as np
from jax import lax
from jax.experimental import pallas as pl
from jax.experimental.pallas import tpu as pltpu
from jax.sharding import PartitionSpec as P

SLOTS = 16
GROUP = 4
VMEM = 60 * 2**20
ANY = pl.BlockSpec(memory_space=pl.ANY)


def call(kernel, operands, after, *, grid, in_specs, out_specs, out_shape, name, prefetch=0, scratch=(), alias=None):
    inputs, extra = len(operands), len(after)

    def body(*refs):
        kernel(*refs[:inputs], *refs[inputs + extra :])

    return pl.pallas_call(
        body,
        grid_spec=pltpu.PrefetchScalarGridSpec(
            num_scalar_prefetch=prefetch,
            grid=grid,
            in_specs=list(in_specs) + [ANY] * extra,
            out_specs=out_specs,
            scratch_shapes=list(scratch),
        ),
        out_shape=out_shape,
        input_output_aliases=alias or {},
        compiler_params=pltpu.CompilerParams(vmem_limit_bytes=VMEM),
        cost_estimate=pl.CostEstimate(flops=1, transcendentals=0, bytes_accessed=1),
        name=name,
    )(*operands, *after)


def hold(value, after):
    def kernel(value_ref, out_ref):
        pass

    return call(
        kernel, [value], after, grid=(), in_specs=[ANY], out_specs=ANY,
        out_shape=jax.ShapeDtypeStruct(value.shape, value.dtype), name="hold",
        alias={0: 0},
    )


def lane_pick(slot_ref, repeats, shape, rank, first):
    slot = jnp.concatenate([slot_ref[...]] * repeats, axis=0)
    return slot == lax.broadcasted_iota(jnp.int32, shape, 1) // rank + first


def low_rank(row_sets, slot_sets, maps, index, after=()):
    sets = len(row_sets)
    count, width = row_sets[0].shape
    rank = maps.shape[1]
    wide = GROUP * rank
    steps = index.shape[0] // sets // GROUP
    repeats = count // slot_sets[0].shape[0]
    half = count // 2

    def kernel(index_ref, *refs):
        row_refs, slot_refs, map_refs = refs[:sets], refs[sets : 2 * sets], refs[2 * sets : 2 * sets + GROUP]
        out_ref, acc = refs[-2], refs[-1]
        i = pl.program_id(1)
        blocks = jnp.concatenate([ref[0] for ref in map_refs], axis=0)
        for s in range(sets):

            @pl.when(pl.program_id(0) == s)
            def _():
                scores = lax.dot_general(
                    row_refs[s][...], blocks, (((1,), (1,)), ((), ())), preferred_element_type=jnp.float32
                )
                pick = lane_pick(slot_refs[s], repeats, (count, wide), rank, i * GROUP)
                term = jnp.where(pick, scores, 0.0)

                @pl.when(i == 0)
                def _():
                    acc[...] = term

                @pl.when(i > 0)
                def _():
                    acc[...] += term

        @pl.when(i == steps - 1)
        def _():
            summed = acc[:, 0:rank]
            for g in range(1, GROUP):
                summed += acc[:, g * rank : (g + 1) * rank]
            summed = jnp.concatenate([summed[:half], summed[half:]], axis=1)
            out_ref[...] = summed.astype(out_ref.dtype)

    def map_spec(g):
        return pl.BlockSpec((1, rank, width), lambda s, i, index: (index[(s * steps + i) * GROUP + g], 0, 0))

    def whole(array):
        return pl.BlockSpec(array.shape, lambda s, i, index: (0, 0))

    return call(
        kernel, [index, *row_sets, *slot_sets] + [maps] * GROUP, after, prefetch=1, grid=(sets, steps),
        in_specs=[whole(rows) for rows in row_sets]
        + [whole(slot) for slot in slot_sets]
        + [map_spec(g) for g in range(GROUP)],
        out_specs=pl.BlockSpec((half, 2 * rank), lambda s, i, index: (s, 0)),
        out_shape=jax.ShapeDtypeStruct((sets * half, 2 * rank), jnp.bfloat16),
        scratch=[pltpu.VMEM((count, wide), jnp.float32)],
        name="low_rank",
    )


def expand(low, slot_sets, maps, index, after=()):
    sets = len(slot_sets)
    rank, width = maps.shape[1:]
    half = low.shape[0] // sets
    count = 2 * half
    wide = GROUP * rank
    steps = index.shape[0] // sets // GROUP
    repeats = count // slot_sets[0].shape[0]

    def kernel(index_ref, low_ref, *refs):
        slot_refs, map_refs = refs[:sets], refs[sets : sets + GROUP]
        out_refs, acc = refs[sets + GROUP : -1], refs[-1]
        i = pl.program_id(1)
        blocks = jnp.concatenate([ref[0] for ref in map_refs], axis=0)
        packed = low_ref[...]
        tiled = jnp.concatenate([packed[:, :rank]] * GROUP, axis=1)
        tiled = jnp.concatenate([tiled, jnp.concatenate([packed[:, rank:]] * GROUP, axis=1)], axis=0)
        for s in range(sets):

            @pl.when(pl.program_id(0) == s)
            def _():
                pick = lane_pick(slot_refs[s], repeats, (count, wide), rank, i * GROUP)
                picked = jnp.where(pick, tiled, jnp.zeros_like(tiled))
                term = jnp.dot(picked, blocks, preferred_element_type=jnp.float32)

                @pl.when(i == 0)
                def _():
                    acc[...] = term

                @pl.when((i > 0) & (i < steps - 1))
                def _():
                    acc[...] += term

                @pl.when(i == steps - 1)
                def _():
                    out_refs[s][...] = (acc[...] + term).astype(out_refs[s].dtype)

    def map_spec(g):
        return pl.BlockSpec((1, rank, width), lambda s, i, index: (index[(s * steps + i) * GROUP + g], 0, 0))

    whole = pl.BlockSpec((count, width), lambda s, i, index: (0, 0))
    return call(
        kernel, [index, low, *slot_sets] + [maps] * GROUP, after, prefetch=1, grid=(sets, steps),
        in_specs=[pl.BlockSpec((half, 2 * rank), lambda s, i, index: (s, 0))]
        + [pl.BlockSpec(slot.shape, lambda s, i, index: (0, 0)) for slot in slot_sets]
        + [map_spec(g) for g in range(GROUP)],
        out_specs=[whole] * sets,
        out_shape=[
            jax.ShapeDtypeStruct((count, width), jnp.bfloat16 if s else jnp.float32) for s in range(sets)
        ],
        scratch=[pltpu.VMEM((count, width), jnp.float32)],
        name="expand",
    )


def products(rows, weight, at, after=()):
    width = rows.shape[1]
    count = first_rows(rows)
    blocks = at.shape[0]
    size = weight.shape[1] // lax.axis_size("tensor")
    tile = min(512, size)
    half = size // tile

    def kernel(at_ref, rows_ref, weight_ref, *out_refs):
        value = jnp.dot(rows_ref[...], weight_ref[...], preferred_element_type=jnp.float32)
        value = value.astype(rows.dtype)
        for b in range(blocks):

            @pl.when(pl.program_id(0) // half == b)
            def _():
                out_refs[b][...] = value

    def out_spec(b):
        return pl.BlockSpec((count, tile), lambda i, at: (0, jnp.clip(i - b * half, 0, half - 1)))

    return call(
        kernel, [at, rows, weight], after, prefetch=1, grid=(blocks * half,),
        in_specs=[
            pl.BlockSpec((count, width), lambda i, at: (0, 0)),
            pl.BlockSpec((width, tile), lambda i, at: (0, at[i // half] * half + i % half)),
        ],
        out_specs=[out_spec(b) for b in range(blocks)],
        out_shape=[jax.ShapeDtypeStruct((count, size), rows.dtype)] * blocks,
        name="products",
    )


def few_products(rows, weight, at, after=()):
    width = rows.shape[1]
    few = rows.shape[0] - first_rows(rows)
    pairs = at.shape[0]
    size = 2 * weight.shape[1] // lax.axis_size("tensor")
    tile = min(1024, size)
    half = size // tile

    def kernel(at_ref, rows_ref, weight_ref, sent_ref, kept_ref):
        value = jnp.dot(rows_ref[...], weight_ref[...], preferred_element_type=jnp.float32)
        value = value.astype(rows.dtype)

        @pl.when(pl.program_id(0) < pairs - 1)
        def _():
            sent_ref[...] = value

        @pl.when(pl.program_id(0) == pairs - 1)
        def _():
            kept_ref[...] = value

    def sent_at(b, i, at):
        done = b == pairs - 1
        return (jnp.where(done, pairs - 2, b), jnp.where(done, half - 1, i))

    return call(
        kernel, [at, rows, weight], after, prefetch=1, grid=(pairs, half),
        in_specs=[
            pl.BlockSpec((few, width), lambda b, i, at: (rows.shape[0] // few - 1, 0)),
            pl.BlockSpec((width, tile), lambda b, i, at: (0, at[b] * half + i)),
        ],
        out_specs=[
            pl.BlockSpec((few, tile), sent_at),
            pl.BlockSpec((few, tile), lambda b, i, at: (0, jnp.where(b == pairs - 1, i, 0))),
        ],
        out_shape=[
            jax.ShapeDtypeStruct(((pairs - 1) * few, size), rows.dtype),
            jax.ShapeDtypeStruct((few, size), rows.dtype),
        ],
        name="few_products",
    )


def first_rows(rows):
    return rows.shape[0] - rows.shape[0] // 6


def total(terms, tile=128, dtype=jnp.bfloat16, after=()):
    blocks = len(terms[0][1])
    width = terms[0][0].shape[1]
    table = np.asarray([list(places) for _, places in terms], np.int32)

    def kernel(table_ref, *refs):
        value = refs[0][...].astype(jnp.float32)
        for ref in refs[1:-1]:
            value += ref[...].astype(jnp.float32)
        refs[-1][...] = value.astype(dtype)

    def spec(t):
        return pl.BlockSpec((tile, width), lambda i, table: (table[t, i], 0))

    return call(
        kernel, [jnp.asarray(table)] + [term for term, _ in terms], after, prefetch=1, grid=(blocks,),
        in_specs=[spec(t) for t in range(len(terms))],
        out_specs=pl.BlockSpec((tile, width), lambda i, table: (i, 0)),
        out_shape=jax.ShapeDtypeStruct((blocks * tile, width), dtype),
        name="total",
    )


def finish(head, arrived, tail):
    high, width = head.shape
    low = tail.shape[0]
    blocks = high // low

    def kernel(head_ref, *refs):
        tail_ref, out_ref = refs[-2], refs[-1]
        i = pl.program_id(0)

        @pl.when(i < blocks)
        def _():
            value = head_ref[...]
            for ref in refs[:-2]:
                value += ref[...].astype(jnp.float32)
            out_ref[...] = value.astype(out_ref.dtype)

        @pl.when(i == blocks)
        def _():
            out_ref[...] = tail_ref[...]

    spec = pl.BlockSpec((low, width), lambda i: (jnp.minimum(i, blocks - 1), 0))
    return call(
        kernel, [head, *arrived, tail], (), grid=(blocks + 1,),
        in_specs=[spec] * (1 + len(arrived)) + [pl.BlockSpec((low, width), lambda i: (0, 0))],
        out_specs=pl.BlockSpec((low, width), lambda i: (i, 0)),
        out_shape=jax.ShapeDtypeStruct((high + low, width), tail.dtype),
        name="finish",
    )


def line_plan(nz):
    order = np.zeros((nz, nz), np.int32)
    for z in range(nz):
        def need(j):
            if j == z:
                return (2 * nz, 0)
            return (nz - 1 - j + z, j) if j > z else (nz - 1 - z + j, nz - j)

        order[z] = sorted(range(nz), key=need)
    return order


def on_device(attention_result, tenant, projection_weight, adapter_down_maps, adapter_up_maps):
    steps, row_count, width = attention_result.shape
    local_adapters = adapter_down_maps.shape[0]
    owners = lax.axis_size("dp")
    me = lax.axis_index("dp")
    n = lax.axis_size("tensor")
    nz = n // 2
    place = lax.axis_index("tensor")
    z, y = place // 2, place % 2
    order = line_plan(nz)
    my_order = jnp.asarray(order)[z]
    out_width = projection_weight.shape[1] // n

    def swap_y(value):
        return lax.ppermute(value, "tensor", [(t, t ^ 1) for t in range(n)])

    def hop(value, h):
        pairs = []
        for side in range(2):
            pairs.append((h * 2 + side, (h + 1) * 2 + side))
            pairs.append(((nz - 1 - h) * 2 + side, (nz - 2 - h) * 2 + side))
        return lax.ppermute(value, "tensor", pairs)

    def slot_of(h, m):
        return list(order[h]).index(nz - 1 - m)

    rows = attention_result.reshape(steps * row_count, width)
    total_rows = steps * row_count
    most = first_rows(rows)
    few = total_rows - most
    last = [()]

    def then(kernel, *operands, **options):
        out = kernel(*operands, after=last[0], **options)
        last[0] = (out[0] if isinstance(out, (tuple, list)) else out,)
        return out

    slot_range = jnp.arange(SLOTS, dtype=jnp.int32)
    ids = jnp.arange(local_adapters, dtype=jnp.int32)

    def slots(row_ids, owner):
        hit = row_ids[:, None] - owner * local_adapters == ids[None, :]
        used = jnp.any(hit, axis=0)
        position = jnp.sum(
            (used[None, :] & (ids[None, :] < ids[:, None])).astype(jnp.int32), axis=1
        )
        names = jnp.sum(
            jnp.where(used[None, :] & (position[None, :] == slot_range[:, None]), ids[None, :], 0),
            axis=1,
        )
        row_slot = jnp.sum(jnp.where(hit, position[None, :] + 1, 0), axis=1) - 1
        return names, row_slot[:, None]

    away = [my_order[k] * 2 + 1 - y for k in range(nz)]
    own = [my_order[k] * 2 + y for k in range(nz)]
    every = range(most // 128)
    held_y, own_part, from_y, arrived = {}, {}, {}, {}

    def multiply(aways, owns):
        at = jnp.stack([away[k] for k in aways] + [own[k] for k in owns])
        parts = then(products, rows, projection_weight, at)
        held_y.update(zip(aways, parts))
        own_part.update(zip(owns, parts[len(aways) :]))

    def line(h, m):
        k = slot_of(h, m)
        terms = [(own_part[k], every), (from_y[k], every)]
        if h:
            terms.append((arrived[h - 1, m], every))
        arrived[h, m] = hop(then(total, terms), h)

    few_arrived = []

    def few_line():
        h = len(few_arrived)
        if h == 0:
            few_arrived.append(hop(few_sent, 0))
        else:
            blocks = range(nz - 1 - h)
            terms = [(few_sent, [slot_of(h, m) for m in blocks]), (few_arrived[h - 1], blocks)]
            few_arrived.append(hop(then(total, terms, few), h))

    def pass_on(value, shift):
        return lax.ppermute(value, "dp", [(i, (i + shift) % owners) for i in range(owners)])

    row_ids = [tenant] + [pass_on(tenant, shift) for shift in range(1, owners)]
    row_sets = [rows] + [pass_on(rows, shift) for shift in range(1, owners)]
    multiply([0], [])
    from_y[0] = swap_y(held_y[0])
    few_sent, few_kept = then(few_products, rows, projection_weight, my_order)
    few_line()
    named = [slots(some_ids, me) for some_ids in row_ids]
    names = jnp.concatenate([which for which, _ in named])
    slot_sets = [row_slot for _, row_slot in named]
    low = then(low_rank, row_sets, slot_sets, adapter_down_maps, names)
    swaps = []
    while 1 << len(swaps) < n:
        swaps.append(1 << len(swaps))

    def low_step():
        nonlocal low
        if swaps:
            bit = swaps.pop(0)
            other = lax.ppermute(low, "tensor", [(t, t ^ bit) for t in range(n)])
            blocks = range(low.shape[0] // 128)
            low = then(total, [(low, blocks), (other, blocks)])

    multiply([1], [0])
    from_y[1] = swap_y(held_y[1])
    multiply(range(2, nz), range(1, nz))
    started = 2

    def start_y():
        nonlocal started
        if started < nz:
            from_y[started] = swap_y(hold(held_y[started], last[0]))
            started += 1

    low_step()
    line(0, 0)
    start_y()
    few_line()
    deltas = None
    for when in range(1, 2 * nz - 3):
        low_step()
        if not swaps and deltas is None:
            deltas = then(expand, low, slot_sets, adapter_up_maps, names)
        for h in range(nz - 1):
            if 0 <= when - h < nz - 1 - h:
                line(h, when - h)
                if h == 0:
                    start_y()
        if len(few_arrived) < nz - 1:
            few_line()
    while len(few_arrived) < nz - 1:
        few_line()
    while swaps:
        low_step()
    if deltas is None:
        deltas = then(expand, low, slot_sets, adapter_up_maps, names)
    delta = [deltas[0]] + [pass_on(deltas[shift], -shift) for shift in range(1, owners)]
    few_sum = then(
        total, [(few_kept, [0])] + [(few_arrived[h], [nz - 2 - h]) for h in range(nz - 1)], few
    )
    few_away = lax.dynamic_slice(few_sum, (0, (1 - y) * out_width), (few, out_width))
    few_own = lax.dynamic_slice(few_sum, (0, y * out_width), (few, out_width))
    few_other = swap_y(few_away)
    few_out = few_own.astype(jnp.float32) + few_other.astype(jnp.float32)
    for term in delta:
        few_out = few_out + term[most:].astype(jnp.float32)
    terms = [(own_part[nz - 1], every), (from_y[nz - 1], every)] + [(term, every) for term in delta]
    head = then(total, terms, 128, jnp.float32)
    out = finish(head, [arrived[h, nz - 2 - h] for h in range(nz - 1)], few_out.astype(jnp.bfloat16))
    return out.reshape(steps, row_count, out_width)


def solution(mesh):
    placed = (
        P(None, ("groups", "dp"), "tensor"),
        P(("groups", "dp")),
        P("tensor", None),
        P(("groups", "dp"), None, "tensor"),
        P(("groups", "dp"), None, "tensor"),
    )
    return jax.shard_map(
        on_device,
        mesh=mesh,
        in_specs=placed,
        out_specs=P(None, ("groups", "dp"), "tensor"),
        check_vma=False,
    )
```

```python
import jax
import jax.numpy as jnp
import numpy as np
from jax import lax
from jax.experimental import pallas as pl
from jax.experimental.pallas import tpu as pltpu
from jax.sharding import PartitionSpec as P

SLOTS = 16
LANES = 128
CHUNK = 256
PARTS = 2
LOW_WITH = (0, PARTS - 1)
VMEM = 50 * 2**20
ANY = pl.BlockSpec(memory_space=pl.ANY)


def call(kernel, operands, after, *, in_specs, out_specs, out_shape, name, prefetch=0, scratch=(), alias=None):
    inputs, extra = len(operands), len(after)

    def body(*refs):
        kernel(*refs[:inputs], *refs[inputs + extra :])

    return pl.pallas_call(
        body,
        grid_spec=pltpu.PrefetchScalarGridSpec(
            num_scalar_prefetch=prefetch,
            grid=(),
            in_specs=list(in_specs) + [ANY] * extra,
            out_specs=out_specs,
            scratch_shapes=list(scratch),
        ),
        out_shape=out_shape,
        input_output_aliases=alias or {},
        compiler_params=pltpu.CompilerParams(vmem_limit_bytes=VMEM),
        cost_estimate=pl.CostEstimate(flops=1, transcendentals=0, bytes_accessed=1),
        name=name,
    )(*operands, *after)


def hold(value, after):
    def kernel(value_ref, out_ref):
        pass

    return call(
        kernel, [value], after, in_specs=[ANY], out_specs=ANY,
        out_shape=jax.ShapeDtypeStruct(value.shape, value.dtype), name="hold", alias={0: 0},
    )


def products(rows, weight, starts, size, outs, tail=None, after=()):
    count, width = rows.shape
    blocks = starts.shape[0]
    chunks = [(at, min(CHUNK, size - at)) for at in range(0, size, CHUNK)]
    low = min(first for _, first, _ in outs)
    high = max(first + some for _, first, some in outs)
    upper = (high - low) // 32 * 16
    row_parts = [(0, upper), (upper, high - low - upper)]
    tails = [] if tail is None else [tail]
    heights = [some for _, _, some in outs]
    for array in tails:
        heights[-1] += array.shape[0]

    def kernel(starts_ref, rows_ref, weight_ref, *refs):
        tail_refs, refs = refs[: len(tails)], refs[len(tails) :]
        out_refs, (x, w, *refs) = refs[: len(outs)], refs[len(outs) :]
        stage, (x_sems, w_sems, out_sems, tail_sems) = refs[: len(outs)], refs[len(outs) :]
        x_copies = [
            pltpu.make_async_copy(
                rows_ref.at[pl.ds(low + at, some)], x.at[pl.ds(at, some)], x_sems.at[i]
            )
            for i, (at, some) in enumerate(row_parts)
        ]
        w_copies = [
            [
                pltpu.make_async_copy(
                    weight_ref.at[:, pl.ds(pl.multiple_of(starts_ref[b] + at, LANES), extent)],
                    w.at[b, :, pl.ds(at, extent)],
                    w_sems.at[b, c],
                )
                for c, (at, extent) in enumerate(chunks)
            ]
            for b in range(blocks)
        ]
        x_copies[0].start()
        w_copies[0][0].start()
        x_copies[1].start()
        for b in range(blocks):
            for c in range(len(chunks)):
                if b or c:
                    w_copies[b][c].start()
        stores = []
        for ref in tail_refs:
            below = pl.ds(outs[-1][2], ref.shape[0])
            read = pltpu.make_async_copy(ref, stage[-1].at[below], tail_sems.at[0])
            read.start()
            read.wait()
            stores.append(pltpu.make_async_copy(stage[-1].at[below], out_refs[-1].at[below], tail_sems.at[1]))
            stores[-1].start()
        for copy in x_copies:
            copy.wait()
        for b in range(blocks):
            for c, (at, extent) in enumerate(chunks):
                w_copies[b][c].wait()
                for o, (index, first, some) in enumerate(outs):
                    if index == b:
                        value = jnp.dot(
                            x[first - low : first - low + some, :], w[b, :, at : at + extent],
                            preferred_element_type=jnp.float32,
                        )
                        stage[o][:some, at : at + extent] = value.astype(rows.dtype)
                        store = pltpu.make_async_copy(
                            stage[o].at[pl.ds(0, some), pl.ds(at, extent)],
                            out_refs[o].at[pl.ds(0, some), pl.ds(at, extent)],
                            out_sems.at[o, c],
                        )
                        store.start()
                        stores.append(store)
        for store in stores:
            store.wait()

    shapes = [(height, size) for height in heights]
    return call(
        kernel, [starts, rows, weight] + tails, after, prefetch=1,
        in_specs=[ANY] * (2 + len(tails)),
        out_specs=[ANY] * len(outs),
        out_shape=[jax.ShapeDtypeStruct(shape, rows.dtype) for shape in shapes],
        scratch=[pltpu.VMEM((high - low, width), rows.dtype), pltpu.VMEM((blocks, width, size), rows.dtype)]
        + [pltpu.VMEM(shape, rows.dtype) for shape in shapes]
        + [
            pltpu.SemaphoreType.DMA((2,)),
            pltpu.SemaphoreType.DMA((blocks, len(chunks))),
            pltpu.SemaphoreType.DMA((len(outs), len(chunks))),
            pltpu.SemaphoreType.DMA((2,)),
        ],
        name="products",
    )


def total(runs, dtype=jnp.bfloat16, into=None, after=()):
    width = runs[0][1][0][0].shape[1]
    height = sum(some for some, _ in runs)
    rows_in_all, first, so_far = into or (height, 0, None)
    tiles = []
    at = 0
    for r, (some, terms) in enumerate(runs):
        size = -(-some // 32) * 16 if some * width > 2**17 else some
        for skip in range(0, some, size):
            tiles.append((r, skip, min(size, some - skip), at + skip))
        at += some
    operands = [term for _, terms in runs for term, _ in terms]
    before = [] if so_far is None else [so_far]
    most_terms = max(len(terms) for _, terms in runs)
    of_run = np.cumsum([0] + [len(terms) for _, terms in runs])

    def kernel(*refs):
        term_refs, out_ref = refs[: len(operands)], refs[len(operands) + len(before)]
        refs = refs[len(operands) + len(before) + 1 :]
        bufs, (stage, in_sems, out_sems) = refs[: len(operands)], refs[len(operands) :]
        reads, writes = [], []
        for n, (r, skip, size, place) in enumerate(tiles):
            reads.append(
                [
                    pltpu.make_async_copy(
                        term_refs[of_run[r] + t].at[pl.ds(start + skip, size)],
                        bufs[of_run[r] + t].at[pl.ds(skip, size)],
                        in_sems.at[t, n],
                    )
                    for t, (_, start) in enumerate(runs[r][1])
                ]
            )
            writes.append(
                pltpu.make_async_copy(
                    stage.at[pl.ds(place, size)], out_ref.at[pl.ds(first + place, size)], out_sems.at[n]
                )
            )
        for some in reads:
            for read in some:
                read.start()
        for n, (r, skip, size, place) in enumerate(tiles):
            for read in reads[n]:
                read.wait()
            value = None
            for t in range(len(runs[r][1])):
                part = bufs[of_run[r] + t][skip : skip + size, :].astype(jnp.float32)
                value = part if value is None else value + part
            stage[place : place + size, :] = value.astype(dtype)
            writes[n].start()
        for write in writes:
            write.wait()

    return call(
        kernel, operands + before, after,
        in_specs=[ANY] * (len(operands) + len(before)),
        out_specs=ANY,
        out_shape=jax.ShapeDtypeStruct((rows_in_all, width), dtype),
        scratch=[pltpu.VMEM((some, width), term.dtype) for some, terms in runs for term, _ in terms]
        + [
            pltpu.VMEM((height, width), dtype),
            pltpu.SemaphoreType.DMA((most_terms, len(tiles))),
            pltpu.SemaphoreType.DMA((len(tiles),)),
        ],
        alias={len(operands): 0} if before else None,
        name="total",
    )


def lane_pick(slot_ref, repeats, shape, rank, first):
    slot = jnp.concatenate([slot_ref[...]] * repeats, axis=0)
    return slot == lax.broadcasted_iota(jnp.int32, shape, 1) // rank + first


def block_copies(index_ref, maps_ref, buf, sems, sets, rank):
    each = index_ref.shape[0] // sets
    return [
        [
            pltpu.make_async_copy(
                maps_ref.at[index_ref[s * each + i]], buf.at[pl.ds((s * each + i) * rank, rank)],
                sems.at[s * each + i],
            )
            for i in range(each)
        ]
        for s in range(sets)
    ]


def low_rank(row_sets, slot_sets, maps, index, wide, after=()):
    sets = len(row_sets)
    count, width = row_sets[0].shape
    rank = maps.shape[1]
    span = index.shape[0] // sets * rank
    repeats = count // slot_sets[0].shape[0]
    half = count // 2
    group = 256
    tall = sets * half * 2 * rank // wide

    def kernel(index_ref, *refs):
        row_refs, slot_refs, maps_ref, out_ref = refs[:sets], refs[sets : 2 * sets], refs[2 * sets], refs[2 * sets + 1]
        rows_buf, maps_buf, row_sems, map_sems = refs[2 * sets + 2 :]
        row_copies = [
            pltpu.make_async_copy(row_refs[s], rows_buf.at[s], row_sems.at[s]) for s in range(sets)
        ]
        map_copies = block_copies(index_ref, maps_ref, maps_buf, map_sems, sets, rank)
        for s in range(sets):
            row_copies[s].start()
            for copy in map_copies[s]:
                copy.start()
        for s in range(sets):
            row_copies[s].wait()
            for copy in map_copies[s]:
                copy.wait()
            acc = None
            for at in range(0, span, group):
                scores = lax.dot_general(
                    rows_buf[s], maps_buf[s * span + at : s * span + at + group],
                    (((1,), (1,)), ((), ())), preferred_element_type=jnp.float32,
                )
                pick = lane_pick(slot_refs[s], repeats, (count, group), rank, at // rank)
                term = jnp.where(pick, scores, 0.0)
                acc = term if acc is None else acc + term
            summed = acc[:, 0:rank]
            for g in range(1, group // rank):
                summed += acc[:, g * rank : (g + 1) * rank]
            summed = summed.astype(out_ref.dtype)
            for b in range(half // tall):
                lanes = slice((s * half // tall + b) * 2 * rank, (s * half // tall + b + 1) * 2 * rank)
                both = [summed[start + b * tall : start + (b + 1) * tall] for start in (0, half)]
                out_ref[:, lanes] = jnp.concatenate(both, axis=1)

    return call(
        kernel, [index, *row_sets, *slot_sets, maps], after, prefetch=1,
        in_specs=[ANY] * sets + [pl.BlockSpec(memory_space=pltpu.VMEM)] * sets + [ANY],
        out_specs=pl.BlockSpec(memory_space=pltpu.VMEM),
        out_shape=jax.ShapeDtypeStruct((tall, wide), jnp.bfloat16),
        scratch=[
            pltpu.VMEM((sets, count, width), row_sets[0].dtype),
            pltpu.VMEM((sets * span, width), maps.dtype),
            pltpu.SemaphoreType.DMA((sets,)),
            pltpu.SemaphoreType.DMA((index.shape[0],)),
        ],
        name="low_rank",
    )


def expand(low, slot_sets, maps, index, parts, after=()):
    sets = len(slot_sets)
    rank, width = maps.shape[1:]
    tall = low.shape[0]
    half = low.size // sets // (2 * rank)
    count = 2 * half
    span = index.shape[0] // sets * rank
    repeats = count // slot_sets[0].shape[0]
    outs = [(s, first, some) for s in range(1, sets) for first, some in parts]
    outs.append((0, 0, count))

    def kernel(index_ref, low_ref, *refs):
        slot_refs, maps_ref, out_refs = refs[:sets], refs[sets], refs[sets + 1 : sets + 1 + len(outs)]
        stages, (maps_buf, map_sems, out_sems) = (
            refs[sets + 1 + len(outs) : sets + 1 + 2 * len(outs)], refs[sets + 1 + 2 * len(outs) :]
        )
        map_copies = block_copies(index_ref, maps_ref, maps_buf, map_sems, sets, rank)
        writes = [pltpu.make_async_copy(stages[o], out_refs[o], out_sems.at[o]) for o in range(len(outs))]
        order = list(range(1, sets)) + [0]
        for s in order:
            for copy in map_copies[s]:
                copy.start()
        for s in order:
            lanes = [(s * half // tall + b) * 2 * rank for b in range(half // tall)]
            mine = jnp.concatenate(
                [low_ref[:, at + side : at + side + rank] for side in (0, rank) for at in lanes], axis=0
            )
            tiled = jnp.concatenate([mine] * (span // rank), axis=1)
            pick = lane_pick(slot_refs[s], repeats, (count, span), rank, 0)
            picked = jnp.where(pick, tiled, jnp.zeros_like(tiled))
            for copy in map_copies[s]:
                copy.wait()
            for o, (which, first, some) in enumerate(outs):
                if which == s:
                    for at in range(0, width, CHUNK):
                        value = jnp.dot(
                            picked[first : first + some], maps_buf[s * span : (s + 1) * span, at : at + CHUNK],
                            preferred_element_type=jnp.float32,
                        )
                        stages[o][:, at : at + CHUNK] = value.astype(stages[o].dtype)
                    writes[o].start()
        for write in writes:
            write.wait()

    kinds = [jax.ShapeDtypeStruct((some, width), jnp.bfloat16 if s else jnp.float32) for s, _, some in outs]
    done = call(
        kernel, [index, low, *slot_sets, maps], after, prefetch=1,
        in_specs=[pl.BlockSpec(memory_space=pltpu.VMEM)] * (1 + sets) + [ANY],
        out_specs=[ANY] * len(outs),
        out_shape=kinds,
        scratch=[pltpu.VMEM(kind.shape, kind.dtype) for kind in kinds]
        + [
            pltpu.VMEM((sets * span, width), maps.dtype),
            pltpu.SemaphoreType.DMA((index.shape[0],)),
            pltpu.SemaphoreType.DMA((len(outs),)),
        ],
        name="expand",
    )
    return [done[-1]] + [done[s * len(parts) : (s + 1) * len(parts)] for s in range(sets - 1)]


def line_plan(nz):
    order = np.zeros((nz, nz), np.int32)
    for z in range(nz):
        def need(j):
            if j == z:
                return (2 * nz, 0)
            return (nz - 1 - j + z, j) if j > z else (nz - 1 - z + j, nz - j)

        order[z] = sorted(range(nz), key=need)
    return order


def on_device(attention_result, tenant, projection_weight, adapter_down_maps, adapter_up_maps):
    steps, row_count, width = attention_result.shape
    local_adapters = adapter_down_maps.shape[0]
    owners = lax.axis_size("dp")
    me = lax.axis_index("dp")
    n = lax.axis_size("tensor")
    nz = n // 2
    place = lax.axis_index("tensor")
    z, y = place // 2, place % 2
    order = line_plan(nz)
    my_order = jnp.asarray(order)[z]
    out_width = projection_weight.shape[1] // n

    def swap_y(value):
        return lax.ppermute(value, "tensor", [(t, t ^ 1) for t in range(n)])

    def hop(value, h):
        pairs = []
        for side in range(2):
            pairs.append((h * 2 + side, (h + 1) * 2 + side))
            pairs.append(((nz - 1 - h) * 2 + side, (nz - 2 - h) * 2 + side))
        return lax.ppermute(value, "tensor", pairs)

    def slot_of(h, m):
        return list(order[h]).index(nz - 1 - m)

    def pass_on(value, shift):
        return lax.ppermute(value, "dp", [(i, (i + shift) % owners) for i in range(owners)])

    rows = attention_result.reshape(steps * row_count, width)
    count = steps * row_count
    last = [()]

    def then(kernel, *operands, **options):
        out = kernel(*operands, after=last[0], **options)
        last[0] = (out[0] if isinstance(out, (tuple, list)) else out,)
        return out

    slot_range = jnp.arange(SLOTS, dtype=jnp.int32)
    ids = jnp.arange(local_adapters, dtype=jnp.int32)

    def slots(row_ids, owner):
        hit = row_ids[:, None] - owner * local_adapters == ids[None, :]
        used = jnp.any(hit, axis=0)
        position = jnp.sum(
            (used[None, :] & (ids[None, :] < ids[:, None])).astype(jnp.int32), axis=1
        )
        names = jnp.sum(
            jnp.where(used[None, :] & (position[None, :] == slot_range[:, None]), ids[None, :], 0),
            axis=1,
        )
        row_slot = jnp.sum(jnp.where(hit, position[None, :] + 1, 0), axis=1) - 1
        return names, row_slot[:, None]

    away = [(my_order[k] * 2 + 1 - y) * out_width for k in range(nz)]
    own = [(my_order[k] * 2 + y) * out_width for k in range(nz)]
    low_rows = 2 * (owners * count // 2) * adapter_down_maps.shape[1] // out_width
    even = [(p * count // PARTS, count // PARTS) for p in range(PARTS)]
    uneven = [(0, count // 2 + low_rows), (count // 2 + low_rows, count // 2 - low_rows)]
    away_part, own_all, from_y, sums, arrived = {}, {}, {}, {}, {}

    def split(k):
        return uneven if k == 0 else even

    def add_up(span, terms, extra=(), dtype=jnp.bfloat16, into=None):
        low_row, high_row = span[0], span[0] + span[1]
        cuts = {low_row, high_row}
        for term in terms:
            for at, some, _, _ in term:
                cuts.update(row for row in (at, at + some) if low_row < row < high_row)
        cuts = sorted(cuts)
        runs = []
        for begin, end in zip(cuts, cuts[1:]):
            here = [
                (array, row + begin - at) for term in terms for at, some, array, row in term if at <= begin < at + some
            ]
            runs.append((end - begin, here))
        return then(total, runs + list(extra), dtype, into)

    def whole(array):
        return [(0, count, array, 0)]

    def parts_of(arrays, cut):
        return [(at, some, array, 0) for (at, some), array in zip(cut, arrays)]

    def multiply(aways, owns, tail=None):
        ks = sorted({k for k, _ in aways})
        starts = jnp.stack([away[k] for k in ks] + [own[k] for k in owns])
        outs = [(ks.index(k), *split(k)[p]) for k, p in aways]
        outs += [(len(ks) + i, 0, count) for i in range(len(owns))]
        done = then(products, rows, projection_weight, starts, out_width, outs, tail)
        away_part.update(zip(aways, done))
        own_all.update(zip(owns, done[len(aways) :]))

    def start_y(i):
        k, p = divmod(i, PARTS)
        if k < nz:
            value = away_part[k, p]
            from_y[k, p] = swap_y(hold(value, last[0]) if i >= PARTS else value)

    def y_parts(k):
        return [(*split(k)[p], from_y[k, p], 0) for p in range(PARTS) if (k, p) in from_y]

    def sum_parts(k):
        return [(*split(k)[p], sums[k, p], 0) for p in range(PARTS) if (k, p) in sums]

    def cut_of(h, m):
        return uneven if m == 0 and h <= 1 else even

    def arrived_parts(h, m):
        return [(*cut_of(h, m)[p], arrived[h, m, p], 0) for p in range(PARTS) if (h, m, p) in arrived]

    def line(h, m, p):
        k = slot_of(h, m)
        span = cut_of(h, m)[p]
        low_too = m == 0 and h <= 1 and p == LOW_WITH[1]
        if h == 0:
            extra = [(low_rows, [(low, 0), (from_y[k, p], span[1])])] if low_too else []
            value = sums[k, p] = add_up(span, [whole(own_all[k]), y_parts(k)], extra)
        else:
            extra = [(low_rows, [(sums[k, p], span[1]), (arrived[h - 1, m, p], span[1])])] if low_too else []
            value = add_up(span, [sum_parts(k), arrived_parts(h - 1, m)], extra)
        arrived[h, m, p] = hop(value, h)

    def line_order():
        ready, free = {}, {}
        steps = [(h, m, p) for h in range(nz - 1) for m in range(nz - 1 - h) for p in range(PARTS)]
        for h, m, p in sorted(steps, key=lambda step: (step[0], step[1] * PARTS + step[2])):
            there = slot_of(h, m) * PARTS + p + 1.0
            if h:
                there = max(there, ready[h - 1, m, p, "end"])
            ready[h, m, p] = there
            free[h] = max(there, free.get(h, 0.0)) + 1.0
            ready[h, m, p, "end"] = free[h]
        return sorted(steps, key=lambda step: (ready[step], step[0]))

    row_ids = [tenant] + [pass_on(tenant, shift) for shift in range(1, owners)]
    row_sets = [rows] + [pass_on(rows, shift) for shift in range(1, owners)]
    multiply([(0, p) for p in range(PARTS - 1)], [])
    for i in range(PARTS - 1):
        start_y(i)
    named = [slots(some_ids, me) for some_ids in row_ids]
    names = jnp.concatenate([which for which, _ in named])
    slot_sets = [row_slot for _, row_slot in named]
    low = then(low_rank, row_sets, slot_sets, adapter_down_maps, names, out_width)
    multiply([LOW_WITH], [], low)
    start_y(PARTS - 1)
    multiply([(1, p) for p in range(PARTS)], [0])
    low_sum = None

    deltas = None
    started = PARTS
    for h, m, p in line_order():
        if h == 0 and (slot_of(0, m), p) == (2, 0) and nz > 2:
            low_at = uneven[LOW_WITH[1]][1]
            pieces = [(sums[LOW_WITH], low_at)]
            for step in range(nz - 1):
                if step >= 2:
                    prefix = then(total, [(low_rows, [pieces[0], pieces[-1]])])
                    pieces.append((hop(prefix, step), 0))
                else:
                    pieces.append((arrived[step, 0, LOW_WITH[1]], low_at))
            low_sum = then(total, [(low_rows, pieces)])
        line(h, m, p)
        if h == 0:
            start_y(started)
            started += 1
            if started == PARTS + 1:
                multiply([(k, q) for k in range(2, nz) for q in range(PARTS)], range(1, nz))
        if low_sum is not None and deltas is None:
            deltas = then(expand, low_sum, slot_sets, adapter_up_maps, names, even)
            back = {}
            for shift in range(1, owners):
                for q in range(PARTS):
                    back[shift, q] = pass_on(deltas[shift][q], -shift)
    head = [whole(own_all[nz - 1]), whole(deltas[0])]
    head += [parts_of([back[shift, q] for q in range(PARTS)], even) for shift in range(1, owners)]
    out = None
    for span in even:
        most = add_up(span, head + [arrived_parts(h, nz - 2 - h) for h in range(nz - 1)], dtype=jnp.float32)
        out = add_up(span, [[(*span, most, 0)], y_parts(nz - 1)], into=(count, span[0], out))
    return out.reshape(steps, row_count, out_width)


def solution(mesh):
    placed = (
        P(None, ("groups", "dp"), "tensor"),
        P(("groups", "dp")),
        P("tensor", None),
        P(("groups", "dp"), None, "tensor"),
        P(("groups", "dp"), None, "tensor"),
    )
    return jax.shard_map(
        on_device,
        mesh=mesh,
        in_specs=placed,
        out_specs=P(None, ("groups", "dp"), "tensor"),
        check_vma=False,
    )
```

```python
import jax
import jax.numpy as jnp
import numpy as np
from jax import lax
from jax.experimental import pallas as pl
from jax.experimental.pallas import tpu as pltpu
from jax.sharding import PartitionSpec as P

SLOTS = 16
LANES = 128
CHUNK = 512
PARTS = 2
LOW_WITH = (0, PARTS - 1)
VMEM = 50 * 2**20
ANY = pl.BlockSpec(memory_space=pl.ANY)


def call(kernel, operands, after, *, in_specs, out_specs, out_shape, name, prefetch=0, scratch=(), alias=None):
    inputs, extra = len(operands), len(after)

    def body(*refs):
        kernel(*refs[:inputs], *refs[inputs + extra :])

    return pl.pallas_call(
        body,
        grid_spec=pltpu.PrefetchScalarGridSpec(
            num_scalar_prefetch=prefetch,
            grid=(),
            in_specs=list(in_specs) + [ANY] * extra,
            out_specs=out_specs,
            scratch_shapes=list(scratch),
        ),
        out_shape=out_shape,
        input_output_aliases=alias or {},
        compiler_params=pltpu.CompilerParams(vmem_limit_bytes=VMEM),
        cost_estimate=pl.CostEstimate(flops=1, transcendentals=0, bytes_accessed=1),
        name=name,
    )(*operands, *after)


def hold(value, after):
    def kernel(value_ref, out_ref):
        pass

    return call(
        kernel, [value], after, in_specs=[ANY], out_specs=ANY,
        out_shape=jax.ShapeDtypeStruct(value.shape, value.dtype), name="hold", alias={0: 0},
    )


def products(rows, weight, starts, size, outs, tail=None, chunk=1024, after=()):
    count, width = rows.shape
    blocks = starts.shape[0]
    chunks = [(at, min(chunk, size - at)) for at in range(0, size, chunk)]
    low = min(first for _, first, _ in outs)
    high = max(first + some for _, first, some in outs)
    upper = (high - low) // 32 * 16
    row_parts = [(0, upper), (upper, high - low - upper)]
    tails = [] if tail is None else [tail]
    heights = [some for _, _, some in outs]
    for array in tails:
        heights[-1] += array.shape[0]

    def kernel(starts_ref, rows_ref, weight_ref, *refs):
        tail_refs, refs = refs[: len(tails)], refs[len(tails) :]
        out_refs, (x, w, *refs) = refs[: len(outs)], refs[len(outs) :]
        stage, (x_sems, w_sems, out_sems, tail_sems) = refs[: len(outs)], refs[len(outs) :]
        x_copies = [
            pltpu.make_async_copy(
                rows_ref.at[pl.ds(low + at, some)], x.at[pl.ds(at, some)], x_sems.at[i]
            )
            for i, (at, some) in enumerate(row_parts)
        ]
        w_copies = [
            [
                pltpu.make_async_copy(
                    weight_ref.at[:, pl.ds(pl.multiple_of(starts_ref[b] + at, LANES), extent)],
                    w.at[b, :, pl.ds(at, extent)],
                    w_sems.at[b, c],
                )
                for c, (at, extent) in enumerate(chunks)
            ]
            for b in range(blocks)
        ]
        x_copies[0].start()
        w_copies[0][0].start()
        x_copies[1].start()
        for b in range(blocks):
            for c in range(len(chunks)):
                if b or c:
                    w_copies[b][c].start()
        stores = []
        for ref in tail_refs:
            below = pl.ds(outs[-1][2], ref.shape[0])
            read = pltpu.make_async_copy(ref, stage[-1].at[below], tail_sems.at[0])
            read.start()
            read.wait()
            stores.append(pltpu.make_async_copy(stage[-1].at[below], out_refs[-1].at[below], tail_sems.at[1]))
            stores[-1].start()
        for copy in x_copies:
            copy.wait()
        for b in range(blocks):
            for c, (at, extent) in enumerate(chunks):
                w_copies[b][c].wait()
                for o, (index, first, some) in enumerate(outs):
                    if index == b:
                        value = jnp.dot(
                            x[first - low : first - low + some, :], w[b, :, at : at + extent],
                            preferred_element_type=jnp.float32,
                        )
                        stage[o][:some, at : at + extent] = value.astype(rows.dtype)
                        store = pltpu.make_async_copy(
                            stage[o].at[pl.ds(0, some), pl.ds(at, extent)],
                            out_refs[o].at[pl.ds(0, some), pl.ds(at, extent)],
                            out_sems.at[o, c],
                        )
                        store.start()
                        stores.append(store)
        for store in stores:
            store.wait()

    shapes = [(height, size) for height in heights]
    return call(
        kernel, [starts, rows, weight] + tails, after, prefetch=1,
        in_specs=[ANY] * (2 + len(tails)),
        out_specs=[ANY] * len(outs),
        out_shape=[jax.ShapeDtypeStruct(shape, rows.dtype) for shape in shapes],
        scratch=[pltpu.VMEM((high - low, width), rows.dtype), pltpu.VMEM((blocks, width, size), rows.dtype)]
        + [pltpu.VMEM(shape, rows.dtype) for shape in shapes]
        + [
            pltpu.SemaphoreType.DMA((2,)),
            pltpu.SemaphoreType.DMA((blocks, len(chunks))),
            pltpu.SemaphoreType.DMA((len(outs), len(chunks))),
            pltpu.SemaphoreType.DMA((2,)),
        ],
        name="products",
    )


def total(runs, dtype=jnp.bfloat16, into=None, after=()):
    width = runs[0][1][0][0].shape[1]
    height = sum(some for some, _ in runs)
    rows_in_all, first, so_far = into or (height, 0, None)
    tiles = []
    at = 0
    for r, (some, terms) in enumerate(runs):
        size = -(-some // 32) * 16 if some * width > 2**17 else some
        for skip in range(0, some, size):
            tiles.append((r, skip, min(size, some - skip), at + skip))
        at += some
    operands = [term for _, terms in runs for term, _ in terms]
    before = [] if so_far is None else [so_far]
    most_terms = max(len(terms) for _, terms in runs)
    of_run = np.cumsum([0] + [len(terms) for _, terms in runs])

    def kernel(*refs):
        term_refs, out_ref = refs[: len(operands)], refs[len(operands) + len(before)]
        refs = refs[len(operands) + len(before) + 1 :]
        bufs, (stage, in_sems, out_sems) = refs[: len(operands)], refs[len(operands) :]
        reads, writes = [], []
        for n, (r, skip, size, place) in enumerate(tiles):
            reads.append(
                [
                    pltpu.make_async_copy(
                        term_refs[of_run[r] + t].at[pl.ds(start + skip, size)],
                        bufs[of_run[r] + t].at[pl.ds(skip, size)],
                        in_sems.at[t, n],
                    )
                    for t, (_, start) in enumerate(runs[r][1])
                ]
            )
            writes.append(
                pltpu.make_async_copy(
                    stage.at[pl.ds(place, size)], out_ref.at[pl.ds(first + place, size)], out_sems.at[n]
                )
            )
        for some in reads:
            for read in some:
                read.start()
        for n, (r, skip, size, place) in enumerate(tiles):
            for read in reads[n]:
                read.wait()
            value = None
            for t in range(len(runs[r][1])):
                part = bufs[of_run[r] + t][skip : skip + size, :].astype(jnp.float32)
                value = part if value is None else value + part
            stage[place : place + size, :] = value.astype(dtype)
            writes[n].start()
        for write in writes:
            write.wait()

    return call(
        kernel, operands + before, after,
        in_specs=[ANY] * (len(operands) + len(before)),
        out_specs=ANY,
        out_shape=jax.ShapeDtypeStruct((rows_in_all, width), dtype),
        scratch=[pltpu.VMEM((some, width), term.dtype) for some, terms in runs for term, _ in terms]
        + [
            pltpu.VMEM((height, width), dtype),
            pltpu.SemaphoreType.DMA((most_terms, len(tiles))),
            pltpu.SemaphoreType.DMA((len(tiles),)),
        ],
        alias={len(operands): 0} if before else None,
        name="total",
    )


def lane_pick(slot_ref, repeats, shape, rank, first):
    slot = jnp.concatenate([slot_ref[...]] * repeats, axis=0)
    return slot == lax.broadcasted_iota(jnp.int32, shape, 1) // rank + first


def block_copies(index_ref, maps_ref, buf, sems, sets, rank):
    each = index_ref.shape[0] // sets
    return [
        [
            pltpu.make_async_copy(
                maps_ref.at[index_ref[s * each + i]], buf.at[pl.ds((s * each + i) * rank, rank)],
                sems.at[s * each + i],
            )
            for i in range(each)
        ]
        for s in range(sets)
    ]


def low_rank(row_sets, slot_sets, maps, index, wide, after=()):
    sets = len(row_sets)
    count, width = row_sets[0].shape
    rank = maps.shape[1]
    span = index.shape[0] // sets * rank
    repeats = count // slot_sets[0].shape[0]
    half = count // 2
    group = 256
    tall = sets * half * 2 * rank // wide

    def kernel(index_ref, *refs):
        row_refs, slot_refs, maps_ref, out_ref = refs[:sets], refs[sets : 2 * sets], refs[2 * sets], refs[2 * sets + 1]
        rows_buf, maps_buf, row_sems, map_sems = refs[2 * sets + 2 :]
        row_copies = [
            pltpu.make_async_copy(row_refs[s], rows_buf.at[s], row_sems.at[s]) for s in range(sets)
        ]
        map_copies = block_copies(index_ref, maps_ref, maps_buf, map_sems, sets, rank)
        for s in range(sets):
            row_copies[s].start()
            for copy in map_copies[s]:
                copy.start()
        for s in range(sets):
            row_copies[s].wait()
            for copy in map_copies[s]:
                copy.wait()
            acc = None
            for at in range(0, span, group):
                scores = lax.dot_general(
                    rows_buf[s], maps_buf[s * span + at : s * span + at + group],
                    (((1,), (1,)), ((), ())), preferred_element_type=jnp.float32,
                )
                pick = lane_pick(slot_refs[s], repeats, (count, group), rank, at // rank)
                term = jnp.where(pick, scores, 0.0)
                acc = term if acc is None else acc + term
            summed = acc[:, 0:rank]
            for g in range(1, group // rank):
                summed += acc[:, g * rank : (g + 1) * rank]
            summed = summed.astype(out_ref.dtype)
            for b in range(half // tall):
                lanes = slice((s * half // tall + b) * 2 * rank, (s * half // tall + b + 1) * 2 * rank)
                both = [summed[start + b * tall : start + (b + 1) * tall] for start in (0, half)]
                out_ref[:, lanes] = jnp.concatenate(both, axis=1)

    return call(
        kernel, [index, *row_sets, *slot_sets, maps], after, prefetch=1,
        in_specs=[ANY] * sets + [pl.BlockSpec(memory_space=pltpu.VMEM)] * sets + [ANY],
        out_specs=pl.BlockSpec(memory_space=pltpu.VMEM),
        out_shape=jax.ShapeDtypeStruct((tall, wide), jnp.bfloat16),
        scratch=[
            pltpu.VMEM((sets, count, width), row_sets[0].dtype),
            pltpu.VMEM((sets * span, width), maps.dtype),
            pltpu.SemaphoreType.DMA((sets,)),
            pltpu.SemaphoreType.DMA((index.shape[0],)),
        ],
        name="low_rank",
    )


def expand(low, slot_sets, maps, index, after=()):
    sets = len(slot_sets)
    rank, width = maps.shape[1:]
    tall = low.shape[0]
    half = low.size // sets // (2 * rank)
    count = 2 * half
    span = index.shape[0] // sets * rank
    repeats = count // slot_sets[0].shape[0]

    outs = [(0, 0, count)] + [
        (s, p * count // PARTS, count // PARTS) for s in range(1, sets) for p in range(PARTS)
    ]

    def kernel(index_ref, low_ref, *refs):
        slot_refs, maps_ref, out_refs = refs[:sets], refs[sets], refs[sets + 1 : sets + 1 + len(outs)]
        stage, maps_buf, map_sems, out_sems = refs[sets + 1 + len(outs) :]
        map_copies = block_copies(index_ref, maps_ref, maps_buf, map_sems, sets, rank)
        writes = [
            pltpu.make_async_copy(stage.at[s, pl.ds(first, some)], out_refs[o], out_sems.at[o])
            for o, (s, first, some) in enumerate(outs)
        ]
        order = list(range(1, sets)) + [0]
        for s in order:
            for copy in map_copies[s]:
                copy.start()
        for s in order:
            lanes = [(s * half // tall + b) * 2 * rank for b in range(half // tall)]
            mine = jnp.concatenate(
                [low_ref[:, at + side : at + side + rank] for side in (0, rank) for at in lanes], axis=0
            )
            tiled = jnp.concatenate([mine] * (span // rank), axis=1)
            pick = lane_pick(slot_refs[s], repeats, (count, span), rank, 0)
            picked = jnp.where(pick, tiled, jnp.zeros_like(tiled))
            for copy in map_copies[s]:
                copy.wait()
            for at in range(0, width, CHUNK):
                value = jnp.dot(
                    picked, maps_buf[s * span : (s + 1) * span, at : at + CHUNK], preferred_element_type=jnp.float32
                )
                stage[s, :, at : at + CHUNK] = value.astype(stage.dtype)
            for o, (which, _, _) in enumerate(outs):
                if which == s:
                    writes[o].start()
        for write in writes:
            write.wait()

    return call(
        kernel, [index, low, *slot_sets, maps], after, prefetch=1,
        in_specs=[pl.BlockSpec(memory_space=pltpu.VMEM)] * (1 + sets) + [ANY],
        out_specs=[ANY] * len(outs),
        out_shape=[jax.ShapeDtypeStruct((some, width), jnp.bfloat16) for _, _, some in outs],
        scratch=[
            pltpu.VMEM((sets, count, width), jnp.bfloat16),
            pltpu.VMEM((sets * span, width), maps.dtype),
            pltpu.SemaphoreType.DMA((index.shape[0],)),
            pltpu.SemaphoreType.DMA((len(outs),)),
        ],
        name="expand",
    )


def line_plan(nz):
    order = np.zeros((nz, nz), np.int32)
    for z in range(nz):
        def need(j):
            if j == z:
                return (2 * nz, 0)
            return (nz - 1 - j + z, j) if j > z else (nz - 1 - z + j, nz - j)

        order[z] = sorted(range(nz), key=need)
    return order


def on_device(attention_result, tenant, projection_weight, adapter_down_maps, adapter_up_maps):
    steps, row_count, width = attention_result.shape
    local_adapters = adapter_down_maps.shape[0]
    owners = lax.axis_size("dp")
    me = lax.axis_index("dp")
    n = lax.axis_size("tensor")
    nz = n // 2
    place = lax.axis_index("tensor")
    z, y = place // 2, place % 2
    order = line_plan(nz)
    my_order = jnp.asarray(order)[z]
    out_width = projection_weight.shape[1] // n

    def swap_y(value):
        return lax.ppermute(value, "tensor", [(t, t ^ 1) for t in range(n)])

    def hop(value, h):
        pairs = []
        for side in range(2):
            pairs.append((h * 2 + side, (h + 1) * 2 + side))
            pairs.append(((nz - 1 - h) * 2 + side, (nz - 2 - h) * 2 + side))
        return lax.ppermute(value, "tensor", pairs)

    def slot_of(h, m):
        return list(order[h]).index(nz - 1 - m)

    def pass_on(value, shift):
        return lax.ppermute(value, "dp", [(i, (i + shift) % owners) for i in range(owners)])

    rows = attention_result.reshape(steps * row_count, width)
    count = steps * row_count
    last = [()]

    def then(kernel, *operands, **options):
        out = kernel(*operands, after=last[0], **options)
        last[0] = (out[0] if isinstance(out, (tuple, list)) else out,)
        return out

    slot_range = jnp.arange(SLOTS, dtype=jnp.int32)
    ids = jnp.arange(local_adapters, dtype=jnp.int32)

    def slots(row_ids, owner):
        hit = row_ids[:, None] - owner * local_adapters == ids[None, :]
        used = jnp.any(hit, axis=0)
        position = jnp.sum(
            (used[None, :] & (ids[None, :] < ids[:, None])).astype(jnp.int32), axis=1
        )
        names = jnp.sum(
            jnp.where(used[None, :] & (position[None, :] == slot_range[:, None]), ids[None, :], 0),
            axis=1,
        )
        row_slot = jnp.sum(jnp.where(hit, position[None, :] + 1, 0), axis=1) - 1
        return names, row_slot[:, None]

    away = [(my_order[k] * 2 + 1 - y) * out_width for k in range(nz)]
    own = [(my_order[k] * 2 + y) * out_width for k in range(nz)]
    low_rows = 2 * (owners * count // 2) * adapter_down_maps.shape[1] // out_width
    even = [(p * count // PARTS, count // PARTS) for p in range(PARTS)]
    uneven = [(0, count // 2 + low_rows), (count // 2 + low_rows, count // 2 - low_rows)]
    away_part, own_all, from_y, sums, arrived = {}, {}, {}, {}, {}

    def split(k):
        return uneven if k == 0 else [(0, count)]

    def add_up(span, terms, extra=(), dtype=jnp.bfloat16, into=None):
        low_row, high_row = span[0], span[0] + span[1]
        cuts = {low_row, high_row}
        for term in terms:
            for at, some, _, _ in term:
                cuts.update(row for row in (at, at + some) if low_row < row < high_row)
        cuts = sorted(cuts)
        runs = []
        for begin, end in zip(cuts, cuts[1:]):
            here = [
                (array, row + begin - at) for term in terms for at, some, array, row in term if at <= begin < at + some
            ]
            runs.append((end - begin, here))
        return then(total, runs + list(extra), dtype, into)

    def whole(array):
        return [(0, count, array, 0)]

    def multiply(aways, owns, tail=None, chunk=1024):
        ks = sorted({k for k, _ in aways})
        starts = jnp.stack([away[k] for k in ks] + [own[k] for k in owns])
        outs = [(ks.index(k), *split(k)[p]) for k, p in aways]
        outs += [(len(ks) + i, 0, count) for i in range(len(owns))]
        done = then(products, rows, projection_weight, starts, out_width, outs, tail, chunk)
        away_part.update(zip(aways, done))
        own_all.update(zip(owns, done[len(aways) :]))

    def start_y(k, p, after=None):
        value = away_part[k, p]
        from_y[k, p] = swap_y(value if after is None else hold(value, after))

    def y_parts(k):
        return [(*cut, from_y[k, p], 0) for p, cut in enumerate(split(k)) if (k, p) in from_y]

    def sum_parts(k):
        return [(*cut, sums[k, p], 0) for p, cut in enumerate(cut_of(0, k)) if (k, p) in sums]

    def cut_of(h, m):
        return uneven if m == 0 and h <= 1 else [(0, count)]

    def arrived_parts(h, m):
        return [(*cut, arrived[h, m, p], 0) for p, cut in enumerate(cut_of(h, m)) if (h, m, p) in arrived]

    def line(h, m, p):
        k = slot_of(h, m)
        span = cut_of(h, m)[p]
        low_too = m == 0 and h <= 1 and p == LOW_WITH[1]
        if h == 0:
            extra = [(low_rows, [(low, 0), (from_y[k, p], span[1])])] if low_too else []
            value = sums[k, p] = add_up(span, [whole(own_all[k]), y_parts(k)], extra)
        else:
            extra = [(low_rows, [(sums[k, p], span[1]), (arrived[h - 1, m, p], span[1])])] if low_too else []
            value = add_up(span, [sum_parts(k), arrived_parts(h - 1, m)], extra)
        arrived[h, m, p] = hop(value, h)

    def line_order():
        ready, free = {}, {}
        steps = [(h, m, p) for h in range(nz - 1) for m in range(nz - 1 - h) for p in range(len(cut_of(h, m)))]
        for h, m, p in sorted(steps, key=lambda step: (step[0], step[1], step[2])):
            k = slot_of(h, m)
            there = (k + 1.0) * count if k or p else 1.0 * cut_of(0, 0)[0][1]
            if h:
                above = range(len(cut_of(h - 1, m)))
                there = max(there, max(ready[h - 1, m, q, "end"] for q in above if q == p or len(above) != len(cut_of(h, m))))
            ready[h, m, p] = there
            free[h] = max(there, free.get(h, 0.0)) + cut_of(h, m)[p][1]
            ready[h, m, p, "end"] = free[h]
        return sorted(steps, key=lambda step: (ready[step], step[0]))

    row_ids = [tenant] + [pass_on(tenant, shift) for shift in range(1, owners)]
    row_sets = [rows] + [pass_on(rows, shift) for shift in range(1, owners)]
    multiply([(0, 0)], [], chunk=512)
    start_y(0, 0)
    named = [slots(some_ids, me) for some_ids in row_ids]
    names = jnp.concatenate([which for which, _ in named])
    slot_sets = [row_slot for _, row_slot in named]
    low = then(low_rank, row_sets, slot_sets, adapter_down_maps, names, out_width)
    multiply([LOW_WITH], [], low, chunk=512)
    start_y(*LOW_WITH)
    multiply([(1, 0)], [0])
    start_y(1, 0)
    for h, m, p in line_order():
        k = slot_of(h, m)
        line(h, m, p)
        if h == 0:
            if k == 0 and p == 0:
                multiply([(2, 0)] if nz > 2 else [], [1])
            elif k == 0:
                if nz > 2:
                    start_y(2, 0, last[0])
                multiply([(j, 0) for j in range(3, nz)], range(2, nz))
            elif p == len(cut_of(h, m)) - 1 and k + 2 < nz:
                start_y(k + 2, 0, last[0])
        if (h, k) == (0, 1):
            low_at = uneven[LOW_WITH[1]][1]
            pieces = [(sums[LOW_WITH], low_at)]
            for step in range(nz - 1):
                if step >= 2:
                    prefix = then(total, [(low_rows, [pieces[0], pieces[-1]])])
                    pieces.append((hop(prefix, step), 0))
                else:
                    pieces.append((arrived[step, 0, LOW_WITH[1]], low_at))
            low_sum = then(total, [(low_rows, pieces)])
            deltas = then(expand, low_sum, slot_sets, adapter_up_maps, names)
            back = [
                [(*cut, pass_on(deltas[1 + (shift - 1) * PARTS + p], -shift), 0) for p, cut in enumerate(even)]
                for shift in range(1, owners)
            ]
    span = (0, count)
    most = add_up(span, [whole(own_all[nz - 1]), whole(deltas[0]), y_parts(nz - 1)] + back, dtype=jnp.float32)
    out = add_up(span, [whole(most)] + [arrived_parts(h, nz - 2 - h) for h in range(nz - 1)])
    return out.reshape(steps, row_count, out_width)


def solution(mesh):
    placed = (
        P(None, ("groups", "dp"), "tensor"),
        P(("groups", "dp")),
        P("tensor", None),
        P(("groups", "dp"), None, "tensor"),
        P(("groups", "dp"), None, "tensor"),
    )
    return jax.shard_map(
        on_device,
        mesh=mesh,
        in_specs=placed,
        out_specs=P(None, ("groups", "dp"), "tensor"),
        check_vma=False,
    )
```

```python
import jax
import jax.numpy as jnp
import numpy as np
from jax import lax
from jax.experimental import pallas as pl
from jax.experimental.pallas import tpu as pltpu
from jax.sharding import PartitionSpec as P

SLOTS = 16
LANES = 128
CHUNK = 512
PARTS = 2
LOW_WITH = (0, PARTS - 1)
VMEM = 63 * 2**20
ANY = pl.BlockSpec(memory_space=pl.ANY)


def call(kernel, operands, after, *, in_specs, out_specs, out_shape, name, prefetch=0, scratch=(), alias=None):
    inputs, extra = len(operands), len(after)

    def body(*refs):
        kernel(*refs[:inputs], *refs[inputs + extra :])

    return pl.pallas_call(
        body,
        grid_spec=pltpu.PrefetchScalarGridSpec(
            num_scalar_prefetch=prefetch,
            grid=(),
            in_specs=list(in_specs) + [ANY] * extra,
            out_specs=out_specs,
            scratch_shapes=list(scratch),
        ),
        out_shape=out_shape,
        input_output_aliases=alias or {},
        compiler_params=pltpu.CompilerParams(vmem_limit_bytes=VMEM),
        cost_estimate=pl.CostEstimate(flops=1, transcendentals=0, bytes_accessed=1),
        name=name,
    )(*operands, *after)


def hold(value, after=()):
    def kernel(value_ref, out_ref):
        pass

    return call(
        kernel, [value], after, in_specs=[ANY], out_specs=ANY,
        out_shape=jax.ShapeDtypeStruct(value.shape, value.dtype), name="hold", alias={0: 0},
    )


def products(rows, weight, starts, size, outs, tail=None, chunk=1024, after=()):
    count, width = rows.shape
    blocks = starts.shape[0]
    chunks = [(at, min(chunk, size - at)) for at in range(0, size, chunk)]
    used = [segment for out in outs for segment in out if segment]
    low = min(first for _, first, _ in used)
    high = max(first + some for _, first, some in used)
    upper = (high - low) // 32 * 16
    row_parts = [(0, upper), (upper, high - low - upper)]
    tails = [] if tail is None else [tail]
    heights, places, tail_places = [], [], []
    for o, out in enumerate(outs):
        at = 0
        for segment in out:
            if segment:
                places.append((o, at, segment))
                at += segment[2]
            else:
                tail_places.append((o, at))
                at += tail.shape[0]
        heights.append(at)

    def kernel(starts_ref, rows_ref, weight_ref, *refs):
        tail_refs, refs = refs[: len(tails)], refs[len(tails) :]
        out_refs, (x, w, *refs) = refs[: len(outs)], refs[len(outs) :]
        stage, (x_sems, w_sems, out_sems, tail_sems) = refs[: len(outs)], refs[len(outs) :]
        x_copies = [
            pltpu.make_async_copy(
                rows_ref.at[pl.ds(low + at, some)], x.at[pl.ds(at, some)], x_sems.at[i]
            )
            for i, (at, some) in enumerate(row_parts)
        ]
        w_copies = [
            [
                pltpu.make_async_copy(
                    weight_ref.at[:, pl.ds(pl.multiple_of(starts_ref[b] + at, LANES), extent)],
                    w.at[b, :, pl.ds(at, extent)],
                    w_sems.at[b, c],
                )
                for c, (at, extent) in enumerate(chunks)
            ]
            for b in range(blocks)
        ]
        x_copies[0].start()
        w_copies[0][0].start()
        x_copies[1].start()
        for b in range(blocks):
            for c in range(len(chunks)):
                if b or c:
                    w_copies[b][c].start()
        stores = []
        for i, (o, at) in enumerate(tail_places):
            below = pl.ds(at, tail.shape[0])
            read = pltpu.make_async_copy(tail_refs[0], stage[o].at[below], tail_sems.at[0, i])
            read.start()
            read.wait()
            stores.append(pltpu.make_async_copy(stage[o].at[below], out_refs[o].at[below], tail_sems.at[1, i]))
            stores[-1].start()
        for copy in x_copies:
            copy.wait()
        for b in range(blocks):
            for c, (at, extent) in enumerate(chunks):
                w_copies[b][c].wait()
                for n, (o, place, (index, first, some)) in enumerate(places):
                    if index == b:
                        value = jnp.dot(
                            x[first - low : first - low + some, :], w[b, :, at : at + extent],
                            preferred_element_type=jnp.float32,
                        )
                        stage[o][place : place + some, at : at + extent] = value.astype(rows.dtype)
                        store = pltpu.make_async_copy(
                            stage[o].at[pl.ds(place, some), pl.ds(at, extent)],
                            out_refs[o].at[pl.ds(place, some), pl.ds(at, extent)],
                            out_sems.at[n, c],
                        )
                        store.start()
                        stores.append(store)
        for store in stores:
            store.wait()

    shapes = [(height, size) for height in heights]
    return call(
        kernel, [starts, rows, weight] + tails, after, prefetch=1,
        in_specs=[ANY] * (2 + len(tails)),
        out_specs=[ANY] * len(outs),
        out_shape=[jax.ShapeDtypeStruct(shape, rows.dtype) for shape in shapes],
        scratch=[pltpu.VMEM((high - low, width), rows.dtype), pltpu.VMEM((blocks, width, size), rows.dtype)]
        + [pltpu.VMEM(shape, rows.dtype) for shape in shapes]
        + [
            pltpu.SemaphoreType.DMA((2,)),
            pltpu.SemaphoreType.DMA((blocks, len(chunks))),
            pltpu.SemaphoreType.DMA((len(places), len(chunks))),
            pltpu.SemaphoreType.DMA((2, max(1, len(tail_places)))),
        ],
        name="products",
    )


def total(runs, dtype=jnp.bfloat16, into=None, after=()):
    width = runs[0][1][0][0].shape[1]
    height = sum(some for some, _ in runs)
    rows_in_all, first, so_far = into or (height, 0, None)
    tiles = []
    at = 0
    for r, (some, terms) in enumerate(runs):
        size = -(-some // 32) * 16 if some * width > 2**17 else some
        for skip in range(0, some, size):
            tiles.append((r, skip, min(size, some - skip), at + skip))
        at += some
    operands = [term for _, terms in runs for term, _ in terms]
    before = [] if so_far is None else [so_far]
    most_terms = max(len(terms) for _, terms in runs)
    of_run = np.cumsum([0] + [len(terms) for _, terms in runs])

    def kernel(*refs):
        term_refs, out_ref = refs[: len(operands)], refs[len(operands) + len(before)]
        refs = refs[len(operands) + len(before) + 1 :]
        bufs, (stage, in_sems, out_sems) = refs[: len(operands)], refs[len(operands) :]
        reads, writes = [], []
        for n, (r, skip, size, place) in enumerate(tiles):
            reads.append(
                [
                    pltpu.make_async_copy(
                        term_refs[of_run[r] + t].at[pl.ds(start + skip, size)],
                        bufs[of_run[r] + t].at[pl.ds(skip, size)],
                        in_sems.at[t, n],
                    )
                    for t, (_, start) in enumerate(runs[r][1])
                ]
            )
            writes.append(
                pltpu.make_async_copy(
                    stage.at[pl.ds(place, size)], out_ref.at[pl.ds(first + place, size)], out_sems.at[n]
                )
            )
        for some in reads:
            for read in some:
                read.start()
        for n, (r, skip, size, place) in enumerate(tiles):
            for read in reads[n]:
                read.wait()
            value = None
            for t in range(len(runs[r][1])):
                part = bufs[of_run[r] + t][skip : skip + size, :].astype(jnp.float32)
                value = part if value is None else value + part
            stage[place : place + size, :] = value.astype(dtype)
            writes[n].start()
        for write in writes:
            write.wait()

    return call(
        kernel, operands + before, after,
        in_specs=[ANY] * (len(operands) + len(before)),
        out_specs=ANY,
        out_shape=jax.ShapeDtypeStruct((rows_in_all, width), dtype),
        scratch=[pltpu.VMEM((some, width), term.dtype) for some, terms in runs for term, _ in terms]
        + [
            pltpu.VMEM((height, width), dtype),
            pltpu.SemaphoreType.DMA((most_terms, len(tiles))),
            pltpu.SemaphoreType.DMA((len(tiles),)),
        ],
        alias={len(operands): 0} if before else None,
        name="total",
    )


def lane_pick(slot_ref, repeats, shape, rank, first):
    slot = jnp.concatenate([slot_ref[...]] * repeats, axis=0)
    return slot == lax.broadcasted_iota(jnp.int32, shape, 1) // rank + first


def block_copies(index_ref, maps_ref, buf, sems, sets, rank):
    each = index_ref.shape[0] // sets
    return [
        [
            pltpu.make_async_copy(
                maps_ref.at[index_ref[s * each + i]], buf.at[pl.ds((s * each + i) * rank, rank)],
                sems.at[s * each + i],
            )
            for i in range(each)
        ]
        for s in range(sets)
    ]


def low_rank(row_sets, slot_sets, maps, index, wide, after=()):
    sets = len(row_sets)
    count, width = row_sets[0].shape
    rank = maps.shape[1]
    span = index.shape[0] // sets * rank
    repeats = count // slot_sets[0].shape[0]
    half = count // 2
    group = 256
    tall = sets * half * 2 * rank // wide

    def kernel(index_ref, *refs):
        row_refs, slot_refs, maps_ref, out_ref = refs[:sets], refs[sets : 2 * sets], refs[2 * sets], refs[2 * sets + 1]
        rows_buf, maps_buf, row_sems, map_sems = refs[2 * sets + 2 :]
        row_copies = [
            pltpu.make_async_copy(row_refs[s], rows_buf.at[s], row_sems.at[s]) for s in range(sets)
        ]
        map_copies = block_copies(index_ref, maps_ref, maps_buf, map_sems, sets, rank)
        for s in range(sets):
            row_copies[s].start()
            for copy in map_copies[s]:
                copy.start()
        for s in range(sets):
            row_copies[s].wait()
            for copy in map_copies[s]:
                copy.wait()
            acc = None
            for at in range(0, span, group):
                scores = lax.dot_general(
                    rows_buf[s], maps_buf[s * span + at : s * span + at + group],
                    (((1,), (1,)), ((), ())), preferred_element_type=jnp.float32,
                )
                pick = lane_pick(slot_refs[s], repeats, (count, group), rank, at // rank)
                term = jnp.where(pick, scores, 0.0)
                acc = term if acc is None else acc + term
            summed = acc[:, 0:rank]
            for g in range(1, group // rank):
                summed += acc[:, g * rank : (g + 1) * rank]
            summed = summed.astype(out_ref.dtype)
            for b in range(half // tall):
                lanes = slice((s * half // tall + b) * 2 * rank, (s * half // tall + b + 1) * 2 * rank)
                both = [summed[start + b * tall : start + (b + 1) * tall] for start in (0, half)]
                out_ref[:, lanes] = jnp.concatenate(both, axis=1)

    return call(
        kernel, [index, *row_sets, *slot_sets, maps], after, prefetch=1,
        in_specs=[ANY] * sets + [pl.BlockSpec(memory_space=pltpu.VMEM)] * sets + [ANY],
        out_specs=pl.BlockSpec(memory_space=pltpu.VMEM),
        out_shape=jax.ShapeDtypeStruct((tall, wide), jnp.bfloat16),
        scratch=[
            pltpu.VMEM((sets, count, width), row_sets[0].dtype),
            pltpu.VMEM((sets * span, width), maps.dtype),
            pltpu.SemaphoreType.DMA((sets,)),
            pltpu.SemaphoreType.DMA((index.shape[0],)),
        ],
        name="low_rank",
    )


def expand(low, slot_sets, maps, index, after=()):
    sets = len(slot_sets)
    rank, width = maps.shape[1:]
    tall = low.shape[0]
    half = low.size // sets // (2 * rank)
    count = 2 * half
    span = index.shape[0] // sets * rank
    repeats = count // slot_sets[0].shape[0]

    outs = [(0, 0, count)] + [
        (s, p * count // PARTS, count // PARTS) for s in range(1, sets) for p in range(PARTS)
    ]

    def kernel(index_ref, low_ref, *refs):
        slot_refs, maps_ref, out_refs = refs[:sets], refs[sets], refs[sets + 1 : sets + 1 + len(outs)]
        stage, maps_buf, map_sems, out_sems = refs[sets + 1 + len(outs) :]
        map_copies = block_copies(index_ref, maps_ref, maps_buf, map_sems, sets, rank)
        writes = [
            pltpu.make_async_copy(stage.at[s, pl.ds(first, some)], out_refs[o], out_sems.at[o])
            for o, (s, first, some) in enumerate(outs)
        ]
        order = list(range(1, sets)) + [0]
        for s in order:
            for copy in map_copies[s]:
                copy.start()
        for s in order:
            lanes = [(s * half // tall + b) * 2 * rank for b in range(half // tall)]
            mine = jnp.concatenate(
                [low_ref[:, at + side : at + side + rank] for side in (0, rank) for at in lanes], axis=0
            )
            tiled = jnp.concatenate([mine] * (span // rank), axis=1)
            pick = lane_pick(slot_refs[s], repeats, (count, span), rank, 0)
            picked = jnp.where(pick, tiled, jnp.zeros_like(tiled))
            for copy in map_copies[s]:
                copy.wait()
            for at in range(0, width, CHUNK):
                value = jnp.dot(
                    picked, maps_buf[s * span : (s + 1) * span, at : at + CHUNK], preferred_element_type=jnp.float32
                )
                stage[s, :, at : at + CHUNK] = value.astype(stage.dtype)
            for o, (which, _, _) in enumerate(outs):
                if which == s:
                    writes[o].start()
        for write in writes:
            write.wait()

    return call(
        kernel, [index, low, *slot_sets, maps], after, prefetch=1,
        in_specs=[pl.BlockSpec(memory_space=pltpu.VMEM)] * (1 + sets) + [ANY],
        out_specs=[ANY] * len(outs),
        out_shape=[jax.ShapeDtypeStruct((some, width), jnp.bfloat16) for _, _, some in outs],
        scratch=[
            pltpu.VMEM((sets, count, width), jnp.bfloat16),
            pltpu.VMEM((sets * span, width), maps.dtype),
            pltpu.SemaphoreType.DMA((index.shape[0],)),
            pltpu.SemaphoreType.DMA((len(outs),)),
        ],
        name="expand",
    )


def line_plan(nz):
    order = np.zeros((nz, nz), np.int32)
    for z in range(nz):
        def need(j):
            if j == z:
                return (2 * nz, 0)
            return (nz - 1 - j + z, j) if j > z else (nz - 1 - z + j, nz - j)

        order[z] = sorted(range(nz), key=need)
    return order


def on_device(attention_result, tenant, projection_weight, adapter_down_maps, adapter_up_maps):
    steps, row_count, width = attention_result.shape
    local_adapters = adapter_down_maps.shape[0]
    owners = lax.axis_size("dp")
    me = lax.axis_index("dp")
    n = lax.axis_size("tensor")
    nz = n // 2
    place = lax.axis_index("tensor")
    z, y = place // 2, place % 2
    order = line_plan(nz)
    my_order = jnp.asarray(order)[z]
    out_width = projection_weight.shape[1] // n

    def sum_y(value):
        pairs = [[t, t + 1] for t in range(0, n, 2)]
        return lax.psum_scatter(value, "tensor", scatter_dimension=0, axis_index_groups=pairs, tiled=True)

    def hop(value, h):
        pairs = []
        for side in range(2):
            pairs.append((h * 2 + side, (h + 1) * 2 + side))
            pairs.append(((nz - 1 - h) * 2 + side, (nz - 2 - h) * 2 + side))
        return lax.ppermute(value, "tensor", pairs)

    def slot_of(h, m):
        return list(order[h]).index(nz - 1 - m)

    def pass_on(value, shift):
        return lax.ppermute(value, "dp", [(i, (i + shift) % owners) for i in range(owners)])

    rows = attention_result.reshape(steps * row_count, width)
    count = steps * row_count
    last = [()]

    def then(kernel, *operands, **options):
        out = kernel(*operands, after=last[0], **options)
        last[0] = (out[0] if isinstance(out, (tuple, list)) else out,)
        return out

    slot_range = jnp.arange(SLOTS, dtype=jnp.int32)
    ids = jnp.arange(local_adapters, dtype=jnp.int32)

    def slots(row_ids, owner):
        hit = row_ids[:, None] - owner * local_adapters == ids[None, :]
        used = jnp.any(hit, axis=0)
        position = jnp.sum(
            (used[None, :] & (ids[None, :] < ids[:, None])).astype(jnp.int32), axis=1
        )
        names = jnp.sum(
            jnp.where(used[None, :] & (position[None, :] == slot_range[:, None]), ids[None, :], 0),
            axis=1,
        )
        row_slot = jnp.sum(jnp.where(hit, position[None, :] + 1, 0), axis=1) - 1
        return names, row_slot[:, None]

    low_rows = 2 * (owners * count // 2) * adapter_down_maps.shape[1] // out_width
    even = [(p * count // PARTS, count // PARTS) for p in range(PARTS)]
    uneven = [(0, count // 2 + low_rows), (count // 2 + low_rows, count // 2 - low_rows)]
    sums, arrived = {}, {}

    def split(k):
        return uneven if k == 0 else [(0, count)]

    def add_up(span, terms, extra=(), dtype=jnp.bfloat16, into=None):
        low_row, high_row = span[0], span[0] + span[1]
        cuts = {low_row, high_row}
        for term in terms:
            for at, some, _, _ in term:
                cuts.update(row for row in (at, at + some) if low_row < row < high_row)
        cuts = sorted(cuts)
        runs = []
        for begin, end in zip(cuts, cuts[1:]):
            here = [
                (array, row + begin - at) for term in terms for at, some, array, row in term if at <= begin < at + some
            ]
            runs.append((end - begin, here))
        return then(total, runs + list(extra), dtype, into)

    def whole(array):
        return [(0, count, array, 0)]

    def multiply(k, p, tail=None, chunk=1024):
        first, some = split(k)[p]
        starts = jnp.stack([(my_order[k] * 2 + side) * out_width for side in range(2)])
        extra = [] if tail is None else [None]
        outs = [[(0, first, some), *extra, (1, first, some), *extra]]
        sums[k, p] = sum_y(then(products, rows, projection_weight, starts, out_width, outs, tail, chunk)[0])

    def sum_parts(k):
        return [(*cut, sums[k, p], 0) for p, cut in enumerate(split(k))]

    def cut_of(h, m):
        return uneven if m == 0 and h <= 1 else [(0, count)]

    def arrived_parts(h, m):
        return [(*cut, arrived[h, m, p], 0) for p, cut in enumerate(cut_of(h, m)) if (h, m, p) in arrived]

    def line(h, m, p):
        k = slot_of(h, m)
        span = cut_of(h, m)[p]
        low_too = m == 0 and h <= 1 and p == LOW_WITH[1]
        if h == 0:
            value = then(hold, sums[k, p])
        else:
            extra = [(low_rows, [(sums[k, p], span[1]), (arrived[h - 1, m, p], span[1])])] if low_too else []
            value = add_up(span, [sum_parts(k), arrived_parts(h - 1, m)], extra)
        arrived[h, m, p] = hop(value, h)

    def line_order():
        ready, free = {}, {}
        steps = [(h, m, p) for h in range(nz - 1) for m in range(nz - 1 - h) for p in range(len(cut_of(h, m)))]
        for h, m, p in sorted(steps, key=lambda step: (step[0], step[1], step[2])):
            k = slot_of(h, m)
            there = (k + 1.0) * count if k or p else 1.0 * cut_of(0, 0)[0][1]
            if h:
                above = range(len(cut_of(h - 1, m)))
                there = max(there, max(ready[h - 1, m, q, "end"] for q in above if q == p or len(above) != len(cut_of(h, m))))
            ready[h, m, p] = there
            free[h] = max(there, free.get(h, 0.0)) + cut_of(h, m)[p][1]
            ready[h, m, p, "end"] = free[h]
        return sorted(steps, key=lambda step: (ready[step], step[0]))

    row_ids = [tenant] + [pass_on(tenant, shift) for shift in range(1, owners)]
    row_sets = [rows] + [pass_on(rows, shift) for shift in range(1, owners)]
    multiply(0, 0, chunk=512)
    named = [slots(some_ids, me) for some_ids in row_ids]
    names = jnp.concatenate([which for which, _ in named])
    slot_sets = [row_slot for _, row_slot in named]
    low = then(low_rank, row_sets, slot_sets, adapter_down_maps, names, out_width)
    multiply(*LOW_WITH, low, chunk=512)
    for k in range(1, nz):
        multiply(k, 0)
    for h, m, p in line_order():
        k = slot_of(h, m)
        line(h, m, p)
        if (h, k) == (0, 1):
            low_at = uneven[LOW_WITH[1]][1]
            pieces = [(sums[LOW_WITH], low_at)]
            for step in range(nz - 1):
                if step >= 2:
                    prefix = then(total, [(low_rows, [pieces[0], pieces[-1]])])
                    pieces.append((hop(prefix, step), 0))
                else:
                    pieces.append((arrived[step, 0, LOW_WITH[1]], low_at))
            low_sum = then(total, [(low_rows, pieces)])
            deltas = then(expand, low_sum, slot_sets, adapter_up_maps, names)
            back = [
                [(*cut, pass_on(deltas[1 + (shift - 1) * PARTS + p], -shift), 0) for p, cut in enumerate(even)]
                for shift in range(1, owners)
            ]
    span = (0, count)
    head = add_up(span, [whole(deltas[0]), sum_parts(nz - 1)] + back, dtype=jnp.float32)
    out = add_up(span, [whole(head)] + [arrived_parts(h, nz - 2 - h) for h in range(nz - 1)])
    return out.reshape(steps, row_count, out_width)


def solution(mesh):
    placed = (
        P(None, ("groups", "dp"), "tensor"),
        P(("groups", "dp")),
        P("tensor", None),
        P(("groups", "dp"), None, "tensor"),
        P(("groups", "dp"), None, "tensor"),
    )
    return jax.shard_map(
        on_device,
        mesh=mesh,
        in_specs=placed,
        out_specs=P(None, ("groups", "dp"), "tensor"),
        check_vma=False,
    )
```

```python
import jax
import jax.numpy as jnp
import numpy as np
from jax import lax
from jax.experimental import pallas as pl
from jax.experimental.pallas import tpu as pltpu
from jax.sharding import PartitionSpec as P

SLOTS = 16
LANES = 128
CHUNK = 512
PARTS = 2
LOW_WITH = (0, PARTS - 1)
HEAD_AFTER = (2, 0)
VMEM = 63 * 2**20
ANY = pl.BlockSpec(memory_space=pl.ANY)


def call(kernel, operands, after, *, in_specs, out_specs, out_shape, name, prefetch=0, scratch=(), alias=None):
    inputs, extra = len(operands), len(after)

    def body(*refs):
        kernel(*refs[:inputs], *refs[inputs + extra :])

    return pl.pallas_call(
        body,
        grid_spec=pltpu.PrefetchScalarGridSpec(
            num_scalar_prefetch=prefetch,
            grid=(),
            in_specs=list(in_specs) + [ANY] * extra,
            out_specs=out_specs,
            scratch_shapes=list(scratch),
        ),
        out_shape=out_shape,
        input_output_aliases=alias or {},
        compiler_params=pltpu.CompilerParams(vmem_limit_bytes=VMEM),
        cost_estimate=pl.CostEstimate(flops=1, transcendentals=0, bytes_accessed=1),
        name=name,
    )(*operands, *after)


def hold(value, after):
    def kernel(value_ref, out_ref):
        pass

    return call(
        kernel, [value], after, in_specs=[ANY], out_specs=ANY,
        out_shape=jax.ShapeDtypeStruct(value.shape, value.dtype), name="hold", alias={0: 0},
    )


def products(rows, weight, starts, size, outs, tail=None, chunk=1024, after=()):
    count, width = rows.shape
    blocks = starts.shape[0]
    chunks = [(at, min(chunk, size - at)) for at in range(0, size, chunk)]
    low = min(first for _, first, _ in outs)
    high = max(first + some for _, first, some in outs)
    upper = (high - low) // 32 * 16
    row_parts = [(0, upper), (upper, high - low - upper)]
    tails = [] if tail is None else [tail]
    heights = [some for _, _, some in outs]
    for array in tails:
        heights[-1] += array.shape[0]

    def kernel(starts_ref, rows_ref, weight_ref, *refs):
        tail_refs, refs = refs[: len(tails)], refs[len(tails) :]
        out_refs, (x, w, *refs) = refs[: len(outs)], refs[len(outs) :]
        stage, (x_sems, w_sems, out_sems, tail_sems) = refs[: len(outs)], refs[len(outs) :]
        x_copies = [
            pltpu.make_async_copy(
                rows_ref.at[pl.ds(low + at, some)], x.at[pl.ds(at, some)], x_sems.at[i]
            )
            for i, (at, some) in enumerate(row_parts)
        ]
        w_copies = [
            [
                pltpu.make_async_copy(
                    weight_ref.at[:, pl.ds(pl.multiple_of(starts_ref[b] + at, LANES), extent)],
                    w.at[b, :, pl.ds(at, extent)],
                    w_sems.at[b, c],
                )
                for c, (at, extent) in enumerate(chunks)
            ]
            for b in range(blocks)
        ]
        x_copies[0].start()
        w_copies[0][0].start()
        x_copies[1].start()
        for b in range(blocks):
            for c in range(len(chunks)):
                if b or c:
                    w_copies[b][c].start()
        stores = []
        for ref in tail_refs:
            below = pl.ds(outs[-1][2], ref.shape[0])
            read = pltpu.make_async_copy(ref, stage[-1].at[below], tail_sems.at[0])
            read.start()
            read.wait()
            stores.append(pltpu.make_async_copy(stage[-1].at[below], out_refs[-1].at[below], tail_sems.at[1]))
            stores[-1].start()
        for copy in x_copies:
            copy.wait()
        for b in range(blocks):
            for c, (at, extent) in enumerate(chunks):
                w_copies[b][c].wait()
                for o, (index, first, some) in enumerate(outs):
                    if index == b:
                        value = jnp.dot(
                            x[first - low : first - low + some, :], w[b, :, at : at + extent],
                            preferred_element_type=jnp.float32,
                        )
                        stage[o][:some, at : at + extent] = value.astype(rows.dtype)
                        store = pltpu.make_async_copy(
                            stage[o].at[pl.ds(0, some), pl.ds(at, extent)],
                            out_refs[o].at[pl.ds(0, some), pl.ds(at, extent)],
                            out_sems.at[o, c],
                        )
                        store.start()
                        stores.append(store)
        for store in stores:
            store.wait()

    shapes = [(height, size) for height in heights]
    return call(
        kernel, [starts, rows, weight] + tails, after, prefetch=1,
        in_specs=[ANY] * (2 + len(tails)),
        out_specs=[ANY] * len(outs),
        out_shape=[jax.ShapeDtypeStruct(shape, rows.dtype) for shape in shapes],
        scratch=[pltpu.VMEM((high - low, width), rows.dtype), pltpu.VMEM((blocks, width, size), rows.dtype)]
        + [pltpu.VMEM(shape, rows.dtype) for shape in shapes]
        + [
            pltpu.SemaphoreType.DMA((2,)),
            pltpu.SemaphoreType.DMA((blocks, len(chunks))),
            pltpu.SemaphoreType.DMA((len(outs), len(chunks))),
            pltpu.SemaphoreType.DMA((2,)),
        ],
        name="products",
    )


def total(runs, dtype=jnp.bfloat16, into=None, after=()):
    width = runs[0][1][0][0].shape[1]
    height = sum(some for some, _ in runs)
    rows_in_all, first, so_far = into or (height, 0, None)
    tiles = []
    at = 0
    for r, (some, terms) in enumerate(runs):
        size = -(-some // 32) * 16 if some * width > 2**17 else some
        for skip in range(0, some, size):
            tiles.append((r, skip, min(size, some - skip), at + skip))
        at += some
    operands = [term for _, terms in runs for term, _ in terms]
    before = [] if so_far is None else [so_far]
    most_terms = max(len(terms) for _, terms in runs)
    of_run = np.cumsum([0] + [len(terms) for _, terms in runs])

    def kernel(*refs):
        term_refs, out_ref = refs[: len(operands)], refs[len(operands) + len(before)]
        refs = refs[len(operands) + len(before) + 1 :]
        bufs, (stage, in_sems, out_sems) = refs[: len(operands)], refs[len(operands) :]
        reads, writes = [], []
        for n, (r, skip, size, place) in enumerate(tiles):
            reads.append(
                [
                    pltpu.make_async_copy(
                        term_refs[of_run[r] + t].at[pl.ds(start + skip, size)],
                        bufs[of_run[r] + t].at[pl.ds(skip, size)],
                        in_sems.at[t, n],
                    )
                    for t, (_, start) in enumerate(runs[r][1])
                ]
            )
            writes.append(
                pltpu.make_async_copy(
                    stage.at[pl.ds(place, size)], out_ref.at[pl.ds(first + place, size)], out_sems.at[n]
                )
            )
        for some in reads:
            for read in some:
                read.start()
        for n, (r, skip, size, place) in enumerate(tiles):
            for read in reads[n]:
                read.wait()
            value = None
            for t in range(len(runs[r][1])):
                part = bufs[of_run[r] + t][skip : skip + size, :].astype(jnp.float32)
                value = part if value is None else value + part
            stage[place : place + size, :] = value.astype(dtype)
            writes[n].start()
        for write in writes:
            write.wait()

    return call(
        kernel, operands + before, after,
        in_specs=[ANY] * (len(operands) + len(before)),
        out_specs=ANY,
        out_shape=jax.ShapeDtypeStruct((rows_in_all, width), dtype),
        scratch=[pltpu.VMEM((some, width), term.dtype) for some, terms in runs for term, _ in terms]
        + [
            pltpu.VMEM((height, width), dtype),
            pltpu.SemaphoreType.DMA((most_terms, len(tiles))),
            pltpu.SemaphoreType.DMA((len(tiles),)),
        ],
        alias={len(operands): 0} if before else None,
        name="total",
    )


def lane_pick(slot_ref, repeats, shape, rank, first):
    slot = jnp.concatenate([slot_ref[...]] * repeats, axis=0)
    return slot == lax.broadcasted_iota(jnp.int32, shape, 1) // rank + first


def block_copies(index_ref, maps_ref, buf, sems, sets, rank):
    each = index_ref.shape[0] // sets
    return [
        [
            pltpu.make_async_copy(
                maps_ref.at[index_ref[s * each + i]], buf.at[pl.ds((s * each + i) * rank, rank)],
                sems.at[s * each + i],
            )
            for i in range(each)
        ]
        for s in range(sets)
    ]


def low_rank(row_sets, slot_sets, maps, index, wide, after=()):
    sets = len(row_sets)
    count, width = row_sets[0].shape
    rank = maps.shape[1]
    span = index.shape[0] // sets * rank
    repeats = count // slot_sets[0].shape[0]
    half = count // 2
    group = 256
    tall = sets * half * 2 * rank // wide

    def kernel(index_ref, *refs):
        row_refs, slot_refs, maps_ref, out_ref = refs[:sets], refs[sets : 2 * sets], refs[2 * sets], refs[2 * sets + 1]
        rows_buf, maps_buf, row_sems, map_sems = refs[2 * sets + 2 :]
        row_copies = [
            pltpu.make_async_copy(row_refs[s], rows_buf.at[s], row_sems.at[s]) for s in range(sets)
        ]
        map_copies = block_copies(index_ref, maps_ref, maps_buf, map_sems, sets, rank)
        for s in range(sets):
            row_copies[s].start()
            for copy in map_copies[s]:
                copy.start()
        for s in range(sets):
            row_copies[s].wait()
            for copy in map_copies[s]:
                copy.wait()
            acc = None
            for at in range(0, span, group):
                scores = lax.dot_general(
                    rows_buf[s], maps_buf[s * span + at : s * span + at + group],
                    (((1,), (1,)), ((), ())), preferred_element_type=jnp.float32,
                )
                pick = lane_pick(slot_refs[s], repeats, (count, group), rank, at // rank)
                term = jnp.where(pick, scores, 0.0)
                acc = term if acc is None else acc + term
            summed = acc[:, 0:rank]
            for g in range(1, group // rank):
                summed += acc[:, g * rank : (g + 1) * rank]
            summed = summed.astype(out_ref.dtype)
            for b in range(half // tall):
                lanes = slice((s * half // tall + b) * 2 * rank, (s * half // tall + b + 1) * 2 * rank)
                both = [summed[start + b * tall : start + (b + 1) * tall] for start in (0, half)]
                out_ref[:, lanes] = jnp.concatenate(both, axis=1)

    return call(
        kernel, [index, *row_sets, *slot_sets, maps], after, prefetch=1,
        in_specs=[ANY] * sets + [pl.BlockSpec(memory_space=pltpu.VMEM)] * sets + [ANY],
        out_specs=pl.BlockSpec(memory_space=pltpu.VMEM),
        out_shape=jax.ShapeDtypeStruct((tall, wide), jnp.bfloat16),
        scratch=[
            pltpu.VMEM((sets, count, width), row_sets[0].dtype),
            pltpu.VMEM((sets * span, width), maps.dtype),
            pltpu.SemaphoreType.DMA((sets,)),
            pltpu.SemaphoreType.DMA((index.shape[0],)),
        ],
        name="low_rank",
    )


def expand(low, slot_sets, maps, index, places, after=()):
    sets = len(slot_sets)
    rank, width = maps.shape[1:]
    tall = low.shape[0]
    half = low.size // sets // (2 * rank)
    count = 2 * half
    span = index.shape[0] // sets * rank
    repeats = count // slot_sets[0].shape[0]

    def kernel(index_ref, places_ref, low_ref, *refs):
        slot_refs, maps_ref, out_ref = refs[:sets], refs[sets], refs[sets + 1]
        stage, maps_buf, map_sems, out_sems = refs[sets + 2 :]
        map_copies = block_copies(index_ref, maps_ref, maps_buf, map_sems, sets, rank)
        writes = [
            pltpu.make_async_copy(
                stage.at[s], out_ref.at[pl.ds(pl.multiple_of(places_ref[s] * count, count), count)], out_sems.at[s]
            )
            for s in range(sets)
        ]
        for s in range(sets):
            for copy in map_copies[s]:
                copy.start()
        for s in range(sets):
            lanes = [(s * half // tall + b) * 2 * rank for b in range(half // tall)]
            mine = jnp.concatenate(
                [low_ref[:, at + side : at + side + rank] for side in (0, rank) for at in lanes], axis=0
            )
            tiled = jnp.concatenate([mine] * (span // rank), axis=1)
            pick = lane_pick(slot_refs[s], repeats, (count, span), rank, 0)
            picked = jnp.where(pick, tiled, jnp.zeros_like(tiled))
            for copy in map_copies[s]:
                copy.wait()
            for at in range(0, width, CHUNK):
                value = jnp.dot(
                    picked, maps_buf[s * span : (s + 1) * span, at : at + CHUNK], preferred_element_type=jnp.float32
                )
                stage[s, :, at : at + CHUNK] = value.astype(stage.dtype)
            writes[s].start()
        for write in writes:
            write.wait()

    return call(
        kernel, [index, places, low, *slot_sets, maps], after, prefetch=2,
        in_specs=[pl.BlockSpec(memory_space=pltpu.VMEM)] * (1 + sets) + [ANY],
        out_specs=ANY,
        out_shape=jax.ShapeDtypeStruct((sets * count, width), jnp.bfloat16),
        scratch=[
            pltpu.VMEM((sets, count, width), jnp.bfloat16),
            pltpu.VMEM((sets * span, width), maps.dtype),
            pltpu.SemaphoreType.DMA((index.shape[0],)),
            pltpu.SemaphoreType.DMA((sets,)),
        ],
        name="expand",
    )


def line_plan(nz):
    order = np.zeros((nz, nz), np.int32)
    for z in range(nz):
        def need(j):
            if j == z:
                return (2 * nz, 0)
            return (nz - 1 - j + z, j) if j > z else (nz - 1 - z + j, nz - j)

        order[z] = sorted(range(nz), key=need)
    return order


def on_device(attention_result, tenant, projection_weight, adapter_down_maps, adapter_up_maps):
    steps, row_count, width = attention_result.shape
    local_adapters = adapter_down_maps.shape[0]
    owners = lax.axis_size("dp")
    me = lax.axis_index("dp")
    n = lax.axis_size("tensor")
    nz = n // 2
    place = lax.axis_index("tensor")
    z, y = place // 2, place % 2
    order = line_plan(nz)
    my_order = jnp.asarray(order)[z]
    out_width = projection_weight.shape[1] // n

    def swap_y(value):
        return lax.ppermute(value, "tensor", [(t, t ^ 1) for t in range(n)])

    def hop(value, h):
        pairs = []
        for side in range(2):
            pairs.append((h * 2 + side, (h + 1) * 2 + side))
            pairs.append(((nz - 1 - h) * 2 + side, (nz - 2 - h) * 2 + side))
        return lax.ppermute(value, "tensor", pairs)

    def slot_of(h, m):
        return list(order[h]).index(nz - 1 - m)

    def pass_on(value, shift):
        return lax.ppermute(value, "dp", [(i, (i + shift) % owners) for i in range(owners)])

    rows = attention_result.reshape(steps * row_count, width)
    count = steps * row_count
    last = [()]

    def then(kernel, *operands, **options):
        out = kernel(*operands, after=last[0], **options)
        last[0] = (out[0] if isinstance(out, (tuple, list)) else out,)
        return out

    slot_range = jnp.arange(SLOTS, dtype=jnp.int32)
    ids = jnp.arange(local_adapters, dtype=jnp.int32)

    def slots(row_ids, owner):
        hit = row_ids[:, None] - owner * local_adapters == ids[None, :]
        used = jnp.any(hit, axis=0)
        position = jnp.sum(
            (used[None, :] & (ids[None, :] < ids[:, None])).astype(jnp.int32), axis=1
        )
        names = jnp.sum(
            jnp.where(used[None, :] & (position[None, :] == slot_range[:, None]), ids[None, :], 0),
            axis=1,
        )
        row_slot = jnp.sum(jnp.where(hit, position[None, :] + 1, 0), axis=1) - 1
        return names, row_slot[:, None]

    away = [(my_order[k] * 2 + 1 - y) * out_width for k in range(nz)]
    own = [(my_order[k] * 2 + y) * out_width for k in range(nz)]
    low_rows = 2 * (owners * count // 2) * adapter_down_maps.shape[1] // out_width
    even = [(p * count // PARTS, count // PARTS) for p in range(PARTS)]
    uneven = [(0, count // 2 + low_rows), (count // 2 + low_rows, count // 2 - low_rows)]
    away_part, own_all, from_y, sums, arrived = {}, {}, {}, {}, {}

    def split(k):
        return uneven if k == 0 else [(0, count)]

    def add_up(span, terms, extra=(), dtype=jnp.bfloat16, into=None):
        low_row, high_row = span[0], span[0] + span[1]
        cuts = {low_row, high_row}
        for term in terms:
            for at, some, _, _ in term:
                cuts.update(row for row in (at, at + some) if low_row < row < high_row)
        cuts = sorted(cuts)
        runs = []
        for begin, end in zip(cuts, cuts[1:]):
            here = [
                (array, row + begin - at) for term in terms for at, some, array, row in term if at <= begin < at + some
            ]
            runs.append((end - begin, here))
        return then(total, runs + list(extra), dtype, into)

    def whole(array):
        return [(0, count, array, 0)]

    def multiply(aways, owns, tail=None, chunk=1024):
        ks = sorted({k for k, _ in aways})
        starts = jnp.stack([away[k] for k in ks] + [own[k] for k in owns])
        outs = [(ks.index(k), *split(k)[p]) for k, p in aways]
        outs += [(len(ks) + i, 0, count) for i in range(len(owns))]
        done = then(products, rows, projection_weight, starts, out_width, outs, tail, chunk)
        away_part.update(zip(aways, done))
        own_all.update(zip(owns, done[len(aways) :]))

    def start_y(k, p, after=None):
        value = away_part[k, p]
        from_y[k, p] = swap_y(value if after is None else hold(value, after))

    def y_parts(k):
        return [(*cut, from_y[k, p], 0) for p, cut in enumerate(split(k)) if (k, p) in from_y]

    def sum_parts(k):
        return [(*cut, sums[k, p], 0) for p, cut in enumerate(cut_of(0, k)) if (k, p) in sums]

    def cut_of(h, m):
        if m == 0 and h <= 1:
            return uneven
        return even if m == 1 else [(0, count)]

    def arrived_parts(h, m):
        return [(*cut, arrived[h, m, p], 0) for p, cut in enumerate(cut_of(h, m)) if (h, m, p) in arrived]

    def line(h, m, p):
        k = slot_of(h, m)
        span = cut_of(h, m)[p]
        low_too = m == 0 and h <= 1 and p == LOW_WITH[1]
        if h == 0:
            extra = [(low_rows, [(low, 0), (from_y[k, p], span[1])])] if low_too else []
            value = sums[k, p] = add_up(span, [whole(own_all[k]), y_parts(k)], extra)
        else:
            extra = [(low_rows, [(sums[k, p], span[1]), (arrived[h - 1, m, p], span[1])])] if low_too else []
            value = add_up(span, [sum_parts(k), arrived_parts(h - 1, m)], extra)
        arrived[h, m, p] = hop(value, h)

    def line_order():
        ready, free = {}, {}
        steps = [(h, m, p) for h in range(nz - 1) for m in range(nz - 1 - h) for p in range(len(cut_of(h, m)))]
        for h, m, p in sorted(steps, key=lambda step: (step[0], step[1], step[2])):
            k = slot_of(h, m)
            there = (k + 1.0) * count if k or p else 1.0 * cut_of(0, 0)[0][1]
            if h:
                above = range(len(cut_of(h - 1, m)))
                there = max(there, max(ready[h - 1, m, q, "end"] for q in above if q == p or len(above) != len(cut_of(h, m))))
            ready[h, m, p] = there
            free[h] = max(there, free.get(h, 0.0)) + cut_of(h, m)[p][1]
            ready[h, m, p, "end"] = free[h]
        return sorted(steps, key=lambda step: (ready[step], step[0]))

    row_ids = [tenant] + [pass_on(tenant, shift) for shift in range(1, owners)]
    row_sets = [rows] + [pass_on(rows, shift) for shift in range(1, owners)]
    multiply([(0, 0)], [], chunk=512)
    start_y(0, 0)
    named = [slots(some_ids, me) for some_ids in row_ids]
    names = jnp.concatenate([which for which, _ in named])
    slot_sets = [row_slot for _, row_slot in named]
    low = then(low_rank, row_sets, slot_sets, adapter_down_maps, names, out_width)
    multiply([LOW_WITH], [], low, chunk=512)
    start_y(*LOW_WITH)
    multiply([(1, 0)], [0])
    start_y(1, 0)
    for h, m, p in line_order():
        k = slot_of(h, m)
        line(h, m, p)
        if h == 0:
            if k == 0 and p == 0:
                multiply([(2, 0)] if nz > 2 else [], [1])
            elif k == 0:
                if nz > 2:
                    start_y(2, 0, last[0])
                multiply([(j, 0) for j in range(3, nz)], range(2, nz))
            elif p == len(cut_of(h, m)) - 1 and k + 2 < nz:
                start_y(k + 2, 0, last[0])
        if (h, k, p) == (0, 1, len(cut_of(h, m)) - 1):
            low_at = uneven[LOW_WITH[1]][1]
            pieces = [(sums[LOW_WITH], low_at)]
            for step in range(nz - 1):
                if step >= 2:
                    prefix = then(total, [(low_rows, [pieces[0], pieces[-1]])])
                    pieces.append((hop(prefix, step), 0))
                else:
                    pieces.append((arrived[step, 0, LOW_WITH[1]], low_at))
        if (h, m, p) == (1, 1, 0):
            low_sum = then(total, [(low_rows, pieces)])
            places = jnp.stack([(me - shift) % owners for shift in range(owners)])
            deltas = then(expand, low_sum, slot_sets, adapter_up_maps, names, places)
            delta = lax.psum_scatter(deltas, "dp", scatter_dimension=0, tiled=True)
        if (h, m) == (HEAD_AFTER if nz > 2 else (0, 0)) and p == len(cut_of(h, m)) - 1:
            head = add_up((0, count), [whole(own_all[nz - 1]), whole(delta)], dtype=jnp.float32)
    span = (0, count)
    early = [arrived_parts(h, nz - 2 - h) for h in range(1, nz - 2)]
    late = [arrived_parts(h, nz - 2 - h) for h in range(nz - 1) if not 1 <= h < nz - 2]
    most = add_up(span, [whole(head), y_parts(nz - 1)] + early, dtype=jnp.float32)
    out = add_up(span, [whole(most)] + late)
    return out.reshape(steps, row_count, out_width)


def solution(mesh):
    placed = (
        P(None, ("groups", "dp"), "tensor"),
        P(("groups", "dp")),
        P("tensor", None),
        P(("groups", "dp"), None, "tensor"),
        P(("groups", "dp"), None, "tensor"),
    )
    return jax.shard_map(
        on_device,
        mesh=mesh,
        in_specs=placed,
        out_specs=P(None, ("groups", "dp"), "tensor"),
        check_vma=False,
    )
```

```python
import jax
import jax.numpy as jnp
import numpy as np
from jax import lax
from jax.experimental import pallas as pl
from jax.experimental.pallas import tpu as pltpu
from jax.sharding import PartitionSpec as P

SLOTS = 16
LANES = 128
CHUNK = 512
PARTS = 2
VMEM = 63 * 2**20
ANY = pl.BlockSpec(memory_space=pl.ANY)


def call(kernel, operands, after, *, in_specs, out_specs, out_shape, name, prefetch=0, scratch=(), alias=None):
    inputs, extra = len(operands), len(after)

    def body(*refs):
        kernel(*refs[:inputs], *refs[inputs + extra :])

    return pl.pallas_call(
        body,
        grid_spec=pltpu.PrefetchScalarGridSpec(
            num_scalar_prefetch=prefetch,
            grid=(),
            in_specs=list(in_specs) + [ANY] * extra,
            out_specs=out_specs,
            scratch_shapes=list(scratch),
        ),
        out_shape=out_shape,
        input_output_aliases=alias or {},
        compiler_params=pltpu.CompilerParams(vmem_limit_bytes=VMEM),
        cost_estimate=pl.CostEstimate(flops=1, transcendentals=0, bytes_accessed=1),
        name=name,
    )(*operands, *after)


def hold(value, after):
    def kernel(value_ref, out_ref):
        pass

    return call(
        kernel, [value], after, in_specs=[ANY], out_specs=ANY,
        out_shape=jax.ShapeDtypeStruct(value.shape, value.dtype), name="hold", alias={0: 0},
    )


def products(rows, weight, starts, names, size, outs, tail=None, chunk=1024, after=()):
    count, width = rows.shape
    blocks = len(names)
    chunks = [(at, min(chunk, size - at)) for at in range(0, size, chunk)]
    used = [segment for out in outs for segment in out if segment]
    low = min(first for _, first, _ in used)
    high = max(first + some for _, first, some in used)
    upper = (high - low) // 32 * 16
    row_parts = [(0, upper), (upper, high - low - upper)]
    tails = [] if tail is None else [tail]
    heights, places, tail_places = [], [], []
    for o, out in enumerate(outs):
        at = 0
        for segment in out:
            if segment:
                places.append((o, at, segment))
                at += segment[2]
            else:
                tail_places.append((o, at))
                at += tail.shape[0]
        heights.append(at)

    def kernel(starts_ref, rows_ref, weight_ref, *refs):
        tail_refs, refs = refs[: len(tails)], refs[len(tails) :]
        out_refs, (x, w, *refs) = refs[: len(outs)], refs[len(outs) :]
        stage, (x_sems, w_sems, out_sems, tail_sems) = refs[: len(outs)], refs[len(outs) :]
        x_copies = [
            pltpu.make_async_copy(
                rows_ref.at[pl.ds(low + at, some)], x.at[pl.ds(at, some)], x_sems.at[i]
            )
            for i, (at, some) in enumerate(row_parts)
        ]
        w_copies = [
            [
                pltpu.make_async_copy(
                    weight_ref.at[:, pl.ds(pl.multiple_of(starts_ref[names[b]] + at, LANES), extent)],
                    w.at[b, :, pl.ds(at, extent)],
                    w_sems.at[b, c],
                )
                for c, (at, extent) in enumerate(chunks)
            ]
            for b in range(blocks)
        ]
        x_copies[0].start()
        w_copies[0][0].start()
        x_copies[1].start()
        for b in range(blocks):
            for c in range(len(chunks)):
                if b or c:
                    w_copies[b][c].start()
        stores = []
        for i, (o, at) in enumerate(tail_places):
            below = pl.ds(at, tail.shape[0])
            read = pltpu.make_async_copy(tail_refs[0], stage[o].at[below], tail_sems.at[0, i])
            read.start()
            read.wait()
            stores.append(pltpu.make_async_copy(stage[o].at[below], out_refs[o].at[below], tail_sems.at[1, i]))
            stores[-1].start()
        for copy in x_copies:
            copy.wait()
        for b in range(blocks):
            for c, (at, extent) in enumerate(chunks):
                w_copies[b][c].wait()
                for n, (o, place, (index, first, some)) in enumerate(places):
                    if index == b:
                        value = jnp.dot(
                            x[first - low : first - low + some, :], w[b, :, at : at + extent],
                            preferred_element_type=jnp.float32,
                        )
                        stage[o][place : place + some, at : at + extent] = value.astype(rows.dtype)
                        store = pltpu.make_async_copy(
                            stage[o].at[pl.ds(place, some), pl.ds(at, extent)],
                            out_refs[o].at[pl.ds(place, some), pl.ds(at, extent)],
                            out_sems.at[n, c],
                        )
                        store.start()
                        stores.append(store)
        for store in stores:
            store.wait()

    shapes = [(height, size) for height in heights]
    return call(
        kernel, [starts, rows, weight] + tails, after, prefetch=1,
        in_specs=[ANY] * (2 + len(tails)),
        out_specs=[ANY] * len(outs),
        out_shape=[jax.ShapeDtypeStruct(shape, rows.dtype) for shape in shapes],
        scratch=[pltpu.VMEM((high - low, width), rows.dtype), pltpu.VMEM((blocks, width, size), rows.dtype)]
        + [pltpu.VMEM(shape, rows.dtype) for shape in shapes]
        + [
            pltpu.SemaphoreType.DMA((2,)),
            pltpu.SemaphoreType.DMA((blocks, len(chunks))),
            pltpu.SemaphoreType.DMA((len(places), len(chunks))),
            pltpu.SemaphoreType.DMA((2, max(1, len(tail_places)))),
        ],
        name="products",
    )


def total(runs, dtype=jnp.bfloat16, into=None, after=()):
    width = runs[0][1][0][0].shape[1]
    height = sum(some for some, _ in runs)
    rows_in_all, first, so_far = into or (height, 0, None)
    tiles = []
    at = 0
    for r, (some, terms) in enumerate(runs):
        size = -(-some // 32) * 16 if some * width > 2**17 else some
        for skip in range(0, some, size):
            tiles.append((r, skip, min(size, some - skip), at + skip))
        at += some
    operands = [term for _, terms in runs for term, _ in terms]
    before = [] if so_far is None else [so_far]
    most_terms = max(len(terms) for _, terms in runs)
    of_run = np.cumsum([0] + [len(terms) for _, terms in runs])

    def kernel(*refs):
        term_refs, out_ref = refs[: len(operands)], refs[len(operands) + len(before)]
        refs = refs[len(operands) + len(before) + 1 :]
        bufs, (stage, in_sems, out_sems) = refs[: len(operands)], refs[len(operands) :]
        reads, writes = [], []
        for n, (r, skip, size, place) in enumerate(tiles):
            reads.append(
                [
                    pltpu.make_async_copy(
                        term_refs[of_run[r] + t].at[pl.ds(start + skip, size)],
                        bufs[of_run[r] + t].at[pl.ds(skip, size)],
                        in_sems.at[t, n],
                    )
                    for t, (_, start) in enumerate(runs[r][1])
                ]
            )
            writes.append(
                pltpu.make_async_copy(
                    stage.at[pl.ds(place, size)], out_ref.at[pl.ds(first + place, size)], out_sems.at[n]
                )
            )
        for some in reads:
            for read in some:
                read.start()
        for n, (r, skip, size, place) in enumerate(tiles):
            for read in reads[n]:
                read.wait()
            value = None
            for t in range(len(runs[r][1])):
                part = bufs[of_run[r] + t][skip : skip + size, :].astype(jnp.float32)
                value = part if value is None else value + part
            stage[place : place + size, :] = value.astype(dtype)
            writes[n].start()
        for write in writes:
            write.wait()

    return call(
        kernel, operands + before, after,
        in_specs=[ANY] * (len(operands) + len(before)),
        out_specs=ANY,
        out_shape=jax.ShapeDtypeStruct((rows_in_all, width), dtype),
        scratch=[pltpu.VMEM((some, width), term.dtype) for some, terms in runs for term, _ in terms]
        + [
            pltpu.VMEM((height, width), dtype),
            pltpu.SemaphoreType.DMA((most_terms, len(tiles))),
            pltpu.SemaphoreType.DMA((len(tiles),)),
        ],
        alias={len(operands): 0} if before else None,
        name="total",
    )


def lane_pick(slot_ref, repeats, shape, rank, first):
    slot = jnp.concatenate([slot_ref[...]] * repeats, axis=0)
    return slot == lax.broadcasted_iota(jnp.int32, shape, 1) // rank + first


def block_copies(index_ref, maps_ref, buf, sems, sets, rank):
    each = index_ref.shape[0] // sets
    return [
        [
            pltpu.make_async_copy(
                maps_ref.at[index_ref[s * each + i]], buf.at[pl.ds((s * each + i) * rank, rank)],
                sems.at[s * each + i],
            )
            for i in range(each)
        ]
        for s in range(sets)
    ]


def low_rank(row_sets, slot_sets, maps, index, wide, after=()):
    sets = len(row_sets)
    count, width = row_sets[0].shape
    rank = maps.shape[1]
    span = index.shape[0] // sets * rank
    repeats = count // slot_sets[0].shape[0]
    half = count // 2
    group = 256
    tall = sets * half * 2 * rank // wide

    def kernel(index_ref, *refs):
        row_refs, slot_refs, maps_ref, out_ref = refs[:sets], refs[sets : 2 * sets], refs[2 * sets], refs[2 * sets + 1]
        rows_buf, maps_buf, row_sems, map_sems = refs[2 * sets + 2 :]
        row_copies = [
            pltpu.make_async_copy(row_refs[s], rows_buf.at[s], row_sems.at[s]) for s in range(sets)
        ]
        map_copies = block_copies(index_ref, maps_ref, maps_buf, map_sems, sets, rank)
        for s in range(sets):
            row_copies[s].start()
            for copy in map_copies[s]:
                copy.start()
        for s in range(sets):
            row_copies[s].wait()
            for copy in map_copies[s]:
                copy.wait()
            acc = None
            for at in range(0, span, group):
                scores = lax.dot_general(
                    rows_buf[s], maps_buf[s * span + at : s * span + at + group],
                    (((1,), (1,)), ((), ())), preferred_element_type=jnp.float32,
                )
                pick = lane_pick(slot_refs[s], repeats, (count, group), rank, at // rank)
                term = jnp.where(pick, scores, 0.0)
                acc = term if acc is None else acc + term
            summed = acc[:, 0:rank]
            for g in range(1, group // rank):
                summed += acc[:, g * rank : (g + 1) * rank]
            summed = summed.astype(out_ref.dtype)
            for b in range(half // tall):
                lanes = slice((s * half // tall + b) * 2 * rank, (s * half // tall + b + 1) * 2 * rank)
                both = [summed[start + b * tall : start + (b + 1) * tall] for start in (0, half)]
                out_ref[:, lanes] = jnp.concatenate(both, axis=1)

    return call(
        kernel, [index, *row_sets, *slot_sets, maps], after, prefetch=1,
        in_specs=[ANY] * sets + [pl.BlockSpec(memory_space=pltpu.VMEM)] * sets + [ANY],
        out_specs=pl.BlockSpec(memory_space=pltpu.VMEM),
        out_shape=jax.ShapeDtypeStruct((tall, wide), jnp.bfloat16),
        scratch=[
            pltpu.VMEM((sets, count, width), row_sets[0].dtype),
            pltpu.VMEM((sets * span, width), maps.dtype),
            pltpu.SemaphoreType.DMA((sets,)),
            pltpu.SemaphoreType.DMA((index.shape[0],)),
        ],
        name="low_rank",
    )


def expand(low, slot_sets, maps, index, after=()):
    sets = len(slot_sets)
    rank, width = maps.shape[1:]
    tall = low.shape[0]
    half = low.size // sets // (2 * rank)
    count = 2 * half
    span = index.shape[0] // sets * rank
    repeats = count // slot_sets[0].shape[0]

    outs = [(0, 0, count)] + [
        (s, p * count // PARTS, count // PARTS) for s in range(1, sets) for p in range(PARTS)
    ]

    def kernel(index_ref, low_ref, *refs):
        slot_refs, maps_ref, out_refs = refs[:sets], refs[sets], refs[sets + 1 : sets + 1 + len(outs)]
        stage, maps_buf, map_sems, out_sems = refs[sets + 1 + len(outs) :]
        map_copies = block_copies(index_ref, maps_ref, maps_buf, map_sems, sets, rank)
        writes = [
            pltpu.make_async_copy(stage.at[s, pl.ds(first, some)], out_refs[o], out_sems.at[o])
            for o, (s, first, some) in enumerate(outs)
        ]
        order = list(range(1, sets)) + [0]
        for s in order:
            for copy in map_copies[s]:
                copy.start()
        for s in order:
            lanes = [(s * half // tall + b) * 2 * rank for b in range(half // tall)]
            mine = jnp.concatenate(
                [low_ref[:, at + side : at + side + rank] for side in (0, rank) for at in lanes], axis=0
            )
            tiled = jnp.concatenate([mine] * (span // rank), axis=1)
            pick = lane_pick(slot_refs[s], repeats, (count, span), rank, 0)
            picked = jnp.where(pick, tiled, jnp.zeros_like(tiled))
            for copy in map_copies[s]:
                copy.wait()
            for at in range(0, width, CHUNK):
                value = jnp.dot(
                    picked, maps_buf[s * span : (s + 1) * span, at : at + CHUNK], preferred_element_type=jnp.float32
                )
                stage[s, :, at : at + CHUNK] = value.astype(stage.dtype)
            for o, (which, _, _) in enumerate(outs):
                if which == s:
                    writes[o].start()
        for write in writes:
            write.wait()

    return call(
        kernel, [index, low, *slot_sets, maps], after, prefetch=1,
        in_specs=[pl.BlockSpec(memory_space=pltpu.VMEM)] * (1 + sets) + [ANY],
        out_specs=[ANY] * len(outs),
        out_shape=[jax.ShapeDtypeStruct((some, width), jnp.bfloat16) for _, _, some in outs],
        scratch=[
            pltpu.VMEM((sets, count, width), jnp.bfloat16),
            pltpu.VMEM((sets * span, width), maps.dtype),
            pltpu.SemaphoreType.DMA((index.shape[0],)),
            pltpu.SemaphoreType.DMA((len(outs),)),
        ],
        name="expand",
    )


def line_plan(nz):
    order = np.zeros((nz, nz), np.int32)
    for z in range(nz):
        def need(j):
            if j == z:
                return (2 * nz, 0)
            return (nz - 1 - j + z, j) if j > z else (nz - 1 - z + j, nz - j)

        order[z] = sorted(range(nz), key=need)
    return order


def on_device(attention_result, tenant, projection_weight, adapter_down_maps, adapter_up_maps):
    steps, row_count, width = attention_result.shape
    local_adapters = adapter_down_maps.shape[0]
    owners = lax.axis_size("dp")
    me = lax.axis_index("dp")
    n = lax.axis_size("tensor")
    nz = n // 2
    place = lax.axis_index("tensor")
    order = line_plan(nz)
    out_width = projection_weight.shape[1] // n

    def swap_y(value):
        return lax.ppermute(value, "tensor", [(t, t ^ 1) for t in range(n)])

    def hop(value, h):
        pairs = []
        for side in range(2):
            pairs.append((h * 2 + side, (h + 1) * 2 + side))
            pairs.append(((nz - 1 - h) * 2 + side, (nz - 2 - h) * 2 + side))
        return lax.ppermute(value, "tensor", pairs)

    def slot_of(h, m):
        return list(order[h]).index(nz - 1 - m)

    def pass_on(value, shift):
        return lax.ppermute(value, "dp", [(i, (i + shift) % owners) for i in range(owners)])

    rows = attention_result.reshape(steps * row_count, width)
    count = steps * row_count
    last = [()]

    def then(kernel, *operands, **options):
        out = kernel(*operands, after=last[0], **options)
        last[0] = (out[0] if isinstance(out, (tuple, list)) else out,)
        return out

    slot_range = jnp.arange(SLOTS, dtype=jnp.int32)
    ids = jnp.arange(local_adapters, dtype=jnp.int32)

    def slots(row_ids, owner):
        hit = row_ids[:, None] - owner * local_adapters == ids[None, :]
        used = jnp.any(hit, axis=0)
        position = jnp.sum(
            (used[None, :] & (ids[None, :] < ids[:, None])).astype(jnp.int32), axis=1
        )
        names = jnp.sum(
            jnp.where(used[None, :] & (position[None, :] == slot_range[:, None]), ids[None, :], 0),
            axis=1,
        )
        row_slot = jnp.sum(jnp.where(hit, position[None, :] + 1, 0), axis=1) - 1
        return names, row_slot[:, None]

    blocks = [[(order[t // 2][k] * 2 + side) for side in (1 - t % 2, t % 2) for k in range(nz)] for t in range(n)]
    starts = jnp.asarray(np.asarray(blocks, np.int32) * out_width)[place]
    low_rows = 2 * (owners * count // 2) * adapter_down_maps.shape[1] // out_width
    even = [(p * count // PARTS, count // PARTS) for p in range(PARTS)]
    away_all, own_all, from_y, sums, arrived = {}, {}, {}, {}, {}

    def add_up(span, terms, extra=(), dtype=jnp.bfloat16, into=None):
        low_row, high_row = span[0], span[0] + span[1]
        cuts = {low_row, high_row}
        for term in terms:
            for at, some, _, _ in term:
                cuts.update(row for row in (at, at + some) if low_row < row < high_row)
        cuts = sorted(cuts)
        runs = []
        for begin, end in zip(cuts, cuts[1:]):
            here = [
                (array, row + begin - at) for term in terms for at, some, array, row in term if at <= begin < at + some
            ]
            runs.append((end - begin, here))
        return then(total, runs + list(extra), dtype, into)

    def whole(array):
        return [(0, count, array, 0)]

    def multiply(outs, tail=None, chunk=1024):
        names = sorted({segment[0] for out in outs for segment in out if segment}, key=str)
        outs = [[segment and (names.index(segment[0]), *segment[1:]) for segment in out] for out in outs]
        columns = [k + (nz if kind == "own" else 0) for kind, k in names]
        return then(products, rows, projection_weight, starts, columns, out_width, outs, tail, chunk)

    def all_of(kind, k):
        return [((kind, k), 0, count)]

    def start_y(k):
        from_y[k] = swap_y(hold(away_all[k], last[0]) if k else away_all[k])

    def y_parts(k):
        return whole(from_y[k])

    def sum_parts(k):
        return [(*cut, sums[k, p], 0) for p, cut in enumerate(cut_of(0, k)) if (k, p) in sums]

    def cut_of(h, m):
        return even if m <= 1 and h <= 1 else [(0, count)]

    def arrived_parts(h, m):
        return [(*cut, arrived[h, m, p], 0) for p, cut in enumerate(cut_of(h, m)) if (h, m, p) in arrived]

    def line(h, m, p):
        k = slot_of(h, m)
        span = cut_of(h, m)[p]
        if h == 0:
            value = sums[k, p] = add_up(span, [whole(own_all[k]), y_parts(k)])
        else:
            value = add_up(span, [sum_parts(k), arrived_parts(h - 1, m)])
        arrived[h, m, p] = hop(value, h)

    def line_order():
        ready, free = {}, {}
        steps = [(h, m, p) for h in range(nz - 1) for m in range(nz - 1 - h) for p in range(len(cut_of(h, m)))]
        for h, m, p in sorted(steps, key=lambda step: (step[0], step[1], step[2])):
            k = slot_of(h, m)
            there = (k + 1.0) * count
            if h:
                above = range(len(cut_of(h - 1, m)))
                there = max(there, max(ready[h - 1, m, q, "end"] for q in above if q == p or len(above) != len(cut_of(h, m))))
            ready[h, m, p] = there
            free[h] = max(there, free.get(h, 0.0)) + cut_of(h, m)[p][1]
            ready[h, m, p, "end"] = free[h]
        return sorted(steps, key=lambda step: (ready[step], step[0] and nz - step[0]))

    row_ids = [tenant] + [pass_on(tenant, shift) for shift in range(1, owners)]
    row_sets = [rows] + [pass_on(rows, shift) for shift in range(1, owners)]
    away_all[0] = multiply([all_of("away", 0)], chunk=512)[0]
    start_y(0)
    named = [slots(some_ids, me) for some_ids in row_ids]
    names = jnp.concatenate([which for which, _ in named])
    slot_sets = [row_slot for _, row_slot in named]
    low = then(low_rank, row_sets, slot_sets, adapter_down_maps, names, out_width)
    bits = [1 << i for i in range(1, 16) if 1 << i < n] + [1]

    def send_low():
        bit = bits.pop(0)
        return lax.ppermute(low, "tensor", [(t, t ^ bit) for t in range(n)])

    def add_low(other):
        return then(total, [(low_rows, [(low, 0), (other, 0)])])

    k = 0
    while len(bits) > 1:
        other = send_low()
        if k < 2:
            own_all[k] = multiply([all_of("own", k)])[0]
            k += 1
        low = add_low(other)
    other = send_low()
    away_all[1], *rest = multiply([all_of("away", 1)] + [all_of("own", j) for j in range(k, 2)])
    own_all.update(zip(range(k, 2), rest))
    if nz > 2:
        away_all[2], own_all[2] = multiply([all_of("away", 2), all_of("own", 2)])
    low = add_low(other)
    start_y(1)
    for h, m, p in line_order():
        k = slot_of(h, m)
        if (h, m, p) == (1, 1, 1):
            last[0] += (arrived[1, 1, 0],)
        line(h, m, p)
        if h == 0 and p == len(cut_of(h, m)) - 1 and k + 2 < nz:
            start_y(k + 2)
        if (h, k, p) == (0, 0, len(cut_of(h, m)) - 1):
            for j in range(3, nz):
                away_all[j], own_all[j] = multiply([all_of("away", j), all_of("own", j)])
            deltas = then(expand, low, slot_sets, adapter_up_maps, names)
            back = [
                [(*cut, pass_on(deltas[1 + (shift - 1) * PARTS + p], -shift), 0) for p, cut in enumerate(even)]
                for shift in range(1, owners)
            ]
        if (h, m, p) == (1, 0, 0) or nz == 2:
            head = add_up((0, count), [whole(own_all[nz - 1]), whole(deltas[0])] + back, dtype=jnp.float32)
    span = (0, count)
    early = [arrived_parts(h, nz - 2 - h) for h in range(1, nz - 2)]
    late = [arrived_parts(h, nz - 2 - h) for h in range(nz - 1) if not 1 <= h < nz - 2]
    most = add_up(span, [whole(head), y_parts(nz - 1)] + early, dtype=jnp.float32)
    out = add_up(span, [whole(most)] + late)
    return out.reshape(steps, row_count, out_width)


def solution(mesh):
    placed = (
        P(None, ("groups", "dp"), "tensor"),
        P(("groups", "dp")),
        P("tensor", None),
        P(("groups", "dp"), None, "tensor"),
        P(("groups", "dp"), None, "tensor"),
    )
    return jax.shard_map(
        on_device,
        mesh=mesh,
        in_specs=placed,
        out_specs=P(None, ("groups", "dp"), "tensor"),
        check_vma=False,
    )
```

```python
import jax
import jax.numpy as jnp
import numpy as np
from jax import lax
from jax.experimental import pallas as pl
from jax.experimental.pallas import tpu as pltpu
from jax.sharding import PartitionSpec as P

SLOTS = 16
LANES = 128
CHUNK = 512
PARTS = 2
LOW_WITH = (0, PARTS - 1)
HEAD_AFTER = (2, 0)
VMEM = 50 * 2**20
ANY = pl.BlockSpec(memory_space=pl.ANY)


def call(kernel, operands, after, *, in_specs, out_specs, out_shape, name, prefetch=0, scratch=(), alias=None):
    inputs, extra = len(operands), len(after)

    def body(*refs):
        kernel(*refs[:inputs], *refs[inputs + extra :])

    return pl.pallas_call(
        body,
        grid_spec=pltpu.PrefetchScalarGridSpec(
            num_scalar_prefetch=prefetch,
            grid=(),
            in_specs=list(in_specs) + [ANY] * extra,
            out_specs=out_specs,
            scratch_shapes=list(scratch),
        ),
        out_shape=out_shape,
        input_output_aliases=alias or {},
        compiler_params=pltpu.CompilerParams(vmem_limit_bytes=VMEM),
        cost_estimate=pl.CostEstimate(flops=1, transcendentals=0, bytes_accessed=1),
        name=name,
    )(*operands, *after)


def hold(value, after):
    def kernel(value_ref, out_ref):
        pass

    return call(
        kernel, [value], after, in_specs=[ANY], out_specs=ANY,
        out_shape=jax.ShapeDtypeStruct(value.shape, value.dtype), name="hold", alias={0: 0},
    )


def products(rows, weight, starts, names, size, outs, tail=None, chunk=1024, after=()):
    count, width = rows.shape
    blocks = len(names)
    chunks = [(at, min(chunk, size - at)) for at in range(0, size, chunk)]
    low = min(first for _, first, _ in outs)
    high = max(first + some for _, first, some in outs)
    upper = (high - low) // 32 * 16
    row_parts = [(0, upper), (upper, high - low - upper)]
    tails = [] if tail is None else [tail]
    heights = [some for _, _, some in outs]
    for array in tails:
        heights[-1] += array.shape[0]

    def kernel(starts_ref, rows_ref, weight_ref, *refs):
        tail_refs, refs = refs[: len(tails)], refs[len(tails) :]
        out_refs, (x, w, *refs) = refs[: len(outs)], refs[len(outs) :]
        stage, (x_sems, w_sems, out_sems, tail_sems) = refs[: len(outs)], refs[len(outs) :]
        x_copies = [
            pltpu.make_async_copy(
                rows_ref.at[pl.ds(low + at, some)], x.at[pl.ds(at, some)], x_sems.at[i]
            )
            for i, (at, some) in enumerate(row_parts)
        ]
        w_copies = [
            [
                pltpu.make_async_copy(
                    weight_ref.at[:, pl.ds(pl.multiple_of(starts_ref[names[b]] + at, LANES), extent)],
                    w.at[b, :, pl.ds(at, extent)],
                    w_sems.at[b, c],
                )
                for c, (at, extent) in enumerate(chunks)
            ]
            for b in range(blocks)
        ]
        x_copies[0].start()
        w_copies[0][0].start()
        x_copies[1].start()
        for b in range(blocks):
            for c in range(len(chunks)):
                if b or c:
                    w_copies[b][c].start()
        stores = []
        for ref in tail_refs:
            below = pl.ds(outs[-1][2], ref.shape[0])
            read = pltpu.make_async_copy(ref, stage[-1].at[below], tail_sems.at[0])
            read.start()
            read.wait()
            stores.append(pltpu.make_async_copy(stage[-1].at[below], out_refs[-1].at[below], tail_sems.at[1]))
            stores[-1].start()
        for copy in x_copies:
            copy.wait()
        for b in range(blocks):
            for c, (at, extent) in enumerate(chunks):
                w_copies[b][c].wait()
                for o, (index, first, some) in enumerate(outs):
                    if index == b:
                        value = jnp.dot(
                            x[first - low : first - low + some, :], w[b, :, at : at + extent],
                            preferred_element_type=jnp.float32,
                        )
                        stage[o][:some, at : at + extent] = value.astype(rows.dtype)
                        store = pltpu.make_async_copy(
                            stage[o].at[pl.ds(0, some), pl.ds(at, extent)],
                            out_refs[o].at[pl.ds(0, some), pl.ds(at, extent)],
                            out_sems.at[o, c],
                        )
                        store.start()
                        stores.append(store)
        for store in stores:
            store.wait()

    shapes = [(height, size) for height in heights]
    return call(
        kernel, [starts, rows, weight] + tails, after, prefetch=1,
        in_specs=[ANY] * (2 + len(tails)),
        out_specs=[ANY] * len(outs),
        out_shape=[jax.ShapeDtypeStruct(shape, rows.dtype) for shape in shapes],
        scratch=[pltpu.VMEM((high - low, width), rows.dtype), pltpu.VMEM((blocks, width, size), rows.dtype)]
        + [pltpu.VMEM(shape, rows.dtype) for shape in shapes]
        + [
            pltpu.SemaphoreType.DMA((2,)),
            pltpu.SemaphoreType.DMA((blocks, len(chunks))),
            pltpu.SemaphoreType.DMA((len(outs), len(chunks))),
            pltpu.SemaphoreType.DMA((2,)),
        ],
        name="products",
    )


def total(runs, dtype=jnp.bfloat16, into=None, after=()):
    width = runs[0][1][0][0].shape[1]
    height = sum(some for some, _ in runs)
    rows_in_all, first, so_far = into or (height, 0, None)
    tiles = []
    at = 0
    for r, (some, terms) in enumerate(runs):
        size = -(-some // 32) * 16 if some * width > 2**17 else some
        for skip in range(0, some, size):
            tiles.append((r, skip, min(size, some - skip), at + skip))
        at += some
    operands = [term for _, terms in runs for term, _ in terms]
    before = [] if so_far is None else [so_far]
    most_terms = max(len(terms) for _, terms in runs)
    of_run = np.cumsum([0] + [len(terms) for _, terms in runs])

    def kernel(*refs):
        term_refs, out_ref = refs[: len(operands)], refs[len(operands) + len(before)]
        refs = refs[len(operands) + len(before) + 1 :]
        bufs, (stage, in_sems, out_sems) = refs[: len(operands)], refs[len(operands) :]
        reads, writes = [], []
        for n, (r, skip, size, place) in enumerate(tiles):
            reads.append(
                [
                    pltpu.make_async_copy(
                        term_refs[of_run[r] + t].at[pl.ds(start + skip, size)],
                        bufs[of_run[r] + t].at[pl.ds(skip, size)],
                        in_sems.at[t, n],
                    )
                    for t, (_, start) in enumerate(runs[r][1])
                ]
            )
            writes.append(
                pltpu.make_async_copy(
                    stage.at[pl.ds(place, size)], out_ref.at[pl.ds(first + place, size)], out_sems.at[n]
                )
            )
        for some in reads:
            for read in some:
                read.start()
        for n, (r, skip, size, place) in enumerate(tiles):
            for read in reads[n]:
                read.wait()
            value = None
            for t in range(len(runs[r][1])):
                part = bufs[of_run[r] + t][skip : skip + size, :].astype(jnp.float32)
                value = part if value is None else value + part
            stage[place : place + size, :] = value.astype(dtype)
            writes[n].start()
        for write in writes:
            write.wait()

    return call(
        kernel, operands + before, after,
        in_specs=[ANY] * (len(operands) + len(before)),
        out_specs=ANY,
        out_shape=jax.ShapeDtypeStruct((rows_in_all, width), dtype),
        scratch=[pltpu.VMEM((some, width), term.dtype) for some, terms in runs for term, _ in terms]
        + [
            pltpu.VMEM((height, width), dtype),
            pltpu.SemaphoreType.DMA((most_terms, len(tiles))),
            pltpu.SemaphoreType.DMA((len(tiles),)),
        ],
        alias={len(operands): 0} if before else None,
        name="total",
    )


def lane_pick(slot_ref, repeats, shape, rank, first):
    slot = jnp.concatenate([slot_ref[...]] * repeats, axis=0)
    return slot == lax.broadcasted_iota(jnp.int32, shape, 1) // rank + first


def block_copies(index_ref, maps_ref, buf, sems, sets, rank):
    each = index_ref.shape[0] // sets
    return [
        [
            pltpu.make_async_copy(
                maps_ref.at[index_ref[s * each + i]], buf.at[pl.ds((s * each + i) * rank, rank)],
                sems.at[s * each + i],
            )
            for i in range(each)
        ]
        for s in range(sets)
    ]


def low_rank(row_sets, slot_sets, maps, index, wide, after=()):
    sets = len(row_sets)
    count, width = row_sets[0].shape
    rank = maps.shape[1]
    span = index.shape[0] // sets * rank
    repeats = count // slot_sets[0].shape[0]
    half = count // 2
    group = 256
    tall = sets * half * 2 * rank // wide

    def kernel(index_ref, *refs):
        row_refs, slot_refs, maps_ref, out_ref = refs[:sets], refs[sets : 2 * sets], refs[2 * sets], refs[2 * sets + 1]
        rows_buf, maps_buf, row_sems, map_sems = refs[2 * sets + 2 :]
        row_copies = [
            pltpu.make_async_copy(row_refs[s], rows_buf.at[s], row_sems.at[s]) for s in range(sets)
        ]
        map_copies = block_copies(index_ref, maps_ref, maps_buf, map_sems, sets, rank)
        for s in range(sets):
            row_copies[s].start()
            for copy in map_copies[s]:
                copy.start()
        for s in range(sets):
            row_copies[s].wait()
            for copy in map_copies[s]:
                copy.wait()
            acc = None
            for at in range(0, span, group):
                scores = lax.dot_general(
                    rows_buf[s], maps_buf[s * span + at : s * span + at + group],
                    (((1,), (1,)), ((), ())), preferred_element_type=jnp.float32,
                )
                pick = lane_pick(slot_refs[s], repeats, (count, group), rank, at // rank)
                term = jnp.where(pick, scores, 0.0)
                acc = term if acc is None else acc + term
            summed = acc[:, 0:rank]
            for g in range(1, group // rank):
                summed += acc[:, g * rank : (g + 1) * rank]
            summed = summed.astype(out_ref.dtype)
            for b in range(half // tall):
                lanes = slice((s * half // tall + b) * 2 * rank, (s * half // tall + b + 1) * 2 * rank)
                both = [summed[start + b * tall : start + (b + 1) * tall] for start in (0, half)]
                out_ref[:, lanes] = jnp.concatenate(both, axis=1)

    return call(
        kernel, [index, *row_sets, *slot_sets, maps], after, prefetch=1,
        in_specs=[ANY] * sets + [pl.BlockSpec(memory_space=pltpu.VMEM)] * sets + [ANY],
        out_specs=pl.BlockSpec(memory_space=pltpu.VMEM),
        out_shape=jax.ShapeDtypeStruct((tall, wide), jnp.bfloat16),
        scratch=[
            pltpu.VMEM((sets, count, width), row_sets[0].dtype),
            pltpu.VMEM((sets * span, width), maps.dtype),
            pltpu.SemaphoreType.DMA((sets,)),
            pltpu.SemaphoreType.DMA((index.shape[0],)),
        ],
        name="low_rank",
    )


def expand(low, slot_sets, maps, index, after=()):
    sets = len(slot_sets)
    rank, width = maps.shape[1:]
    tall = low.shape[0]
    half = low.size // sets // (2 * rank)
    count = 2 * half
    span = index.shape[0] // sets * rank
    repeats = count // slot_sets[0].shape[0]

    outs = [(0, 0, count)] + [
        (s, p * count // PARTS, count // PARTS) for s in range(1, sets) for p in range(PARTS)
    ]

    def kernel(index_ref, low_ref, *refs):
        slot_refs, maps_ref, out_refs = refs[:sets], refs[sets], refs[sets + 1 : sets + 1 + len(outs)]
        stage, maps_buf, map_sems, out_sems = refs[sets + 1 + len(outs) :]
        map_copies = block_copies(index_ref, maps_ref, maps_buf, map_sems, sets, rank)
        writes = [
            pltpu.make_async_copy(stage.at[s, pl.ds(first, some)], out_refs[o], out_sems.at[o])
            for o, (s, first, some) in enumerate(outs)
        ]
        order = list(range(1, sets)) + [0]
        for s in order:
            for copy in map_copies[s]:
                copy.start()
        for s in order:
            lanes = [(s * half // tall + b) * 2 * rank for b in range(half // tall)]
            mine = jnp.concatenate(
                [low_ref[:, at + side : at + side + rank] for side in (0, rank) for at in lanes], axis=0
            )
            tiled = jnp.concatenate([mine] * (span // rank), axis=1)
            pick = lane_pick(slot_refs[s], repeats, (count, span), rank, 0)
            picked = jnp.where(pick, tiled, jnp.zeros_like(tiled))
            for copy in map_copies[s]:
                copy.wait()
            for at in range(0, width, CHUNK):
                value = jnp.dot(
                    picked, maps_buf[s * span : (s + 1) * span, at : at + CHUNK], preferred_element_type=jnp.float32
                )
                stage[s, :, at : at + CHUNK] = value.astype(stage.dtype)
            for o, (which, _, _) in enumerate(outs):
                if which == s:
                    writes[o].start()
        for write in writes:
            write.wait()

    return call(
        kernel, [index, low, *slot_sets, maps], after, prefetch=1,
        in_specs=[pl.BlockSpec(memory_space=pltpu.VMEM)] * (1 + sets) + [ANY],
        out_specs=[ANY] * len(outs),
        out_shape=[jax.ShapeDtypeStruct((some, width), jnp.bfloat16) for _, _, some in outs],
        scratch=[
            pltpu.VMEM((sets, count, width), jnp.bfloat16),
            pltpu.VMEM((sets * span, width), maps.dtype),
            pltpu.SemaphoreType.DMA((index.shape[0],)),
            pltpu.SemaphoreType.DMA((len(outs),)),
        ],
        name="expand",
    )


def line_plan(nz):
    order = np.zeros((nz, nz), np.int32)
    for z in range(nz):
        def need(j):
            if j == z:
                return (2 * nz, 0)
            return (nz - 1 - j + z, j) if j > z else (nz - 1 - z + j, nz - j)

        order[z] = sorted(range(nz), key=need)
    return order


def on_device(attention_result, tenant, projection_weight, adapter_down_maps, adapter_up_maps):
    steps, row_count, width = attention_result.shape
    local_adapters = adapter_down_maps.shape[0]
    owners = lax.axis_size("dp")
    me = lax.axis_index("dp")
    n = lax.axis_size("tensor")
    nz = n // 2
    place = lax.axis_index("tensor")
    order = line_plan(nz)
    out_width = projection_weight.shape[1] // n

    def swap_y(value):
        return lax.ppermute(value, "tensor", [(t, t ^ 1) for t in range(n)])

    def hop(value, h):
        pairs = []
        for side in range(2):
            pairs.append((h * 2 + side, (h + 1) * 2 + side))
            pairs.append(((nz - 1 - h) * 2 + side, (nz - 2 - h) * 2 + side))
        return lax.ppermute(value, "tensor", pairs)

    def slot_of(h, m):
        return list(order[h]).index(nz - 1 - m)

    def pass_on(value, shift):
        return lax.ppermute(value, "dp", [(i, (i + shift) % owners) for i in range(owners)])

    rows = attention_result.reshape(steps * row_count, width)
    count = steps * row_count
    last = [()]

    def then(kernel, *operands, **options):
        out = kernel(*operands, after=last[0], **options)
        last[0] = (out[0] if isinstance(out, (tuple, list)) else out,)
        return out

    slot_range = jnp.arange(SLOTS, dtype=jnp.int32)
    ids = jnp.arange(local_adapters, dtype=jnp.int32)

    def slots(row_ids, owner):
        hit = row_ids[:, None] - owner * local_adapters == ids[None, :]
        used = jnp.any(hit, axis=0)
        position = jnp.sum(
            (used[None, :] & (ids[None, :] < ids[:, None])).astype(jnp.int32), axis=1
        )
        names = jnp.sum(
            jnp.where(used[None, :] & (position[None, :] == slot_range[:, None]), ids[None, :], 0),
            axis=1,
        )
        row_slot = jnp.sum(jnp.where(hit, position[None, :] + 1, 0), axis=1) - 1
        return names, row_slot[:, None]

    blocks = [[(order[t // 2][k] * 2 + side) for side in (1 - t % 2, t % 2) for k in range(nz)] for t in range(n)]
    starts = jnp.asarray(np.asarray(blocks, np.int32) * out_width)[place]
    low_rows = 2 * (owners * count // 2) * adapter_down_maps.shape[1] // out_width
    even = [(p * count // PARTS, count // PARTS) for p in range(PARTS)]
    uneven = [(0, count // 2 + low_rows), (count // 2 + low_rows, count // 2 - low_rows)]
    away_part, own_all, from_y, sums, arrived = {}, {}, {}, {}, {}

    def split(k):
        return uneven if k == 0 else [(0, count)]

    def add_up(span, terms, extra=(), dtype=jnp.bfloat16, into=None):
        low_row, high_row = span[0], span[0] + span[1]
        cuts = {low_row, high_row}
        for term in terms:
            for at, some, _, _ in term:
                cuts.update(row for row in (at, at + some) if low_row < row < high_row)
        cuts = sorted(cuts)
        runs = []
        for begin, end in zip(cuts, cuts[1:]):
            here = [
                (array, row + begin - at) for term in terms for at, some, array, row in term if at <= begin < at + some
            ]
            runs.append((end - begin, here))
        return then(total, runs + list(extra), dtype, into)

    def whole(array):
        return [(0, count, array, 0)]

    def multiply(aways, owns, tail=None, chunk=1024):
        ks = sorted({k for k, _ in aways})
        names = ks + [nz + k for k in owns]
        outs = [(ks.index(k), *split(k)[p]) for k, p in aways]
        outs += [(len(ks) + i, 0, count) for i in range(len(owns))]
        done = then(products, rows, projection_weight, starts, names, out_width, outs, tail, chunk)
        away_part.update(zip(aways, done))
        own_all.update(zip(owns, done[len(aways) :]))

    def start_y(k, p, after=None):
        value = away_part[k, p]
        from_y[k, p] = swap_y(value if after is None else hold(value, after))

    def y_parts(k):
        return [(*cut, from_y[k, p], 0) for p, cut in enumerate(split(k)) if (k, p) in from_y]

    def sum_parts(k):
        return [(*cut, sums[k, p], 0) for p, cut in enumerate(cut_of(0, k)) if (k, p) in sums]

    def cut_of(h, m):
        if m == 0 and h <= 1:
            return uneven
        return even if m == 1 else [(0, count)]

    def arrived_parts(h, m):
        return [(*cut, arrived[h, m, p], 0) for p, cut in enumerate(cut_of(h, m)) if (h, m, p) in arrived]

    def line(h, m, p):
        k = slot_of(h, m)
        span = cut_of(h, m)[p]
        low_too = m == 0 and h <= 1 and p == LOW_WITH[1]
        if h == 0:
            extra = [(low_rows, [(low, 0), (from_y[k, p], span[1])])] if low_too else []
            value = sums[k, p] = add_up(span, [whole(own_all[k]), y_parts(k)], extra)
        else:
            extra = [(low_rows, [(sums[k, p], span[1]), (arrived[h - 1, m, p], span[1])])] if low_too else []
            value = add_up(span, [sum_parts(k), arrived_parts(h - 1, m)], extra)
        arrived[h, m, p] = hop(value, h)

    def line_order():
        ready, free = {}, {}
        steps = [(h, m, p) for h in range(nz - 1) for m in range(nz - 1 - h) for p in range(len(cut_of(h, m)))]
        for h, m, p in sorted(steps, key=lambda step: (step[0], step[1], step[2])):
            k = slot_of(h, m)
            there = (k + 1.0) * count if k or p else 1.0 * cut_of(0, 0)[0][1]
            if h:
                above = range(len(cut_of(h - 1, m)))
                there = max(there, max(ready[h - 1, m, q, "end"] for q in above if q == p or len(above) != len(cut_of(h, m))))
            ready[h, m, p] = there
            free[h] = max(there, free.get(h, 0.0)) + cut_of(h, m)[p][1]
            ready[h, m, p, "end"] = free[h]
        return sorted(steps, key=lambda step: (ready[step], step[0]))

    row_ids = [tenant] + [pass_on(tenant, shift) for shift in range(1, owners)]
    row_sets = [rows] + [pass_on(rows, shift) for shift in range(1, owners)]
    multiply([(0, 0)], [], chunk=512)
    start_y(0, 0)
    named = [slots(some_ids, me) for some_ids in row_ids]
    names = jnp.concatenate([which for which, _ in named])
    slot_sets = [row_slot for _, row_slot in named]
    low = then(low_rank, row_sets, slot_sets, adapter_down_maps, names, out_width)
    multiply([LOW_WITH], [], low, chunk=512)
    start_y(*LOW_WITH)
    multiply([(1, 0)], [0])
    start_y(1, 0)
    for h, m, p in line_order():
        k = slot_of(h, m)
        if (h, m, p) == (1, 1, 1):
            last[0] += (arrived[1, 1, 0],)
        line(h, m, p)
        if h == 0:
            if k == 0 and p == 0:
                multiply([(2, 0)] if nz > 2 else [], [1])
            elif k == 0:
                if nz > 2:
                    start_y(2, 0, last[0])
                multiply([(j, 0) for j in range(3, nz)], range(2, nz))
            elif p == len(cut_of(h, m)) - 1 and 1 < k < nz - 1:
                start_y(k + 1, 0, last[0])
        if (h, k, p) == (0, 1, len(cut_of(h, m)) - 1):
            low_at = uneven[LOW_WITH[1]][1]
            pieces = [(sums[LOW_WITH], low_at)]
            for step in range(nz - 1):
                if step >= 2:
                    prefix = then(total, [(low_rows, [pieces[0], pieces[-1]])])
                    pieces.append((hop(prefix, step), 0))
                else:
                    pieces.append((arrived[step, 0, LOW_WITH[1]], low_at))
        if (h, m, p) == (1, 1, 0):
            low_sum = then(total, [(low_rows, pieces)])
            deltas = then(expand, low_sum, slot_sets, adapter_up_maps, names)
            back = [
                [(*cut, pass_on(deltas[1 + (shift - 1) * PARTS + p], -shift), 0) for p, cut in enumerate(even)]
                for shift in range(1, owners)
            ]
        if (h, m) == (HEAD_AFTER if nz > 2 else (0, 0)) and p == len(cut_of(h, m)) - 1:
            head = add_up((0, count), [whole(own_all[nz - 1]), whole(deltas[0])] + back, dtype=jnp.float32)
    span = (0, count)
    early = [arrived_parts(h, nz - 2 - h) for h in range(1, nz - 2)]
    late = [arrived_parts(h, nz - 2 - h) for h in range(nz - 1) if not 1 <= h < nz - 2]
    most = add_up(span, [whole(head), y_parts(nz - 1)] + early, dtype=jnp.float32)
    out = add_up(span, [whole(most)] + late)
    return out.reshape(steps, row_count, out_width)


def solution(mesh):
    placed = (
        P(None, ("groups", "dp"), "tensor"),
        P(("groups", "dp")),
        P("tensor", None),
        P(("groups", "dp"), None, "tensor"),
        P(("groups", "dp"), None, "tensor"),
    )
    return jax.shard_map(
        on_device,
        mesh=mesh,
        in_specs=placed,
        out_specs=P(None, ("groups", "dp"), "tensor"),
        check_vma=False,
    )
```

```python
import jax
import jax.numpy as jnp
import numpy as np
from jax import lax
from jax.experimental import pallas as pl
from jax.experimental.pallas import tpu as pltpu
from jax.sharding import PartitionSpec as P

SLOTS = 16
LANES = 128
CHUNK = 512
PARTS = 2
LOW_WITH = (0, PARTS - 1)
LOW_SUM_AFTER = (0, 2, 0)
EXPAND_AFTER = (2, 0, 0)
VMEM = 50 * 2**20
ANY = pl.BlockSpec(memory_space=pl.ANY)


def call(kernel, operands, after, *, in_specs, out_specs, out_shape, name, prefetch=0, scratch=(), alias=None):
    inputs, extra = len(operands), len(after)

    def body(*refs):
        kernel(*refs[:inputs], *refs[inputs + extra :])

    return pl.pallas_call(
        body,
        grid_spec=pltpu.PrefetchScalarGridSpec(
            num_scalar_prefetch=prefetch,
            grid=(),
            in_specs=list(in_specs) + [ANY] * extra,
            out_specs=out_specs,
            scratch_shapes=list(scratch),
        ),
        out_shape=out_shape,
        input_output_aliases=alias or {},
        compiler_params=pltpu.CompilerParams(vmem_limit_bytes=VMEM),
        cost_estimate=pl.CostEstimate(flops=1, transcendentals=0, bytes_accessed=1),
        name=name,
    )(*operands, *after)


def hold(value, after):
    def kernel(value_ref, out_ref):
        pass

    return call(
        kernel, [value], after, in_specs=[ANY], out_specs=ANY,
        out_shape=jax.ShapeDtypeStruct(value.shape, value.dtype), name="hold", alias={0: 0},
    )


def products(rows, weight, starts, names, size, outs, tail=None, chunk=1024, after=()):
    count, width = rows.shape
    blocks = len(names)
    chunks = [(at, min(chunk, size - at)) for at in range(0, size, chunk)]
    low = min(first for _, first, _ in outs)
    high = max(first + some for _, first, some in outs)
    upper = (high - low) // 32 * 16
    row_parts = [(0, upper), (upper, high - low - upper)]
    tails = [] if tail is None else [tail]
    heights = [some for _, _, some in outs]
    for array in tails:
        heights[-1] += array.shape[0]

    def kernel(starts_ref, rows_ref, weight_ref, *refs):
        tail_refs, refs = refs[: len(tails)], refs[len(tails) :]
        out_refs, (x, w, *refs) = refs[: len(outs)], refs[len(outs) :]
        stage, (x_sems, w_sems, out_sems, tail_sems) = refs[: len(outs)], refs[len(outs) :]
        x_copies = [
            pltpu.make_async_copy(
                rows_ref.at[pl.ds(low + at, some)], x.at[pl.ds(at, some)], x_sems.at[i]
            )
            for i, (at, some) in enumerate(row_parts)
        ]
        w_copies = [
            [
                pltpu.make_async_copy(
                    weight_ref.at[:, pl.ds(pl.multiple_of(starts_ref[names[b]] + at, LANES), extent)],
                    w.at[b, :, pl.ds(at, extent)],
                    w_sems.at[b, c],
                )
                for c, (at, extent) in enumerate(chunks)
            ]
            for b in range(blocks)
        ]
        x_copies[0].start()
        w_copies[0][0].start()
        x_copies[1].start()
        for b in range(blocks):
            for c in range(len(chunks)):
                if b or c:
                    w_copies[b][c].start()
        stores = []
        for ref in tail_refs:
            below = pl.ds(outs[-1][2], ref.shape[0])
            read = pltpu.make_async_copy(ref, stage[-1].at[below], tail_sems.at[0])
            read.start()
            read.wait()
            stores.append(pltpu.make_async_copy(stage[-1].at[below], out_refs[-1].at[below], tail_sems.at[1]))
            stores[-1].start()
        for copy in x_copies:
            copy.wait()
        for b in range(blocks):
            for c, (at, extent) in enumerate(chunks):
                w_copies[b][c].wait()
                for o, (index, first, some) in enumerate(outs):
                    if index == b:
                        value = jnp.dot(
                            x[first - low : first - low + some, :], w[b, :, at : at + extent],
                            preferred_element_type=jnp.float32,
                        )
                        stage[o][:some, at : at + extent] = value.astype(rows.dtype)
                        store = pltpu.make_async_copy(
                            stage[o].at[pl.ds(0, some), pl.ds(at, extent)],
                            out_refs[o].at[pl.ds(0, some), pl.ds(at, extent)],
                            out_sems.at[o, c],
                        )
                        store.start()
                        stores.append(store)
        for store in stores:
            store.wait()

    shapes = [(height, size) for height in heights]
    return call(
        kernel, [starts, rows, weight] + tails, after, prefetch=1,
        in_specs=[ANY] * (2 + len(tails)),
        out_specs=[ANY] * len(outs),
        out_shape=[jax.ShapeDtypeStruct(shape, rows.dtype) for shape in shapes],
        scratch=[pltpu.VMEM((high - low, width), rows.dtype), pltpu.VMEM((blocks, width, size), rows.dtype)]
        + [pltpu.VMEM(shape, rows.dtype) for shape in shapes]
        + [
            pltpu.SemaphoreType.DMA((2,)),
            pltpu.SemaphoreType.DMA((blocks, len(chunks))),
            pltpu.SemaphoreType.DMA((len(outs), len(chunks))),
            pltpu.SemaphoreType.DMA((2,)),
        ],
        name="products",
    )


def total(runs, dtype=jnp.bfloat16, into=None, after=()):
    width = runs[0][1][0][0].shape[1]
    height = sum(some for some, _ in runs)
    rows_in_all, first, so_far = into or (height, 0, None)
    tiles = []
    at = 0
    for r, (some, terms) in enumerate(runs):
        size = -(-some // 32) * 16 if some * width > 2**17 else some
        for skip in range(0, some, size):
            tiles.append((r, skip, min(size, some - skip), at + skip))
        at += some
    operands = [term for _, terms in runs for term, _ in terms]
    before = [] if so_far is None else [so_far]
    most_terms = max(len(terms) for _, terms in runs)
    of_run = np.cumsum([0] + [len(terms) for _, terms in runs])

    def kernel(*refs):
        term_refs, out_ref = refs[: len(operands)], refs[len(operands) + len(before)]
        refs = refs[len(operands) + len(before) + 1 :]
        bufs, (stage, in_sems, out_sems) = refs[: len(operands)], refs[len(operands) :]
        reads, writes = [], []
        for n, (r, skip, size, place) in enumerate(tiles):
            reads.append(
                [
                    pltpu.make_async_copy(
                        term_refs[of_run[r] + t].at[pl.ds(start + skip, size)],
                        bufs[of_run[r] + t].at[pl.ds(skip, size)],
                        in_sems.at[t, n],
                    )
                    for t, (_, start) in enumerate(runs[r][1])
                ]
            )
            writes.append(
                pltpu.make_async_copy(
                    stage.at[pl.ds(place, size)], out_ref.at[pl.ds(first + place, size)], out_sems.at[n]
                )
            )
        for some in reads:
            for read in some:
                read.start()
        for n, (r, skip, size, place) in enumerate(tiles):
            for read in reads[n]:
                read.wait()
            value = None
            for t in range(len(runs[r][1])):
                part = bufs[of_run[r] + t][skip : skip + size, :].astype(jnp.float32)
                value = part if value is None else value + part
            stage[place : place + size, :] = value.astype(dtype)
            writes[n].start()
        for write in writes:
            write.wait()

    return call(
        kernel, operands + before, after,
        in_specs=[ANY] * (len(operands) + len(before)),
        out_specs=ANY,
        out_shape=jax.ShapeDtypeStruct((rows_in_all, width), dtype),
        scratch=[pltpu.VMEM((some, width), term.dtype) for some, terms in runs for term, _ in terms]
        + [
            pltpu.VMEM((height, width), dtype),
            pltpu.SemaphoreType.DMA((most_terms, len(tiles))),
            pltpu.SemaphoreType.DMA((len(tiles),)),
        ],
        alias={len(operands): 0} if before else None,
        name="total",
    )


def lane_pick(slot_ref, repeats, shape, rank, first):
    slot = jnp.concatenate([slot_ref[...]] * repeats, axis=0)
    return slot == lax.broadcasted_iota(jnp.int32, shape, 1) // rank + first


def block_copies(index_ref, maps_ref, buf, sems, sets, rank):
    each = index_ref.shape[0] // sets
    return [
        [
            pltpu.make_async_copy(
                maps_ref.at[index_ref[s * each + i]], buf.at[pl.ds((s * each + i) * rank, rank)],
                sems.at[s * each + i],
            )
            for i in range(each)
        ]
        for s in range(sets)
    ]


def low_rank(row_sets, slot_sets, maps, index, wide, after=()):
    sets = len(row_sets)
    count, width = row_sets[0].shape
    rank = maps.shape[1]
    span = index.shape[0] // sets * rank
    repeats = count // slot_sets[0].shape[0]
    half = count // 2
    group = 256
    tall = sets * half * 2 * rank // wide

    def kernel(index_ref, *refs):
        row_refs, slot_refs, maps_ref, out_ref = refs[:sets], refs[sets : 2 * sets], refs[2 * sets], refs[2 * sets + 1]
        rows_buf, maps_buf, row_sems, map_sems = refs[2 * sets + 2 :]
        row_copies = [
            pltpu.make_async_copy(row_refs[s], rows_buf.at[s], row_sems.at[s]) for s in range(sets)
        ]
        map_copies = block_copies(index_ref, maps_ref, maps_buf, map_sems, sets, rank)
        for s in range(sets):
            row_copies[s].start()
            for copy in map_copies[s]:
                copy.start()
        for s in range(sets):
            row_copies[s].wait()
            for copy in map_copies[s]:
                copy.wait()
            acc = None
            for at in range(0, span, group):
                scores = lax.dot_general(
                    rows_buf[s], maps_buf[s * span + at : s * span + at + group],
                    (((1,), (1,)), ((), ())), preferred_element_type=jnp.float32,
                )
                pick = lane_pick(slot_refs[s], repeats, (count, group), rank, at // rank)
                term = jnp.where(pick, scores, 0.0)
                acc = term if acc is None else acc + term
            summed = acc[:, 0:rank]
            for g in range(1, group // rank):
                summed += acc[:, g * rank : (g + 1) * rank]
            summed = summed.astype(out_ref.dtype)
            for b in range(half // tall):
                lanes = slice((s * half // tall + b) * 2 * rank, (s * half // tall + b + 1) * 2 * rank)
                both = [summed[start + b * tall : start + (b + 1) * tall] for start in (0, half)]
                out_ref[:, lanes] = jnp.concatenate(both, axis=1)

    return call(
        kernel, [index, *row_sets, *slot_sets, maps], after, prefetch=1,
        in_specs=[ANY] * sets + [pl.BlockSpec(memory_space=pltpu.VMEM)] * sets + [ANY],
        out_specs=pl.BlockSpec(memory_space=pltpu.VMEM),
        out_shape=jax.ShapeDtypeStruct((tall, wide), jnp.bfloat16),
        scratch=[
            pltpu.VMEM((sets, count, width), row_sets[0].dtype),
            pltpu.VMEM((sets * span, width), maps.dtype),
            pltpu.SemaphoreType.DMA((sets,)),
            pltpu.SemaphoreType.DMA((index.shape[0],)),
        ],
        name="low_rank",
    )


def expand(low, slot_sets, maps, index, after=()):
    sets = len(slot_sets)
    rank, width = maps.shape[1:]
    tall = low.shape[0]
    half = low.size // sets // (2 * rank)
    count = 2 * half
    span = index.shape[0] // sets * rank
    repeats = count // slot_sets[0].shape[0]

    outs = [(0, 0, count)] + [
        (s, p * count // PARTS, count // PARTS) for s in range(1, sets) for p in range(PARTS)
    ]

    def kernel(index_ref, low_ref, *refs):
        slot_refs, maps_ref, out_refs = refs[:sets], refs[sets], refs[sets + 1 : sets + 1 + len(outs)]
        stage, maps_buf, map_sems, out_sems = refs[sets + 1 + len(outs) :]
        map_copies = block_copies(index_ref, maps_ref, maps_buf, map_sems, sets, rank)
        writes = [
            pltpu.make_async_copy(stage.at[s, pl.ds(first, some)], out_refs[o], out_sems.at[o])
            for o, (s, first, some) in enumerate(outs)
        ]
        order = list(range(1, sets)) + [0]
        for s in order:
            for copy in map_copies[s]:
                copy.start()
        for s in order:
            lanes = [(s * half // tall + b) * 2 * rank for b in range(half // tall)]
            mine = jnp.concatenate(
                [low_ref[:, at + side : at + side + rank] for side in (0, rank) for at in lanes], axis=0
            )
            tiled = jnp.concatenate([mine] * (span // rank), axis=1)
            pick = lane_pick(slot_refs[s], repeats, (count, span), rank, 0)
            picked = jnp.where(pick, tiled, jnp.zeros_like(tiled))
            for copy in map_copies[s]:
                copy.wait()
            for at in range(0, width, CHUNK):
                value = jnp.dot(
                    picked, maps_buf[s * span : (s + 1) * span, at : at + CHUNK], preferred_element_type=jnp.float32
                )
                stage[s, :, at : at + CHUNK] = value.astype(stage.dtype)
            for o, (which, _, _) in enumerate(outs):
                if which == s:
                    writes[o].start()
        for write in writes:
            write.wait()

    return call(
        kernel, [index, low, *slot_sets, maps], after, prefetch=1,
        in_specs=[pl.BlockSpec(memory_space=pltpu.VMEM)] * (1 + sets) + [ANY],
        out_specs=[ANY] * len(outs),
        out_shape=[jax.ShapeDtypeStruct((some, width), jnp.bfloat16) for _, _, some in outs],
        scratch=[
            pltpu.VMEM((sets, count, width), jnp.bfloat16),
            pltpu.VMEM((sets * span, width), maps.dtype),
            pltpu.SemaphoreType.DMA((index.shape[0],)),
            pltpu.SemaphoreType.DMA((len(outs),)),
        ],
        name="expand",
    )


def line_plan(nz):
    order = np.zeros((nz, nz), np.int32)
    for z in range(nz):
        def need(j):
            if j == z:
                return (2 * nz, 0)
            return (nz - 1 - j + z, j) if j > z else (nz - 1 - z + j, nz - j)

        order[z] = sorted(range(nz), key=need)
    return order


def on_device(attention_result, tenant, projection_weight, adapter_down_maps, adapter_up_maps):
    steps, row_count, width = attention_result.shape
    local_adapters = adapter_down_maps.shape[0]
    owners = lax.axis_size("dp")
    me = lax.axis_index("dp")
    n = lax.axis_size("tensor")
    nz = n // 2
    place = lax.axis_index("tensor")
    order = line_plan(nz)
    out_width = projection_weight.shape[1] // n

    def swap_y(value):
        return lax.ppermute(value, "tensor", [(t, t ^ 1) for t in range(n)])

    def hop(value, h):
        pairs = []
        for side in range(2):
            pairs.append((h * 2 + side, (h + 1) * 2 + side))
            pairs.append(((nz - 1 - h) * 2 + side, (nz - 2 - h) * 2 + side))
        return lax.ppermute(value, "tensor", pairs)

    def slot_of(h, m):
        return list(order[h]).index(nz - 1 - m)

    def pass_on(value, shift):
        return lax.ppermute(value, "dp", [(i, (i + shift) % owners) for i in range(owners)])

    rows = attention_result.reshape(steps * row_count, width)
    count = steps * row_count
    last = [()]

    def then(kernel, *operands, **options):
        out = kernel(*operands, after=last[0], **options)
        last[0] = (out[0] if isinstance(out, (tuple, list)) else out,)
        return out

    slot_range = jnp.arange(SLOTS, dtype=jnp.int32)
    ids = jnp.arange(local_adapters, dtype=jnp.int32)

    def slots(row_ids, owner):
        hit = row_ids[:, None] - owner * local_adapters == ids[None, :]
        used = jnp.any(hit, axis=0)
        position = jnp.sum(
            (used[None, :] & (ids[None, :] < ids[:, None])).astype(jnp.int32), axis=1
        )
        names = jnp.sum(
            jnp.where(used[None, :] & (position[None, :] == slot_range[:, None]), ids[None, :], 0),
            axis=1,
        )
        row_slot = jnp.sum(jnp.where(hit, position[None, :] + 1, 0), axis=1) - 1
        return names, row_slot[:, None]

    blocks = [[(order[t // 2][k] * 2 + side) for side in (1 - t % 2, t % 2) for k in range(nz)] for t in range(n)]
    starts = jnp.asarray(np.asarray(blocks, np.int32) * out_width)[place]
    low_rows = 2 * (owners * count // 2) * adapter_down_maps.shape[1] // out_width
    even = [(p * count // PARTS, count // PARTS) for p in range(PARTS)]
    uneven = [(0, count // 2 + low_rows), (count // 2 + low_rows, count // 2 - low_rows)]
    away_part, own_all, from_y, sums, arrived = {}, {}, {}, {}, {}

    def split(k):
        return uneven if k == 0 else [(0, count)]

    def add_up(span, terms, extra=(), dtype=jnp.bfloat16, into=None):
        low_row, high_row = span[0], span[0] + span[1]
        cuts = {low_row, high_row}
        for term in terms:
            for at, some, _, _ in term:
                cuts.update(row for row in (at, at + some) if low_row < row < high_row)
        cuts = sorted(cuts)
        runs = []
        for begin, end in zip(cuts, cuts[1:]):
            here = [
                (array, row + begin - at) for term in terms for at, some, array, row in term if at <= begin < at + some
            ]
            runs.append((end - begin, here))
        return then(total, runs + list(extra), dtype, into)

    def whole(array):
        return [(0, count, array, 0)]

    def multiply(aways, owns, tail=None, chunk=1024):
        ks = sorted({k for k, _ in aways})
        names = ks + [nz + k for k in owns]
        outs = [(ks.index(k), *split(k)[p]) for k, p in aways]
        outs += [(len(ks) + i, 0, count) for i in range(len(owns))]
        done = then(products, rows, projection_weight, starts, names, out_width, outs, tail, chunk)
        away_part.update(zip(aways, done))
        own_all.update(zip(owns, done[len(aways) :]))

    def start_y(k, p, after=None):
        value = away_part[k, p]
        from_y[k, p] = swap_y(value if after is None else hold(value, after))

    def y_parts(k):
        return [(*cut, from_y[k, p], 0) for p, cut in enumerate(split(k)) if (k, p) in from_y]

    def sum_parts(k):
        return [(*cut, sums[k, p], 0) for p, cut in enumerate(cut_of(0, k)) if (k, p) in sums]

    def cut_of(h, m):
        if m == 0 and h <= 1:
            return uneven
        return even if m == 1 else [(0, count)]

    def arrived_parts(h, m):
        return [(*cut, arrived[h, m, p], 0) for p, cut in enumerate(cut_of(h, m)) if (h, m, p) in arrived]

    def line(h, m, p):
        k = slot_of(h, m)
        span = cut_of(h, m)[p]
        low_too = m == 0 and h <= 1 and p == LOW_WITH[1]
        if h == 0:
            extra = [(low_rows, [(low, 0), (from_y[k, p], span[1])])] if low_too else []
            value = sums[k, p] = add_up(span, [whole(own_all[k]), y_parts(k)], extra)
        else:
            extra = [(low_rows, [(sums[k, p], span[1]), (arrived[h - 1, m, p], span[1])])] if low_too else []
            value = add_up(span, [sum_parts(k), arrived_parts(h - 1, m)], extra)
        arrived[h, m, p] = hop(value, h)

    def line_order():
        ready, free = {}, {}
        steps = [(h, m, p) for h in range(nz - 1) for m in range(nz - 1 - h) for p in range(len(cut_of(h, m)))]
        for h, m, p in sorted(steps, key=lambda step: (step[0], step[1], step[2])):
            k = slot_of(h, m)
            there = (k + 1.0) * count if k or p else 1.0 * cut_of(0, 0)[0][1]
            if h:
                above = range(len(cut_of(h - 1, m)))
                there = max(there, max(ready[h - 1, m, q, "end"] for q in above if q == p or len(above) != len(cut_of(h, m))))
            ready[h, m, p] = there
            free[h] = max(there, free.get(h, 0.0)) + cut_of(h, m)[p][1]
            ready[h, m, p, "end"] = free[h]
        return sorted(steps, key=lambda step: (ready[step], step[0]))

    row_ids = [tenant] + [pass_on(tenant, shift) for shift in range(1, owners)]
    row_sets = [rows] + [pass_on(rows, shift) for shift in range(1, owners)]
    multiply([(0, 0)], [], chunk=512)
    start_y(0, 0)
    named = [slots(some_ids, me) for some_ids in row_ids]
    names = jnp.concatenate([which for which, _ in named])
    slot_sets = [row_slot for _, row_slot in named]
    low = then(low_rank, row_sets, slot_sets, adapter_down_maps, names, out_width)
    multiply([LOW_WITH], [], low, chunk=512)
    start_y(*LOW_WITH)
    multiply([(1, 0)], [0])
    start_y(1, 0)
    low_sum = deltas = None
    for h, m, p in line_order():
        k = slot_of(h, m)
        if (h, m, p) == (1, 1, 1):
            last[0] += (arrived[1, 1, 0],)
        line(h, m, p)
        if h == 0:
            if k == 0 and p == 0:
                multiply([(2, 0)] if nz > 2 else [], [1])
            elif k == 0:
                if nz > 2:
                    start_y(2, 0, last[0])
                multiply([(j, 0) for j in range(3, nz)], range(2, nz))
            elif p == len(cut_of(h, m)) - 1 and k + 2 < nz:
                start_y(k + 2, 0, last[0])
        if (h, k, p) == (0, 1, len(cut_of(h, m)) - 1):
            low_at = uneven[LOW_WITH[1]][1]
            pieces = [(sums[LOW_WITH], low_at)]
            for step in range(nz - 1):
                if step >= 2:
                    prefix = then(total, [(low_rows, [pieces[0], pieces[-1]])])
                    pieces.append((hop(prefix, step), 0))
                else:
                    pieces.append((arrived[step, 0, LOW_WITH[1]], low_at))
        if (h, m, p) == LOW_SUM_AFTER:
            low_sum = then(total, [(low_rows, pieces)])
        if deltas is None and low_sum is not None and EXPAND_AFTER in arrived:
            deltas = then(expand, low_sum, slot_sets, adapter_up_maps, names)
            back = [
                [(*cut, pass_on(deltas[1 + (shift - 1) * PARTS + p], -shift), 0) for p, cut in enumerate(even)]
                for shift in range(1, owners)
            ]
    span = (0, count)
    early = [arrived_parts(h, nz - 2 - h) for h in range(1, nz - 2)]
    late = [arrived_parts(h, nz - 2 - h) for h in range(nz - 1) if not 1 <= h < nz - 2]
    most = add_up(span, [whole(own_all[nz - 1]), whole(deltas[0]), y_parts(nz - 1)] + early, dtype=jnp.float32)
    out = add_up(span, [whole(most)] + back + late)
    return out.reshape(steps, row_count, out_width)


def solution(mesh):
    placed = (
        P(None, ("groups", "dp"), "tensor"),
        P(("groups", "dp")),
        P("tensor", None),
        P(("groups", "dp"), None, "tensor"),
        P(("groups", "dp"), None, "tensor"),
    )
    return jax.shard_map(
        on_device,
        mesh=mesh,
        in_specs=placed,
        out_specs=P(None, ("groups", "dp"), "tensor"),
        check_vma=False,
    )
```

```python
import jax
import jax.numpy as jnp
import numpy as np
from jax import lax
from jax.experimental import pallas as pl
from jax.experimental.pallas import tpu as pltpu
from jax.sharding import PartitionSpec as P

SLOTS = 16
LANES = 128
CHUNK = 512
PARTS = 2
LOW_WITH = (0, PARTS - 1)
LOW_SUM_AFTER = (0, 2, 0)
EXPAND_AFTER = (2, 0, 0)
VMEM = 50 * 2**20
ANY = pl.BlockSpec(memory_space=pl.ANY)


def call(kernel, operands, after, *, in_specs, out_specs, out_shape, name, prefetch=0, scratch=(), alias=None):
    inputs, extra = len(operands), len(after)

    def body(*refs):
        kernel(*refs[:inputs], *refs[inputs + extra :])

    return pl.pallas_call(
        body,
        grid_spec=pltpu.PrefetchScalarGridSpec(
            num_scalar_prefetch=prefetch,
            grid=(),
            in_specs=list(in_specs) + [ANY] * extra,
            out_specs=out_specs,
            scratch_shapes=list(scratch),
        ),
        out_shape=out_shape,
        input_output_aliases=alias or {},
        compiler_params=pltpu.CompilerParams(vmem_limit_bytes=VMEM),
        cost_estimate=pl.CostEstimate(flops=1, transcendentals=0, bytes_accessed=1),
        name=name,
    )(*operands, *after)


def hold(value, after):
    def kernel(value_ref, out_ref):
        pass

    return call(
        kernel, [value], after, in_specs=[ANY], out_specs=ANY,
        out_shape=jax.ShapeDtypeStruct(value.shape, value.dtype), name="hold", alias={0: 0},
    )


def products(rows, weight, starts, names, size, outs, tail=None, chunk=1024, after=()):
    count, width = rows.shape
    blocks = len(names)
    chunks = [(at, min(chunk, size - at)) for at in range(0, size, chunk)]
    low = min(first for _, first, _ in outs)
    high = max(first + some for _, first, some in outs)
    upper = (high - low) // 32 * 16
    row_parts = [(0, upper), (upper, high - low - upper)]
    tails = [] if tail is None else [tail]
    heights = [some for _, _, some in outs]
    for array in tails:
        heights[-1] += array.shape[0]

    def kernel(starts_ref, rows_ref, weight_ref, *refs):
        tail_refs, refs = refs[: len(tails)], refs[len(tails) :]
        out_refs, (x, w, *refs) = refs[: len(outs)], refs[len(outs) :]
        stage, (x_sems, w_sems, out_sems, tail_sems) = refs[: len(outs)], refs[len(outs) :]
        x_copies = [
            pltpu.make_async_copy(
                rows_ref.at[pl.ds(low + at, some)], x.at[pl.ds(at, some)], x_sems.at[i]
            )
            for i, (at, some) in enumerate(row_parts)
        ]
        w_copies = [
            [
                pltpu.make_async_copy(
                    weight_ref.at[:, pl.ds(pl.multiple_of(starts_ref[names[b]] + at, LANES), extent)],
                    w.at[b, :, pl.ds(at, extent)],
                    w_sems.at[b, c],
                )
                for c, (at, extent) in enumerate(chunks)
            ]
            for b in range(blocks)
        ]
        x_copies[0].start()
        w_copies[0][0].start()
        x_copies[1].start()
        for b in range(blocks):
            for c in range(len(chunks)):
                if b or c:
                    w_copies[b][c].start()
        stores = []
        for ref in tail_refs:
            below = pl.ds(outs[-1][2], ref.shape[0])
            read = pltpu.make_async_copy(ref, stage[-1].at[below], tail_sems.at[0])
            read.start()
            read.wait()
            stores.append(pltpu.make_async_copy(stage[-1].at[below], out_refs[-1].at[below], tail_sems.at[1]))
            stores[-1].start()
        for copy in x_copies:
            copy.wait()
        for b in range(blocks):
            for c, (at, extent) in enumerate(chunks):
                w_copies[b][c].wait()
                for o, (index, first, some) in enumerate(outs):
                    if index == b:
                        value = jnp.dot(
                            x[first - low : first - low + some, :], w[b, :, at : at + extent],
                            preferred_element_type=jnp.float32,
                        )
                        stage[o][:some, at : at + extent] = value.astype(rows.dtype)
                        store = pltpu.make_async_copy(
                            stage[o].at[pl.ds(0, some), pl.ds(at, extent)],
                            out_refs[o].at[pl.ds(0, some), pl.ds(at, extent)],
                            out_sems.at[o, c],
                        )
                        store.start()
                        stores.append(store)
        for store in stores:
            store.wait()

    shapes = [(height, size) for height in heights]
    return call(
        kernel, [starts, rows, weight] + tails, after, prefetch=1,
        in_specs=[ANY] * (2 + len(tails)),
        out_specs=[ANY] * len(outs),
        out_shape=[jax.ShapeDtypeStruct(shape, rows.dtype) for shape in shapes],
        scratch=[pltpu.VMEM((high - low, width), rows.dtype), pltpu.VMEM((blocks, width, size), rows.dtype)]
        + [pltpu.VMEM(shape, rows.dtype) for shape in shapes]
        + [
            pltpu.SemaphoreType.DMA((2,)),
            pltpu.SemaphoreType.DMA((blocks, len(chunks))),
            pltpu.SemaphoreType.DMA((len(outs), len(chunks))),
            pltpu.SemaphoreType.DMA((2,)),
        ],
        name="products",
    )


def total(runs, dtype=jnp.bfloat16, into=None, after=()):
    width = runs[0][1][0][0].shape[1]
    height = sum(some for some, _ in runs)
    rows_in_all, first, so_far = into or (height, 0, None)
    tiles = []
    at = 0
    for r, (some, terms) in enumerate(runs):
        size = -(-some // 32) * 16 if some * width > 2**17 else some
        for skip in range(0, some, size):
            tiles.append((r, skip, min(size, some - skip), at + skip))
        at += some
    operands = [term for _, terms in runs for term, _ in terms]
    before = [] if so_far is None else [so_far]
    most_terms = max(len(terms) for _, terms in runs)
    of_run = np.cumsum([0] + [len(terms) for _, terms in runs])

    def kernel(*refs):
        term_refs, out_ref = refs[: len(operands)], refs[len(operands) + len(before)]
        refs = refs[len(operands) + len(before) + 1 :]
        bufs, (stage, in_sems, out_sems) = refs[: len(operands)], refs[len(operands) :]
        reads, writes = [], []
        for n, (r, skip, size, place) in enumerate(tiles):
            reads.append(
                [
                    pltpu.make_async_copy(
                        term_refs[of_run[r] + t].at[pl.ds(start + skip, size)],
                        bufs[of_run[r] + t].at[pl.ds(skip, size)],
                        in_sems.at[t, n],
                    )
                    for t, (_, start) in enumerate(runs[r][1])
                ]
            )
            writes.append(
                pltpu.make_async_copy(
                    stage.at[pl.ds(place, size)], out_ref.at[pl.ds(first + place, size)], out_sems.at[n]
                )
            )
        for some in reads:
            for read in some:
                read.start()
        for n, (r, skip, size, place) in enumerate(tiles):
            for read in reads[n]:
                read.wait()
            value = None
            for t in range(len(runs[r][1])):
                part = bufs[of_run[r] + t][skip : skip + size, :].astype(jnp.float32)
                value = part if value is None else value + part
            stage[place : place + size, :] = value.astype(dtype)
            writes[n].start()
        for write in writes:
            write.wait()

    return call(
        kernel, operands + before, after,
        in_specs=[ANY] * (len(operands) + len(before)),
        out_specs=ANY,
        out_shape=jax.ShapeDtypeStruct((rows_in_all, width), dtype),
        scratch=[pltpu.VMEM((some, width), term.dtype) for some, terms in runs for term, _ in terms]
        + [
            pltpu.VMEM((height, width), dtype),
            pltpu.SemaphoreType.DMA((most_terms, len(tiles))),
            pltpu.SemaphoreType.DMA((len(tiles),)),
        ],
        alias={len(operands): 0} if before else None,
        name="total",
    )


def lane_pick(slot_ref, repeats, shape, rank, first):
    slot = jnp.concatenate([slot_ref[...]] * repeats, axis=0)
    return slot == lax.broadcasted_iota(jnp.int32, shape, 1) // rank + first


def block_copies(index_ref, maps_ref, buf, sems, sets, rank):
    each = index_ref.shape[0] // sets
    return [
        [
            pltpu.make_async_copy(
                maps_ref.at[index_ref[s * each + i]], buf.at[pl.ds((s * each + i) * rank, rank)],
                sems.at[s * each + i],
            )
            for i in range(each)
        ]
        for s in range(sets)
    ]


def low_rank(row_sets, slot_sets, maps, index, wide, after=()):
    sets = len(row_sets)
    count, width = row_sets[0].shape
    rank = maps.shape[1]
    span = index.shape[0] // sets * rank
    repeats = count // slot_sets[0].shape[0]
    half = count // 2
    group = 256
    tall = sets * half * 2 * rank // wide

    def kernel(index_ref, *refs):
        row_refs, slot_refs, maps_ref, out_ref = refs[:sets], refs[sets : 2 * sets], refs[2 * sets], refs[2 * sets + 1]
        rows_buf, maps_buf, row_sems, map_sems = refs[2 * sets + 2 :]
        row_copies = [
            pltpu.make_async_copy(row_refs[s], rows_buf.at[s], row_sems.at[s]) for s in range(sets)
        ]
        map_copies = block_copies(index_ref, maps_ref, maps_buf, map_sems, sets, rank)
        for s in range(sets):
            row_copies[s].start()
            for copy in map_copies[s]:
                copy.start()
        for s in range(sets):
            row_copies[s].wait()
            for copy in map_copies[s]:
                copy.wait()
            acc = None
            for at in range(0, span, group):
                scores = lax.dot_general(
                    rows_buf[s], maps_buf[s * span + at : s * span + at + group],
                    (((1,), (1,)), ((), ())), preferred_element_type=jnp.float32,
                )
                pick = lane_pick(slot_refs[s], repeats, (count, group), rank, at // rank)
                term = jnp.where(pick, scores, 0.0)
                acc = term if acc is None else acc + term
            summed = acc[:, 0:rank]
            for g in range(1, group // rank):
                summed += acc[:, g * rank : (g + 1) * rank]
            summed = summed.astype(out_ref.dtype)
            for b in range(half // tall):
                lanes = slice((s * half // tall + b) * 2 * rank, (s * half // tall + b + 1) * 2 * rank)
                both = [summed[start + b * tall : start + (b + 1) * tall] for start in (0, half)]
                out_ref[:, lanes] = jnp.concatenate(both, axis=1)

    return call(
        kernel, [index, *row_sets, *slot_sets, maps], after, prefetch=1,
        in_specs=[ANY] * sets + [pl.BlockSpec(memory_space=pltpu.VMEM)] * sets + [ANY],
        out_specs=pl.BlockSpec(memory_space=pltpu.VMEM),
        out_shape=jax.ShapeDtypeStruct((tall, wide), jnp.bfloat16),
        scratch=[
            pltpu.VMEM((sets, count, width), row_sets[0].dtype),
            pltpu.VMEM((sets * span, width), maps.dtype),
            pltpu.SemaphoreType.DMA((sets,)),
            pltpu.SemaphoreType.DMA((index.shape[0],)),
        ],
        name="low_rank",
    )


def expand(low, slot_sets, maps, index, after=()):
    sets = len(slot_sets)
    rank, width = maps.shape[1:]
    tall = low.shape[0]
    half = low.size // sets // (2 * rank)
    count = 2 * half
    span = index.shape[0] // sets * rank
    repeats = count // slot_sets[0].shape[0]

    outs = [(0, 0, count)] + [
        (s, p * count // PARTS, count // PARTS) for s in range(1, sets) for p in range(PARTS)
    ]

    def kernel(index_ref, low_ref, *refs):
        slot_refs, maps_ref, out_refs = refs[:sets], refs[sets], refs[sets + 1 : sets + 1 + len(outs)]
        stage, maps_buf, map_sems, out_sems = refs[sets + 1 + len(outs) :]
        map_copies = block_copies(index_ref, maps_ref, maps_buf, map_sems, sets, rank)
        writes = [
            pltpu.make_async_copy(stage.at[s, pl.ds(first, some)], out_refs[o], out_sems.at[o])
            for o, (s, first, some) in enumerate(outs)
        ]
        order = list(range(1, sets)) + [0]
        for s in order:
            for copy in map_copies[s]:
                copy.start()
        for s in order:
            lanes = [(s * half // tall + b) * 2 * rank for b in range(half // tall)]
            mine = jnp.concatenate(
                [low_ref[:, at + side : at + side + rank] for side in (0, rank) for at in lanes], axis=0
            )
            tiled = jnp.concatenate([mine] * (span // rank), axis=1)
            pick = lane_pick(slot_refs[s], repeats, (count, span), rank, 0)
            picked = jnp.where(pick, tiled, jnp.zeros_like(tiled))
            for copy in map_copies[s]:
                copy.wait()
            for at in range(0, width, CHUNK):
                value = jnp.dot(
                    picked, maps_buf[s * span : (s + 1) * span, at : at + CHUNK], preferred_element_type=jnp.float32
                )
                stage[s, :, at : at + CHUNK] = value.astype(stage.dtype)
            for o, (which, _, _) in enumerate(outs):
                if which == s:
                    writes[o].start()
        for write in writes:
            write.wait()

    return call(
        kernel, [index, low, *slot_sets, maps], after, prefetch=1,
        in_specs=[pl.BlockSpec(memory_space=pltpu.VMEM)] * (1 + sets) + [ANY],
        out_specs=[ANY] * len(outs),
        out_shape=[jax.ShapeDtypeStruct((some, width), jnp.bfloat16) for _, _, some in outs],
        scratch=[
            pltpu.VMEM((sets, count, width), jnp.bfloat16),
            pltpu.VMEM((sets * span, width), maps.dtype),
            pltpu.SemaphoreType.DMA((index.shape[0],)),
            pltpu.SemaphoreType.DMA((len(outs),)),
        ],
        name="expand",
    )


def line_plan(nz):
    order = np.zeros((nz, nz), np.int32)
    for z in range(nz):
        def need(j):
            if j == z:
                return (2 * nz, 0)
            return (nz - 1 - j + z, j) if j > z else (nz - 1 - z + j, nz - j)

        order[z] = sorted(range(nz), key=need)
    return order


def on_device(attention_result, tenant, projection_weight, adapter_down_maps, adapter_up_maps):
    steps, row_count, width = attention_result.shape
    local_adapters = adapter_down_maps.shape[0]
    owners = lax.axis_size("dp")
    me = lax.axis_index("dp")
    n = lax.axis_size("tensor")
    nz = n // 2
    place = lax.axis_index("tensor")
    order = line_plan(nz)
    out_width = projection_weight.shape[1] // n

    def swap_y(value):
        return lax.ppermute(value, "tensor", [(t, t ^ 1) for t in range(n)])

    def hop(value, h):
        pairs = []
        for side in range(2):
            pairs.append((h * 2 + side, (h + 1) * 2 + side))
            pairs.append(((nz - 1 - h) * 2 + side, (nz - 2 - h) * 2 + side))
        return lax.ppermute(value, "tensor", pairs)

    def slot_of(h, m):
        return list(order[h]).index(nz - 1 - m)

    def pass_on(value, shift):
        return lax.ppermute(value, "dp", [(i, (i + shift) % owners) for i in range(owners)])

    rows = attention_result.reshape(steps * row_count, width)
    count = steps * row_count
    last = [()]

    def then(kernel, *operands, **options):
        out = kernel(*operands, after=last[0], **options)
        last[0] = (out[0] if isinstance(out, (tuple, list)) else out,)
        return out

    slot_range = jnp.arange(SLOTS, dtype=jnp.int32)
    ids = jnp.arange(local_adapters, dtype=jnp.int32)

    def slots(row_ids, owner):
        hit = row_ids[:, None] - owner * local_adapters == ids[None, :]
        used = jnp.any(hit, axis=0)
        position = jnp.sum(
            (used[None, :] & (ids[None, :] < ids[:, None])).astype(jnp.int32), axis=1
        )
        names = jnp.sum(
            jnp.where(used[None, :] & (position[None, :] == slot_range[:, None]), ids[None, :], 0),
            axis=1,
        )
        row_slot = jnp.sum(jnp.where(hit, position[None, :] + 1, 0), axis=1) - 1
        return names, row_slot[:, None]

    blocks = [[(order[t // 2][k] * 2 + side) for side in (1 - t % 2, t % 2) for k in range(nz)] for t in range(n)]
    starts = jnp.asarray(np.asarray(blocks, np.int32) * out_width)[place]
    low_rows = 2 * (owners * count // 2) * adapter_down_maps.shape[1] // out_width
    even = [(p * count // PARTS, count // PARTS) for p in range(PARTS)]
    uneven = [(0, (count + low_rows) // 2), ((count + low_rows) // 2, (count - low_rows) // 2)]
    away_part, own_all, from_y, sums, arrived = {}, {}, {}, {}, {}

    def split(k):
        return uneven if k == 0 else [(0, count)]

    def add_up(span, terms, extra=(), dtype=jnp.bfloat16, into=None):
        low_row, high_row = span[0], span[0] + span[1]
        cuts = {low_row, high_row}
        for term in terms:
            for at, some, _, _ in term:
                cuts.update(row for row in (at, at + some) if low_row < row < high_row)
        cuts = sorted(cuts)
        runs = []
        for begin, end in zip(cuts, cuts[1:]):
            here = [
                (array, row + begin - at) for term in terms for at, some, array, row in term if at <= begin < at + some
            ]
            runs.append((end - begin, here))
        return then(total, runs + list(extra), dtype, into)

    def whole(array):
        return [(0, count, array, 0)]

    def multiply(aways, owns, tail=None, chunk=1024):
        ks = sorted({k for k, _ in aways})
        names = ks + [nz + k for k in owns]
        outs = [(ks.index(k), *split(k)[p]) for k, p in aways]
        outs += [(len(ks) + i, 0, count) for i in range(len(owns))]
        done = then(products, rows, projection_weight, starts, names, out_width, outs, tail, chunk)
        away_part.update(zip(aways, done))
        own_all.update(zip(owns, done[len(aways) :]))

    def start_y(k, p, after=None):
        value = away_part[k, p]
        from_y[k, p] = swap_y(value if after is None else hold(value, after))

    def y_parts(k):
        return [(*cut, from_y[k, p], 0) for p, cut in enumerate(split(k)) if (k, p) in from_y]

    def sum_parts(k):
        return [(*cut, sums[k, p], 0) for p, cut in enumerate(cut_of(0, k)) if (k, p) in sums]

    def cut_of(h, m):
        if m == 0 and h <= 1:
            return uneven
        return even if m == 1 else [(0, count)]

    def arrived_parts(h, m):
        return [(*cut, arrived[h, m, p], 0) for p, cut in enumerate(cut_of(h, m)) if (h, m, p) in arrived]

    def line(h, m, p):
        k = slot_of(h, m)
        span = cut_of(h, m)[p]
        low_too = m == 0 and h <= 1 and p == LOW_WITH[1]
        if h == 0:
            extra = [(low_rows, [(low, 0), (from_y[k, p], span[1])])] if low_too else []
            value = sums[k, p] = add_up(span, [whole(own_all[k]), y_parts(k)], extra)
        else:
            extra = [(low_rows, [(sums[k, p], span[1]), (arrived[h - 1, m, p], span[1])])] if low_too else []
            value = add_up(span, [sum_parts(k), arrived_parts(h - 1, m)], extra)
        arrived[h, m, p] = hop(value, h)

    def line_order():
        ready, free = {}, {}
        steps = [(h, m, p) for h in range(nz - 1) for m in range(nz - 1 - h) for p in range(len(cut_of(h, m)))]
        for h, m, p in sorted(steps, key=lambda step: (step[0], step[1], step[2])):
            k = slot_of(h, m)
            there = (k + 1.0) * count if k or p else 1.0 * cut_of(0, 0)[0][1]
            if h:
                above = range(len(cut_of(h - 1, m)))
                there = max(there, max(ready[h - 1, m, q, "end"] for q in above if q == p or len(above) != len(cut_of(h, m))))
            ready[h, m, p] = there
            free[h] = max(there, free.get(h, 0.0)) + cut_of(h, m)[p][1]
            ready[h, m, p, "end"] = free[h]
        return sorted(steps, key=lambda step: (ready[step], step[0]))

    row_ids = [tenant] + [pass_on(tenant, shift) for shift in range(1, owners)]
    row_sets = [rows] + [pass_on(rows, shift) for shift in range(1, owners)]
    multiply([(0, 0)], [], chunk=512)
    start_y(0, 0)
    named = [slots(some_ids, me) for some_ids in row_ids]
    names = jnp.concatenate([which for which, _ in named])
    slot_sets = [row_slot for _, row_slot in named]
    low = then(low_rank, row_sets, slot_sets, adapter_down_maps, names, out_width)
    multiply([LOW_WITH], [], low, chunk=512)
    start_y(*LOW_WITH)
    multiply([(1, 0)], [0])
    start_y(1, 0)
    low_sum = deltas = None
    for h, m, p in line_order():
        k = slot_of(h, m)
        line(h, m, p)
        if h == 0:
            if k == 0 and p == 0:
                multiply([(2, 0)] if nz > 2 else [], [1])
            elif k == 0:
                if nz > 2:
                    start_y(2, 0, last[0])
                multiply([(j, 0) for j in range(3, nz)], range(2, nz))
            elif p == len(cut_of(h, m)) - 1 and k + 2 < nz:
                start_y(k + 2, 0, last[0])
        if (h, k, p) == (0, 1, len(cut_of(h, m)) - 1):
            low_at = uneven[LOW_WITH[1]][1]
            pieces = [(sums[LOW_WITH], low_at)]
            last[0] += (arrived[1, 0, 0],) if nz > 2 else ()
            for step in range(nz - 1):
                if step >= 2:
                    prefix = then(total, [(low_rows, [pieces[0], pieces[-1]])])
                    pieces.append((hop(prefix, step), 0))
                else:
                    pieces.append((arrived[step, 0, LOW_WITH[1]], low_at))
        if (h, m, p) == LOW_SUM_AFTER:
            low_sum = then(total, [(low_rows, pieces)])
        if deltas is None and low_sum is not None and EXPAND_AFTER in arrived:
            last[0] += (arrived[1, 1, 0],) if nz > 2 else ()
            deltas = then(expand, low_sum, slot_sets, adapter_up_maps, names)
            back = [
                [(*cut, pass_on(deltas[1 + (shift - 1) * PARTS + p], -shift), 0) for p, cut in enumerate(even)]
                for shift in range(1, owners)
            ]
    span = (0, count)
    early = [arrived_parts(h, nz - 2 - h) for h in range(1, nz - 2)]
    late = [arrived_parts(h, nz - 2 - h) for h in range(nz - 1) if not 1 <= h < nz - 2]
    most = add_up(span, [whole(own_all[nz - 1]), whole(deltas[0]), y_parts(nz - 1)] + early, dtype=jnp.float32)
    out = add_up(span, [whole(most)] + back + late)
    return out.reshape(steps, row_count, out_width)


def solution(mesh):
    placed = (
        P(None, ("groups", "dp"), "tensor"),
        P(("groups", "dp")),
        P("tensor", None),
        P(("groups", "dp"), None, "tensor"),
        P(("groups", "dp"), None, "tensor"),
    )
    return jax.shard_map(
        on_device,
        mesh=mesh,
        in_specs=placed,
        out_specs=P(None, ("groups", "dp"), "tensor"),
        check_vma=False,
    )
```

```python
import jax
import jax.numpy as jnp
import numpy as np
from jax import lax
from jax.experimental import pallas as pl
from jax.experimental.pallas import tpu as pltpu
from jax.sharding import PartitionSpec as P

SLOTS = 16
LANES = 128
CHUNK = 512
PARTS = 2
LOW_WITH = (0, PARTS - 1)
LOW_SUM_AFTER = (0, 2, 0)
EXPAND_AFTER = (1, 1, 1)
VMEM = 50 * 2**20
ANY = pl.BlockSpec(memory_space=pl.ANY)


def call(kernel, operands, after, *, in_specs, out_specs, out_shape, name, prefetch=0, scratch=(), alias=None):
    inputs, extra = len(operands), len(after)

    def body(*refs):
        kernel(*refs[:inputs], *refs[inputs + extra :])

    return pl.pallas_call(
        body,
        grid_spec=pltpu.PrefetchScalarGridSpec(
            num_scalar_prefetch=prefetch,
            grid=(),
            in_specs=list(in_specs) + [ANY] * extra,
            out_specs=out_specs,
            scratch_shapes=list(scratch),
        ),
        out_shape=out_shape,
        input_output_aliases=alias or {},
        compiler_params=pltpu.CompilerParams(vmem_limit_bytes=VMEM),
        cost_estimate=pl.CostEstimate(flops=1, transcendentals=0, bytes_accessed=1),
        name=name,
    )(*operands, *after)


def hold(value, after):
    def kernel(value_ref, out_ref):
        pass

    return call(
        kernel, [value], after, in_specs=[ANY], out_specs=ANY,
        out_shape=jax.ShapeDtypeStruct(value.shape, value.dtype), name="hold", alias={0: 0},
    )


def products(rows, weight, starts, names, size, outs, tail=None, chunk=1024, after=()):
    count, width = rows.shape
    blocks = len(names)
    chunks = [(at, min(chunk, size - at)) for at in range(0, size, chunk)]
    low = min(first for _, first, _ in outs)
    high = max(first + some for _, first, some in outs)
    upper = (high - low) // 32 * 16
    row_parts = [(0, upper), (upper, high - low - upper)]
    tails = [] if tail is None else [tail]
    heights = [some for _, _, some in outs]
    for array in tails:
        heights[-1] += array.shape[0]

    def kernel(starts_ref, rows_ref, weight_ref, *refs):
        tail_refs, refs = refs[: len(tails)], refs[len(tails) :]
        out_refs, (x, w, *refs) = refs[: len(outs)], refs[len(outs) :]
        stage, (x_sems, w_sems, out_sems, tail_sems) = refs[: len(outs)], refs[len(outs) :]
        x_copies = [
            pltpu.make_async_copy(
                rows_ref.at[pl.ds(low + at, some)], x.at[pl.ds(at, some)], x_sems.at[i]
            )
            for i, (at, some) in enumerate(row_parts)
        ]
        w_copies = [
            [
                pltpu.make_async_copy(
                    weight_ref.at[:, pl.ds(pl.multiple_of(starts_ref[names[b]] + at, LANES), extent)],
                    w.at[b, :, pl.ds(at, extent)],
                    w_sems.at[b, c],
                )
                for c, (at, extent) in enumerate(chunks)
            ]
            for b in range(blocks)
        ]
        x_copies[0].start()
        w_copies[0][0].start()
        x_copies[1].start()
        for b in range(blocks):
            for c in range(len(chunks)):
                if b or c:
                    w_copies[b][c].start()
        stores = []
        for ref in tail_refs:
            below = pl.ds(outs[-1][2], ref.shape[0])
            read = pltpu.make_async_copy(ref, stage[-1].at[below], tail_sems.at[0])
            read.start()
            read.wait()
            stores.append(pltpu.make_async_copy(stage[-1].at[below], out_refs[-1].at[below], tail_sems.at[1]))
            stores[-1].start()
        for copy in x_copies:
            copy.wait()
        for b in range(blocks):
            for c, (at, extent) in enumerate(chunks):
                w_copies[b][c].wait()
                for o, (index, first, some) in enumerate(outs):
                    if index == b:
                        value = jnp.dot(
                            x[first - low : first - low + some, :], w[b, :, at : at + extent],
                            preferred_element_type=jnp.float32,
                        )
                        stage[o][:some, at : at + extent] = value.astype(rows.dtype)
                        store = pltpu.make_async_copy(
                            stage[o].at[pl.ds(0, some), pl.ds(at, extent)],
                            out_refs[o].at[pl.ds(0, some), pl.ds(at, extent)],
                            out_sems.at[o, c],
                        )
                        store.start()
                        stores.append(store)
        for store in stores:
            store.wait()

    shapes = [(height, size) for height in heights]
    return call(
        kernel, [starts, rows, weight] + tails, after, prefetch=1,
        in_specs=[ANY] * (2 + len(tails)),
        out_specs=[ANY] * len(outs),
        out_shape=[jax.ShapeDtypeStruct(shape, rows.dtype) for shape in shapes],
        scratch=[pltpu.VMEM((high - low, width), rows.dtype), pltpu.VMEM((blocks, width, size), rows.dtype)]
        + [pltpu.VMEM(shape, rows.dtype) for shape in shapes]
        + [
            pltpu.SemaphoreType.DMA((2,)),
            pltpu.SemaphoreType.DMA((blocks, len(chunks))),
            pltpu.SemaphoreType.DMA((len(outs), len(chunks))),
            pltpu.SemaphoreType.DMA((2,)),
        ],
        name="products",
    )


def total(runs, dtype=jnp.bfloat16, into=None, after=()):
    width = runs[0][1][0][0].shape[1]
    height = sum(some for some, _ in runs)
    rows_in_all, first, so_far = into or (height, 0, None)
    tiles = []
    at = 0
    for r, (some, terms) in enumerate(runs):
        split = 4 if some * len(terms) > 2000 else 2 if some * width > 2**17 else 1
        size = -(-some // (16 * split)) * 16
        for skip in range(0, some, size):
            tiles.append((r, skip, min(size, some - skip), at + skip))
        at += some
    operands = [term for _, terms in runs for term, _ in terms]
    before = [] if so_far is None else [so_far]
    most_terms = max(len(terms) for _, terms in runs)
    of_run = np.cumsum([0] + [len(terms) for _, terms in runs])

    def kernel(*refs):
        term_refs, out_ref = refs[: len(operands)], refs[len(operands) + len(before)]
        refs = refs[len(operands) + len(before) + 1 :]
        bufs, (stage, in_sems, out_sems) = refs[: len(operands)], refs[len(operands) :]
        reads, writes = [], []
        for n, (r, skip, size, place) in enumerate(tiles):
            reads.append(
                [
                    pltpu.make_async_copy(
                        term_refs[of_run[r] + t].at[pl.ds(start + skip, size)],
                        bufs[of_run[r] + t].at[pl.ds(skip, size)],
                        in_sems.at[t, n],
                    )
                    for t, (_, start) in enumerate(runs[r][1])
                ]
            )
            writes.append(
                pltpu.make_async_copy(
                    stage.at[pl.ds(place, size)], out_ref.at[pl.ds(first + place, size)], out_sems.at[n]
                )
            )
        for some in reads:
            for read in some:
                read.start()
        for n, (r, skip, size, place) in enumerate(tiles):
            for read in reads[n]:
                read.wait()
            value = None
            for t in range(len(runs[r][1])):
                part = bufs[of_run[r] + t][skip : skip + size, :].astype(jnp.float32)
                value = part if value is None else value + part
            stage[place : place + size, :] = value.astype(dtype)
            writes[n].start()
        for write in writes:
            write.wait()

    return call(
        kernel, operands + before, after,
        in_specs=[ANY] * (len(operands) + len(before)),
        out_specs=ANY,
        out_shape=jax.ShapeDtypeStruct((rows_in_all, width), dtype),
        scratch=[pltpu.VMEM((some, width), term.dtype) for some, terms in runs for term, _ in terms]
        + [
            pltpu.VMEM((height, width), dtype),
            pltpu.SemaphoreType.DMA((most_terms, len(tiles))),
            pltpu.SemaphoreType.DMA((len(tiles),)),
        ],
        alias={len(operands): 0} if before else None,
        name="total",
    )


def lane_pick(slot_ref, repeats, shape, rank, first):
    slot = jnp.concatenate([slot_ref[...]] * repeats, axis=0)
    return slot == lax.broadcasted_iota(jnp.int32, shape, 1) // rank + first


def block_copies(index_ref, maps_ref, buf, sems, sets, rank):
    each = index_ref.shape[0] // sets
    return [
        [
            pltpu.make_async_copy(
                maps_ref.at[index_ref[s * each + i]], buf.at[pl.ds((s * each + i) * rank, rank)],
                sems.at[s * each + i],
            )
            for i in range(each)
        ]
        for s in range(sets)
    ]


def low_rank(row_sets, slot_sets, maps, index, wide, after=()):
    sets = len(row_sets)
    count, width = row_sets[0].shape
    rank = maps.shape[1]
    span = index.shape[0] // sets * rank
    repeats = count // slot_sets[0].shape[0]
    half = count // 2
    group = 256
    tall = sets * half * 2 * rank // wide

    def kernel(index_ref, *refs):
        row_refs, slot_refs, maps_ref, out_ref = refs[:sets], refs[sets : 2 * sets], refs[2 * sets], refs[2 * sets + 1]
        rows_buf, maps_buf, row_sems, map_sems = refs[2 * sets + 2 :]
        row_copies = [
            pltpu.make_async_copy(row_refs[s], rows_buf.at[s], row_sems.at[s]) for s in range(sets)
        ]
        map_copies = block_copies(index_ref, maps_ref, maps_buf, map_sems, sets, rank)
        for s in range(sets):
            row_copies[s].start()
            for copy in map_copies[s]:
                copy.start()
        for s in range(sets):
            row_copies[s].wait()
            for copy in map_copies[s]:
                copy.wait()
            acc = None
            for at in range(0, span, group):
                scores = lax.dot_general(
                    rows_buf[s], maps_buf[s * span + at : s * span + at + group],
                    (((1,), (1,)), ((), ())), preferred_element_type=jnp.float32,
                )
                pick = lane_pick(slot_refs[s], repeats, (count, group), rank, at // rank)
                term = jnp.where(pick, scores, 0.0)
                acc = term if acc is None else acc + term
            summed = acc[:, 0:rank]
            for g in range(1, group // rank):
                summed += acc[:, g * rank : (g + 1) * rank]
            summed = summed.astype(out_ref.dtype)
            for b in range(half // tall):
                lanes = slice((s * half // tall + b) * 2 * rank, (s * half // tall + b + 1) * 2 * rank)
                both = [summed[start + b * tall : start + (b + 1) * tall] for start in (0, half)]
                out_ref[:, lanes] = jnp.concatenate(both, axis=1)

    return call(
        kernel, [index, *row_sets, *slot_sets, maps], after, prefetch=1,
        in_specs=[ANY] * sets + [pl.BlockSpec(memory_space=pltpu.VMEM)] * sets + [ANY],
        out_specs=pl.BlockSpec(memory_space=pltpu.VMEM),
        out_shape=jax.ShapeDtypeStruct((tall, wide), jnp.bfloat16),
        scratch=[
            pltpu.VMEM((sets, count, width), row_sets[0].dtype),
            pltpu.VMEM((sets * span, width), maps.dtype),
            pltpu.SemaphoreType.DMA((sets,)),
            pltpu.SemaphoreType.DMA((index.shape[0],)),
        ],
        name="low_rank",
    )


def expand(low, slot_sets, maps, index, after=()):
    sets = len(slot_sets)
    rank, width = maps.shape[1:]
    tall = low.shape[0]
    half = low.size // sets // (2 * rank)
    count = 2 * half
    span = index.shape[0] // sets * rank
    repeats = count // slot_sets[0].shape[0]

    outs = [(0, 0, count)] + [
        (s, p * count // PARTS, count // PARTS) for s in range(1, sets) for p in range(PARTS)
    ]

    def kernel(index_ref, low_ref, *refs):
        slot_refs, maps_ref, out_refs = refs[:sets], refs[sets], refs[sets + 1 : sets + 1 + len(outs)]
        stage, maps_buf, map_sems, out_sems = refs[sets + 1 + len(outs) :]
        map_copies = block_copies(index_ref, maps_ref, maps_buf, map_sems, sets, rank)
        writes = [
            pltpu.make_async_copy(stage.at[s, pl.ds(first, some)], out_refs[o], out_sems.at[o])
            for o, (s, first, some) in enumerate(outs)
        ]
        order = list(range(1, sets)) + [0]
        for s in order:
            for copy in map_copies[s]:
                copy.start()
        for s in order:
            lanes = [(s * half // tall + b) * 2 * rank for b in range(half // tall)]
            mine = jnp.concatenate(
                [low_ref[:, at + side : at + side + rank] for side in (0, rank) for at in lanes], axis=0
            )
            tiled = jnp.concatenate([mine] * (span // rank), axis=1)
            pick = lane_pick(slot_refs[s], repeats, (count, span), rank, 0)
            picked = jnp.where(pick, tiled, jnp.zeros_like(tiled))
            for copy in map_copies[s]:
                copy.wait()
            for at in range(0, width, CHUNK):
                value = jnp.dot(
                    picked, maps_buf[s * span : (s + 1) * span, at : at + CHUNK], preferred_element_type=jnp.float32
                )
                stage[s, :, at : at + CHUNK] = value.astype(stage.dtype)
            for o, (which, _, _) in enumerate(outs):
                if which == s:
                    writes[o].start()
        for write in writes:
            write.wait()

    return call(
        kernel, [index, low, *slot_sets, maps], after, prefetch=1,
        in_specs=[pl.BlockSpec(memory_space=pltpu.VMEM)] * (1 + sets) + [ANY],
        out_specs=[ANY] * len(outs),
        out_shape=[jax.ShapeDtypeStruct((some, width), jnp.bfloat16) for _, _, some in outs],
        scratch=[
            pltpu.VMEM((sets, count, width), jnp.bfloat16),
            pltpu.VMEM((sets * span, width), maps.dtype),
            pltpu.SemaphoreType.DMA((index.shape[0],)),
            pltpu.SemaphoreType.DMA((len(outs),)),
        ],
        name="expand",
    )


def line_plan(nz):
    order = np.zeros((nz, nz), np.int32)
    for z in range(nz):
        def need(j):
            if j == z:
                return (2 * nz, 0)
            return (nz - 1 - j + z, j) if j > z else (nz - 1 - z + j, nz - j)

        order[z] = sorted(range(nz), key=need)
    return order


def on_device(attention_result, tenant, projection_weight, adapter_down_maps, adapter_up_maps):
    steps, row_count, width = attention_result.shape
    local_adapters = adapter_down_maps.shape[0]
    owners = lax.axis_size("dp")
    me = lax.axis_index("dp")
    n = lax.axis_size("tensor")
    nz = n // 2
    place = lax.axis_index("tensor")
    order = line_plan(nz)
    out_width = projection_weight.shape[1] // n

    def swap_y(value):
        return lax.ppermute(value, "tensor", [(t, t ^ 1) for t in range(n)])

    def hop(value, h):
        pairs = []
        for side in range(2):
            pairs.append((h * 2 + side, (h + 1) * 2 + side))
            pairs.append(((nz - 1 - h) * 2 + side, (nz - 2 - h) * 2 + side))
        return lax.ppermute(value, "tensor", pairs)

    def slot_of(h, m):
        return list(order[h]).index(nz - 1 - m)

    def pass_on(value, shift):
        return lax.ppermute(value, "dp", [(i, (i + shift) % owners) for i in range(owners)])

    rows = attention_result.reshape(steps * row_count, width)
    count = steps * row_count
    last = [()]

    def then(kernel, *operands, **options):
        out = kernel(*operands, after=last[0], **options)
        last[0] = (out[0] if isinstance(out, (tuple, list)) else out,)
        return out

    slot_range = jnp.arange(SLOTS, dtype=jnp.int32)
    ids = jnp.arange(local_adapters, dtype=jnp.int32)

    def slots(row_ids, owner):
        hit = row_ids[:, None] - owner * local_adapters == ids[None, :]
        used = jnp.any(hit, axis=0)
        position = jnp.sum(
            (used[None, :] & (ids[None, :] < ids[:, None])).astype(jnp.int32), axis=1
        )
        names = jnp.sum(
            jnp.where(used[None, :] & (position[None, :] == slot_range[:, None]), ids[None, :], 0),
            axis=1,
        )
        row_slot = jnp.sum(jnp.where(hit, position[None, :] + 1, 0), axis=1) - 1
        return names, row_slot[:, None]

    blocks = [[(order[t // 2][k] * 2 + side) for side in (1 - t % 2, t % 2) for k in range(nz)] for t in range(n)]
    starts = jnp.asarray(np.asarray(blocks, np.int32) * out_width)[place]
    low_rows = 2 * (owners * count // 2) * adapter_down_maps.shape[1] // out_width
    even = [(p * count // PARTS, count // PARTS) for p in range(PARTS)]
    uneven = [(0, (count + low_rows) // 2), ((count + low_rows) // 2, (count - low_rows) // 2)]
    away_part, own_all, from_y, sums, arrived = {}, {}, {}, {}, {}

    def split(k):
        return uneven if k == 0 else [(0, count)]

    def add_up(span, terms, extra=(), dtype=jnp.bfloat16, into=None):
        low_row, high_row = span[0], span[0] + span[1]
        cuts = {low_row, high_row}
        for term in terms:
            for at, some, _, _ in term:
                cuts.update(row for row in (at, at + some) if low_row < row < high_row)
        cuts = sorted(cuts)
        runs = []
        for begin, end in zip(cuts, cuts[1:]):
            here = [
                (array, row + begin - at) for term in terms for at, some, array, row in term if at <= begin < at + some
            ]
            runs.append((end - begin, here))
        return then(total, runs + list(extra), dtype, into)

    def whole(array):
        return [(0, count, array, 0)]

    def multiply(aways, owns, tail=None, chunk=1024):
        ks = sorted({k for k, _ in aways})
        names = ks + [nz + k for k in owns]
        outs = [(ks.index(k), *split(k)[p]) for k, p in aways]
        outs += [(len(ks) + i, 0, count) for i in range(len(owns))]
        done = then(products, rows, projection_weight, starts, names, out_width, outs, tail, chunk)
        away_part.update(zip(aways, done))
        own_all.update(zip(owns, done[len(aways) :]))

    def start_y(k, p, after=None):
        value = away_part[k, p]
        from_y[k, p] = swap_y(value if after is None else hold(value, after))

    def y_parts(k):
        return [(*cut, from_y[k, p], 0) for p, cut in enumerate(split(k)) if (k, p) in from_y]

    def sum_parts(k):
        return [(*cut, sums[k, p], 0) for p, cut in enumerate(cut_of(0, k)) if (k, p) in sums]

    def cut_of(h, m):
        if m == 0 and h <= 1:
            return uneven
        return even if m == 1 else [(0, count)]

    def arrived_parts(h, m):
        return [(*cut, arrived[h, m, p], 0) for p, cut in enumerate(cut_of(h, m)) if (h, m, p) in arrived]

    def line(h, m, p):
        k = slot_of(h, m)
        span = cut_of(h, m)[p]
        low_too = m == 0 and h <= 1 and p == LOW_WITH[1]
        if h == 0:
            extra = [(low_rows, [(low, 0), (from_y[k, p], span[1])])] if low_too else []
            value = sums[k, p] = add_up(span, [whole(own_all[k]), y_parts(k)], extra)
        else:
            extra = [(low_rows, [(sums[k, p], span[1]), (arrived[h - 1, m, p], span[1])])] if low_too else []
            value = add_up(span, [sum_parts(k), arrived_parts(h - 1, m)], extra)
        arrived[h, m, p] = hop(value, h)

    def line_order():
        ready, free = {}, {}
        steps = [(h, m, p) for h in range(nz - 1) for m in range(nz - 1 - h) for p in range(len(cut_of(h, m)))]
        for h, m, p in sorted(steps, key=lambda step: (step[0], step[1], step[2])):
            k = slot_of(h, m)
            there = (k + 1.0) * count if k or p else 1.0 * cut_of(0, 0)[0][1]
            if h:
                above = range(len(cut_of(h - 1, m)))
                there = max(there, max(ready[h - 1, m, q, "end"] for q in above if q == p or len(above) != len(cut_of(h, m))))
            ready[h, m, p] = there
            free[h] = max(there, free.get(h, 0.0)) + cut_of(h, m)[p][1]
            ready[h, m, p, "end"] = free[h]
        return sorted(steps, key=lambda step: (ready[step], step[0] and nz - step[0]))

    row_ids = [tenant] + [pass_on(tenant, shift) for shift in range(1, owners)]
    row_sets = [rows] + [pass_on(rows, shift) for shift in range(1, owners)]
    multiply([(0, 0)], [], chunk=512)
    start_y(0, 0)
    named = [slots(some_ids, me) for some_ids in row_ids]
    names = jnp.concatenate([which for which, _ in named])
    slot_sets = [row_slot for _, row_slot in named]
    low = then(low_rank, row_sets, slot_sets, adapter_down_maps, names, out_width)
    multiply([LOW_WITH], [], low, chunk=512)
    start_y(*LOW_WITH)
    multiply([(1, 0)], [0])
    start_y(1, 0)
    low_sum = deltas = None
    for h, m, p in line_order():
        k = slot_of(h, m)
        line(h, m, p)
        if h == 0:
            if k == 0 and p == 0:
                multiply([(2, 0)] if nz > 2 else [], [1])
            elif k == 0:
                if nz > 2:
                    start_y(2, 0, last[0])
                multiply([(j, 0) for j in range(3, nz)], range(2, nz))
            elif p == len(cut_of(h, m)) - 1 and k + 2 < nz:
                start_y(k + 2, 0, last[0])
        if (h, k, p) == (0, 1, len(cut_of(h, m)) - 1):
            low_at = uneven[LOW_WITH[1]][1]
            pieces = [(sums[LOW_WITH], low_at)]
            last[0] += (arrived[1, 0, 0],) if nz > 2 else ()
            for step in range(nz - 1):
                if step >= 2:
                    prefix = then(total, [(low_rows, [pieces[0], pieces[-1]])])
                    pieces.append((hop(prefix, step), 0))
                else:
                    pieces.append((arrived[step, 0, LOW_WITH[1]], low_at))
        if (h, m, p) == LOW_SUM_AFTER:
            low_sum = then(total, [(low_rows, pieces)])
        if deltas is None and low_sum is not None and EXPAND_AFTER in arrived:
            last[0] += (arrived[1, 1, 0],) if nz > 2 else ()
            deltas = then(expand, low_sum, slot_sets, adapter_up_maps, names)
            back = [
                [(*cut, pass_on(deltas[1 + (shift - 1) * PARTS + p], -shift), 0) for p, cut in enumerate(even)]
                for shift in range(1, owners)
            ]
    span = (0, count)
    early = [arrived_parts(h, nz - 2 - h) for h in range(1, nz - 2)]
    late = [arrived_parts(h, nz - 2 - h) for h in range(nz - 1) if not 1 <= h < nz - 2]
    most = add_up(span, [whole(own_all[nz - 1]), whole(deltas[0]), y_parts(nz - 1)] + early)
    out = add_up(span, [whole(most)] + back + late)
    return out.reshape(steps, row_count, out_width)


def solution(mesh):
    placed = (
        P(None, ("groups", "dp"), "tensor"),
        P(("groups", "dp")),
        P("tensor", None),
        P(("groups", "dp"), None, "tensor"),
        P(("groups", "dp"), None, "tensor"),
    )
    return jax.shard_map(
        on_device,
        mesh=mesh,
        in_specs=placed,
        out_specs=P(None, ("groups", "dp"), "tensor"),
        check_vma=False,
    )
```

```python
import jax
import jax.numpy as jnp
import numpy as np
from jax import lax
from jax.experimental import pallas as pl
from jax.experimental.pallas import tpu as pltpu
from jax.sharding import PartitionSpec as P

SLOTS = 16
LANES = 128
CHUNK = 512
PARTS = 2
LOW_WITH = (0, PARTS - 1)
LOW_SUM_AFTER = (0, 2, 0)
EXPAND_AFTER = (1, 1, 1)
VMEM = 50 * 2**20
ANY = pl.BlockSpec(memory_space=pl.ANY)


def call(kernel, operands, after, *, in_specs, out_specs, out_shape, name, prefetch=0, scratch=(), alias=None):
    inputs, extra = len(operands), len(after)

    def body(*refs):
        kernel(*refs[:inputs], *refs[inputs + extra :])

    return pl.pallas_call(
        body,
        grid_spec=pltpu.PrefetchScalarGridSpec(
            num_scalar_prefetch=prefetch,
            grid=(),
            in_specs=list(in_specs) + [ANY] * extra,
            out_specs=out_specs,
            scratch_shapes=list(scratch),
        ),
        out_shape=out_shape,
        input_output_aliases=alias or {},
        compiler_params=pltpu.CompilerParams(vmem_limit_bytes=VMEM),
        cost_estimate=pl.CostEstimate(flops=1, transcendentals=0, bytes_accessed=1),
        name=name,
    )(*operands, *after)


def hold(value, after):
    def kernel(value_ref, out_ref):
        pass

    return call(
        kernel, [value], after, in_specs=[ANY], out_specs=ANY,
        out_shape=jax.ShapeDtypeStruct(value.shape, value.dtype), name="hold", alias={0: 0},
    )


def products(rows, weight, starts, names, size, outs, tail=None, chunk=1024, after=()):
    count, width = rows.shape
    blocks = len(names)
    chunks = [(at, min(chunk, size - at)) for at in range(0, size, chunk)]
    low = min(first for _, first, _ in outs)
    high = max(first + some for _, first, some in outs)
    upper = (high - low) // 32 * 16
    row_parts = [(0, upper), (upper, high - low - upper)]
    tails = [] if tail is None else [tail]
    heights = [some for _, _, some in outs]
    for array in tails:
        heights[-1] += array.shape[0]

    def kernel(starts_ref, rows_ref, weight_ref, *refs):
        tail_refs, refs = refs[: len(tails)], refs[len(tails) :]
        out_refs, (x, w, *refs) = refs[: len(outs)], refs[len(outs) :]
        stage, (x_sems, w_sems, out_sems, tail_sems) = refs[: len(outs)], refs[len(outs) :]
        x_copies = [
            pltpu.make_async_copy(
                rows_ref.at[pl.ds(low + at, some)], x.at[pl.ds(at, some)], x_sems.at[i]
            )
            for i, (at, some) in enumerate(row_parts)
        ]
        w_copies = [
            [
                pltpu.make_async_copy(
                    weight_ref.at[:, pl.ds(pl.multiple_of(starts_ref[names[b]] + at, LANES), extent)],
                    w.at[b, :, pl.ds(at, extent)],
                    w_sems.at[b, c],
                )
                for c, (at, extent) in enumerate(chunks)
            ]
            for b in range(blocks)
        ]
        x_copies[0].start()
        w_copies[0][0].start()
        x_copies[1].start()
        for b in range(blocks):
            for c in range(len(chunks)):
                if b or c:
                    w_copies[b][c].start()
        stores = []
        for ref in tail_refs:
            below = pl.ds(outs[-1][2], ref.shape[0])
            read = pltpu.make_async_copy(ref, stage[-1].at[below], tail_sems.at[0])
            read.start()
            read.wait()
            stores.append(pltpu.make_async_copy(stage[-1].at[below], out_refs[-1].at[below], tail_sems.at[1]))
            stores[-1].start()
        for copy in x_copies:
            copy.wait()
        for b in range(blocks):
            for c, (at, extent) in enumerate(chunks):
                w_copies[b][c].wait()
                for o, (index, first, some) in enumerate(outs):
                    if index == b:
                        value = jnp.dot(
                            x[first - low : first - low + some, :], w[b, :, at : at + extent],
                            preferred_element_type=jnp.float32,
                        )
                        stage[o][:some, at : at + extent] = value.astype(rows.dtype)
                        store = pltpu.make_async_copy(
                            stage[o].at[pl.ds(0, some), pl.ds(at, extent)],
                            out_refs[o].at[pl.ds(0, some), pl.ds(at, extent)],
                            out_sems.at[o, c],
                        )
                        store.start()
                        stores.append(store)
        for store in stores:
            store.wait()

    shapes = [(height, size) for height in heights]
    return call(
        kernel, [starts, rows, weight] + tails, after, prefetch=1,
        in_specs=[ANY] * (2 + len(tails)),
        out_specs=[ANY] * len(outs),
        out_shape=[jax.ShapeDtypeStruct(shape, rows.dtype) for shape in shapes],
        scratch=[pltpu.VMEM((high - low, width), rows.dtype), pltpu.VMEM((blocks, width, size), rows.dtype)]
        + [pltpu.VMEM(shape, rows.dtype) for shape in shapes]
        + [
            pltpu.SemaphoreType.DMA((2,)),
            pltpu.SemaphoreType.DMA((blocks, len(chunks))),
            pltpu.SemaphoreType.DMA((len(outs), len(chunks))),
            pltpu.SemaphoreType.DMA((2,)),
        ],
        name="products",
    )


def total(runs, dtype=jnp.bfloat16, into=None, after=()):
    width = runs[0][1][0][0].shape[1]
    height = sum(some for some, _ in runs)
    rows_in_all, first, so_far = into or (height, 0, None)
    tiles = []
    at = 0
    for r, (some, terms) in enumerate(runs):
        split = 4 if some * len(terms) > 2000 else 2 if some * width > 2**17 else 1
        size = -(-some // (16 * split)) * 16
        for skip in range(0, some, size):
            tiles.append((r, skip, min(size, some - skip), at + skip))
        at += some
    operands = [term for _, terms in runs for term, _ in terms]
    before = [] if so_far is None else [so_far]
    most_terms = max(len(terms) for _, terms in runs)
    of_run = np.cumsum([0] + [len(terms) for _, terms in runs])

    def kernel(*refs):
        term_refs, out_ref = refs[: len(operands)], refs[len(operands) + len(before)]
        refs = refs[len(operands) + len(before) + 1 :]
        bufs, (stage, in_sems, out_sems) = refs[: len(operands)], refs[len(operands) :]
        reads, writes = [], []
        for n, (r, skip, size, place) in enumerate(tiles):
            reads.append(
                [
                    pltpu.make_async_copy(
                        term_refs[of_run[r] + t].at[pl.ds(start + skip, size)],
                        bufs[of_run[r] + t].at[pl.ds(skip, size)],
                        in_sems.at[t, n],
                    )
                    for t, (_, start) in enumerate(runs[r][1])
                ]
            )
            writes.append(
                pltpu.make_async_copy(
                    stage.at[pl.ds(place, size)], out_ref.at[pl.ds(first + place, size)], out_sems.at[n]
                )
            )
        for some in reads:
            for read in some:
                read.start()
        for n, (r, skip, size, place) in enumerate(tiles):
            for read in reads[n]:
                read.wait()
            value = None
            for t in range(len(runs[r][1])):
                part = bufs[of_run[r] + t][skip : skip + size, :].astype(jnp.float32)
                value = part if value is None else value + part
            stage[place : place + size, :] = value.astype(dtype)
            writes[n].start()
        for write in writes:
            write.wait()

    return call(
        kernel, operands + before, after,
        in_specs=[ANY] * (len(operands) + len(before)),
        out_specs=ANY,
        out_shape=jax.ShapeDtypeStruct((rows_in_all, width), dtype),
        scratch=[pltpu.VMEM((some, width), term.dtype) for some, terms in runs for term, _ in terms]
        + [
            pltpu.VMEM((height, width), dtype),
            pltpu.SemaphoreType.DMA((most_terms, len(tiles))),
            pltpu.SemaphoreType.DMA((len(tiles),)),
        ],
        alias={len(operands): 0} if before else None,
        name="total",
    )


def lane_pick(slot_ref, repeats, shape, rank, first):
    slot = jnp.concatenate([slot_ref[...]] * repeats, axis=0)
    return slot == lax.broadcasted_iota(jnp.int32, shape, 1) // rank + first


def block_copies(index_ref, maps_ref, buf, sems, sets, rank):
    each = index_ref.shape[0] // sets
    return [
        [
            pltpu.make_async_copy(
                maps_ref.at[index_ref[s * each + i]], buf.at[pl.ds((s * each + i) * rank, rank)],
                sems.at[s * each + i],
            )
            for i in range(each)
        ]
        for s in range(sets)
    ]


def low_rank(row_sets, slot_sets, maps, index, wide, after=()):
    sets = len(row_sets)
    count, width = row_sets[0].shape
    rank = maps.shape[1]
    span = index.shape[0] // sets * rank
    repeats = count // slot_sets[0].shape[0]
    half = count // 2
    group = 256
    tall = sets * half * 2 * rank // wide

    def kernel(index_ref, *refs):
        row_refs, slot_refs, maps_ref, out_ref = refs[:sets], refs[sets : 2 * sets], refs[2 * sets], refs[2 * sets + 1]
        rows_buf, maps_buf, row_sems, map_sems = refs[2 * sets + 2 :]
        row_copies = [
            pltpu.make_async_copy(row_refs[s], rows_buf.at[s], row_sems.at[s]) for s in range(sets)
        ]
        map_copies = block_copies(index_ref, maps_ref, maps_buf, map_sems, sets, rank)
        for s in range(sets):
            row_copies[s].start()
            for copy in map_copies[s]:
                copy.start()
        for s in range(sets):
            row_copies[s].wait()
            for copy in map_copies[s]:
                copy.wait()
            acc = None
            for at in range(0, span, group):
                scores = lax.dot_general(
                    rows_buf[s], maps_buf[s * span + at : s * span + at + group],
                    (((1,), (1,)), ((), ())), preferred_element_type=jnp.float32,
                )
                pick = lane_pick(slot_refs[s], repeats, (count, group), rank, at // rank)
                term = jnp.where(pick, scores, 0.0)
                acc = term if acc is None else acc + term
            summed = acc[:, 0:rank]
            for g in range(1, group // rank):
                summed += acc[:, g * rank : (g + 1) * rank]
            summed = summed.astype(out_ref.dtype)
            for b in range(half // tall):
                lanes = slice((s * half // tall + b) * 2 * rank, (s * half // tall + b + 1) * 2 * rank)
                both = [summed[start + b * tall : start + (b + 1) * tall] for start in (0, half)]
                out_ref[:, lanes] = jnp.concatenate(both, axis=1)

    return call(
        kernel, [index, *row_sets, *slot_sets, maps], after, prefetch=1,
        in_specs=[ANY] * sets + [pl.BlockSpec(memory_space=pltpu.VMEM)] * sets + [ANY],
        out_specs=pl.BlockSpec(memory_space=pltpu.VMEM),
        out_shape=jax.ShapeDtypeStruct((tall, wide), jnp.bfloat16),
        scratch=[
            pltpu.VMEM((sets, count, width), row_sets[0].dtype),
            pltpu.VMEM((sets * span, width), maps.dtype),
            pltpu.SemaphoreType.DMA((sets,)),
            pltpu.SemaphoreType.DMA((index.shape[0],)),
        ],
        name="low_rank",
    )


def expand(low, slot_sets, maps, index, after=()):
    sets = len(slot_sets)
    rank, width = maps.shape[1:]
    tall = low.shape[0]
    half = low.size // sets // (2 * rank)
    count = 2 * half
    span = index.shape[0] // sets * rank
    repeats = count // slot_sets[0].shape[0]

    outs = [(0, 0, count)] + [
        (s, p * count // PARTS, count // PARTS) for s in range(1, sets) for p in range(PARTS)
    ]

    def kernel(index_ref, low_ref, *refs):
        slot_refs, maps_ref, out_refs = refs[:sets], refs[sets], refs[sets + 1 : sets + 1 + len(outs)]
        stage, maps_buf, map_sems, out_sems = refs[sets + 1 + len(outs) :]
        map_copies = block_copies(index_ref, maps_ref, maps_buf, map_sems, sets, rank)
        writes = [
            pltpu.make_async_copy(stage.at[s, pl.ds(first, some)], out_refs[o], out_sems.at[o])
            for o, (s, first, some) in enumerate(outs)
        ]
        order = list(range(1, sets)) + [0]
        for s in order:
            for copy in map_copies[s]:
                copy.start()
        for s in order:
            lanes = [(s * half // tall + b) * 2 * rank for b in range(half // tall)]
            mine = jnp.concatenate(
                [low_ref[:, at + side : at + side + rank] for side in (0, rank) for at in lanes], axis=0
            )
            tiled = jnp.concatenate([mine] * (span // rank), axis=1)
            pick = lane_pick(slot_refs[s], repeats, (count, span), rank, 0)
            picked = jnp.where(pick, tiled, jnp.zeros_like(tiled))
            for copy in map_copies[s]:
                copy.wait()
            for at in range(0, width, CHUNK):
                value = jnp.dot(
                    picked, maps_buf[s * span : (s + 1) * span, at : at + CHUNK], preferred_element_type=jnp.float32
                )
                stage[s, :, at : at + CHUNK] = value.astype(stage.dtype)
            for o, (which, _, _) in enumerate(outs):
                if which == s:
                    writes[o].start()
        for write in writes:
            write.wait()

    return call(
        kernel, [index, low, *slot_sets, maps], after, prefetch=1,
        in_specs=[pl.BlockSpec(memory_space=pltpu.VMEM)] * (1 + sets) + [ANY],
        out_specs=[ANY] * len(outs),
        out_shape=[jax.ShapeDtypeStruct((some, width), jnp.bfloat16) for _, _, some in outs],
        scratch=[
            pltpu.VMEM((sets, count, width), jnp.bfloat16),
            pltpu.VMEM((sets * span, width), maps.dtype),
            pltpu.SemaphoreType.DMA((index.shape[0],)),
            pltpu.SemaphoreType.DMA((len(outs),)),
        ],
        name="expand",
    )


def line_plan(nz):
    order = np.zeros((nz, nz), np.int32)
    for z in range(nz):
        def need(j):
            if j == z:
                return (2 * nz, 0)
            return (nz - 1 - j + z, j) if j > z else (nz - 1 - z + j, nz - j)

        order[z] = sorted(range(nz), key=need)
    return order


def on_device(attention_result, tenant, projection_weight, adapter_down_maps, adapter_up_maps):
    steps, row_count, width = attention_result.shape
    local_adapters = adapter_down_maps.shape[0]
    owners = lax.axis_size("dp")
    me = lax.axis_index("dp")
    n = lax.axis_size("tensor")
    nz = n // 2
    place = lax.axis_index("tensor")
    order = line_plan(nz)
    out_width = projection_weight.shape[1] // n

    def swap_y(value):
        return lax.ppermute(value, "tensor", [(t, t ^ 1) for t in range(n)])

    def hop(value, h):
        pairs = []
        for side in range(2):
            pairs.append((h * 2 + side, (h + 1) * 2 + side))
            pairs.append(((nz - 1 - h) * 2 + side, (nz - 2 - h) * 2 + side))
        return lax.ppermute(value, "tensor", pairs)

    def slot_of(h, m):
        return list(order[h]).index(nz - 1 - m)

    def pass_on(value, shift):
        return lax.ppermute(value, "dp", [(i, (i + shift) % owners) for i in range(owners)])

    rows = attention_result.reshape(steps * row_count, width)
    count = steps * row_count
    last = [()]

    def then(kernel, *operands, **options):
        out = kernel(*operands, after=last[0], **options)
        last[0] = (out[0] if isinstance(out, (tuple, list)) else out,)
        return out

    slot_range = jnp.arange(SLOTS, dtype=jnp.int32)
    ids = jnp.arange(local_adapters, dtype=jnp.int32)

    def slots(row_ids, owner):
        hit = row_ids[:, None] - owner * local_adapters == ids[None, :]
        used = jnp.any(hit, axis=0)
        position = jnp.sum(
            (used[None, :] & (ids[None, :] < ids[:, None])).astype(jnp.int32), axis=1
        )
        names = jnp.sum(
            jnp.where(used[None, :] & (position[None, :] == slot_range[:, None]), ids[None, :], 0),
            axis=1,
        )
        row_slot = jnp.sum(jnp.where(hit, position[None, :] + 1, 0), axis=1) - 1
        return names, row_slot[:, None]

    blocks = [[(order[t // 2][k] * 2 + side) for side in (1 - t % 2, t % 2) for k in range(nz)] for t in range(n)]
    starts = jnp.asarray(np.asarray(blocks, np.int32) * out_width)[place]
    low_rows = 2 * (owners * count // 2) * adapter_down_maps.shape[1] // out_width
    even = [(p * count // PARTS, count // PARTS) for p in range(PARTS)]
    uneven = [(0, (count + low_rows) // 2), ((count + low_rows) // 2, (count - low_rows) // 2)]
    away_part, own_all, from_y, sums, arrived = {}, {}, {}, {}, {}

    def split(k):
        return uneven if k == 0 else [(0, count)]

    def add_up(span, terms, extra=(), dtype=jnp.bfloat16, into=None):
        low_row, high_row = span[0], span[0] + span[1]
        cuts = {low_row, high_row}
        for term in terms:
            for at, some, _, _ in term:
                cuts.update(row for row in (at, at + some) if low_row < row < high_row)
        cuts = sorted(cuts)
        runs = []
        for begin, end in zip(cuts, cuts[1:]):
            here = [
                (array, row + begin - at) for term in terms for at, some, array, row in term if at <= begin < at + some
            ]
            runs.append((end - begin, here))
        return then(total, runs + list(extra), dtype, into)

    def whole(array):
        return [(0, count, array, 0)]

    def multiply(aways, owns, tail=None, chunk=1024):
        ks = sorted({k for k, _ in aways})
        names = ks + [nz + k for k in owns]
        outs = [(ks.index(k), *split(k)[p]) for k, p in aways]
        outs += [(len(ks) + i, 0, count) for i in range(len(owns))]
        done = then(products, rows, projection_weight, starts, names, out_width, outs, tail, chunk)
        away_part.update(zip(aways, done))
        own_all.update(zip(owns, done[len(aways) :]))

    def start_y(k, p, after=None):
        value = away_part[k, p]
        from_y[k, p] = swap_y(value if after is None else hold(value, after))

    def y_parts(k):
        return [(*cut, from_y[k, p], 0) for p, cut in enumerate(split(k)) if (k, p) in from_y]

    def sum_parts(k):
        return [(*cut, sums[k, p], 0) for p, cut in enumerate(cut_of(0, k)) if (k, p) in sums]

    def cut_of(h, m):
        if m == 0 and h <= 1:
            return uneven
        return [(0, count * 7 // 16), (count * 7 // 16, count * 9 // 16)] if m == 1 else [(0, count)]

    def arrived_parts(h, m):
        return [(*cut, arrived[h, m, p], 0) for p, cut in enumerate(cut_of(h, m)) if (h, m, p) in arrived]

    def line(h, m, p):
        k = slot_of(h, m)
        span = cut_of(h, m)[p]
        low_too = m == 0 and h <= 1 and p == LOW_WITH[1]
        if h == 0:
            extra = [(low_rows, [(low, 0), (from_y[k, p], span[1])])] if low_too else []
            value = sums[k, p] = add_up(span, [whole(own_all[k]), y_parts(k)], extra)
        else:
            extra = [(low_rows, [(sums[k, p], span[1]), (arrived[h - 1, m, p], span[1])])] if low_too else []
            value = add_up(span, [sum_parts(k), arrived_parts(h - 1, m)], extra)
        arrived[h, m, p] = hop(value, h)

    def line_order():
        ready, free = {}, {}
        steps = [(h, m, p) for h in range(nz - 1) for m in range(nz - 1 - h) for p in range(len(cut_of(h, m)))]
        for h, m, p in sorted(steps, key=lambda step: (step[0], step[1], step[2])):
            k = slot_of(h, m)
            there = (k + 1.0) * count if k or p else 1.0 * cut_of(0, 0)[0][1]
            if h:
                above = range(len(cut_of(h - 1, m)))
                there = max(there, max(ready[h - 1, m, q, "end"] for q in above if q == p or len(above) != len(cut_of(h, m))))
            ready[h, m, p] = there
            free[h] = max(there, free.get(h, 0.0)) + cut_of(h, m)[p][1]
            ready[h, m, p, "end"] = free[h]
        return sorted(steps, key=lambda step: (ready[step], step[0] and nz - step[0]))

    row_ids = [tenant] + [pass_on(tenant, shift) for shift in range(1, owners)]
    row_sets = [rows] + [pass_on(rows, shift) for shift in range(1, owners)]
    multiply([(0, 0)], [], chunk=512)
    start_y(0, 0)
    named = [slots(some_ids, me) for some_ids in row_ids]
    names = jnp.concatenate([which for which, _ in named])
    slot_sets = [row_slot for _, row_slot in named]
    low = then(low_rank, row_sets, slot_sets, adapter_down_maps, names, out_width)
    multiply([LOW_WITH], [], low, chunk=512)
    start_y(*LOW_WITH)
    multiply([(1, 0)], [0])
    start_y(1, 0)
    low_sum = deltas = None
    for h, m, p in line_order():
        k = slot_of(h, m)
        line(h, m, p)
        if h == 0:
            if k == 0 and p == 0:
                multiply([(2, 0)] if nz > 2 else [], [1])
            elif k == 0:
                if nz > 2:
                    start_y(2, 0, last[0])
                multiply([(j, 0) for j in range(3, nz)], range(2, nz))
            elif p == len(cut_of(h, m)) - 1 and k + 2 < nz:
                start_y(k + 2, 0, last[0])
        if (h, k, p) == (0, 1, len(cut_of(h, m)) - 1):
            low_at = uneven[LOW_WITH[1]][1]
            pieces = [(sums[LOW_WITH], low_at)]
            last[0] += (arrived[1, 0, 0],) if nz > 2 else ()
            for step in range(nz - 1):
                if step >= 2:
                    prefix = then(total, [(low_rows, [pieces[0], pieces[-1]])])
                    pieces.append((hop(prefix, step), 0))
                else:
                    pieces.append((arrived[step, 0, LOW_WITH[1]], low_at))
        if (h, m, p) == LOW_SUM_AFTER:
            low_sum = then(total, [(low_rows, pieces)])
        if deltas is None and low_sum is not None and EXPAND_AFTER in arrived:
            last[0] += (arrived[1, 1, 0],) if nz > 2 else ()
            deltas = then(expand, low_sum, slot_sets, adapter_up_maps, names)
            back = [
                [(*cut, pass_on(deltas[1 + (shift - 1) * PARTS + p], -shift), 0) for p, cut in enumerate(even)]
                for shift in range(1, owners)
            ]
    span = (0, count)
    early = [arrived_parts(h, nz - 2 - h) for h in range(1, nz - 2)]
    late = [arrived_parts(h, nz - 2 - h) for h in range(nz - 1) if not 1 <= h < nz - 2]
    most = add_up(span, [whole(own_all[nz - 1]), whole(deltas[0]), y_parts(nz - 1)] + early)
    out = add_up(span, [whole(most)] + back + late)
    return out.reshape(steps, row_count, out_width)


def solution(mesh):
    placed = (
        P(None, ("groups", "dp"), "tensor"),
        P(("groups", "dp")),
        P("tensor", None),
        P(("groups", "dp"), None, "tensor"),
        P(("groups", "dp"), None, "tensor"),
    )
    return jax.shard_map(
        on_device,
        mesh=mesh,
        in_specs=placed,
        out_specs=P(None, ("groups", "dp"), "tensor"),
        check_vma=False,
    )
```

```python
import jax
import jax.numpy as jnp
import numpy as np
from jax import lax
from jax.experimental import pallas as pl
from jax.experimental.pallas import tpu as pltpu
from jax.sharding import PartitionSpec as P

SLOTS = 16
LANES = 128
CHUNK = 512
PARTS = 2
LOW_WITH = (0, PARTS - 1)
LOW_SUM_AFTER = (0, 2, 0)
EXPAND_AFTER = (1, 1, 1)
VMEM = 50 * 2**20
ANY = pl.BlockSpec(memory_space=pl.ANY)


def call(kernel, operands, after, *, in_specs, out_specs, out_shape, name, prefetch=0, scratch=(), alias=None, vmem=VMEM):
    inputs, extra = len(operands), len(after)

    def body(*refs):
        kernel(*refs[:inputs], *refs[inputs + extra :])

    return pl.pallas_call(
        body,
        grid_spec=pltpu.PrefetchScalarGridSpec(
            num_scalar_prefetch=prefetch,
            grid=(),
            in_specs=list(in_specs) + [ANY] * extra,
            out_specs=out_specs,
            scratch_shapes=list(scratch),
        ),
        out_shape=out_shape,
        input_output_aliases=alias or {},
        compiler_params=pltpu.CompilerParams(vmem_limit_bytes=vmem),
        cost_estimate=pl.CostEstimate(flops=1, transcendentals=0, bytes_accessed=1),
        name=name,
    )(*operands, *after)


def hold(value, after):
    def kernel(value_ref, out_ref):
        pass

    return call(
        kernel, [value], after, in_specs=[ANY], out_specs=ANY,
        out_shape=jax.ShapeDtypeStruct(value.shape, value.dtype), name="hold", alias={0: 0},
    )


def products(rows, weight, starts, names, size, outs, tail=None, chunk=1024, vmem=VMEM, after=()):
    count, width = rows.shape
    blocks = len(names)
    chunks = [(at, min(chunk, size - at)) for at in range(0, size, chunk)]
    low = min(first for _, first, _ in outs)
    high = max(first + some for _, first, some in outs)
    upper = (high - low) // 32 * 16
    row_parts = [(0, upper), (upper, high - low - upper)]
    tails = [] if tail is None else [tail]
    heights = [some for _, _, some in outs]
    for array in tails:
        heights[-1] += array.shape[0]

    def kernel(starts_ref, rows_ref, weight_ref, *refs):
        tail_refs, refs = refs[: len(tails)], refs[len(tails) :]
        out_refs, (x, w, *refs) = refs[: len(outs)], refs[len(outs) :]
        stage, (x_sems, w_sems, out_sems, tail_sems) = refs[: len(outs)], refs[len(outs) :]
        x_copies = [
            pltpu.make_async_copy(
                rows_ref.at[pl.ds(low + at, some)], x.at[pl.ds(at, some)], x_sems.at[i]
            )
            for i, (at, some) in enumerate(row_parts)
        ]
        w_copies = [
            [
                pltpu.make_async_copy(
                    weight_ref.at[:, pl.ds(pl.multiple_of(starts_ref[names[b]] + at, LANES), extent)],
                    w.at[b, :, pl.ds(at, extent)],
                    w_sems.at[b, c],
                )
                for c, (at, extent) in enumerate(chunks)
            ]
            for b in range(blocks)
        ]
        x_copies[0].start()
        w_copies[0][0].start()
        x_copies[1].start()
        for b in range(blocks):
            for c in range(len(chunks)):
                if b or c:
                    w_copies[b][c].start()
        stores = []
        for ref in tail_refs:
            below = pl.ds(outs[-1][2], ref.shape[0])
            read = pltpu.make_async_copy(ref, stage[-1].at[below], tail_sems.at[0])
            read.start()
            read.wait()
            stores.append(pltpu.make_async_copy(stage[-1].at[below], out_refs[-1].at[below], tail_sems.at[1]))
            stores[-1].start()
        for copy in x_copies:
            copy.wait()
        for b in range(blocks):
            for c, (at, extent) in enumerate(chunks):
                w_copies[b][c].wait()
                for o, (index, first, some) in enumerate(outs):
                    if index == b:
                        value = jnp.dot(
                            x[first - low : first - low + some, :], w[b, :, at : at + extent],
                            preferred_element_type=jnp.float32,
                        )
                        stage[o][:some, at : at + extent] = value.astype(rows.dtype)
                        store = pltpu.make_async_copy(
                            stage[o].at[pl.ds(0, some), pl.ds(at, extent)],
                            out_refs[o].at[pl.ds(0, some), pl.ds(at, extent)],
                            out_sems.at[o, c],
                        )
                        store.start()
                        stores.append(store)
        for store in stores:
            store.wait()

    shapes = [(height, size) for height in heights]
    return call(
        kernel, [starts, rows, weight] + tails, after, prefetch=1,
        in_specs=[ANY] * (2 + len(tails)),
        out_specs=[ANY] * len(outs),
        out_shape=[jax.ShapeDtypeStruct(shape, rows.dtype) for shape in shapes],
        scratch=[pltpu.VMEM((high - low, width), rows.dtype), pltpu.VMEM((blocks, width, size), rows.dtype)]
        + [pltpu.VMEM(shape, rows.dtype) for shape in shapes]
        + [
            pltpu.SemaphoreType.DMA((2,)),
            pltpu.SemaphoreType.DMA((blocks, len(chunks))),
            pltpu.SemaphoreType.DMA((len(outs), len(chunks))),
            pltpu.SemaphoreType.DMA((2,)),
        ],
        name="products", vmem=vmem,
    )


def total(runs, dtype=jnp.bfloat16, into=None, after=()):
    width = runs[0][1][0][0].shape[1]
    height = sum(some for some, _ in runs)
    rows_in_all, first, so_far = into or (height, 0, None)
    tiles = []
    at = 0
    for r, (some, terms) in enumerate(runs):
        split = 4 if some * len(terms) > 2000 else 2 if some * width > 2**17 else 1
        size = -(-some // (16 * split)) * 16
        for skip in range(0, some, size):
            tiles.append((r, skip, min(size, some - skip), at + skip))
        at += some
    operands = [term for _, terms in runs for term, _ in terms]
    before = [] if so_far is None else [so_far]
    most_terms = max(len(terms) for _, terms in runs)
    of_run = np.cumsum([0] + [len(terms) for _, terms in runs])

    def kernel(*refs):
        term_refs, out_ref = refs[: len(operands)], refs[len(operands) + len(before)]
        refs = refs[len(operands) + len(before) + 1 :]
        bufs, (stage, in_sems, out_sems) = refs[: len(operands)], refs[len(operands) :]
        reads, writes = [], []
        for n, (r, skip, size, place) in enumerate(tiles):
            reads.append(
                [
                    pltpu.make_async_copy(
                        term_refs[of_run[r] + t].at[pl.ds(start + skip, size)],
                        bufs[of_run[r] + t].at[pl.ds(skip, size)],
                        in_sems.at[t, n],
                    )
                    for t, (_, start) in enumerate(runs[r][1])
                ]
            )
            writes.append(
                pltpu.make_async_copy(
                    stage.at[pl.ds(place, size)], out_ref.at[pl.ds(first + place, size)], out_sems.at[n]
                )
            )
        for some in reads:
            for read in some:
                read.start()
        for n, (r, skip, size, place) in enumerate(tiles):
            for read in reads[n]:
                read.wait()
            value = None
            for t in range(len(runs[r][1])):
                part = bufs[of_run[r] + t][skip : skip + size, :].astype(jnp.float32)
                value = part if value is None else value + part
            stage[place : place + size, :] = value.astype(dtype)
            writes[n].start()
        for write in writes:
            write.wait()

    return call(
        kernel, operands + before, after,
        in_specs=[ANY] * (len(operands) + len(before)),
        out_specs=ANY,
        out_shape=jax.ShapeDtypeStruct((rows_in_all, width), dtype),
        scratch=[pltpu.VMEM((some, width), term.dtype) for some, terms in runs for term, _ in terms]
        + [
            pltpu.VMEM((height, width), dtype),
            pltpu.SemaphoreType.DMA((most_terms, len(tiles))),
            pltpu.SemaphoreType.DMA((len(tiles),)),
        ],
        alias={len(operands): 0} if before else None,
        name="total",
    )


def lane_pick(slot_ref, repeats, shape, rank, first):
    slot = jnp.concatenate([slot_ref[...]] * repeats, axis=0)
    return slot == lax.broadcasted_iota(jnp.int32, shape, 1) // rank + first


def block_copies(index_ref, maps_ref, buf, sems, sets, rank):
    each = index_ref.shape[0] // sets
    return [
        [
            pltpu.make_async_copy(
                maps_ref.at[index_ref[s * each + i]], buf.at[pl.ds((s * each + i) * rank, rank)],
                sems.at[s * each + i],
            )
            for i in range(each)
        ]
        for s in range(sets)
    ]


def low_rank(row_sets, slot_sets, maps, index, wide, after=()):
    sets = len(row_sets)
    count, width = row_sets[0].shape
    rank = maps.shape[1]
    span = index.shape[0] // sets * rank
    repeats = count // slot_sets[0].shape[0]
    half = count // 2
    group = 256
    tall = sets * half * 2 * rank // wide

    def kernel(index_ref, *refs):
        row_refs, slot_refs, maps_ref, out_ref = refs[:sets], refs[sets : 2 * sets], refs[2 * sets], refs[2 * sets + 1]
        rows_buf, maps_buf, row_sems, map_sems = refs[2 * sets + 2 :]
        row_copies = [
            pltpu.make_async_copy(row_refs[s], rows_buf.at[s], row_sems.at[s]) for s in range(sets)
        ]
        map_copies = block_copies(index_ref, maps_ref, maps_buf, map_sems, sets, rank)
        for s in range(sets):
            row_copies[s].start()
            for copy in map_copies[s]:
                copy.start()
        for s in range(sets):
            row_copies[s].wait()
            for copy in map_copies[s]:
                copy.wait()
            acc = None
            for at in range(0, span, group):
                scores = lax.dot_general(
                    rows_buf[s], maps_buf[s * span + at : s * span + at + group],
                    (((1,), (1,)), ((), ())), preferred_element_type=jnp.float32,
                )
                pick = lane_pick(slot_refs[s], repeats, (count, group), rank, at // rank)
                term = jnp.where(pick, scores, 0.0)
                acc = term if acc is None else acc + term
            summed = acc[:, 0:rank]
            for g in range(1, group // rank):
                summed += acc[:, g * rank : (g + 1) * rank]
            summed = summed.astype(out_ref.dtype)
            for b in range(half // tall):
                lanes = slice((s * half // tall + b) * 2 * rank, (s * half // tall + b + 1) * 2 * rank)
                both = [summed[start + b * tall : start + (b + 1) * tall] for start in (0, half)]
                out_ref[:, lanes] = jnp.concatenate(both, axis=1)

    return call(
        kernel, [index, *row_sets, *slot_sets, maps], after, prefetch=1,
        in_specs=[ANY] * sets + [pl.BlockSpec(memory_space=pltpu.VMEM)] * sets + [ANY],
        out_specs=pl.BlockSpec(memory_space=pltpu.VMEM),
        out_shape=jax.ShapeDtypeStruct((tall, wide), jnp.bfloat16),
        scratch=[
            pltpu.VMEM((sets, count, width), row_sets[0].dtype),
            pltpu.VMEM((sets * span, width), maps.dtype),
            pltpu.SemaphoreType.DMA((sets,)),
            pltpu.SemaphoreType.DMA((index.shape[0],)),
        ],
        name="low_rank",
    )


def expand(low, slot_sets, maps, index, after=()):
    sets = len(slot_sets)
    rank, width = maps.shape[1:]
    tall = low.shape[0]
    half = low.size // sets // (2 * rank)
    count = 2 * half
    span = index.shape[0] // sets * rank
    repeats = count // slot_sets[0].shape[0]

    outs = [(0, 0, count)] + [
        (s, p * count // PARTS, count // PARTS) for s in range(1, sets) for p in range(PARTS)
    ]

    def kernel(index_ref, low_ref, *refs):
        slot_refs, maps_ref, out_refs = refs[:sets], refs[sets], refs[sets + 1 : sets + 1 + len(outs)]
        stage, maps_buf, map_sems, out_sems = refs[sets + 1 + len(outs) :]
        map_copies = block_copies(index_ref, maps_ref, maps_buf, map_sems, sets, rank)
        writes = [
            pltpu.make_async_copy(stage.at[s, pl.ds(first, some)], out_refs[o], out_sems.at[o])
            for o, (s, first, some) in enumerate(outs)
        ]
        order = list(range(1, sets)) + [0]
        for s in order:
            for copy in map_copies[s]:
                copy.start()
        for s in order:
            lanes = [(s * half // tall + b) * 2 * rank for b in range(half // tall)]
            mine = jnp.concatenate(
                [low_ref[:, at + side : at + side + rank] for side in (0, rank) for at in lanes], axis=0
            )
            tiled = jnp.concatenate([mine] * (span // rank), axis=1)
            pick = lane_pick(slot_refs[s], repeats, (count, span), rank, 0)
            picked = jnp.where(pick, tiled, jnp.zeros_like(tiled))
            for copy in map_copies[s]:
                copy.wait()
            for at in range(0, width, CHUNK):
                value = jnp.dot(
                    picked, maps_buf[s * span : (s + 1) * span, at : at + CHUNK], preferred_element_type=jnp.float32
                )
                stage[s, :, at : at + CHUNK] = value.astype(stage.dtype)
            for o, (which, _, _) in enumerate(outs):
                if which == s:
                    writes[o].start()
        for write in writes:
            write.wait()

    return call(
        kernel, [index, low, *slot_sets, maps], after, prefetch=1,
        in_specs=[pl.BlockSpec(memory_space=pltpu.VMEM)] * (1 + sets) + [ANY],
        out_specs=[ANY] * len(outs),
        out_shape=[jax.ShapeDtypeStruct((some, width), jnp.bfloat16) for _, _, some in outs],
        scratch=[
            pltpu.VMEM((sets, count, width), jnp.bfloat16),
            pltpu.VMEM((sets * span, width), maps.dtype),
            pltpu.SemaphoreType.DMA((index.shape[0],)),
            pltpu.SemaphoreType.DMA((len(outs),)),
        ],
        name="expand",
    )


def line_plan(nz):
    order = np.zeros((nz, nz), np.int32)
    for z in range(nz):
        def need(j):
            if j == z:
                return (2 * nz, 0)
            return (nz - 1 - j + z, j) if j > z else (nz - 1 - z + j, nz - j)

        order[z] = sorted(range(nz), key=need)
    return order


def on_device(attention_result, tenant, projection_weight, adapter_down_maps, adapter_up_maps):
    steps, row_count, width = attention_result.shape
    local_adapters = adapter_down_maps.shape[0]
    owners = lax.axis_size("dp")
    me = lax.axis_index("dp")
    n = lax.axis_size("tensor")
    nz = n // 2
    place = lax.axis_index("tensor")
    order = line_plan(nz)
    out_width = projection_weight.shape[1] // n

    def swap_y(value):
        return lax.ppermute(value, "tensor", [(t, t ^ 1) for t in range(n)])

    def hop(value, h):
        pairs = []
        for side in range(2):
            pairs.append((h * 2 + side, (h + 1) * 2 + side))
            pairs.append(((nz - 1 - h) * 2 + side, (nz - 2 - h) * 2 + side))
        return lax.ppermute(value, "tensor", pairs)

    def slot_of(h, m):
        return list(order[h]).index(nz - 1 - m)

    def pass_on(value, shift):
        return lax.ppermute(value, "dp", [(i, (i + shift) % owners) for i in range(owners)])

    rows = attention_result.reshape(steps * row_count, width)
    count = steps * row_count
    last = [()]

    def then(kernel, *operands, **options):
        out = kernel(*operands, after=last[0], **options)
        last[0] = (out[0] if isinstance(out, (tuple, list)) else out,)
        return out

    slot_range = jnp.arange(SLOTS, dtype=jnp.int32)
    ids = jnp.arange(local_adapters, dtype=jnp.int32)

    def slots(row_ids, owner):
        hit = row_ids[:, None] - owner * local_adapters == ids[None, :]
        used = jnp.any(hit, axis=0)
        position = jnp.sum(
            (used[None, :] & (ids[None, :] < ids[:, None])).astype(jnp.int32), axis=1
        )
        names = jnp.sum(
            jnp.where(used[None, :] & (position[None, :] == slot_range[:, None]), ids[None, :], 0),
            axis=1,
        )
        row_slot = jnp.sum(jnp.where(hit, position[None, :] + 1, 0), axis=1) - 1
        return names, row_slot[:, None]

    blocks = [[(order[t // 2][k] * 2 + side) for side in (1 - t % 2, t % 2) for k in range(nz)] for t in range(n)]
    starts = jnp.asarray(np.asarray(blocks, np.int32) * out_width)[place]
    low_rows = 2 * (owners * count // 2) * adapter_down_maps.shape[1] // out_width
    even = [(p * count // PARTS, count // PARTS) for p in range(PARTS)]
    uneven = [(0, (count + low_rows) // 2), ((count + low_rows) // 2, (count - low_rows) // 2)]
    away_part, own_all, from_y, sums, arrived = {}, {}, {}, {}, {}

    def split(k):
        return uneven if k == 0 else [(0, count)]

    def add_up(span, terms, extra=(), dtype=jnp.bfloat16, into=None):
        low_row, high_row = span[0], span[0] + span[1]
        cuts = {low_row, high_row}
        for term in terms:
            for at, some, _, _ in term:
                cuts.update(row for row in (at, at + some) if low_row < row < high_row)
        cuts = sorted(cuts)
        runs = []
        for begin, end in zip(cuts, cuts[1:]):
            here = [
                (array, row + begin - at) for term in terms for at, some, array, row in term if at <= begin < at + some
            ]
            runs.append((end - begin, here))
        return then(total, runs + list(extra), dtype, into)

    def whole(array):
        return [(0, count, array, 0)]

    def multiply(aways, owns, tail=None, chunk=1024, vmem=VMEM):
        ks = sorted({k for k, _ in aways})
        names = ks + [nz + k for k in owns]
        outs = [(ks.index(k), *split(k)[p]) for k, p in aways]
        outs += [(len(ks) + i, 0, count) for i in range(len(owns))]
        done = then(products, rows, projection_weight, starts, names, out_width, outs, tail, chunk, vmem)
        away_part.update(zip(aways, done))
        own_all.update(zip(owns, done[len(aways) :]))

    def start_y(k, p, after=None):
        value = away_part[k, p]
        from_y[k, p] = swap_y(value if after is None else hold(value, after))

    def y_parts(k):
        return [(*cut, from_y[k, p], 0) for p, cut in enumerate(split(k)) if (k, p) in from_y]

    def sum_parts(k):
        return [(*cut, sums[k, p], 0) for p, cut in enumerate(cut_of(0, k)) if (k, p) in sums]

    def cut_of(h, m):
        if m == 0 and h <= 1:
            return uneven
        return [(0, count * 8 // 16), (count * 8 // 16, count * 8 // 16)] if m == 1 else [(0, count)]

    def arrived_parts(h, m):
        return [(*cut, arrived[h, m, p], 0) for p, cut in enumerate(cut_of(h, m)) if (h, m, p) in arrived]

    def line(h, m, p):
        k = slot_of(h, m)
        span = cut_of(h, m)[p]
        low_too = m == 0 and h <= 1 and p == LOW_WITH[1]
        if h == 0:
            extra = [(low_rows, [(low, 0), (from_y[k, p], span[1])])] if low_too else []
            value = sums[k, p] = add_up(span, [whole(own_all[k]), y_parts(k)], extra)
        else:
            extra = [(low_rows, [(sums[k, p], span[1]), (arrived[h - 1, m, p], span[1])])] if low_too else []
            value = add_up(span, [sum_parts(k), arrived_parts(h - 1, m)], extra)
        arrived[h, m, p] = hop(value, h)

    def line_order():
        ready, free = {}, {}
        steps = [(h, m, p) for h in range(nz - 1) for m in range(nz - 1 - h) for p in range(len(cut_of(h, m)))]
        for h, m, p in sorted(steps, key=lambda step: (step[0], step[1], step[2])):
            k = slot_of(h, m)
            there = (k + 1.0) * count if k or p else 1.0 * cut_of(0, 0)[0][1]
            if h:
                above = range(len(cut_of(h - 1, m)))
                there = max(there, max(ready[h - 1, m, q, "end"] for q in above if q == p or len(above) != len(cut_of(h, m))))
            ready[h, m, p] = there
            free[h] = max(there, free.get(h, 0.0)) + cut_of(h, m)[p][1]
            ready[h, m, p, "end"] = free[h]
        return sorted(steps, key=lambda step: (ready[step], step[0] and nz - step[0]))

    row_ids = [tenant] + [pass_on(tenant, shift) for shift in range(1, owners)]
    row_sets = [rows] + [pass_on(rows, shift) for shift in range(1, owners)]
    multiply([(0, 0)], [], chunk=512, vmem=VMEM + 13 * 2**20)
    start_y(0, 0)
    named = [slots(some_ids, me) for some_ids in row_ids]
    names = jnp.concatenate([which for which, _ in named])
    slot_sets = [row_slot for _, row_slot in named]
    low = then(low_rank, row_sets, slot_sets, adapter_down_maps, names, out_width)
    multiply([LOW_WITH], [], low, chunk=512)
    start_y(*LOW_WITH)
    multiply([(1, 0)], [0])
    start_y(1, 0)
    low_sum = deltas = None
    for h, m, p in line_order():
        k = slot_of(h, m)
        if (h, m, p) == (2, 0, 0) and nz == 4:
            last[0] += (arrived[0, 1, 1],)
        line(h, m, p)
        if h == 0:
            if k == 0 and p == 0:
                multiply([(2, 0)] if nz > 2 else [], [1])
            elif k == 0:
                if nz > 2:
                    start_y(2, 0, last[0])
                multiply([(j, 0) for j in range(3, nz)], range(2, nz))
            elif p == len(cut_of(h, m)) - 1 and k + 2 < nz:
                start_y(k + 2, 0, last[0])
        if (h, k, p) == (0, 1, len(cut_of(h, m)) - 1):
            low_at = uneven[LOW_WITH[1]][1]
            pieces = [(sums[LOW_WITH], low_at)]
            last[0] += (arrived[1, 0, 0],) if nz > 2 else ()
            for step in range(nz - 1):
                if step >= 2:
                    prefix = then(total, [(low_rows, [pieces[0], pieces[-1]])])
                    pieces.append((hop(prefix, step), 0))
                else:
                    pieces.append((arrived[step, 0, LOW_WITH[1]], low_at))
        if (h, m, p) == LOW_SUM_AFTER:
            low_sum = then(total, [(low_rows, pieces)])
        if deltas is None and low_sum is not None and EXPAND_AFTER in arrived:
            last[0] += (arrived[1, 1, 0],) if nz > 2 else ()
            deltas = then(expand, low_sum, slot_sets, adapter_up_maps, names)
            back = [
                [(*cut, pass_on(deltas[1 + (shift - 1) * PARTS + p], -shift), 0) for p, cut in enumerate(even)]
                for shift in range(1, owners)
            ]
    span = (0, count)
    early = [arrived_parts(h, nz - 2 - h) for h in range(1, nz - 2)]
    late = [arrived_parts(h, nz - 2 - h) for h in range(nz - 1) if not 1 <= h < nz - 2]
    most = add_up(span, [whole(own_all[nz - 1]), whole(deltas[0]), y_parts(nz - 1)] + early)
    out = add_up(span, [whole(most)] + back + late)
    return out.reshape(steps, row_count, out_width)


def solution(mesh):
    placed = (
        P(None, ("groups", "dp"), "tensor"),
        P(("groups", "dp")),
        P("tensor", None),
        P(("groups", "dp"), None, "tensor"),
        P(("groups", "dp"), None, "tensor"),
    )
    return jax.shard_map(
        on_device,
        mesh=mesh,
        in_specs=placed,
        out_specs=P(None, ("groups", "dp"), "tensor"),
        check_vma=False,
    )
```

```python
import jax
import jax.numpy as jnp
import numpy as np
from jax import lax
from jax.experimental import pallas as pl
from jax.experimental.pallas import tpu as pltpu
from jax.sharding import PartitionSpec as P

SLOTS = 16
LANES = 128
CHUNK = 512
PARTS = 2
LOW_WITH = (0, PARTS - 1)
LOW_SUM_AFTER = (0, 2, 0)
EXPAND_AFTER = (1, 1, 1)
VMEM = 50 * 2**20
ANY = pl.BlockSpec(memory_space=pl.ANY)


def call(kernel, operands, after, *, in_specs, out_specs, out_shape, name, prefetch=0, scratch=(), alias=None, vmem=VMEM):
    inputs, extra = len(operands), len(after)

    def body(*refs):
        kernel(*refs[:inputs], *refs[inputs + extra :])

    return pl.pallas_call(
        body,
        grid_spec=pltpu.PrefetchScalarGridSpec(
            num_scalar_prefetch=prefetch,
            grid=(),
            in_specs=list(in_specs) + [ANY] * extra,
            out_specs=out_specs,
            scratch_shapes=list(scratch),
        ),
        out_shape=out_shape,
        input_output_aliases=alias or {},
        compiler_params=pltpu.CompilerParams(vmem_limit_bytes=vmem),
        cost_estimate=pl.CostEstimate(flops=1, transcendentals=0, bytes_accessed=1),
        name=name,
    )(*operands, *after)


def hold(value, after):
    def kernel(value_ref, out_ref):
        pass

    return call(
        kernel, [value], after, in_specs=[ANY], out_specs=ANY,
        out_shape=jax.ShapeDtypeStruct(value.shape, value.dtype), name="hold", alias={0: 0},
    )


def products(rows, weight, starts, names, size, outs, tail=None, chunk=1024, vmem=VMEM, after=()):
    count, width = rows.shape
    blocks = len(names)
    chunks = [(at, min(chunk, size - at)) for at in range(0, size, chunk)]
    low = min(first for _, first, _ in outs)
    high = max(first + some for _, first, some in outs)
    upper = (high - low) // 32 * 16
    row_parts = [(0, upper), (upper, high - low - upper)]
    tails = [] if tail is None else [tail]
    heights = [some for _, _, some in outs]
    for array in tails:
        heights[-1] += array.shape[0]

    def kernel(starts_ref, rows_ref, weight_ref, *refs):
        tail_refs, refs = refs[: len(tails)], refs[len(tails) :]
        out_refs, (x, w, *refs) = refs[: len(outs)], refs[len(outs) :]
        stage, (x_sems, w_sems, out_sems, tail_sems) = refs[: len(outs)], refs[len(outs) :]
        x_copies = [
            pltpu.make_async_copy(
                rows_ref.at[pl.ds(low + at, some)], x.at[pl.ds(at, some)], x_sems.at[i]
            )
            for i, (at, some) in enumerate(row_parts)
        ]
        w_copies = [
            [
                pltpu.make_async_copy(
                    weight_ref.at[:, pl.ds(pl.multiple_of(starts_ref[names[b]] + at, LANES), extent)],
                    w.at[b, :, pl.ds(at, extent)],
                    w_sems.at[b, c],
                )
                for c, (at, extent) in enumerate(chunks)
            ]
            for b in range(blocks)
        ]
        x_copies[0].start()
        w_copies[0][0].start()
        x_copies[1].start()
        for b in range(blocks):
            for c in range(len(chunks)):
                if b or c:
                    w_copies[b][c].start()
        stores = []
        for ref in tail_refs:
            below = pl.ds(outs[-1][2], ref.shape[0])
            read = pltpu.make_async_copy(ref, stage[-1].at[below], tail_sems.at[0])
            read.start()
            read.wait()
            stores.append(pltpu.make_async_copy(stage[-1].at[below], out_refs[-1].at[below], tail_sems.at[1]))
            stores[-1].start()
        for copy in x_copies:
            copy.wait()
        for b in range(blocks):
            for c, (at, extent) in enumerate(chunks):
                w_copies[b][c].wait()
                for o, (index, first, some) in enumerate(outs):
                    if index == b:
                        value = jnp.dot(
                            x[first - low : first - low + some, :], w[b, :, at : at + extent],
                            preferred_element_type=jnp.float32,
                        )
                        stage[o][:some, at : at + extent] = value.astype(rows.dtype)
                        store = pltpu.make_async_copy(
                            stage[o].at[pl.ds(0, some), pl.ds(at, extent)],
                            out_refs[o].at[pl.ds(0, some), pl.ds(at, extent)],
                            out_sems.at[o, c],
                        )
                        store.start()
                        stores.append(store)
        for store in stores:
            store.wait()

    shapes = [(height, size) for height in heights]
    return call(
        kernel, [starts, rows, weight] + tails, after, prefetch=1,
        in_specs=[ANY] * (2 + len(tails)),
        out_specs=[ANY] * len(outs),
        out_shape=[jax.ShapeDtypeStruct(shape, rows.dtype) for shape in shapes],
        scratch=[pltpu.VMEM((high - low, width), rows.dtype), pltpu.VMEM((blocks, width, size), rows.dtype)]
        + [pltpu.VMEM(shape, rows.dtype) for shape in shapes]
        + [
            pltpu.SemaphoreType.DMA((2,)),
            pltpu.SemaphoreType.DMA((blocks, len(chunks))),
            pltpu.SemaphoreType.DMA((len(outs), len(chunks))),
            pltpu.SemaphoreType.DMA((2,)),
        ],
        name="products", vmem=vmem,
    )


def total(runs, dtype=jnp.bfloat16, into=None, after=()):
    width = runs[0][1][0][0].shape[1]
    height = sum(some for some, _ in runs)
    rows_in_all, first, so_far = into or (height, 0, None)
    tiles = []
    at = 0
    for r, (some, terms) in enumerate(runs):
        split = 4 if some * len(terms) > 2000 else 2 if some * width > 2**17 else 1
        size = -(-some // (16 * split)) * 16
        for skip in range(0, some, size):
            tiles.append((r, skip, min(size, some - skip), at + skip))
        at += some
    operands = [term for _, terms in runs for term, _ in terms]
    before = [] if so_far is None else [so_far]
    most_terms = max(len(terms) for _, terms in runs)
    of_run = np.cumsum([0] + [len(terms) for _, terms in runs])

    def kernel(*refs):
        term_refs, out_ref = refs[: len(operands)], refs[len(operands) + len(before)]
        refs = refs[len(operands) + len(before) + 1 :]
        bufs, (stage, in_sems, out_sems) = refs[: len(operands)], refs[len(operands) :]
        reads, writes = [], []
        for n, (r, skip, size, place) in enumerate(tiles):
            reads.append(
                [
                    pltpu.make_async_copy(
                        term_refs[of_run[r] + t].at[pl.ds(start + skip, size)],
                        bufs[of_run[r] + t].at[pl.ds(skip, size)],
                        in_sems.at[t, n],
                    )
                    for t, (_, start) in enumerate(runs[r][1])
                ]
            )
            writes.append(
                pltpu.make_async_copy(
                    stage.at[pl.ds(place, size)], out_ref.at[pl.ds(first + place, size)], out_sems.at[n]
                )
            )
        for some in reads:
            for read in some:
                read.start()
        for n, (r, skip, size, place) in enumerate(tiles):
            for read in reads[n]:
                read.wait()
            value = None
            for t in range(len(runs[r][1])):
                part = bufs[of_run[r] + t][skip : skip + size, :].astype(jnp.float32)
                value = part if value is None else value + part
            stage[place : place + size, :] = value.astype(dtype)
            writes[n].start()
        for write in writes:
            write.wait()

    return call(
        kernel, operands + before, after,
        in_specs=[ANY] * (len(operands) + len(before)),
        out_specs=ANY,
        out_shape=jax.ShapeDtypeStruct((rows_in_all, width), dtype),
        scratch=[pltpu.VMEM((some, width), term.dtype) for some, terms in runs for term, _ in terms]
        + [
            pltpu.VMEM((height, width), dtype),
            pltpu.SemaphoreType.DMA((most_terms, len(tiles))),
            pltpu.SemaphoreType.DMA((len(tiles),)),
        ],
        alias={len(operands): 0} if before else None,
        name="total",
    )


def lane_pick(slot_ref, repeats, shape, rank, first):
    slot = jnp.concatenate([slot_ref[...]] * repeats, axis=0)
    return slot == lax.broadcasted_iota(jnp.int32, shape, 1) // rank + first


def block_copies(index_ref, maps_ref, buf, sems, sets, rank):
    each = index_ref.shape[0] // sets
    return [
        [
            pltpu.make_async_copy(
                maps_ref.at[index_ref[s * each + i]], buf.at[pl.ds((s * each + i) * rank, rank)],
                sems.at[s * each + i],
            )
            for i in range(each)
        ]
        for s in range(sets)
    ]


def low_rank(row_sets, slot_sets, maps, index, wide, after=()):
    sets = len(row_sets)
    count, width = row_sets[0].shape
    rank = maps.shape[1]
    span = index.shape[0] // sets * rank
    repeats = count // slot_sets[0].shape[0]
    half = count // 2
    group = 256
    tall = half * 2 * rank // wide

    def kernel(index_ref, *refs):
        row_refs, slot_refs, maps_ref = refs[:sets], refs[sets : 2 * sets], refs[2 * sets]
        out_refs, (rows_buf, maps_buf, row_sems, map_sems) = refs[2 * sets + 1 : 3 * sets + 1], refs[3 * sets + 1 :]
        row_copies = [
            pltpu.make_async_copy(row_refs[s], rows_buf.at[s], row_sems.at[s]) for s in range(sets)
        ]
        map_copies = block_copies(index_ref, maps_ref, maps_buf, map_sems, sets, rank)
        for s in range(sets):
            row_copies[s].start()
            for copy in map_copies[s]:
                copy.start()
        for s in range(sets):
            row_copies[s].wait()
            for copy in map_copies[s]:
                copy.wait()
            acc = None
            for at in range(0, span, group):
                scores = lax.dot_general(
                    rows_buf[s], maps_buf[s * span + at : s * span + at + group],
                    (((1,), (1,)), ((), ())), preferred_element_type=jnp.float32,
                )
                pick = lane_pick(slot_refs[s], repeats, (count, group), rank, at // rank)
                term = jnp.where(pick, scores, 0.0)
                acc = term if acc is None else acc + term
            summed = acc[:, 0:rank]
            for g in range(1, group // rank):
                summed += acc[:, g * rank : (g + 1) * rank]
            summed = summed.astype(out_refs[s].dtype)
            for b in range(half // tall):
                lanes = slice(b * 2 * rank, (b + 1) * 2 * rank)
                both = [summed[start + b * tall : start + (b + 1) * tall] for start in (0, half)]
                out_refs[s][:, lanes] = jnp.concatenate(both, axis=1)

    return call(
        kernel, [index, *row_sets, *slot_sets, maps], after, prefetch=1,
        in_specs=[ANY] * sets + [pl.BlockSpec(memory_space=pltpu.VMEM)] * sets + [ANY],
        out_specs=[pl.BlockSpec(memory_space=pltpu.VMEM)] * sets,
        out_shape=[jax.ShapeDtypeStruct((tall, wide), jnp.bfloat16)] * sets,
        scratch=[
            pltpu.VMEM((sets, count, width), row_sets[0].dtype),
            pltpu.VMEM((sets * span, width), maps.dtype),
            pltpu.SemaphoreType.DMA((sets,)),
            pltpu.SemaphoreType.DMA((index.shape[0],)),
        ],
        name="low_rank",
    )


def expand(low_sets, slot_sets, maps, index, after=()):
    sets = len(slot_sets)
    rank, width = maps.shape[1:]
    tall = low_sets[0].shape[0]
    half = low_sets[0].size // (2 * rank)
    count = 2 * half
    span = index.shape[0] // sets * rank
    repeats = count // slot_sets[0].shape[0]

    outs = [(0, 0, count)] + [
        (s, p * count // PARTS, count // PARTS) for s in range(1, sets) for p in range(PARTS)
    ]

    def kernel(index_ref, *refs):
        low_refs, refs = refs[:sets], refs[sets:]
        slot_refs, maps_ref, out_refs = refs[:sets], refs[sets], refs[sets + 1 : sets + 1 + len(outs)]
        stage, maps_buf, map_sems, out_sems = refs[sets + 1 + len(outs) :]
        map_copies = block_copies(index_ref, maps_ref, maps_buf, map_sems, sets, rank)
        writes = [
            pltpu.make_async_copy(stage.at[s, pl.ds(first, some)], out_refs[o], out_sems.at[o])
            for o, (s, first, some) in enumerate(outs)
        ]
        order = list(range(1, sets)) + [0]
        for s in order:
            for copy in map_copies[s]:
                copy.start()
        for s in order:
            lanes = [b * 2 * rank for b in range(half // tall)]
            mine = jnp.concatenate(
                [low_refs[s][:, at + side : at + side + rank] for side in (0, rank) for at in lanes], axis=0
            )
            tiled = jnp.concatenate([mine] * (span // rank), axis=1)
            pick = lane_pick(slot_refs[s], repeats, (count, span), rank, 0)
            picked = jnp.where(pick, tiled, jnp.zeros_like(tiled))
            for copy in map_copies[s]:
                copy.wait()
            for at in range(0, width, CHUNK):
                value = jnp.dot(
                    picked, maps_buf[s * span : (s + 1) * span, at : at + CHUNK], preferred_element_type=jnp.float32
                )
                stage[s, :, at : at + CHUNK] = value.astype(stage.dtype)
            for o, (which, _, _) in enumerate(outs):
                if which == s:
                    writes[o].start()
        for write in writes:
            write.wait()

    return call(
        kernel, [index, *low_sets, *slot_sets, maps], after, prefetch=1,
        in_specs=[pl.BlockSpec(memory_space=pltpu.VMEM)] * (2 * sets) + [ANY],
        out_specs=[ANY] * len(outs),
        out_shape=[jax.ShapeDtypeStruct((some, width), jnp.bfloat16) for _, _, some in outs],
        scratch=[
            pltpu.VMEM((sets, count, width), jnp.bfloat16),
            pltpu.VMEM((sets * span, width), maps.dtype),
            pltpu.SemaphoreType.DMA((index.shape[0],)),
            pltpu.SemaphoreType.DMA((len(outs),)),
        ],
        name="expand",
    )


def line_plan(nz):
    order = np.zeros((nz, nz), np.int32)
    for z in range(nz):
        def need(j):
            if j == z:
                return (2 * nz, 0)
            return (nz - 1 - j + z, j) if j > z else (nz - 1 - z + j, nz - j)

        order[z] = sorted(range(nz), key=need)
    return order


def on_device(attention_result, tenant, projection_weight, adapter_down_maps, adapter_up_maps):
    steps, row_count, width = attention_result.shape
    local_adapters = adapter_down_maps.shape[0]
    owners = lax.axis_size("dp")
    me = lax.axis_index("dp")
    n = lax.axis_size("tensor")
    nz = n // 2
    place = lax.axis_index("tensor")
    order = line_plan(nz)
    out_width = projection_weight.shape[1] // n

    def swap_y(value):
        return lax.ppermute(value, "tensor", [(t, t ^ 1) for t in range(n)])

    def hop(value, h):
        pairs = []
        for side in range(2):
            pairs.append((h * 2 + side, (h + 1) * 2 + side))
            pairs.append(((nz - 1 - h) * 2 + side, (nz - 2 - h) * 2 + side))
        return lax.ppermute(value, "tensor", pairs)

    def slot_of(h, m):
        return list(order[h]).index(nz - 1 - m)

    def pass_on(value, shift):
        return lax.ppermute(value, "dp", [(i, (i + shift) % owners) for i in range(owners)])

    rows = attention_result.reshape(steps * row_count, width)
    count = steps * row_count
    last = [()]

    def then(kernel, *operands, **options):
        out = kernel(*operands, after=last[0], **options)
        last[0] = (out[0] if isinstance(out, (tuple, list)) else out,)
        return out

    slot_range = jnp.arange(SLOTS, dtype=jnp.int32)
    ids = jnp.arange(local_adapters, dtype=jnp.int32)

    def slots(row_ids, owner):
        hit = row_ids[:, None] - owner * local_adapters == ids[None, :]
        used = jnp.any(hit, axis=0)
        position = jnp.sum(
            (used[None, :] & (ids[None, :] < ids[:, None])).astype(jnp.int32), axis=1
        )
        names = jnp.sum(
            jnp.where(used[None, :] & (position[None, :] == slot_range[:, None]), ids[None, :], 0),
            axis=1,
        )
        row_slot = jnp.sum(jnp.where(hit, position[None, :] + 1, 0), axis=1) - 1
        return names, row_slot[:, None]

    blocks = [[(order[t // 2][k] * 2 + side) for side in (1 - t % 2, t % 2) for k in range(nz)] for t in range(n)]
    starts = jnp.asarray(np.asarray(blocks, np.int32) * out_width)[place]
    low_rows = count * adapter_down_maps.shape[1] // out_width
    even = [(p * count // PARTS, count // PARTS) for p in range(PARTS)]
    high_part = -(-(count + low_rows) // 32) * 16
    uneven = [(0, high_part), (high_part, count - high_part)]
    away_part, own_all, from_y, sums, arrived = {}, {}, {}, {}, {}

    def split(k):
        return uneven if k == 0 else [(0, count)]

    def add_up(span, terms, extra=(), dtype=jnp.bfloat16, into=None):
        low_row, high_row = span[0], span[0] + span[1]
        cuts = {low_row, high_row}
        for term in terms:
            for at, some, _, _ in term:
                cuts.update(row for row in (at, at + some) if low_row < row < high_row)
        cuts = sorted(cuts)
        runs = []
        for begin, end in zip(cuts, cuts[1:]):
            here = [
                (array, row + begin - at) for term in terms for at, some, array, row in term if at <= begin < at + some
            ]
            runs.append((end - begin, here))
        return then(total, runs + list(extra), dtype, into)

    def whole(array):
        return [(0, count, array, 0)]

    def multiply(aways, owns, tail=None, chunk=1024, vmem=VMEM):
        ks = sorted({k for k, _ in aways})
        names = ks + [nz + k for k in owns]
        outs = [(ks.index(k), *split(k)[p]) for k, p in aways]
        outs += [(len(ks) + i, 0, count) for i in range(len(owns))]
        done = then(products, rows, projection_weight, starts, names, out_width, outs, tail, chunk, vmem)
        away_part.update(zip(aways, done))
        own_all.update(zip(owns, done[len(aways) :]))

    def start_y(k, p, after=None):
        value = away_part[k, p]
        from_y[k, p] = swap_y(value if after is None else hold(value, after))

    def y_parts(k):
        return [(*cut, from_y[k, p], 0) for p, cut in enumerate(split(k)) if (k, p) in from_y]

    def sum_parts(k):
        return [(*cut, sums[k, p], 0) for p, cut in enumerate(cut_of(0, k)) if (k, p) in sums]

    def cut_of(h, m):
        if m == 0 and h <= 1:
            return uneven
        return [(0, count * 8 // 16), (count * 8 // 16, count * 8 // 16)] if m == 1 else [(0, count)]

    def arrived_parts(h, m):
        return [(*cut, arrived[h, m, p], 0) for p, cut in enumerate(cut_of(h, m)) if (h, m, p) in arrived]

    def line(h, m, p):
        k = slot_of(h, m)
        span = cut_of(h, m)[p]
        low_too = m == 0 and h <= 1 and p == LOW_WITH[1]
        if h == 0:
            extra = [(low_rows, [(low, 0), (from_y[k, p], span[1])])] if low_too else []
            value = sums[k, p] = add_up(span, [whole(own_all[k]), y_parts(k)], extra)
        else:
            extra = [(low_rows, [(sums[k, p], span[1]), (arrived[h - 1, m, p], span[1])])] if low_too else []
            value = add_up(span, [sum_parts(k), arrived_parts(h - 1, m)], extra)
        arrived[h, m, p] = hop(value, h)

    def line_order():
        ready, free = {}, {}
        steps = [(h, m, p) for h in range(nz - 1) for m in range(nz - 1 - h) for p in range(len(cut_of(h, m)))]
        for h, m, p in sorted(steps, key=lambda step: (step[0], step[1], step[2])):
            k = slot_of(h, m)
            there = (k + 1.0) * count if k or p else 1.0 * cut_of(0, 0)[0][1]
            if h:
                above = range(len(cut_of(h - 1, m)))
                there = max(there, max(ready[h - 1, m, q, "end"] for q in above if q == p or len(above) != len(cut_of(h, m))))
            ready[h, m, p] = there
            free[h] = max(there, free.get(h, 0.0)) + cut_of(h, m)[p][1]
            ready[h, m, p, "end"] = free[h]
        return sorted(steps, key=lambda step: (ready[step], step[0] and nz - step[0]))

    row_ids = [tenant] + [pass_on(tenant, shift) for shift in range(1, owners)]
    row_sets = [rows] + [pass_on(rows, shift) for shift in range(1, owners)]
    multiply([(0, 0)], [], chunk=512, vmem=VMEM + 13 * 2**20)
    start_y(0, 0)
    named = [slots(some_ids, me) for some_ids in row_ids]
    names = jnp.concatenate([which for which, _ in named])
    slot_sets = [row_slot for _, row_slot in named]
    low_sets = then(low_rank, row_sets, slot_sets, adapter_down_maps, names, out_width)
    low_terms = [(low_sets[0], 0)] + [(pass_on(low_sets[s], -s), 0) for s in range(1, owners)]
    low = then(total, [(low_rows, low_terms)])
    multiply([LOW_WITH], [], low, chunk=512)
    start_y(*LOW_WITH)
    multiply([(1, 0)], [0])
    start_y(1, 0)
    low_sum = deltas = None
    for h, m, p in line_order():
        k = slot_of(h, m)
        if (h, m, p) == (2, 0, 0) and nz == 4:
            last[0] += (arrived[0, 1, 1],)
        line(h, m, p)
        if h == 0:
            if k == 0 and p == 0:
                multiply([(2, 0)] if nz > 2 else [], [1])
            elif k == 0:
                if nz > 2:
                    start_y(2, 0, last[0])
                multiply([(j, 0) for j in range(3, nz)], range(2, nz))
            elif p == len(cut_of(h, m)) - 1 and k + 2 < nz:
                start_y(k + 2, 0, last[0])
        if (h, k, p) == (0, 1, len(cut_of(h, m)) - 1):
            low_at = uneven[LOW_WITH[1]][1]
            pieces = [(sums[LOW_WITH], low_at)]
            last[0] += (arrived[1, 0, 0],) if nz > 2 else ()
            for step in range(nz - 1):
                if step >= 2:
                    prefix = then(total, [(low_rows, [pieces[0], pieces[-1]])])
                    pieces.append((hop(prefix, step), 0))
                else:
                    pieces.append((arrived[step, 0, LOW_WITH[1]], low_at))
        if (h, m, p) == LOW_SUM_AFTER:
            low_sum = then(total, [(low_rows, pieces)])
            low_back = [low_sum] + [pass_on(low_sum, shift) for shift in range(1, owners)]
        if deltas is None and low_sum is not None and EXPAND_AFTER in arrived:
            last[0] += (arrived[1, 1, 0],) if nz > 2 else ()
            deltas = then(expand, low_back, slot_sets, adapter_up_maps, names)
            back = [
                [(*cut, pass_on(deltas[1 + (shift - 1) * PARTS + p], -shift), 0) for p, cut in enumerate(even)]
                for shift in range(1, owners)
            ]
    span = (0, count)
    early = [arrived_parts(h, nz - 2 - h) for h in range(1, nz - 2)]
    late = [arrived_parts(h, nz - 2 - h) for h in range(nz - 1) if not 1 <= h < nz - 2]
    most = add_up(span, [whole(own_all[nz - 1]), whole(deltas[0]), y_parts(nz - 1)] + early)
    most = add_up(span, [whole(most)] + back + late[:-1])
    out = add_up(span, [whole(most)] + late[-1:])
    return out.reshape(steps, row_count, out_width)


def solution(mesh):
    placed = (
        P(None, ("groups", "dp"), "tensor"),
        P(("groups", "dp")),
        P("tensor", None),
        P(("groups", "dp"), None, "tensor"),
        P(("groups", "dp"), None, "tensor"),
    )
    return jax.shard_map(
        on_device,
        mesh=mesh,
        in_specs=placed,
        out_specs=P(None, ("groups", "dp"), "tensor"),
        check_vma=False,
    )
```

```python
import jax
import jax.numpy as jnp
import numpy as np
from jax import lax
from jax.experimental import pallas as pl
from jax.experimental.pallas import tpu as pltpu
from jax.sharding import PartitionSpec as P

SLOTS = 16
LANES = 128
CHUNK = 512
PARTS = 2
LOW_WITH = (0, PARTS - 1)
LOW_SUM_AFTER = (2, 0, 0)
EXPAND_AFTER = (1, 1, 1)
VMEM = 50 * 2**20
ANY = pl.BlockSpec(memory_space=pl.ANY)


def call(kernel, operands, after, *, in_specs, out_specs, out_shape, name, prefetch=0, scratch=(), alias=None, vmem=VMEM):
    inputs, extra = len(operands), len(after)

    def body(*refs):
        kernel(*refs[:inputs], *refs[inputs + extra :])

    return pl.pallas_call(
        body,
        grid_spec=pltpu.PrefetchScalarGridSpec(
            num_scalar_prefetch=prefetch,
            grid=(),
            in_specs=list(in_specs) + [ANY] * extra,
            out_specs=out_specs,
            scratch_shapes=list(scratch),
        ),
        out_shape=out_shape,
        input_output_aliases=alias or {},
        compiler_params=pltpu.CompilerParams(vmem_limit_bytes=vmem),
        cost_estimate=pl.CostEstimate(flops=1, transcendentals=0, bytes_accessed=1),
        name=name,
    )(*operands, *after)


def hold(value, after):
    def kernel(value_ref, out_ref):
        pass

    return call(
        kernel, [value], after, in_specs=[ANY], out_specs=ANY,
        out_shape=jax.ShapeDtypeStruct(value.shape, value.dtype), name="hold", alias={0: 0},
    )


def products(rows, weight, starts, names, size, outs, tail=None, chunk=1024, vmem=VMEM, after=()):
    count, width = rows.shape
    blocks = len(names)
    chunks = [(at, min(chunk, size - at)) for at in range(0, size, chunk)]
    low = min(first for _, first, _ in outs)
    high = max(first + some for _, first, some in outs)
    upper = (high - low) // 32 * 16
    row_parts = [(0, upper), (upper, high - low - upper)]
    tails = [] if tail is None else [tail]
    heights = [some for _, _, some in outs]
    for array in tails:
        heights[-1] += array.shape[0]

    def kernel(starts_ref, rows_ref, weight_ref, *refs):
        tail_refs, refs = refs[: len(tails)], refs[len(tails) :]
        out_refs, (x, w, *refs) = refs[: len(outs)], refs[len(outs) :]
        stage, (x_sems, w_sems, out_sems, tail_sems) = refs[: len(outs)], refs[len(outs) :]
        x_copies = [
            pltpu.make_async_copy(
                rows_ref.at[pl.ds(low + at, some)], x.at[pl.ds(at, some)], x_sems.at[i]
            )
            for i, (at, some) in enumerate(row_parts)
        ]
        w_copies = [
            [
                pltpu.make_async_copy(
                    weight_ref.at[:, pl.ds(pl.multiple_of(starts_ref[names[b]] + at, LANES), extent)],
                    w.at[b, :, pl.ds(at, extent)],
                    w_sems.at[b, c],
                )
                for c, (at, extent) in enumerate(chunks)
            ]
            for b in range(blocks)
        ]
        x_copies[0].start()
        w_copies[0][0].start()
        x_copies[1].start()
        for b in range(blocks):
            for c in range(len(chunks)):
                if b or c:
                    w_copies[b][c].start()
        stores = []
        for ref in tail_refs:
            below = pl.ds(outs[-1][2], ref.shape[0])
            read = pltpu.make_async_copy(ref, stage[-1].at[below], tail_sems.at[0])
            read.start()
            read.wait()
            stores.append(pltpu.make_async_copy(stage[-1].at[below], out_refs[-1].at[below], tail_sems.at[1]))
            stores[-1].start()
        for copy in x_copies:
            copy.wait()
        for b in range(blocks):
            for c, (at, extent) in enumerate(chunks):
                w_copies[b][c].wait()
                for o, (index, first, some) in enumerate(outs):
                    if index == b:
                        value = jnp.dot(
                            x[first - low : first - low + some, :], w[b, :, at : at + extent],
                            preferred_element_type=jnp.float32,
                        )
                        stage[o][:some, at : at + extent] = value.astype(rows.dtype)
                        store = pltpu.make_async_copy(
                            stage[o].at[pl.ds(0, some), pl.ds(at, extent)],
                            out_refs[o].at[pl.ds(0, some), pl.ds(at, extent)],
                            out_sems.at[o, c],
                        )
                        store.start()
                        stores.append(store)
        for store in stores:
            store.wait()

    shapes = [(height, size) for height in heights]
    return call(
        kernel, [starts, rows, weight] + tails, after, prefetch=1,
        in_specs=[ANY] * (2 + len(tails)),
        out_specs=[ANY] * len(outs),
        out_shape=[jax.ShapeDtypeStruct(shape, rows.dtype) for shape in shapes],
        scratch=[pltpu.VMEM((high - low, width), rows.dtype), pltpu.VMEM((blocks, width, size), rows.dtype)]
        + [pltpu.VMEM(shape, rows.dtype) for shape in shapes]
        + [
            pltpu.SemaphoreType.DMA((2,)),
            pltpu.SemaphoreType.DMA((blocks, len(chunks))),
            pltpu.SemaphoreType.DMA((len(outs), len(chunks))),
            pltpu.SemaphoreType.DMA((2,)),
        ],
        name="products", vmem=vmem,
    )


def total(runs, dtype=jnp.bfloat16, into=None, only=None, after=()):
    width = runs[0][1][0][0].shape[1]
    height = sum(some for some, _ in runs)
    rows_in_all, first, so_far = into or (height, 0, None)
    tiles = []
    at = 0
    for r, (some, terms) in enumerate(runs):
        split = 4 if some * len(terms) > 2000 else 2 if some * width > 2**17 else 1
        size = -(-some // (16 * split)) * 16
        for skip in range(0, some, size):
            tiles.append((r, skip, min(size, some - skip), at + skip))
        at += some
    operands = [term for _, terms in runs for term, _ in terms]
    before = [] if so_far is None else [so_far]
    most_terms = max(len(terms) for _, terms in runs)
    of_run = np.cumsum([0] + [len(terms) for _, terms in runs])

    flags = [] if only is None else [only[0]]

    def kernel(*refs):
        if only is None:
            add(*refs)
        else:
            pl.when(refs[0][only[1]] != 0)(lambda: add(*refs[1:]))

    def add(*refs):
        term_refs, out_ref = refs[: len(operands)], refs[len(operands) + len(before)]
        refs = refs[len(operands) + len(before) + 1 :]
        bufs, (stage, in_sems, out_sems) = refs[: len(operands)], refs[len(operands) :]
        reads, writes = [], []
        for n, (r, skip, size, place) in enumerate(tiles):
            reads.append(
                [
                    pltpu.make_async_copy(
                        term_refs[of_run[r] + t].at[pl.ds(start + skip, size)],
                        bufs[of_run[r] + t].at[pl.ds(skip, size)],
                        in_sems.at[t, n],
                    )
                    for t, (_, start) in enumerate(runs[r][1])
                ]
            )
            writes.append(
                pltpu.make_async_copy(
                    stage.at[pl.ds(place, size)], out_ref.at[pl.ds(first + place, size)], out_sems.at[n]
                )
            )
        for some in reads:
            for read in some:
                read.start()
        for n, (r, skip, size, place) in enumerate(tiles):
            for read in reads[n]:
                read.wait()
            value = None
            for t in range(len(runs[r][1])):
                part = bufs[of_run[r] + t][skip : skip + size, :].astype(jnp.float32)
                value = part if value is None else value + part
            stage[place : place + size, :] = value.astype(dtype)
            writes[n].start()
        for write in writes:
            write.wait()

    return call(
        kernel, flags + operands + before, after, prefetch=len(flags),
        in_specs=[ANY] * (len(operands) + len(before)),
        out_specs=ANY,
        out_shape=jax.ShapeDtypeStruct((rows_in_all, width), dtype),
        scratch=[pltpu.VMEM((some, width), term.dtype) for some, terms in runs for term, _ in terms]
        + [
            pltpu.VMEM((height, width), dtype),
            pltpu.SemaphoreType.DMA((most_terms, len(tiles))),
            pltpu.SemaphoreType.DMA((len(tiles),)),
        ],
        alias={len(flags) + len(operands): 0} if before else None,
        name="total",
    )


def lane_pick(slot_ref, repeats, shape, rank, first):
    slot = jnp.concatenate([slot_ref[...]] * repeats, axis=0)
    return slot == lax.broadcasted_iota(jnp.int32, shape, 1) // rank + first


def block_copies(index_ref, maps_ref, buf, sems, sets, rank):
    each = index_ref.shape[0] // sets
    return [
        [
            pltpu.make_async_copy(
                maps_ref.at[index_ref[s * each + i]], buf.at[pl.ds((s * each + i) * rank, rank)],
                sems.at[s * each + i],
            )
            for i in range(each)
        ]
        for s in range(sets)
    ]


def low_rank(row_sets, slot_sets, maps, index, wide, after=()):
    sets = len(row_sets)
    count, width = row_sets[0].shape
    rank = maps.shape[1]
    span = index.shape[0] // sets * rank
    repeats = count // slot_sets[0].shape[0]
    half = count // 2
    group = 256
    tall = half * 2 * rank // wide

    def kernel(index_ref, *refs):
        row_refs, slot_refs, maps_ref = refs[:sets], refs[sets : 2 * sets], refs[2 * sets]
        out_refs, (rows_buf, maps_buf, row_sems, map_sems) = refs[2 * sets + 1 : 3 * sets + 1], refs[3 * sets + 1 :]
        row_copies = [
            pltpu.make_async_copy(row_refs[s], rows_buf.at[s], row_sems.at[s]) for s in range(sets)
        ]
        map_copies = block_copies(index_ref, maps_ref, maps_buf, map_sems, sets, rank)
        for s in range(sets):
            row_copies[s].start()
            for copy in map_copies[s]:
                copy.start()
        for s in range(sets):
            row_copies[s].wait()
            for copy in map_copies[s]:
                copy.wait()
            acc = None
            for at in range(0, span, group):
                scores = lax.dot_general(
                    rows_buf[s], maps_buf[s * span + at : s * span + at + group],
                    (((1,), (1,)), ((), ())), preferred_element_type=jnp.float32,
                )
                pick = lane_pick(slot_refs[s], repeats, (count, group), rank, at // rank)
                term = jnp.where(pick, scores, 0.0)
                acc = term if acc is None else acc + term
            summed = acc[:, 0:rank]
            for g in range(1, group // rank):
                summed += acc[:, g * rank : (g + 1) * rank]
            summed = summed.astype(out_refs[s].dtype)
            for b in range(half // tall):
                lanes = slice(b * 2 * rank, (b + 1) * 2 * rank)
                both = [summed[start + b * tall : start + (b + 1) * tall] for start in (0, half)]
                out_refs[s][:, lanes] = jnp.concatenate(both, axis=1)

    return call(
        kernel, [index, *row_sets, *slot_sets, maps], after, prefetch=1,
        in_specs=[ANY] * sets + [pl.BlockSpec(memory_space=pltpu.VMEM)] * sets + [ANY],
        out_specs=[pl.BlockSpec(memory_space=pltpu.VMEM)] * sets,
        out_shape=[jax.ShapeDtypeStruct((tall, wide), jnp.bfloat16)] * sets,
        scratch=[
            pltpu.VMEM((sets, count, width), row_sets[0].dtype),
            pltpu.VMEM((sets * span, width), maps.dtype),
            pltpu.SemaphoreType.DMA((sets,)),
            pltpu.SemaphoreType.DMA((index.shape[0],)),
        ],
        name="low_rank",
    )


def expand(low_sets, slot_sets, maps, index, after=()):
    sets = len(slot_sets)
    rank, width = maps.shape[1:]
    tall = low_sets[0].shape[0]
    half = low_sets[0].size // (2 * rank)
    count = 2 * half
    span = index.shape[0] // sets * rank
    repeats = count // slot_sets[0].shape[0]

    outs = [(0, 0, count)] + [
        (s, p * count // PARTS, count // PARTS) for s in range(1, sets) for p in range(PARTS)
    ]

    def kernel(index_ref, *refs):
        low_refs, refs = refs[:sets], refs[sets:]
        slot_refs, maps_ref, out_refs = refs[:sets], refs[sets], refs[sets + 1 : sets + 1 + len(outs)]
        stage, maps_buf, map_sems, out_sems = refs[sets + 1 + len(outs) :]
        map_copies = block_copies(index_ref, maps_ref, maps_buf, map_sems, sets, rank)
        writes = [
            pltpu.make_async_copy(stage.at[s, pl.ds(first, some)], out_refs[o], out_sems.at[o])
            for o, (s, first, some) in enumerate(outs)
        ]
        order = list(range(1, sets)) + [0]
        for s in order:
            for copy in map_copies[s]:
                copy.start()
        for s in order:
            lanes = [b * 2 * rank for b in range(half // tall)]
            mine = jnp.concatenate(
                [low_refs[s][:, at + side : at + side + rank] for side in (0, rank) for at in lanes], axis=0
            )
            tiled = jnp.concatenate([mine] * (span // rank), axis=1)
            pick = lane_pick(slot_refs[s], repeats, (count, span), rank, 0)
            picked = jnp.where(pick, tiled, jnp.zeros_like(tiled))
            for copy in map_copies[s]:
                copy.wait()
            for at in range(0, width, CHUNK):
                value = jnp.dot(
                    picked, maps_buf[s * span : (s + 1) * span, at : at + CHUNK], preferred_element_type=jnp.float32
                )
                stage[s, :, at : at + CHUNK] = value.astype(stage.dtype)
            for o, (which, _, _) in enumerate(outs):
                if which == s:
                    writes[o].start()
        for write in writes:
            write.wait()

    return call(
        kernel, [index, *low_sets, *slot_sets, maps], after, prefetch=1,
        in_specs=[pl.BlockSpec(memory_space=pltpu.VMEM)] * (2 * sets) + [ANY],
        out_specs=[ANY] * len(outs),
        out_shape=[jax.ShapeDtypeStruct((some, width), jnp.bfloat16) for _, _, some in outs],
        scratch=[
            pltpu.VMEM((sets, count, width), jnp.bfloat16),
            pltpu.VMEM((sets * span, width), maps.dtype),
            pltpu.SemaphoreType.DMA((index.shape[0],)),
            pltpu.SemaphoreType.DMA((len(outs),)),
        ],
        name="expand",
    )


def line_plan(nz):
    order = np.zeros((nz, nz), np.int32)
    for z in range(nz):
        def need(j):
            if j == z:
                return (2 * nz, 0)
            return (nz - 1 - j + z, j) if j > z else (nz - 1 - z + j, nz - j)

        order[z] = sorted(range(nz), key=need)
    return order


def on_device(attention_result, tenant, projection_weight, adapter_down_maps, adapter_up_maps):
    steps, row_count, width = attention_result.shape
    local_adapters = adapter_down_maps.shape[0]
    owners = lax.axis_size("dp")
    me = lax.axis_index("dp")
    n = lax.axis_size("tensor")
    nz = n // 2
    place = lax.axis_index("tensor")
    order = line_plan(nz)
    out_width = projection_weight.shape[1] // n

    def swap_y(value):
        return lax.ppermute(value, "tensor", [(t, t ^ 1) for t in range(n)])

    def hop(value, h):
        pairs = []
        for side in range(2):
            pairs.append((h * 2 + side, (h + 1) * 2 + side))
            pairs.append(((nz - 1 - h) * 2 + side, (nz - 2 - h) * 2 + side))
        return lax.ppermute(value, "tensor", pairs)

    def slot_of(h, m):
        return list(order[h]).index(nz - 1 - m)

    def pass_on(value, shift):
        return lax.ppermute(value, "dp", [(i, (i + shift) % owners) for i in range(owners)])

    rows = attention_result.reshape(steps * row_count, width)
    count = steps * row_count
    last = [()]

    def then(kernel, *operands, **options):
        out = kernel(*operands, after=last[0], **options)
        last[0] = (out[0] if isinstance(out, (tuple, list)) else out,)
        return out

    slot_range = jnp.arange(SLOTS, dtype=jnp.int32)
    ids = jnp.arange(local_adapters, dtype=jnp.int32)

    def slots(row_ids, owner):
        hit = row_ids[:, None] - owner * local_adapters == ids[None, :]
        used = jnp.any(hit, axis=0)
        position = jnp.sum(
            (used[None, :] & (ids[None, :] < ids[:, None])).astype(jnp.int32), axis=1
        )
        names = jnp.sum(
            jnp.where(used[None, :] & (position[None, :] == slot_range[:, None]), ids[None, :], 0),
            axis=1,
        )
        row_slot = jnp.sum(jnp.where(hit, position[None, :] + 1, 0), axis=1) - 1
        return names, row_slot[:, None]

    blocks = [[(order[t // 2][k] * 2 + side) for side in (1 - t % 2, t % 2) for k in range(nz)] for t in range(n)]
    sends = [[int(t // 2 in (h, nz - 1 - h)) for h in range(nz - 1)] for t in range(n)]
    table = np.concatenate([np.asarray(blocks, np.int32) * out_width, np.asarray(sends, np.int32)], axis=1)
    starts = jnp.asarray(table)[place]
    low_rows = count * adapter_down_maps.shape[1] // out_width
    even = [(p * count // PARTS, count // PARTS) for p in range(PARTS)]
    high_part = -(-(count + low_rows) // 32) * 16
    uneven = [(0, high_part), (high_part, count - high_part)]
    away_part, own_all, from_y, sums, arrived = {}, {}, {}, {}, {}

    def split(k):
        return uneven if k == 0 else [(0, count)]

    def add_up(span, terms, extra=(), dtype=jnp.bfloat16, only=None):
        low_row, high_row = span[0], span[0] + span[1]
        cuts = {low_row, high_row}
        for term in terms:
            for at, some, _, _ in term:
                cuts.update(row for row in (at, at + some) if low_row < row < high_row)
        cuts = sorted(cuts)
        runs = []
        for begin, end in zip(cuts, cuts[1:]):
            here = [
                (array, row + begin - at) for term in terms for at, some, array, row in term if at <= begin < at + some
            ]
            runs.append((end - begin, here))
        return then(total, runs + list(extra), dtype, None, only)

    def whole(array):
        return [(0, count, array, 0)]

    def multiply(aways, owns, tail=None, chunk=1024, vmem=VMEM):
        ks = sorted({k for k, _ in aways})
        names = ks + [nz + k for k in owns]
        outs = [(ks.index(k), *split(k)[p]) for k, p in aways]
        outs += [(len(ks) + i, 0, count) for i in range(len(owns))]
        done = then(products, rows, projection_weight, starts, names, out_width, outs, tail, chunk, vmem)
        away_part.update(zip(aways, done))
        own_all.update(zip(owns, done[len(aways) :]))

    def start_y(k, p, after=None):
        value = away_part[k, p]
        from_y[k, p] = swap_y(value if after is None else hold(value, after))

    def y_parts(k):
        return [(*cut, from_y[k, p], 0) for p, cut in enumerate(split(k)) if (k, p) in from_y]

    def sum_parts(k):
        return [(*cut, sums[k, p], 0) for p, cut in enumerate(cut_of(0, k)) if (k, p) in sums]

    def cut_of(h, m):
        if m == 0 and h <= 1:
            return uneven
        return [(0, count * 8 // 16), (count * 8 // 16, count * 8 // 16)] if m == 1 else [(0, count)]

    def arrived_parts(h, m):
        return [(*cut, arrived[h, m, p], 0) for p, cut in enumerate(cut_of(h, m)) if (h, m, p) in arrived]

    def line(h, m, p):
        k = slot_of(h, m)
        span = cut_of(h, m)[p]
        low_too = m == 0 and h <= 1 and p == LOW_WITH[1]
        if h == 0:
            extra = [(low_rows, [(low, 0), (from_y[k, p], span[1])])] if low_too else []
            value = sums[k, p] = add_up(span, [whole(own_all[k]), y_parts(k)], extra)
        else:
            extra = [(low_rows, [(sums[k, p], span[1]), (arrived[h - 1, m, p], span[1])])] if low_too else []
            value = add_up(span, [sum_parts(k), arrived_parts(h - 1, m)], extra, only=(starts, 2 * nz + h))
        arrived[h, m, p] = hop(value, h)

    def line_order():
        ready, free = {}, {}
        steps = [(h, m, p) for h in range(nz - 1) for m in range(nz - 1 - h) for p in range(len(cut_of(h, m)))]
        for h, m, p in sorted(steps, key=lambda step: (step[0], step[1], step[2])):
            k = slot_of(h, m)
            there = (k + 1.0) * count if k or p else 1.0 * cut_of(0, 0)[0][1]
            if h:
                above = range(len(cut_of(h - 1, m)))
                there = max(there, max(ready[h - 1, m, q, "end"] for q in above if q == p or len(above) != len(cut_of(h, m))))
            ready[h, m, p] = there
            free[h] = max(there, free.get(h, 0.0)) + cut_of(h, m)[p][1]
            ready[h, m, p, "end"] = free[h]
        return sorted(steps, key=lambda step: (ready[step], step[0] and nz - step[0]))

    row_ids = [tenant] + [pass_on(tenant, shift) for shift in range(1, owners)]
    row_sets = [rows] + [pass_on(rows, shift) for shift in range(1, owners)]
    multiply([(0, 0)], [], chunk=512, vmem=VMEM + 13 * 2**20)
    start_y(0, 0)
    named = [slots(some_ids, me) for some_ids in row_ids]
    names = jnp.concatenate([which for which, _ in named])
    slot_sets = [row_slot for _, row_slot in named]
    low_sets = then(low_rank, row_sets, slot_sets, adapter_down_maps, names, out_width)
    low_terms = [(low_sets[0], 0)] + [(pass_on(low_sets[s], -s), 0) for s in range(1, owners)]
    low = then(total, [(low_rows, low_terms)])
    multiply([LOW_WITH], [], low, chunk=512)
    start_y(*LOW_WITH)
    multiply([(1, 0)], [0])
    start_y(1, 0)
    low_sum = deltas = None
    for h, m, p in line_order():
        k = slot_of(h, m)
        if (h, m, p) == (2, 0, 0) and nz == 4:
            last[0] += (arrived[0, 1, 1], pieces[-1][0])
        line(h, m, p)
        if h == 0:
            if k == 0 and p == 0:
                multiply([(2, 0)] if nz > 2 else [], [1])
            elif k == 0:
                if nz > 2:
                    start_y(2, 0, last[0])
                multiply([(j, 0) for j in range(3, nz)], range(2, nz))
            elif p == len(cut_of(h, m)) - 1 and k + 2 < nz:
                start_y(k + 2, 0, last[0])
        if (h, k, p) == (0, 1, len(cut_of(h, m)) - 1):
            low_at = uneven[LOW_WITH[1]][1]
            pieces = [(sums[LOW_WITH], low_at)]
            last[0] += (arrived[1, 0, 0],) if nz > 2 else ()
            for step in range(nz - 1):
                if step >= 2:
                    prefix = then(total, [(low_rows, [pieces[0], pieces[-1]])], only=(starts, 2 * nz + step))
                    pieces.append((hop(prefix, step), 0))
                else:
                    pieces.append((arrived[step, 0, LOW_WITH[1]], low_at))
        if (h, m, p) == LOW_SUM_AFTER:
            low_sum = then(total, [(low_rows, pieces)])
            low_back = [low_sum] + [pass_on(low_sum, shift) for shift in range(1, owners)]
        if deltas is None and low_sum is not None and EXPAND_AFTER in arrived:
            last[0] += (arrived[1, 1, 0],) if nz > 2 else ()
            deltas = then(expand, low_back, slot_sets, adapter_up_maps, names)
            back = [
                [(*cut, pass_on(deltas[1 + (shift - 1) * PARTS + p], -shift), 0) for p, cut in enumerate(even)]
                for shift in range(1, owners)
            ]
    span = (0, count)
    early = [arrived_parts(h, nz - 2 - h) for h in range(1, nz - 2)]
    late = [arrived_parts(h, nz - 2 - h) for h in range(nz - 1) if not 1 <= h < nz - 2]
    most = add_up(span, [whole(own_all[nz - 1]), whole(deltas[0]), y_parts(nz - 1)] + early)
    most = add_up(span, [whole(most)] + back + late[:-1])
    out = add_up(span, [whole(most)] + late[-1:])
    return out.reshape(steps, row_count, out_width)


def solution(mesh):
    placed = (
        P(None, ("groups", "dp"), "tensor"),
        P(("groups", "dp")),
        P("tensor", None),
        P(("groups", "dp"), None, "tensor"),
        P(("groups", "dp"), None, "tensor"),
    )
    return jax.shard_map(
        on_device,
        mesh=mesh,
        in_specs=placed,
        out_specs=P(None, ("groups", "dp"), "tensor"),
        check_vma=False,
    )
```

```python
import jax
import jax.numpy as jnp
import numpy as np
from jax import lax
from jax.experimental import pallas as pl
from jax.experimental.pallas import tpu as pltpu
from jax.sharding import PartitionSpec as P

SLOTS = 16
LANES = 128
CHUNK = 512
PARTS = 2
LOW_WITH = (0, PARTS - 1)
LOW_SUM_AFTER = (2, 0, 0)
EXPAND_AFTER = (1, 1, 1)
VMEM = 47 * 2**20
ANY = pl.BlockSpec(memory_space=pl.ANY)


def call(kernel, operands, after, *, in_specs, out_specs, out_shape, name, prefetch=0, scratch=(), alias=None, vmem=VMEM):
    inputs, extra = len(operands), len(after)

    def body(*refs):
        kernel(*refs[:inputs], *refs[inputs + extra :])

    return pl.pallas_call(
        body,
        grid_spec=pltpu.PrefetchScalarGridSpec(
            num_scalar_prefetch=prefetch,
            grid=(),
            in_specs=list(in_specs) + [ANY] * extra,
            out_specs=out_specs,
            scratch_shapes=list(scratch),
        ),
        out_shape=out_shape,
        input_output_aliases=alias or {},
        compiler_params=pltpu.CompilerParams(vmem_limit_bytes=vmem),
        cost_estimate=pl.CostEstimate(flops=1, transcendentals=0, bytes_accessed=1),
        name=name,
    )(*operands, *after)


def hold(value, after):
    def kernel(value_ref, out_ref):
        pass

    return call(
        kernel, [value], after, in_specs=[ANY], out_specs=ANY,
        out_shape=jax.ShapeDtypeStruct(value.shape, value.dtype), name="hold", alias={0: 0},
    )


def products(rows, weight, starts, names, size, outs, tail=None, chunk=1024, vmem=VMEM, after=()):
    count, width = rows.shape
    blocks = len(names)
    chunks = [(at, min(chunk, size - at)) for at in range(0, size, chunk)]
    low = min(first for _, first, _ in outs)
    high = max(first + some for _, first, some in outs)
    upper = (high - low) // 32 * 16
    row_parts = [(0, upper), (upper, high - low - upper)]
    tails = [] if tail is None else [tail]
    heights = [some for _, _, some in outs]
    for array in tails:
        heights[-1] += array.shape[0]

    def kernel(starts_ref, rows_ref, weight_ref, *refs):
        tail_refs, refs = refs[: len(tails)], refs[len(tails) :]
        out_refs, (x, w, *refs) = refs[: len(outs)], refs[len(outs) :]
        stage, (x_sems, w_sems, out_sems, tail_sems) = refs[: len(outs)], refs[len(outs) :]
        x_copies = [
            pltpu.make_async_copy(
                rows_ref.at[pl.ds(low + at, some)], x.at[pl.ds(at, some)], x_sems.at[i]
            )
            for i, (at, some) in enumerate(row_parts)
        ]
        w_copies = [
            [
                pltpu.make_async_copy(
                    weight_ref.at[:, pl.ds(pl.multiple_of(starts_ref[names[b]] + at, LANES), extent)],
                    w.at[b, :, pl.ds(at, extent)],
                    w_sems.at[b, c],
                )
                for c, (at, extent) in enumerate(chunks)
            ]
            for b in range(blocks)
        ]
        x_copies[0].start()
        w_copies[0][0].start()
        x_copies[1].start()
        for b in range(blocks):
            for c in range(len(chunks)):
                if b or c:
                    w_copies[b][c].start()
        stores = []
        for ref in tail_refs:
            below = pl.ds(outs[-1][2], ref.shape[0])
            read = pltpu.make_async_copy(ref, stage[-1].at[below], tail_sems.at[0])
            read.start()
            read.wait()
            stores.append(pltpu.make_async_copy(stage[-1].at[below], out_refs[-1].at[below], tail_sems.at[1]))
            stores[-1].start()
        for copy in x_copies:
            copy.wait()
        for b in range(blocks):
            for c, (at, extent) in enumerate(chunks):
                w_copies[b][c].wait()
                for o, (index, first, some) in enumerate(outs):
                    if index == b:
                        value = jnp.dot(
                            x[first - low : first - low + some, :], w[b, :, at : at + extent],
                            preferred_element_type=jnp.float32,
                        )
                        stage[o][:some, at : at + extent] = value.astype(rows.dtype)
                        store = pltpu.make_async_copy(
                            stage[o].at[pl.ds(0, some), pl.ds(at, extent)],
                            out_refs[o].at[pl.ds(0, some), pl.ds(at, extent)],
                            out_sems.at[o, c],
                        )
                        store.start()
                        stores.append(store)
        for store in stores:
            store.wait()

    shapes = [(height, size) for height in heights]
    return call(
        kernel, [starts, rows, weight] + tails, after, prefetch=1,
        in_specs=[ANY] * (2 + len(tails)),
        out_specs=[ANY] * len(outs),
        out_shape=[jax.ShapeDtypeStruct(shape, rows.dtype) for shape in shapes],
        scratch=[pltpu.VMEM((high - low, width), rows.dtype), pltpu.VMEM((blocks, width, size), rows.dtype)]
        + [pltpu.VMEM(shape, rows.dtype) for shape in shapes]
        + [
            pltpu.SemaphoreType.DMA((2,)),
            pltpu.SemaphoreType.DMA((blocks, len(chunks))),
            pltpu.SemaphoreType.DMA((len(outs), len(chunks))),
            pltpu.SemaphoreType.DMA((2,)),
        ],
        name="products", vmem=vmem,
    )


def total(runs, dtype=jnp.bfloat16, into=None, only=None, after=()):
    width = runs[0][1][0][0].shape[1]
    height = sum(some for some, _ in runs)
    rows_in_all, first, so_far = into or (height, 0, None)
    tiles = []
    at = 0
    for r, (some, terms) in enumerate(runs):
        split = 4 if some * len(terms) > 2000 else 2 if some * width > 2**17 else 1
        size = -(-some // (16 * split)) * 16
        for skip in range(0, some, size):
            tiles.append((r, skip, min(size, some - skip), at + skip))
        at += some
    operands = [term for _, terms in runs for term, _ in terms]
    before = [] if so_far is None else [so_far]
    most_terms = max(len(terms) for _, terms in runs)
    of_run = np.cumsum([0] + [len(terms) for _, terms in runs])

    flags = [] if only is None else [only[0]]

    def kernel(*refs):
        if only is None:
            add(*refs)
        else:
            pl.when(refs[0][only[1]] != 0)(lambda: add(*refs[1:]))

    def add(*refs):
        term_refs, out_ref = refs[: len(operands)], refs[len(operands) + len(before)]
        refs = refs[len(operands) + len(before) + 1 :]
        bufs, (stage, in_sems, out_sems) = refs[: len(operands)], refs[len(operands) :]
        reads, writes = [], []
        for n, (r, skip, size, place) in enumerate(tiles):
            reads.append(
                [
                    pltpu.make_async_copy(
                        term_refs[of_run[r] + t].at[pl.ds(start + skip, size)],
                        bufs[of_run[r] + t].at[pl.ds(skip, size)],
                        in_sems.at[t, n],
                    )
                    for t, (_, start) in enumerate(runs[r][1])
                ]
            )
            writes.append(
                pltpu.make_async_copy(
                    stage.at[pl.ds(place, size)], out_ref.at[pl.ds(first + place, size)], out_sems.at[n]
                )
            )
        for some in reads:
            for read in some:
                read.start()
        for n, (r, skip, size, place) in enumerate(tiles):
            for read in reads[n]:
                read.wait()
            value = None
            for t in range(len(runs[r][1])):
                part = bufs[of_run[r] + t][skip : skip + size, :].astype(jnp.float32)
                value = part if value is None else value + part
            stage[place : place + size, :] = value.astype(dtype)
            writes[n].start()
        for write in writes:
            write.wait()

    return call(
        kernel, flags + operands + before, after, prefetch=len(flags),
        in_specs=[ANY] * (len(operands) + len(before)),
        out_specs=ANY,
        out_shape=jax.ShapeDtypeStruct((rows_in_all, width), dtype),
        scratch=[pltpu.VMEM((some, width), term.dtype) for some, terms in runs for term, _ in terms]
        + [
            pltpu.VMEM((height, width), dtype),
            pltpu.SemaphoreType.DMA((most_terms, len(tiles))),
            pltpu.SemaphoreType.DMA((len(tiles),)),
        ],
        alias={len(flags) + len(operands): 0} if before else None,
        name="total",
    )


def lane_pick(slot_ref, repeats, shape, rank, first):
    slot = jnp.concatenate([slot_ref[...]] * repeats, axis=0)
    return slot == lax.broadcasted_iota(jnp.int32, shape, 1) // rank + first


def block_copies(index_ref, maps_ref, buf, sems, sets, rank):
    each = index_ref.shape[0] // sets
    return [
        [
            pltpu.make_async_copy(
                maps_ref.at[index_ref[s * each + i]], buf.at[pl.ds((s * each + i) * rank, rank)],
                sems.at[s * each + i],
            )
            for i in range(each)
        ]
        for s in range(sets)
    ]


def low_rank(row_sets, slot_sets, maps, index, wide, after=()):
    sets = len(row_sets)
    count, width = row_sets[0].shape
    rank = maps.shape[1]
    span = index.shape[0] // sets * rank
    repeats = count // slot_sets[0].shape[0]
    half = count // 2
    group = 256
    tall = half * 2 * rank // wide

    def kernel(index_ref, *refs):
        row_refs, slot_refs, maps_ref = refs[:sets], refs[sets : 2 * sets], refs[2 * sets]
        out_refs, (rows_buf, maps_buf, row_sems, map_sems) = refs[2 * sets + 1 : 3 * sets + 1], refs[3 * sets + 1 :]
        row_copies = [
            pltpu.make_async_copy(row_refs[s], rows_buf.at[s], row_sems.at[s]) for s in range(sets)
        ]
        map_copies = block_copies(index_ref, maps_ref, maps_buf, map_sems, sets, rank)
        for s in range(sets):
            row_copies[s].start()
            for copy in map_copies[s]:
                copy.start()
        for s in range(sets):
            row_copies[s].wait()
            for copy in map_copies[s]:
                copy.wait()
            acc = None
            for at in range(0, span, group):
                scores = lax.dot_general(
                    rows_buf[s], maps_buf[s * span + at : s * span + at + group],
                    (((1,), (1,)), ((), ())), preferred_element_type=jnp.float32,
                )
                pick = lane_pick(slot_refs[s], repeats, (count, group), rank, at // rank)
                term = jnp.where(pick, scores, 0.0)
                acc = term if acc is None else acc + term
            summed = acc[:, 0:rank]
            for g in range(1, group // rank):
                summed += acc[:, g * rank : (g + 1) * rank]
            summed = summed.astype(out_refs[s].dtype)
            for b in range(half // tall):
                lanes = slice(b * 2 * rank, (b + 1) * 2 * rank)
                both = [summed[start + b * tall : start + (b + 1) * tall] for start in (0, half)]
                out_refs[s][:, lanes] = jnp.concatenate(both, axis=1)

    return call(
        kernel, [index, *row_sets, *slot_sets, maps], after, prefetch=1,
        in_specs=[ANY] * sets + [pl.BlockSpec(memory_space=pltpu.VMEM)] * sets + [ANY],
        out_specs=[pl.BlockSpec(memory_space=pltpu.VMEM)] * sets,
        out_shape=[jax.ShapeDtypeStruct((tall, wide), jnp.bfloat16)] * sets,
        scratch=[
            pltpu.VMEM((sets, count, width), row_sets[0].dtype),
            pltpu.VMEM((sets * span, width), maps.dtype),
            pltpu.SemaphoreType.DMA((sets,)),
            pltpu.SemaphoreType.DMA((index.shape[0],)),
        ],
        name="low_rank",
    )


def expand(low_sets, slot_sets, maps, index, after=()):
    sets = len(slot_sets)
    rank, width = maps.shape[1:]
    tall = low_sets[0].shape[0]
    half = low_sets[0].size // (2 * rank)
    count = 2 * half
    span = index.shape[0] // sets * rank
    repeats = count // slot_sets[0].shape[0]

    outs = [(0, 0, count)] + [
        (s, p * count // PARTS, count // PARTS) for s in range(1, sets) for p in range(PARTS)
    ]

    def kernel(index_ref, *refs):
        low_refs, refs = refs[:sets], refs[sets:]
        slot_refs, maps_ref, out_refs = refs[:sets], refs[sets], refs[sets + 1 : sets + 1 + len(outs)]
        stage, maps_buf, map_sems, out_sems = refs[sets + 1 + len(outs) :]
        map_copies = block_copies(index_ref, maps_ref, maps_buf, map_sems, sets, rank)
        writes = [
            pltpu.make_async_copy(stage.at[s, pl.ds(first, some)], out_refs[o], out_sems.at[o])
            for o, (s, first, some) in enumerate(outs)
        ]
        order = list(range(1, sets)) + [0]
        for s in order:
            for copy in map_copies[s]:
                copy.start()
        for s in order:
            lanes = [b * 2 * rank for b in range(half // tall)]
            mine = jnp.concatenate(
                [low_refs[s][:, at + side : at + side + rank] for side in (0, rank) for at in lanes], axis=0
            )
            tiled = jnp.concatenate([mine] * (span // rank), axis=1)
            pick = lane_pick(slot_refs[s], repeats, (count, span), rank, 0)
            picked = jnp.where(pick, tiled, jnp.zeros_like(tiled))
            for copy in map_copies[s]:
                copy.wait()
            for at in range(0, width, CHUNK):
                value = jnp.dot(
                    picked, maps_buf[s * span : (s + 1) * span, at : at + CHUNK], preferred_element_type=jnp.float32
                )
                stage[s, :, at : at + CHUNK] = value.astype(stage.dtype)
            for o, (which, _, _) in enumerate(outs):
                if which == s:
                    writes[o].start()
        for write in writes:
            write.wait()

    return call(
        kernel, [index, *low_sets, *slot_sets, maps], after, prefetch=1,
        in_specs=[pl.BlockSpec(memory_space=pltpu.VMEM)] * (2 * sets) + [ANY],
        out_specs=[ANY] * len(outs),
        out_shape=[jax.ShapeDtypeStruct((some, width), jnp.bfloat16) for _, _, some in outs],
        scratch=[
            pltpu.VMEM((sets, count, width), jnp.bfloat16),
            pltpu.VMEM((sets * span, width), maps.dtype),
            pltpu.SemaphoreType.DMA((index.shape[0],)),
            pltpu.SemaphoreType.DMA((len(outs),)),
        ],
        name="expand",
    )


def line_plan(nz):
    order = np.zeros((nz, nz), np.int32)
    for z in range(nz):
        def need(j):
            if j == z:
                return (2 * nz, 0)
            return (nz - 1 - j + z, j) if j > z else (nz - 1 - z + j, nz - j)

        order[z] = sorted(range(nz), key=need)
    return order


def on_device(attention_result, tenant, projection_weight, adapter_down_maps, adapter_up_maps):
    steps, row_count, width = attention_result.shape
    local_adapters = adapter_down_maps.shape[0]
    owners = lax.axis_size("dp")
    me = lax.axis_index("dp")
    n = lax.axis_size("tensor")
    nz = n // 2
    place = lax.axis_index("tensor")
    order = line_plan(nz)
    out_width = projection_weight.shape[1] // n

    def swap_y(value):
        return lax.ppermute(value, "tensor", [(t, t ^ 1) for t in range(n)])

    def hop(value, h):
        pairs = []
        for side in range(2):
            pairs.append((h * 2 + side, (h + 1) * 2 + side))
            pairs.append(((nz - 1 - h) * 2 + side, (nz - 2 - h) * 2 + side))
        return lax.ppermute(value, "tensor", pairs)

    def slot_of(h, m):
        return list(order[h]).index(nz - 1 - m)

    def pass_on(value, shift):
        return lax.ppermute(value, "dp", [(i, (i + shift) % owners) for i in range(owners)])

    rows = attention_result.reshape(steps * row_count, width)
    count = steps * row_count
    last = [()]

    def then(kernel, *operands, **options):
        out = kernel(*operands, after=last[0], **options)
        last[0] = (out[0] if isinstance(out, (tuple, list)) else out,)
        return out

    slot_range = jnp.arange(SLOTS, dtype=jnp.int32)
    ids = jnp.arange(local_adapters, dtype=jnp.int32)

    def slots(row_ids, owner):
        hit = row_ids[:, None] - owner * local_adapters == ids[None, :]
        used = jnp.any(hit, axis=0)
        position = jnp.sum(
            (used[None, :] & (ids[None, :] < ids[:, None])).astype(jnp.int32), axis=1
        )
        names = jnp.sum(
            jnp.where(used[None, :] & (position[None, :] == slot_range[:, None]), ids[None, :], 0),
            axis=1,
        )
        row_slot = jnp.sum(jnp.where(hit, position[None, :] + 1, 0), axis=1) - 1
        return names, row_slot[:, None]

    blocks = [[(order[t // 2][k] * 2 + side) for side in (1 - t % 2, t % 2) for k in range(nz)] for t in range(n)]
    sends = [[int(t // 2 in (h, nz - 1 - h)) for h in range(nz - 1)] for t in range(n)]
    table = np.concatenate([np.asarray(blocks, np.int32) * out_width, np.asarray(sends, np.int32)], axis=1)
    starts = jnp.asarray(table)[place]
    low_rows = count * adapter_down_maps.shape[1] // out_width
    even = [(p * count // PARTS, count // PARTS) for p in range(PARTS)]
    high_part = -(-(count + low_rows) // 32) * 16
    uneven = [(0, high_part), (high_part, count - high_part)]
    away_part, own_all, from_y, sums, arrived = {}, {}, {}, {}, {}

    def split(k):
        return uneven if k == 0 else [(0, count)]

    def add_up(span, terms, extra=(), dtype=jnp.bfloat16, only=None):
        low_row, high_row = span[0], span[0] + span[1]
        cuts = {low_row, high_row}
        for term in terms:
            for at, some, _, _ in term:
                cuts.update(row for row in (at, at + some) if low_row < row < high_row)
        cuts = sorted(cuts)
        runs = []
        for begin, end in zip(cuts, cuts[1:]):
            here = [
                (array, row + begin - at) for term in terms for at, some, array, row in term if at <= begin < at + some
            ]
            runs.append((end - begin, here))
        return then(total, runs + list(extra), dtype, None, only)

    def whole(array):
        return [(0, count, array, 0)]

    def multiply(aways, owns, tail=None, chunk=1024, vmem=VMEM):
        ks = sorted({k for k, _ in aways})
        names = ks + [nz + k for k in owns]
        outs = [(ks.index(k), *split(k)[p]) for k, p in aways]
        outs += [(len(ks) + i, 0, count) for i in range(len(owns))]
        done = then(products, rows, projection_weight, starts, names, out_width, outs, tail, chunk, vmem)
        away_part.update(zip(aways, done))
        own_all.update(zip(owns, done[len(aways) :]))

    def start_y(k, p, after=None):
        value = away_part[k, p]
        from_y[k, p] = swap_y(value if after is None else hold(value, after))

    def y_parts(k):
        return [(*cut, from_y[k, p], 0) for p, cut in enumerate(split(k)) if (k, p) in from_y]

    def sum_parts(k):
        return [(*cut, sums[k, p], 0) for p, cut in enumerate(cut_of(0, k)) if (k, p) in sums]

    def cut_of(h, m):
        if m == 0 and h <= 1:
            return uneven
        return [(0, count * 8 // 16), (count * 8 // 16, count * 8 // 16)] if m == 1 else [(0, count)]

    def arrived_parts(h, m):
        return [(*cut, arrived[h, m, p], 0) for p, cut in enumerate(cut_of(h, m)) if (h, m, p) in arrived]

    def line(h, m, p):
        k = slot_of(h, m)
        span = cut_of(h, m)[p]
        low_too = m == 0 and h <= 1 and p == LOW_WITH[1]
        if h == 0:
            extra = [(low_rows, [(low, 0), (from_y[k, p], span[1])])] if low_too else []
            value = sums[k, p] = add_up(span, [whole(own_all[k]), y_parts(k)], extra)
        else:
            extra = [(low_rows, [(sums[k, p], span[1]), (arrived[h - 1, m, p], span[1])])] if low_too else []
            value = add_up(span, [sum_parts(k), arrived_parts(h - 1, m)], extra, only=(starts, 2 * nz + h))
        arrived[h, m, p] = hop(value, h)

    def line_order():
        ready, free = {}, {}
        steps = [(h, m, p) for h in range(nz - 1) for m in range(nz - 1 - h) for p in range(len(cut_of(h, m)))]
        for h, m, p in sorted(steps, key=lambda step: (step[0], step[1], step[2])):
            k = slot_of(h, m)
            there = (k + 1.0) * count if k or p else 1.0 * cut_of(0, 0)[0][1]
            if h:
                above = range(len(cut_of(h - 1, m)))
                there = max(there, max(ready[h - 1, m, q, "end"] for q in above if q == p or len(above) != len(cut_of(h, m))))
            ready[h, m, p] = there
            free[h] = max(there, free.get(h, 0.0)) + cut_of(h, m)[p][1]
            ready[h, m, p, "end"] = free[h]
        return sorted(steps, key=lambda step: (ready[step], step[0] and nz - step[0]))

    row_ids = [tenant] + [pass_on(tenant, shift) for shift in range(1, owners)]
    row_sets = [rows] + [pass_on(rows, shift) for shift in range(1, owners)]
    multiply([(0, 0)], [], chunk=512, vmem=VMEM + 16 * 2**20)
    start_y(0, 0)
    named = [slots(some_ids, me) for some_ids in row_ids]
    names = jnp.concatenate([which for which, _ in named])
    slot_sets = [row_slot for _, row_slot in named]
    low_sets = then(low_rank, row_sets, slot_sets, adapter_down_maps, names, out_width)
    low_terms = [(low_sets[0], 0)] + [(pass_on(low_sets[s], -s), 0) for s in range(1, owners)]
    low = then(total, [(low_rows, low_terms)])
    multiply([LOW_WITH], [], low, chunk=512)
    start_y(*LOW_WITH)
    multiply([(1, 0)], [0])
    start_y(1, 0)
    low_sum = deltas = None
    for h, m, p in line_order():
        k = slot_of(h, m)
        if (h, m, p) == (2, 0, 0) and nz == 4:
            last[0] += (arrived[0, 1, 1], pieces[-1][0])
        line(h, m, p)
        if h == 0:
            if k == 0 and p == 0:
                multiply([(2, 0)] if nz > 2 else [], [1])
            elif k == 0:
                if nz > 2:
                    start_y(2, 0, last[0])
                multiply([(j, 0) for j in range(3, nz)], range(2, nz))
            elif p == len(cut_of(h, m)) - 1 and k + 2 < nz:
                start_y(k + 2, 0, last[0])
        if (h, k, p) == (0, 1, len(cut_of(h, m)) - 1):
            low_at = uneven[LOW_WITH[1]][1]
            pieces = [(sums[LOW_WITH], low_at)]
            last[0] += (arrived[1, 0, 0],) if nz > 2 else ()
            for step in range(nz - 1):
                if step >= 2:
                    prefix = then(total, [(low_rows, [pieces[0], pieces[-1]])], only=(starts, 2 * nz + step))
                    pieces.append((hop(prefix, step), 0))
                else:
                    pieces.append((arrived[step, 0, LOW_WITH[1]], low_at))
        if (h, m, p) == LOW_SUM_AFTER:
            low_sum = then(total, [(low_rows, pieces)])
            low_back = [low_sum] + [pass_on(low_sum, shift) for shift in range(1, owners)]
        if deltas is None and low_sum is not None and EXPAND_AFTER in arrived:
            last[0] += (arrived[1, 1, 0],) if nz > 2 else ()
            deltas = then(expand, low_back, slot_sets, adapter_up_maps, names)
            back = [
                [(*cut, pass_on(deltas[1 + (shift - 1) * PARTS + p], -shift), 0) for p, cut in enumerate(even)]
                for shift in range(1, owners)
            ]
    span = (0, count)
    early = [arrived_parts(h, nz - 2 - h) for h in range(1, nz - 2)]
    late = [arrived_parts(h, nz - 2 - h) for h in range(nz - 1) if not 1 <= h < nz - 2]
    most = add_up(span, [whole(own_all[nz - 1]), whole(deltas[0]), y_parts(nz - 1)] + early)
    most = add_up(span, [whole(most)] + back + late[:-1])
    out = add_up(span, [whole(most)] + late[-1:])
    return out.reshape(steps, row_count, out_width)


def solution(mesh):
    placed = (
        P(None, ("groups", "dp"), "tensor"),
        P(("groups", "dp")),
        P("tensor", None),
        P(("groups", "dp"), None, "tensor"),
        P(("groups", "dp"), None, "tensor"),
    )
    return jax.shard_map(
        on_device,
        mesh=mesh,
        in_specs=placed,
        out_specs=P(None, ("groups", "dp"), "tensor"),
        check_vma=False,
    )
```

```python
import jax
import jax.numpy as jnp
import numpy as np
from jax import lax
from jax.experimental import pallas as pl
from jax.experimental.pallas import tpu as pltpu
from jax.sharding import PartitionSpec as P

SLOTS = 16
LANES = 128
CHUNK = 512
PARTS = 2
LOW_WITH = (0, PARTS - 1)
LOW_SUM_AFTER = (2, 0, 0)
EXPAND_AFTER = (1, 1, 1)
VMEM = 47 * 2**20
ANY = pl.BlockSpec(memory_space=pl.ANY)


def call(kernel, operands, after, *, in_specs, out_specs, out_shape, name, prefetch=0, scratch=(), alias=None, vmem=VMEM):
    inputs, extra = len(operands), len(after)

    def body(*refs):
        kernel(*refs[:inputs], *refs[inputs + extra :])

    return pl.pallas_call(
        body,
        grid_spec=pltpu.PrefetchScalarGridSpec(
            num_scalar_prefetch=prefetch,
            grid=(),
            in_specs=list(in_specs) + [ANY] * extra,
            out_specs=out_specs,
            scratch_shapes=list(scratch),
        ),
        out_shape=out_shape,
        input_output_aliases=alias or {},
        compiler_params=pltpu.CompilerParams(vmem_limit_bytes=vmem),
        cost_estimate=pl.CostEstimate(flops=1, transcendentals=0, bytes_accessed=1),
        name=name,
    )(*operands, *after)


def hold(value, after):
    def kernel(value_ref, out_ref):
        pass

    return call(
        kernel, [value], after, in_specs=[ANY], out_specs=ANY,
        out_shape=jax.ShapeDtypeStruct(value.shape, value.dtype), name="hold", alias={0: 0},
    )


def products(rows, weight, starts, names, size, outs, tail=None, chunk=1024, vmem=VMEM, after=()):
    count, width = rows.shape
    blocks = len(names)
    chunks = [(at, min(chunk, size - at)) for at in range(0, size, chunk)]
    low = min(first for _, first, _ in outs)
    high = max(first + some for _, first, some in outs)
    upper = (high - low) // 32 * 16
    row_parts = [(0, upper), (upper, high - low - upper)]
    tails = [] if tail is None else [tail]
    heights = [some for _, _, some in outs]
    for array in tails:
        heights[-1] += array.shape[0]

    def kernel(starts_ref, rows_ref, weight_ref, *refs):
        tail_refs, refs = refs[: len(tails)], refs[len(tails) :]
        out_refs, (x, w, *refs) = refs[: len(outs)], refs[len(outs) :]
        stage, (x_sems, w_sems, out_sems, tail_sems) = refs[: len(outs)], refs[len(outs) :]
        x_copies = [
            pltpu.make_async_copy(
                rows_ref.at[pl.ds(low + at, some)], x.at[pl.ds(at, some)], x_sems.at[i]
            )
            for i, (at, some) in enumerate(row_parts)
        ]
        w_copies = [
            [
                pltpu.make_async_copy(
                    weight_ref.at[:, pl.ds(pl.multiple_of(starts_ref[names[b]] + at, LANES), extent)],
                    w.at[b, :, pl.ds(at, extent)],
                    w_sems.at[b, c],
                )
                for c, (at, extent) in enumerate(chunks)
            ]
            for b in range(blocks)
        ]
        x_copies[0].start()
        w_copies[0][0].start()
        x_copies[1].start()
        for b in range(blocks):
            for c in range(len(chunks)):
                if b or c:
                    w_copies[b][c].start()
        stores = []
        for ref in tail_refs:
            below = pl.ds(outs[-1][2], ref.shape[0])
            read = pltpu.make_async_copy(ref, stage[-1].at[below], tail_sems.at[0])
            read.start()
            read.wait()
            stores.append(pltpu.make_async_copy(stage[-1].at[below], out_refs[-1].at[below], tail_sems.at[1]))
            stores[-1].start()
        for copy in x_copies:
            copy.wait()
        for b in range(blocks):
            for c, (at, extent) in enumerate(chunks):
                w_copies[b][c].wait()
                for o, (index, first, some) in enumerate(outs):
                    if index == b:
                        value = jnp.dot(
                            x[first - low : first - low + some, :], w[b, :, at : at + extent],
                            preferred_element_type=jnp.float32,
                        )
                        stage[o][:some, at : at + extent] = value.astype(rows.dtype)
                        store = pltpu.make_async_copy(
                            stage[o].at[pl.ds(0, some), pl.ds(at, extent)],
                            out_refs[o].at[pl.ds(0, some), pl.ds(at, extent)],
                            out_sems.at[o, c],
                        )
                        store.start()
                        stores.append(store)
        for store in stores:
            store.wait()

    shapes = [(height, size) for height in heights]
    return call(
        kernel, [starts, rows, weight] + tails, after, prefetch=1,
        in_specs=[ANY] * (2 + len(tails)),
        out_specs=[ANY] * len(outs),
        out_shape=[jax.ShapeDtypeStruct(shape, rows.dtype) for shape in shapes],
        scratch=[pltpu.VMEM((high - low, width), rows.dtype), pltpu.VMEM((blocks, width, size), rows.dtype)]
        + [pltpu.VMEM(shape, rows.dtype) for shape in shapes]
        + [
            pltpu.SemaphoreType.DMA((2,)),
            pltpu.SemaphoreType.DMA((blocks, len(chunks))),
            pltpu.SemaphoreType.DMA((len(outs), len(chunks))),
            pltpu.SemaphoreType.DMA((2,)),
        ],
        name="products", vmem=vmem,
    )


def total(runs, dtype=jnp.bfloat16, into=None, only=None, after=()):
    width = runs[0][1][0][0].shape[1]
    height = sum(some for some, _ in runs)
    rows_in_all, first, so_far = into or (height, 0, None)
    tiles = []
    at = 0
    for r, (some, terms) in enumerate(runs):
        split = 4 if some * len(terms) > 2000 else 2 if some * width > 2**17 else 1
        size = -(-some // (16 * split)) * 16
        for skip in range(0, some, size):
            tiles.append((r, skip, min(size, some - skip), at + skip))
        at += some
    operands = [term for _, terms in runs for term, _ in terms]
    before = [] if so_far is None else [so_far]
    most_terms = max(len(terms) for _, terms in runs)
    of_run = np.cumsum([0] + [len(terms) for _, terms in runs])

    flags = [] if only is None else [only[0]]

    def kernel(*refs):
        if only is None:
            add(*refs)
        else:
            pl.when(refs[0][only[1]] != 0)(lambda: add(*refs[1:]))

    def add(*refs):
        term_refs, out_ref = refs[: len(operands)], refs[len(operands) + len(before)]
        refs = refs[len(operands) + len(before) + 1 :]
        bufs, (stage, in_sems, out_sems) = refs[: len(operands)], refs[len(operands) :]
        reads, writes = [], []
        for n, (r, skip, size, place) in enumerate(tiles):
            reads.append(
                [
                    pltpu.make_async_copy(
                        term_refs[of_run[r] + t].at[pl.ds(start + skip, size)],
                        bufs[of_run[r] + t].at[pl.ds(skip, size)],
                        in_sems.at[t, n],
                    )
                    for t, (_, start) in enumerate(runs[r][1])
                ]
            )
            writes.append(
                pltpu.make_async_copy(
                    stage.at[pl.ds(place, size)], out_ref.at[pl.ds(first + place, size)], out_sems.at[n]
                )
            )
        for some in reads:
            for read in some:
                read.start()
        for n, (r, skip, size, place) in enumerate(tiles):
            for read in reads[n]:
                read.wait()
            value = None
            for t in range(len(runs[r][1])):
                part = bufs[of_run[r] + t][skip : skip + size, :].astype(jnp.float32)
                value = part if value is None else value + part
            stage[place : place + size, :] = value.astype(dtype)
            writes[n].start()
        for write in writes:
            write.wait()

    return call(
        kernel, flags + operands + before, after, prefetch=len(flags),
        in_specs=[ANY] * (len(operands) + len(before)),
        out_specs=ANY,
        out_shape=jax.ShapeDtypeStruct((rows_in_all, width), dtype),
        scratch=[pltpu.VMEM((some, width), term.dtype) for some, terms in runs for term, _ in terms]
        + [
            pltpu.VMEM((height, width), dtype),
            pltpu.SemaphoreType.DMA((most_terms, len(tiles))),
            pltpu.SemaphoreType.DMA((len(tiles),)),
        ],
        alias={len(flags) + len(operands): 0} if before else None,
        name="total",
    )


def lane_pick(slot_ref, repeats, shape, rank, first):
    slot = jnp.concatenate([slot_ref[...]] * repeats, axis=0)
    return slot == lax.broadcasted_iota(jnp.int32, shape, 1) // rank + first


def block_copies(index_ref, maps_ref, buf, sems, sets, rank):
    each = index_ref.shape[0] // sets
    return [
        [
            pltpu.make_async_copy(
                maps_ref.at[index_ref[s * each + i]], buf.at[pl.ds((s * each + i) * rank, rank)],
                sems.at[s * each + i],
            )
            for i in range(each)
        ]
        for s in range(sets)
    ]


def low_rank(row_sets, slot_sets, maps, index, wide, after=()):
    sets = len(row_sets)
    count, width = row_sets[0].shape
    rank = maps.shape[1]
    span = index.shape[0] // sets * rank
    repeats = count // slot_sets[0].shape[0]
    half = count // 2
    group = 256
    tall = half * 2 * rank // wide

    def kernel(index_ref, *refs):
        row_refs, slot_refs, maps_ref = refs[:sets], refs[sets : 2 * sets], refs[2 * sets]
        out_refs, (rows_buf, maps_buf, row_sems, map_sems) = refs[2 * sets + 1 : 3 * sets + 1], refs[3 * sets + 1 :]
        row_copies = [
            pltpu.make_async_copy(row_refs[s], rows_buf.at[s], row_sems.at[s]) for s in range(sets)
        ]
        map_copies = block_copies(index_ref, maps_ref, maps_buf, map_sems, sets, rank)
        for s in range(sets):
            row_copies[s].start()
            for copy in map_copies[s]:
                copy.start()
        for s in range(sets):
            row_copies[s].wait()
            for copy in map_copies[s]:
                copy.wait()
            acc = None
            for at in range(0, span, group):
                scores = lax.dot_general(
                    rows_buf[s], maps_buf[s * span + at : s * span + at + group],
                    (((1,), (1,)), ((), ())), preferred_element_type=jnp.float32,
                )
                pick = lane_pick(slot_refs[s], repeats, (count, group), rank, at // rank)
                term = jnp.where(pick, scores, 0.0)
                acc = term if acc is None else acc + term
            summed = acc[:, 0:rank]
            for g in range(1, group // rank):
                summed += acc[:, g * rank : (g + 1) * rank]
            summed = summed.astype(out_refs[s].dtype)
            for b in range(half // tall):
                lanes = slice(b * 2 * rank, (b + 1) * 2 * rank)
                both = [summed[start + b * tall : start + (b + 1) * tall] for start in (0, half)]
                out_refs[s][:, lanes] = jnp.concatenate(both, axis=1)

    return call(
        kernel, [index, *row_sets, *slot_sets, maps], after, prefetch=1,
        in_specs=[ANY] * sets + [pl.BlockSpec(memory_space=pltpu.VMEM)] * sets + [ANY],
        out_specs=[pl.BlockSpec(memory_space=pltpu.VMEM)] * sets,
        out_shape=[jax.ShapeDtypeStruct((tall, wide), jnp.bfloat16)] * sets,
        scratch=[
            pltpu.VMEM((sets, count, width), row_sets[0].dtype),
            pltpu.VMEM((sets * span, width), maps.dtype),
            pltpu.SemaphoreType.DMA((sets,)),
            pltpu.SemaphoreType.DMA((index.shape[0],)),
        ],
        name="low_rank",
    )


def expand(low_sets, slot_sets, maps, index, after=()):
    sets = len(slot_sets)
    rank, width = maps.shape[1:]
    tall = low_sets[0].shape[0]
    half = low_sets[0].size // (2 * rank)
    count = 2 * half
    span = index.shape[0] // sets * rank
    repeats = count // slot_sets[0].shape[0]

    outs = [(0, 0, count)] + [
        (s, p * count // PARTS, count // PARTS) for s in range(1, sets) for p in range(PARTS)
    ]

    def kernel(index_ref, *refs):
        low_refs, refs = refs[:sets], refs[sets:]
        slot_refs, maps_ref, out_refs = refs[:sets], refs[sets], refs[sets + 1 : sets + 1 + len(outs)]
        stage, maps_buf, map_sems, out_sems = refs[sets + 1 + len(outs) :]
        map_copies = block_copies(index_ref, maps_ref, maps_buf, map_sems, sets, rank)
        writes = [
            pltpu.make_async_copy(stage.at[s, pl.ds(first, some)], out_refs[o], out_sems.at[o])
            for o, (s, first, some) in enumerate(outs)
        ]
        order = list(range(1, sets)) + [0]
        for s in order:
            for copy in map_copies[s]:
                copy.start()
        for s in order:
            lanes = [b * 2 * rank for b in range(half // tall)]
            mine = jnp.concatenate(
                [low_refs[s][:, at + side : at + side + rank] for side in (0, rank) for at in lanes], axis=0
            )
            tiled = jnp.concatenate([mine] * (span // rank), axis=1)
            pick = lane_pick(slot_refs[s], repeats, (count, span), rank, 0)
            picked = jnp.where(pick, tiled, jnp.zeros_like(tiled))
            for copy in map_copies[s]:
                copy.wait()
            for at in range(0, width, CHUNK):
                value = jnp.dot(
                    picked, maps_buf[s * span : (s + 1) * span, at : at + CHUNK], preferred_element_type=jnp.float32
                )
                stage[s, :, at : at + CHUNK] = value.astype(stage.dtype)
            for o, (which, _, _) in enumerate(outs):
                if which == s:
                    writes[o].start()
        for write in writes:
            write.wait()

    return call(
        kernel, [index, *low_sets, *slot_sets, maps], after, prefetch=1,
        in_specs=[pl.BlockSpec(memory_space=pltpu.VMEM)] * (2 * sets) + [ANY],
        out_specs=[ANY] * len(outs),
        out_shape=[jax.ShapeDtypeStruct((some, width), jnp.bfloat16) for _, _, some in outs],
        scratch=[
            pltpu.VMEM((sets, count, width), jnp.bfloat16),
            pltpu.VMEM((sets * span, width), maps.dtype),
            pltpu.SemaphoreType.DMA((index.shape[0],)),
            pltpu.SemaphoreType.DMA((len(outs),)),
        ],
        name="expand",
    )


def line_plan(nz):
    order = np.zeros((nz, nz), np.int32)
    for z in range(nz):
        def need(j):
            if j == z:
                return (2 * nz, 0)
            return (nz - 1 - j + z, j) if j > z else (nz - 1 - z + j, nz - j)

        order[z] = sorted(range(nz), key=need)
    return order


def on_device(attention_result, tenant, projection_weight, adapter_down_maps, adapter_up_maps):
    steps, row_count, width = attention_result.shape
    local_adapters = adapter_down_maps.shape[0]
    owners = lax.axis_size("dp")
    me = lax.axis_index("dp")
    n = lax.axis_size("tensor")
    nz = n // 2
    place = lax.axis_index("tensor")
    order = line_plan(nz)
    out_width = projection_weight.shape[1] // n

    def swap_y(value):
        return lax.ppermute(value, "tensor", [(t, t ^ 1) for t in range(n)])

    def hop(value, h):
        pairs = []
        for side in range(2):
            pairs.append((h * 2 + side, (h + 1) * 2 + side))
            pairs.append(((nz - 1 - h) * 2 + side, (nz - 2 - h) * 2 + side))
        return lax.ppermute(value, "tensor", pairs)

    def slot_of(h, m):
        return list(order[h]).index(nz - 1 - m)

    def pass_on(value, shift):
        return lax.ppermute(value, "dp", [(i, (i + shift) % owners) for i in range(owners)])

    rows = attention_result.reshape(steps * row_count, width)
    count = steps * row_count
    last = [()]

    def then(kernel, *operands, **options):
        out = kernel(*operands, after=last[0], **options)
        last[0] = (out[0] if isinstance(out, (tuple, list)) else out,)
        return out

    slot_range = jnp.arange(SLOTS, dtype=jnp.int32)
    ids = jnp.arange(local_adapters, dtype=jnp.int32)

    def slots(row_ids, owner):
        hit = row_ids[:, None] - owner * local_adapters == ids[None, :]
        used = jnp.any(hit, axis=0)
        position = jnp.sum(
            (used[None, :] & (ids[None, :] < ids[:, None])).astype(jnp.int32), axis=1
        )
        names = jnp.sum(
            jnp.where(used[None, :] & (position[None, :] == slot_range[:, None]), ids[None, :], 0),
            axis=1,
        )
        row_slot = jnp.sum(jnp.where(hit, position[None, :] + 1, 0), axis=1) - 1
        return names, row_slot[:, None]

    blocks = [[(order[t // 2][k] * 2 + side) for side in (1 - t % 2, t % 2) for k in range(nz)] for t in range(n)]
    sends = [[int(t // 2 in (h, nz - 1 - h)) for h in range(nz - 1)] for t in range(n)]
    table = np.concatenate([np.asarray(blocks, np.int32) * out_width, np.asarray(sends, np.int32)], axis=1)
    starts = jnp.asarray(table)[place]
    low_rows = count * adapter_down_maps.shape[1] // out_width
    even = [(p * count // PARTS, count // PARTS) for p in range(PARTS)]
    high_part = -(-(count + low_rows) // 32) * 16
    uneven = [(0, high_part), (high_part, count - high_part)]
    away_part, own_all, from_y, sums, arrived = {}, {}, {}, {}, {}

    def split(k):
        return uneven if k == 0 else [(0, count)]

    def add_up(span, terms, extra=(), dtype=jnp.bfloat16, only=None):
        low_row, high_row = span[0], span[0] + span[1]
        cuts = {low_row, high_row}
        for term in terms:
            for at, some, _, _ in term:
                cuts.update(row for row in (at, at + some) if low_row < row < high_row)
        cuts = sorted(cuts)
        runs = []
        for begin, end in zip(cuts, cuts[1:]):
            here = [
                (array, row + begin - at) for term in terms for at, some, array, row in term if at <= begin < at + some
            ]
            runs.append((end - begin, here))
        return then(total, runs + list(extra), dtype, None, only)

    def whole(array):
        return [(0, count, array, 0)]

    def multiply(aways, owns, tail=None, chunk=1024, vmem=VMEM):
        ks = sorted({k for k, _ in aways})
        names = ks + [nz + k for k in owns]
        outs = [(ks.index(k), *split(k)[p]) for k, p in aways]
        outs += [(len(ks) + i, 0, count) for i in range(len(owns))]
        done = then(products, rows, projection_weight, starts, names, out_width, outs, tail, chunk, vmem)
        away_part.update(zip(aways, done))
        own_all.update(zip(owns, done[len(aways) :]))

    def start_y(k, p, after=None):
        value = away_part[k, p]
        from_y[k, p] = swap_y(value if after is None else hold(value, after))

    def y_parts(k):
        return [(*cut, from_y[k, p], 0) for p, cut in enumerate(split(k)) if (k, p) in from_y]

    def sum_parts(k):
        return [(*cut, sums[k, p], 0) for p, cut in enumerate(cut_of(0, k)) if (k, p) in sums]

    def cut_of(h, m):
        if m == 0 and h <= 1:
            return uneven
        return [(0, count * 8 // 16), (count * 8 // 16, count * 8 // 16)] if m == 1 else [(0, count)]

    def arrived_parts(h, m):
        return [(*cut, arrived[h, m, p], 0) for p, cut in enumerate(cut_of(h, m)) if (h, m, p) in arrived]

    def line(h, m, p):
        k = slot_of(h, m)
        span = cut_of(h, m)[p]
        low_too = m == 0 and h <= 1 and p == LOW_WITH[1]
        if h == 0:
            extra = [(low_rows, [(low, 0), (from_y[k, p], span[1])])] if low_too else []
            value = sums[k, p] = add_up(span, [whole(own_all[k]), y_parts(k)], extra)
        else:
            extra = [(low_rows, [(sums[k, p], span[1]), (arrived[h - 1, m, p], span[1])])] if low_too else []
            value = add_up(span, [sum_parts(k), arrived_parts(h - 1, m)], extra, only=(starts, 2 * nz + h))
        arrived[h, m, p] = hop(value, h)

    def line_order():
        ready, free = {}, {}
        steps = [(h, m, p) for h in range(nz - 1) for m in range(nz - 1 - h) for p in range(len(cut_of(h, m)))]
        for h, m, p in sorted(steps, key=lambda step: (step[0], step[1], step[2])):
            k = slot_of(h, m)
            there = (k + 1.0) * count if k or p else 1.0 * cut_of(0, 0)[0][1]
            if h:
                above = range(len(cut_of(h - 1, m)))
                there = max(there, max(ready[h - 1, m, q, "end"] for q in above if q == p or len(above) != len(cut_of(h, m))))
            ready[h, m, p] = there
            free[h] = max(there, free.get(h, 0.0)) + cut_of(h, m)[p][1]
            ready[h, m, p, "end"] = free[h]
        return sorted(steps, key=lambda step: (ready[step], step[0] and nz - step[0]))

    row_ids = [tenant] + [pass_on(tenant, shift) for shift in range(1, owners)]
    row_sets = [rows] + [pass_on(rows, shift) for shift in range(1, owners)]
    multiply([(0, 0)], [], chunk=512, vmem=VMEM + 16 * 2**20)
    start_y(0, 0)
    named = [slots(some_ids, me) for some_ids in row_ids]
    names = jnp.concatenate([which for which, _ in named])
    slot_sets = [row_slot for _, row_slot in named]
    low_sets = then(low_rank, row_sets, slot_sets, adapter_down_maps, names, out_width)
    low_terms = [(low_sets[0], 0)] + [(pass_on(low_sets[s], -s), 0) for s in range(1, owners)]
    low = then(total, [(low_rows, low_terms)])
    multiply([LOW_WITH], [], low, chunk=512)
    start_y(*LOW_WITH)
    multiply([(1, 0)], [0])
    start_y(1, 0)
    low_sum = deltas = None
    for h, m, p in line_order():
        k = slot_of(h, m)
        if (h, m, p) == (2, 0, 0) and nz == 4:
            last[0] += (pieces[-1][0],)
        line(h, m, p)
        if h == 0:
            if k == 0 and p == 0:
                multiply([(2, 0)] if nz > 2 else [], [1])
            elif k == 0:
                if nz > 2:
                    start_y(2, 0, last[0])
                multiply([(j, 0) for j in range(3, nz)], range(2, nz))
            elif p == len(cut_of(h, m)) - 1 and k + 2 < nz:
                start_y(k + 2, 0, last[0])
        if (h, k, p) == (0, 1, len(cut_of(h, m)) - 1):
            low_at = uneven[LOW_WITH[1]][1]
            pieces = [(sums[LOW_WITH], low_at)]
            last[0] += (arrived[1, 0, 0],) if nz > 2 else ()
            for step in range(nz - 1):
                if step >= 2:
                    prefix = then(total, [(low_rows, [pieces[0], pieces[-1]])], only=(starts, 2 * nz + step))
                    pieces.append((hop(prefix, step), 0))
                else:
                    pieces.append((arrived[step, 0, LOW_WITH[1]], low_at))
        if (h, m, p) == LOW_SUM_AFTER:
            low_sum = then(total, [(low_rows, pieces)])
            low_back = [low_sum] + [pass_on(low_sum, shift) for shift in range(1, owners)]
        if deltas is None and low_sum is not None and EXPAND_AFTER in arrived:
            deltas = then(expand, low_back, slot_sets, adapter_up_maps, names)
            back = [
                [(*cut, pass_on(deltas[1 + (shift - 1) * PARTS + p], -shift), 0) for p, cut in enumerate(even)]
                for shift in range(1, owners)
            ]
    span = (0, count)
    early = [arrived_parts(h, nz - 2 - h) for h in range(1, nz - 2)]
    late = [arrived_parts(h, nz - 2 - h) for h in range(nz - 1) if not 1 <= h < nz - 2]
    most = add_up(span, [whole(own_all[nz - 1]), whole(deltas[0]), y_parts(nz - 1)] + early)
    most = add_up(span, [whole(most)] + back + late[:-1])
    out = add_up(span, [whole(most)] + late[-1:])
    return out.reshape(steps, row_count, out_width)


def solution(mesh):
    placed = (
        P(None, ("groups", "dp"), "tensor"),
        P(("groups", "dp")),
        P("tensor", None),
        P(("groups", "dp"), None, "tensor"),
        P(("groups", "dp"), None, "tensor"),
    )
    return jax.shard_map(
        on_device,
        mesh=mesh,
        in_specs=placed,
        out_specs=P(None, ("groups", "dp"), "tensor"),
        check_vma=False,
    )
```

```python
import jax
import jax.numpy as jnp
import numpy as np
from jax import lax
from jax.experimental import pallas as pl
from jax.experimental.pallas import tpu as pltpu
from jax.sharding import PartitionSpec as P

SLOTS = 16
LANES = 128
CHUNK = 512
PARTS = 2
LOW_WITH = (0, PARTS - 1)
LOW_SUM_AFTER = (2, 0, 0)
EXPAND_AFTER = (1, 1, 1)
VMEM = 47 * 2**20
ANY = pl.BlockSpec(memory_space=pl.ANY)


def call(kernel, operands, after, *, in_specs, out_specs, out_shape, name, prefetch=0, scratch=(), alias=None, vmem=VMEM):
    inputs, extra = len(operands), len(after)

    def body(*refs):
        kernel(*refs[:inputs], *refs[inputs + extra :])

    return pl.pallas_call(
        body,
        grid_spec=pltpu.PrefetchScalarGridSpec(
            num_scalar_prefetch=prefetch,
            grid=(),
            in_specs=list(in_specs) + [ANY] * extra,
            out_specs=out_specs,
            scratch_shapes=list(scratch),
        ),
        out_shape=out_shape,
        input_output_aliases=alias or {},
        compiler_params=pltpu.CompilerParams(vmem_limit_bytes=vmem),
        cost_estimate=pl.CostEstimate(flops=1, transcendentals=0, bytes_accessed=1),
        name=name,
    )(*operands, *after)


def hold(value, after):
    def kernel(value_ref, out_ref):
        pass

    return call(
        kernel, [value], after, in_specs=[ANY], out_specs=ANY,
        out_shape=jax.ShapeDtypeStruct(value.shape, value.dtype), name="hold", alias={0: 0},
    )


def products(rows, weight, starts, names, size, outs, tail=None, chunk=1024, vmem=VMEM, after=()):
    count, width = rows.shape
    blocks = len(names)
    chunks = [(at, min(chunk, size - at)) for at in range(0, size, chunk)]
    low = min(first for _, first, _ in outs)
    high = max(first + some for _, first, some in outs)
    upper = (high - low) // 32 * 16
    row_parts = [(0, upper), (upper, high - low - upper)]
    tails = [] if tail is None else [tail]
    heights = [some for _, _, some in outs]
    for array in tails:
        heights[-1] += array.shape[0]

    def kernel(starts_ref, rows_ref, weight_ref, *refs):
        tail_refs, refs = refs[: len(tails)], refs[len(tails) :]
        out_refs, (x, w, *refs) = refs[: len(outs)], refs[len(outs) :]
        stage, (x_sems, w_sems, out_sems, tail_sems) = refs[: len(outs)], refs[len(outs) :]
        x_copies = [
            pltpu.make_async_copy(
                rows_ref.at[pl.ds(low + at, some)], x.at[pl.ds(at, some)], x_sems.at[i]
            )
            for i, (at, some) in enumerate(row_parts)
        ]
        w_copies = [
            [
                pltpu.make_async_copy(
                    weight_ref.at[:, pl.ds(pl.multiple_of(starts_ref[names[b]] + at, LANES), extent)],
                    w.at[b, :, pl.ds(at, extent)],
                    w_sems.at[b, c],
                )
                for c, (at, extent) in enumerate(chunks)
            ]
            for b in range(blocks)
        ]
        x_copies[0].start()
        w_copies[0][0].start()
        x_copies[1].start()
        for b in range(blocks):
            for c in range(len(chunks)):
                if b or c:
                    w_copies[b][c].start()
        stores = []
        for ref in tail_refs:
            below = pl.ds(outs[-1][2], ref.shape[0])
            read = pltpu.make_async_copy(ref, stage[-1].at[below], tail_sems.at[0])
            read.start()
            read.wait()
            stores.append(pltpu.make_async_copy(stage[-1].at[below], out_refs[-1].at[below], tail_sems.at[1]))
            stores[-1].start()
        for copy in x_copies:
            copy.wait()
        for b in range(blocks):
            for c, (at, extent) in enumerate(chunks):
                w_copies[b][c].wait()
                for o, (index, first, some) in enumerate(outs):
                    if index == b:
                        value = jnp.dot(
                            x[first - low : first - low + some, :], w[b, :, at : at + extent],
                            preferred_element_type=jnp.float32,
                        )
                        stage[o][:some, at : at + extent] = value.astype(rows.dtype)
                        store = pltpu.make_async_copy(
                            stage[o].at[pl.ds(0, some), pl.ds(at, extent)],
                            out_refs[o].at[pl.ds(0, some), pl.ds(at, extent)],
                            out_sems.at[o, c],
                        )
                        store.start()
                        stores.append(store)
        for store in stores:
            store.wait()

    shapes = [(height, size) for height in heights]
    return call(
        kernel, [starts, rows, weight] + tails, after, prefetch=1,
        in_specs=[ANY] * (2 + len(tails)),
        out_specs=[ANY] * len(outs),
        out_shape=[jax.ShapeDtypeStruct(shape, rows.dtype) for shape in shapes],
        scratch=[pltpu.VMEM((high - low, width), rows.dtype), pltpu.VMEM((blocks, width, size), rows.dtype)]
        + [pltpu.VMEM(shape, rows.dtype) for shape in shapes]
        + [
            pltpu.SemaphoreType.DMA((2,)),
            pltpu.SemaphoreType.DMA((blocks, len(chunks))),
            pltpu.SemaphoreType.DMA((len(outs), len(chunks))),
            pltpu.SemaphoreType.DMA((2,)),
        ],
        name="products", vmem=vmem,
    )


def total(runs, dtype=jnp.bfloat16, into=None, only=None, after=()):
    width = runs[0][1][0][0].shape[1]
    height = sum(some for some, _ in runs)
    rows_in_all, first, so_far = into or (height, 0, None)
    tiles = []
    at = 0
    for r, (some, terms) in enumerate(runs):
        split = 4 if some * len(terms) > 2000 else 2 if some * width > 2**17 else 1
        size = -(-some // (16 * split)) * 16
        for skip in range(0, some, size):
            tiles.append((r, skip, min(size, some - skip), at + skip))
        at += some
    operands = [term for _, terms in runs for term, _ in terms]
    before = [] if so_far is None else [so_far]
    most_terms = max(len(terms) for _, terms in runs)
    of_run = np.cumsum([0] + [len(terms) for _, terms in runs])

    flags = [] if only is None else [only[0]]

    def kernel(*refs):
        if only is None:
            add(*refs)
        else:
            pl.when(refs[0][only[1]] != 0)(lambda: add(*refs[1:]))

    def add(*refs):
        term_refs, out_ref = refs[: len(operands)], refs[len(operands) + len(before)]
        refs = refs[len(operands) + len(before) + 1 :]
        bufs, (stage, in_sems, out_sems) = refs[: len(operands)], refs[len(operands) :]
        reads, writes = [], []
        for n, (r, skip, size, place) in enumerate(tiles):
            reads.append(
                [
                    pltpu.make_async_copy(
                        term_refs[of_run[r] + t].at[pl.ds(start + skip, size)],
                        bufs[of_run[r] + t].at[pl.ds(skip, size)],
                        in_sems.at[t, n],
                    )
                    for t, (_, start) in enumerate(runs[r][1])
                ]
            )
            writes.append(
                pltpu.make_async_copy(
                    stage.at[pl.ds(place, size)], out_ref.at[pl.ds(first + place, size)], out_sems.at[n]
                )
            )
        for some in reads:
            for read in some:
                read.start()
        for n, (r, skip, size, place) in enumerate(tiles):
            for read in reads[n]:
                read.wait()
            value = None
            for t in range(len(runs[r][1])):
                part = bufs[of_run[r] + t][skip : skip + size, :].astype(jnp.float32)
                value = part if value is None else value + part
            stage[place : place + size, :] = value.astype(dtype)
            writes[n].start()
        for write in writes:
            write.wait()

    return call(
        kernel, flags + operands + before, after, prefetch=len(flags),
        in_specs=[ANY] * (len(operands) + len(before)),
        out_specs=ANY,
        out_shape=jax.ShapeDtypeStruct((rows_in_all, width), dtype),
        scratch=[pltpu.VMEM((some, width), term.dtype) for some, terms in runs for term, _ in terms]
        + [
            pltpu.VMEM((height, width), dtype),
            pltpu.SemaphoreType.DMA((most_terms, len(tiles))),
            pltpu.SemaphoreType.DMA((len(tiles),)),
        ],
        alias={len(flags) + len(operands): 0} if before else None,
        name="total",
    )


def lane_pick(slot_ref, repeats, shape, rank, first):
    slot = jnp.concatenate([slot_ref[...]] * repeats, axis=0)
    return slot == lax.broadcasted_iota(jnp.int32, shape, 1) // rank + first


def block_copies(index_ref, maps_ref, buf, sems, sets, rank):
    each = index_ref.shape[0] // sets
    return [
        [
            pltpu.make_async_copy(
                maps_ref.at[index_ref[s * each + i]], buf.at[pl.ds((s * each + i) * rank, rank)],
                sems.at[s * each + i],
            )
            for i in range(each)
        ]
        for s in range(sets)
    ]


def low_rank(row_sets, slot_sets, maps, index, wide, after=()):
    sets = len(row_sets)
    count, width = row_sets[0].shape
    rank = maps.shape[1]
    span = index.shape[0] // sets * rank
    repeats = count // slot_sets[0].shape[0]
    half = count // 2
    group = 256
    tall = half * 2 * rank // wide

    def kernel(index_ref, *refs):
        row_refs, slot_refs, maps_ref = refs[:sets], refs[sets : 2 * sets], refs[2 * sets]
        out_refs, (rows_buf, maps_buf, row_sems, map_sems) = refs[2 * sets + 1 : 3 * sets + 1], refs[3 * sets + 1 :]
        row_copies = [
            pltpu.make_async_copy(row_refs[s], rows_buf.at[s], row_sems.at[s]) for s in range(sets)
        ]
        map_copies = block_copies(index_ref, maps_ref, maps_buf, map_sems, sets, rank)
        for s in range(sets):
            row_copies[s].start()
            for copy in map_copies[s]:
                copy.start()
        for s in range(sets):
            row_copies[s].wait()
            for copy in map_copies[s]:
                copy.wait()
            acc = None
            for at in range(0, span, group):
                scores = lax.dot_general(
                    rows_buf[s], maps_buf[s * span + at : s * span + at + group],
                    (((1,), (1,)), ((), ())), preferred_element_type=jnp.float32,
                )
                pick = lane_pick(slot_refs[s], repeats, (count, group), rank, at // rank)
                term = jnp.where(pick, scores, 0.0)
                acc = term if acc is None else acc + term
            summed = acc[:, 0:rank]
            for g in range(1, group // rank):
                summed += acc[:, g * rank : (g + 1) * rank]
            summed = summed.astype(out_refs[s].dtype)
            for b in range(half // tall):
                lanes = slice(b * 2 * rank, (b + 1) * 2 * rank)
                both = [summed[start + b * tall : start + (b + 1) * tall] for start in (0, half)]
                out_refs[s][:, lanes] = jnp.concatenate(both, axis=1)

    return call(
        kernel, [index, *row_sets, *slot_sets, maps], after, prefetch=1,
        in_specs=[ANY] * sets + [pl.BlockSpec(memory_space=pltpu.VMEM)] * sets + [ANY],
        out_specs=[pl.BlockSpec(memory_space=pltpu.VMEM)] * sets,
        out_shape=[jax.ShapeDtypeStruct((tall, wide), jnp.bfloat16)] * sets,
        scratch=[
            pltpu.VMEM((sets, count, width), row_sets[0].dtype),
            pltpu.VMEM((sets * span, width), maps.dtype),
            pltpu.SemaphoreType.DMA((sets,)),
            pltpu.SemaphoreType.DMA((index.shape[0],)),
        ],
        name="low_rank",
    )


def expand(low_sets, slot_sets, maps, index, base, after=()):
    sets = len(slot_sets)
    rank, width = maps.shape[1:]
    tall = low_sets[0].shape[0]
    half = low_sets[0].size // (2 * rank)
    count = 2 * half
    span = index.shape[0] // sets * rank
    repeats = count // slot_sets[0].shape[0]

    outs = [(0, 0, count)] + [
        (s, p * count // PARTS, count // PARTS) for s in range(1, sets) for p in range(PARTS)
    ]

    def kernel(index_ref, *refs):
        low_refs, refs = refs[:sets], refs[sets:]
        slot_refs, maps_ref, base_ref, *refs = refs[:sets], refs[sets], refs[sets + 1], *refs[sets + 2 :]
        out_refs, (stage, maps_buf, map_sems, out_sems) = refs[: len(outs)], refs[len(outs) :]
        map_copies = block_copies(index_ref, maps_ref, maps_buf, map_sems, sets, rank)
        writes = [
            pltpu.make_async_copy(stage.at[s, pl.ds(first, some)], out_refs[o], out_sems.at[o])
            for o, (s, first, some) in enumerate(outs)
        ]
        order = list(range(1, sets)) + [0]
        for s in order:
            for copy in map_copies[s]:
                copy.start()
        for s in order:
            lanes = [b * 2 * rank for b in range(half // tall)]
            mine = jnp.concatenate(
                [low_refs[s][:, at + side : at + side + rank] for side in (0, rank) for at in lanes], axis=0
            )
            tiled = jnp.concatenate([mine] * (span // rank), axis=1)
            pick = lane_pick(slot_refs[s], repeats, (count, span), rank, 0)
            picked = jnp.where(pick, tiled, jnp.zeros_like(tiled))
            for copy in map_copies[s]:
                copy.wait()
            for at in range(0, width, CHUNK):
                value = jnp.dot(
                    picked, maps_buf[s * span : (s + 1) * span, at : at + CHUNK], preferred_element_type=jnp.float32
                )
                if s == 0:
                    value += base_ref[:, at : at + CHUNK].astype(jnp.float32)
                stage[s, :, at : at + CHUNK] = value.astype(stage.dtype)
            for o, (which, _, _) in enumerate(outs):
                if which == s:
                    writes[o].start()
        for write in writes:
            write.wait()

    return call(
        kernel, [index, *low_sets, *slot_sets, maps, base], after, prefetch=1,
        in_specs=[pl.BlockSpec(memory_space=pltpu.VMEM)] * (2 * sets) + [ANY, pl.BlockSpec(memory_space=pltpu.VMEM)],
        out_specs=[ANY] * len(outs),
        out_shape=[jax.ShapeDtypeStruct((some, width), jnp.bfloat16) for _, _, some in outs],
        scratch=[
            pltpu.VMEM((sets, count, width), jnp.bfloat16),
            pltpu.VMEM((sets * span, width), maps.dtype),
            pltpu.SemaphoreType.DMA((index.shape[0],)),
            pltpu.SemaphoreType.DMA((len(outs),)),
        ],
        name="expand",
    )


def line_plan(nz):
    order = np.zeros((nz, nz), np.int32)
    for z in range(nz):
        def need(j):
            if j == z:
                return (2 * nz, 0)
            return (nz - 1 - j + z, j) if j > z else (nz - 1 - z + j, nz - j)

        order[z] = sorted(range(nz), key=need)
    return order


def on_device(attention_result, tenant, projection_weight, adapter_down_maps, adapter_up_maps):
    steps, row_count, width = attention_result.shape
    local_adapters = adapter_down_maps.shape[0]
    owners = lax.axis_size("dp")
    me = lax.axis_index("dp")
    n = lax.axis_size("tensor")
    nz = n // 2
    place = lax.axis_index("tensor")
    order = line_plan(nz)
    out_width = projection_weight.shape[1] // n

    def swap_y(value):
        return lax.ppermute(value, "tensor", [(t, t ^ 1) for t in range(n)])

    def hop(value, h):
        pairs = []
        for side in range(2):
            pairs.append((h * 2 + side, (h + 1) * 2 + side))
            pairs.append(((nz - 1 - h) * 2 + side, (nz - 2 - h) * 2 + side))
        return lax.ppermute(value, "tensor", pairs)

    def slot_of(h, m):
        return list(order[h]).index(nz - 1 - m)

    def pass_on(value, shift):
        return lax.ppermute(value, "dp", [(i, (i + shift) % owners) for i in range(owners)])

    rows = attention_result.reshape(steps * row_count, width)
    count = steps * row_count
    last = [()]

    def then(kernel, *operands, **options):
        out = kernel(*operands, after=last[0], **options)
        last[0] = (out[0] if isinstance(out, (tuple, list)) else out,)
        return out

    slot_range = jnp.arange(SLOTS, dtype=jnp.int32)
    ids = jnp.arange(local_adapters, dtype=jnp.int32)

    def slots(row_ids, owner):
        hit = row_ids[:, None] - owner * local_adapters == ids[None, :]
        used = jnp.any(hit, axis=0)
        position = jnp.sum(
            (used[None, :] & (ids[None, :] < ids[:, None])).astype(jnp.int32), axis=1
        )
        names = jnp.sum(
            jnp.where(used[None, :] & (position[None, :] == slot_range[:, None]), ids[None, :], 0),
            axis=1,
        )
        row_slot = jnp.sum(jnp.where(hit, position[None, :] + 1, 0), axis=1) - 1
        return names, row_slot[:, None]

    blocks = [[(order[t // 2][k] * 2 + side) for side in (1 - t % 2, t % 2) for k in range(nz)] for t in range(n)]
    sends = [[int(t // 2 in (h, nz - 1 - h)) for h in range(nz - 1)] for t in range(n)]
    table = np.concatenate([np.asarray(blocks, np.int32) * out_width, np.asarray(sends, np.int32)], axis=1)
    starts = jnp.asarray(table)[place]
    low_rows = count * adapter_down_maps.shape[1] // out_width
    even = [(p * count // PARTS, count // PARTS) for p in range(PARTS)]
    high_part = -(-(count + low_rows) // 32) * 16
    uneven = [(0, high_part), (high_part, count - high_part)]
    away_part, own_all, from_y, sums, arrived = {}, {}, {}, {}, {}

    def split(k):
        return uneven if k == 0 else [(0, count)]

    def add_up(span, terms, extra=(), dtype=jnp.bfloat16, only=None):
        low_row, high_row = span[0], span[0] + span[1]
        cuts = {low_row, high_row}
        for term in terms:
            for at, some, _, _ in term:
                cuts.update(row for row in (at, at + some) if low_row < row < high_row)
        cuts = sorted(cuts)
        runs = []
        for begin, end in zip(cuts, cuts[1:]):
            here = [
                (array, row + begin - at) for term in terms for at, some, array, row in term if at <= begin < at + some
            ]
            runs.append((end - begin, here))
        return then(total, runs + list(extra), dtype, None, only)

    def whole(array):
        return [(0, count, array, 0)]

    def multiply(aways, owns, tail=None, chunk=1024, vmem=VMEM):
        ks = sorted({k for k, _ in aways})
        names = ks + [nz + k for k in owns]
        outs = [(ks.index(k), *split(k)[p]) for k, p in aways]
        outs += [(len(ks) + i, 0, count) for i in range(len(owns))]
        done = then(products, rows, projection_weight, starts, names, out_width, outs, tail, chunk, vmem)
        away_part.update(zip(aways, done))
        own_all.update(zip(owns, done[len(aways) :]))

    def start_y(k, p, after=None):
        value = away_part[k, p]
        from_y[k, p] = swap_y(value if after is None else hold(value, after))

    def y_parts(k):
        return [(*cut, from_y[k, p], 0) for p, cut in enumerate(split(k)) if (k, p) in from_y]

    def sum_parts(k):
        return [(*cut, sums[k, p], 0) for p, cut in enumerate(cut_of(0, k)) if (k, p) in sums]

    def cut_of(h, m):
        if m == 0 and h <= 1:
            return uneven
        return [(0, count * 8 // 16), (count * 8 // 16, count * 8 // 16)] if m == 1 else [(0, count)]

    def arrived_parts(h, m):
        return [(*cut, arrived[h, m, p], 0) for p, cut in enumerate(cut_of(h, m)) if (h, m, p) in arrived]

    def line(h, m, p):
        k = slot_of(h, m)
        span = cut_of(h, m)[p]
        low_too = m == 0 and h <= 1 and p == LOW_WITH[1]
        if h == 0:
            extra = [(low_rows, [(low, 0), (from_y[k, p], span[1])])] if low_too else []
            value = sums[k, p] = add_up(span, [whole(own_all[k]), y_parts(k)], extra)
        else:
            extra = [(low_rows, [(sums[k, p], span[1]), (arrived[h - 1, m, p], span[1])])] if low_too else []
            value = add_up(span, [sum_parts(k), arrived_parts(h - 1, m)], extra, only=(starts, 2 * nz + h))
        arrived[h, m, p] = hop(value, h)

    def line_order():
        ready, free = {}, {}
        steps = [(h, m, p) for h in range(nz - 1) for m in range(nz - 1 - h) for p in range(len(cut_of(h, m)))]
        for h, m, p in sorted(steps, key=lambda step: (step[0], step[1], step[2])):
            k = slot_of(h, m)
            there = (k + 1.0) * count if k or p else 1.0 * cut_of(0, 0)[0][1]
            if h:
                above = range(len(cut_of(h - 1, m)))
                there = max(there, max(ready[h - 1, m, q, "end"] for q in above if q == p or len(above) != len(cut_of(h, m))))
            ready[h, m, p] = there
            free[h] = max(there, free.get(h, 0.0)) + cut_of(h, m)[p][1]
            ready[h, m, p, "end"] = free[h]
        return sorted(steps, key=lambda step: (ready[step], step[0] and nz - step[0]))

    row_ids = [tenant] + [pass_on(tenant, shift) for shift in range(1, owners)]
    row_sets = [rows] + [pass_on(rows, shift) for shift in range(1, owners)]
    multiply([(0, 0)], [], chunk=512, vmem=VMEM + 16 * 2**20)
    start_y(0, 0)
    named = [slots(some_ids, me) for some_ids in row_ids]
    names = jnp.concatenate([which for which, _ in named])
    slot_sets = [row_slot for _, row_slot in named]
    low_sets = then(low_rank, row_sets, slot_sets, adapter_down_maps, names, out_width)
    low_terms = [(low_sets[0], 0)] + [(pass_on(low_sets[s], -s), 0) for s in range(1, owners)]
    low = then(total, [(low_rows, low_terms)])
    multiply([LOW_WITH], [], low, chunk=512)
    start_y(*LOW_WITH)
    multiply([(1, 0)], [0])
    start_y(1, 0)
    low_sum = deltas = None
    for h, m, p in line_order():
        k = slot_of(h, m)
        if (h, m, p) == (2, 0, 0) and nz == 4:
            last[0] += (pieces[-1][0],)
        line(h, m, p)
        if h == 0:
            if k == 0 and p == 0:
                multiply([(2, 0)] if nz > 2 else [], [1])
            elif k == 0:
                if nz > 2:
                    start_y(2, 0, last[0])
                multiply([(j, 0) for j in range(3, nz)], range(2, nz))
            elif p == len(cut_of(h, m)) - 1 and k + 2 < nz:
                start_y(k + 2, 0, last[0])
        if (h, k, p) == (0, 1, len(cut_of(h, m)) - 1):
            low_at = uneven[LOW_WITH[1]][1]
            pieces = [(sums[LOW_WITH], low_at)]
            last[0] += (arrived[1, 0, 0],) if nz > 2 else ()
            for step in range(nz - 1):
                if step >= 2:
                    prefix = then(total, [(low_rows, [pieces[0], pieces[-1]])], only=(starts, 2 * nz + step))
                    pieces.append((hop(prefix, step), 0))
                else:
                    pieces.append((arrived[step, 0, LOW_WITH[1]], low_at))
        if (h, m, p) == LOW_SUM_AFTER:
            low_sum = then(total, [(low_rows, pieces)])
            low_back = [low_sum] + [pass_on(low_sum, shift) for shift in range(1, owners)]
        if deltas is None and low_sum is not None and EXPAND_AFTER in arrived:
            deltas = then(expand, low_back, slot_sets, adapter_up_maps, names, own_all[nz - 1])
            back = [
                [(*cut, pass_on(deltas[1 + (shift - 1) * PARTS + p], -shift), 0) for p, cut in enumerate(even)]
                for shift in range(1, owners)
            ]
    span = (0, count)
    early = [arrived_parts(h, nz - 2 - h) for h in range(1, nz - 2)]
    late = [arrived_parts(h, nz - 2 - h) for h in range(nz - 1) if not 1 <= h < nz - 2]
    most = add_up(span, [whole(deltas[0]), y_parts(nz - 1)] + early)
    most = add_up(span, [whole(most)] + back + late[:-1])
    out = add_up(span, [whole(most)] + late[-1:])
    return out.reshape(steps, row_count, out_width)


def solution(mesh):
    placed = (
        P(None, ("groups", "dp"), "tensor"),
        P(("groups", "dp")),
        P("tensor", None),
        P(("groups", "dp"), None, "tensor"),
        P(("groups", "dp"), None, "tensor"),
    )
    return jax.shard_map(
        on_device,
        mesh=mesh,
        in_specs=placed,
        out_specs=P(None, ("groups", "dp"), "tensor"),
        check_vma=False,
    )
```
